128 devices in a mesh: depth: 8 (over y, core), seg: 16 (over z, x).
Axes of the slice: x: 4, y: 4, z: 4, core: 2. Of those that a mesh axis runs over, the one named last changes fastest.
Arguments:
- queries: bfloat16 [8, 16, 128, 2560], P('depth', 'seg'), may hold values from -6 to 6, as said below
- keys_values: bfloat16 [8, 16, 2, 128, 512], P('depth', 'seg'), may hold values from -6 to 6
- grad_out: bfloat16 [8, 16, 128, 2560], P('depth', 'seg'), may hold values from -6 to 6
- parents: int32 [7, 16, 1], replicated, may hold values from 0 to 15
Outputs:
- grad_queries: bfloat16 [8, 16, 128, 2560], P('depth', 'seg')
- grad_keys_values: bfloat16 [8, 16, 2, 128, 512], P('depth', 'seg')
The draws below stay inside these ranges and needn't reach their ends.
Inputs may be any that keep to these rules, and one draw needn't show every extreme that they name: `queries`: a few query rows and key rows may be nearly parallel in some draws. `parents`: every column of a level is somebody's parent in some level.
All inputs are finite; a program needn't handle non-finite values.
Results may differ from the reference program's by a relative error of at most 0.012.
Values may be sent and summed in bfloat16 or wider, within the bound.
A program may use at most 128 MiB of HBM per device.

```python
import jax
import jax.numpy as jnp
from jax import lax

HEADS = 20
KV_HEADS = 4
HEAD_DIM = 128
T_SEG = 128
LEVELS = 8
SEGS = 16


def draw_queries(key, part):
    key = jax.random.fold_in(key, 11)
    shape = (LEVELS, SEGS, T_SEG, HEADS * HEAD_DIM)
    base = jnp.clip(jax.random.normal(key, shape, jnp.float32), -4.0, 4.0)
    return base.astype(jnp.bfloat16)


def draw_keys_values(key, part):
    key = jax.random.fold_in(key, 23)
    shape = (LEVELS, SEGS, 2, T_SEG, KV_HEADS * HEAD_DIM)
    base = jnp.clip(jax.random.normal(key, shape, jnp.float32), -4.0, 4.0)
    return base.astype(jnp.bfloat16)


def block_levels(rng, dims, cuts, smallest, largest):
    loudness = 1.0
    for position, blocks in cuts:
        steps = jax.random.uniform(jax.random.fold_in(jax.random.fold_in(rng, 6), position), (blocks,), jnp.float32, smallest / len(cuts), largest / len(cuts))
        loudness = loudness * jnp.repeat(jnp.exp(steps), dims[position] // blocks).reshape((-1,) + (1,) * (len(dims) - 1 - position))
    return loudness


def choose_distinct(rng, rows, number_of, top, lift):
    order = jax.random.permutation(jax.random.fold_in(rng, 1), number_of)
    pull = order
    for power in range(3):
        pull = pull * pull // number_of
    pull = pull * lift // number_of
    tickets = jax.random.randint(jax.random.fold_in(rng, 2), (rows, number_of), 0, 4096) + pull
    holders = jax.random.permutation(jax.random.fold_in(rng, 3), rows)[jnp.arange(number_of) % rows]
    tickets = jnp.where(jnp.arange(rows)[:, None] == holders[None, :], 1 << 14, tickets)
    merit = tickets * number_of + jnp.arange(number_of)
    return lax.top_k(merit.astype(jnp.int32), top)[1].astype(jnp.int32)


def bell_draw(own_key, extent, deviation, most, cuts=(), kind=jnp.bfloat16):
    gain = block_levels(own_key, extent, cuts, -0.22, 0.18) if cuts else 1.0
    values = jax.random.normal(own_key, extent, jnp.float32) * deviation * gain
    return jnp.minimum(jnp.maximum(values, -most), most).astype(kind)


def setup_inputs(seed: int = 0) -> dict:
    arg_keys = jax.random.split(jax.random.key(seed), 5)
    queries = draw_queries(jax.random.fold_in(arg_keys[4], 71), 0)
    keys_values = draw_keys_values(jax.random.fold_in(arg_keys[4], 71), 0)
    grad_out = bell_draw(arg_keys[2], (LEVELS, SEGS, T_SEG, HEADS * HEAD_DIM), 1.0, 6.0, ((0, 8), (1, 16)))
    parents = choose_distinct(arg_keys[3], (LEVELS - 1) * SEGS, SEGS, 1, 1024).reshape((LEVELS - 1, SEGS, 1))
    return {"queries": queries, "keys_values": keys_values, "grad_out": grad_out, "parents": parents}


NEG_FILL = -1.0e30


def ancestor_rows(parents):
    parent_rows = parents[:, :, 0]
    level_count = parent_rows.shape[0] + 1
    seg_count = parent_rows.shape[1]
    level_ids = jnp.arange(level_count)
    current = jnp.broadcast_to(jnp.arange(seg_count, dtype=jnp.int32)[None, :], (level_count, seg_count))
    found = [current]
    for offset in range(1, level_count):
        lifted = parent_rows[jnp.clip(level_ids - offset, 0, level_count - 2)]
        current = jnp.take_along_axis(lifted, current, axis=1).astype(jnp.int32)
        found.append(current)
    return found


def product(form, left, right):
    return jnp.einsum(form, left.astype(jnp.float32), right.astype(jnp.float32), precision=lax.Precision.HIGHEST)


def segment_grads(query_rows, upstream_rows, blocks):
    row_count = query_rows.shape[0]
    group = HEADS // KV_HEADS
    softmax_scale = HEAD_DIM ** -0.5
    query_four = query_rows.reshape(row_count, KV_HEADS, group, HEAD_DIM)
    upstream_four = upstream_rows.reshape(row_count, KV_HEADS, group, HEAD_DIM)
    causal = jnp.arange(row_count)[None, :] <= jnp.arange(row_count)[:, None]
    block_count = blocks.shape[0]

    def logits_of(index):
        keys = blocks[index, 0].reshape(row_count, KV_HEADS, HEAD_DIM)
        raw = softmax_scale * product('tkgd,ukd->kgtu', query_four, keys)
        if index == 0:
            raw = jnp.where(causal, raw, NEG_FILL)
        return raw

    top = logits_of(0).max(-1)
    for index in range(1, block_count):
        top = jnp.maximum(top, logits_of(index).max(-1))
    total = jnp.zeros(top.shape, jnp.float32)
    for index in range(block_count):
        total = total + jnp.exp(logits_of(index) - top[..., None]).sum(-1)
    attended = jnp.zeros((row_count, KV_HEADS, group, HEAD_DIM), jnp.float32)
    for index in range(block_count):
        probs = (jnp.exp(logits_of(index) - top[..., None]) / total[..., None]).astype(jnp.bfloat16)
        values = blocks[index, 1].reshape(row_count, KV_HEADS, HEAD_DIM)
        attended = attended + product('kgtu,ukd->tkgd', probs, values)
    delta = jnp.sum(upstream_four.astype(jnp.float32) * attended, -1).transpose(1, 2, 0)
    grad_query = jnp.zeros((row_count, KV_HEADS, group, HEAD_DIM), jnp.float32)
    terms = []
    for index in range(block_count):
        keys = blocks[index, 0].reshape(row_count, KV_HEADS, HEAD_DIM)
        values = blocks[index, 1].reshape(row_count, KV_HEADS, HEAD_DIM)
        exact = jnp.exp(logits_of(index) - top[..., None]) / total[..., None]
        probs = exact.astype(jnp.bfloat16)
        grad_probs = product('tkgd,ukd->kgtu', upstream_four, values)
        grad_logits = (exact * (grad_probs - delta[..., None])).astype(jnp.bfloat16)
        grad_query = grad_query + softmax_scale * product('kgtu,ukd->tkgd', grad_logits, keys)
        key_term = softmax_scale * product('kgtu,tkgd->ukd', grad_logits, query_four)
        value_term = product('kgtu,tkgd->ukd', probs, upstream_four)
        terms.append(jnp.stack([key_term.reshape(row_count, KV_HEADS * HEAD_DIM), value_term.reshape(row_count, KV_HEADS * HEAD_DIM)]))
    return grad_query.reshape(row_count, HEADS * HEAD_DIM).astype(jnp.bfloat16), jnp.stack(terms)


def reference(queries, keys_values, grad_out, parents):
    found = ancestor_rows(parents)
    accum = [jnp.zeros(keys_values.shape[1:], jnp.float32) for level_index in range(LEVELS)]
    grad_levels = []
    for depth_level in range(LEVELS):
        gathered = [keys_values[depth_level]]
        for offset in range(1, depth_level + 1):
            gathered.append(keys_values[depth_level - offset][found[offset][depth_level]])
        blocks = jnp.stack(gathered, axis=1)

        def one_segment(items):
            return segment_grads(items[0], items[1], items[2])

        grad_query, terms = lax.map(one_segment, (queries[depth_level], grad_out[depth_level], blocks))
        grad_levels.append(grad_query)
        accum[depth_level] = accum[depth_level] + terms[:, 0]
        for offset in range(1, depth_level + 1):
            rounded = lax.optimization_barrier(terms[:, offset].astype(jnp.bfloat16)).astype(jnp.float32)
            accum[depth_level - offset] = accum[depth_level - offset] + jax.ops.segment_sum(rounded, found[offset][depth_level], num_segments=SEGS)
    return jnp.stack(grad_levels), jnp.stack(accum).astype(jnp.bfloat16)
```

```python
import functools

import jax
import jax.numpy as jnp
from jax import lax
from jax.experimental import pallas as pl
from jax.experimental.pallas import tpu as pltpu
from jax.sharding import PartitionSpec as P

HEADS = 20
KV_HEADS = 4
HEAD_DIM = 128
GROUP = HEADS // KV_HEADS
ROWS = 128
LEVELS = 8
SEGS = 16
PIECE = 16
PIECES_PER_PART = ROWS // PIECE
STACK = GROUP * ROWS

NEG_FILL = -1e30
SCALE = HEAD_DIM ** -0.5
EXP2_SCALE = SCALE * 1.4426950408889634
MESH = pl.DeviceIdType.MESH
BF16 = jnp.bfloat16
F32 = jnp.float32


def lanes(index):
    return pl.ds(pl.multiple_of(index * HEAD_DIM, HEAD_DIM), HEAD_DIM)


def rows_of(index, count):
    return pl.ds(pl.multiple_of(index * count, count), count)


def fold(tile):
    return tile.reshape(ROWS // 8, 8, HEAD_DIM)


def kernel(
    parents, queries, keys_values, grad_out, grad_queries, grad_kv,
    anc, pick, spread, pieces, chosen, blocks, terms, term_pieces, own,
    q_stack, g_stack, logits, grad_probs, probs, grad_logits,
    kept, cross_out, cross_in, chain_out, chain_in, final_out, final_in,
    p1_send, p1_recv, up_send, up_recv, p3_send, p3_recv, b1_send, b1_recv,
    x_send, x_recv, c_send, c_recv, f_send, f_recv,
):
    level = lax.axis_index("depth")
    me = lax.axis_index("seg")
    y = level // 2
    core = level % 2
    sibling = 2 * y + 1 - core
    above = 2 * ((y + 1) % 4) + core
    below = 2 * ((y + 3) % 4) + core

    def remote(src, dst, send_sem, recv_sem, device):
        return pltpu.make_async_remote_copy(
            src_ref=src, dst_ref=dst, send_sem=send_sem, recv_sem=recv_sem,
            device_id=device, device_id_type=MESH,
        )

    def wait_bytes(ref, sem):
        pltpu.make_async_copy(ref, ref, sem).wait()

    def per_level(action):
        for count in range(1, LEVELS):
            pl.when(level == count)(functools.partial(action, count))

    barrier = pltpu.get_barrier_semaphore()

    @pl.loop(1, SEGS)
    def _(step):
        pl.semaphore_signal(
            barrier, inc=1, device_id=(level, (me + step) % SEGS), device_id_type=MESH
        )

    for other in (sibling, above, below):
        pl.semaphore_signal(barrier, inc=1, device_id=(other, me), device_id_type=MESH)
    pl.semaphore_wait(barrier, SEGS - 1 + 3)

    def own_rows(part, index, head):
        return keys_values.at[0, 0, part, rows_of(index, PIECE), lanes(head)]

    @pl.loop(0, KV_HEADS)
    def _(head):
        @pl.loop(1, SEGS)
        def _(step):
            peer = (me + step) % SEGS
            remote(
                own_rows(peer // PIECES_PER_PART, peer % PIECES_PER_PART, head),
                pieces.at[head, level, me], p1_send.at[head], p1_recv.at[head],
                (level, peer),
            ).start()

        pltpu.make_async_copy(
            own_rows(me // PIECES_PER_PART, me % PIECES_PER_PART, head),
            pieces.at[head, level, me], p1_recv.at[head],
        ).start()

    @pl.loop(0, SEGS)
    def _(column):
        current = column
        for offset in range(1, LEVELS):
            current = parents[jnp.maximum(level - offset, 0), current]
            anc[offset, column] = current

    @pl.loop(1, level + 1)
    def _(offset):
        lane = lax.broadcasted_iota(jnp.int32, (PIECE, SEGS * PIECE), 1)
        row = lax.broadcasted_iota(jnp.int32, (PIECE, SEGS * PIECE), 0)
        target = lane % PIECE
        lane_column = lane // PIECE
        for column in range(SEGS):
            found = anc[offset, column] * PIECE
            pick[offset, rows_of(column, PIECE), :] = jnp.where(
                lane == found + row, 1.0, 0.0
            ).astype(BF16)
            target = target + jnp.where(lane_column == column, found, 0)
        for column in range(SEGS):
            spread[offset, rows_of(column, PIECE), :] = jnp.where(
                target == row + column * PIECE, 1.0, 0.0
            ).astype(BF16)

    @pl.loop(0, KV_HEADS)
    def _(head):
        blocks[head, 0] = keys_values[0, 0, :, :, lanes(head)]

        @pl.loop(level + 1, LEVELS)
        def _(offset):
            blocks[head, offset] = jnp.zeros((2, ROWS, HEAD_DIM), BF16)

    @pl.loop(level + 1, LEVELS)
    def _(offset):
        probs[rows_of(offset, ROWS), :] = jnp.zeros((ROWS, STACK), BF16)
        grad_logits[rows_of(offset, ROWS), :] = jnp.zeros((ROWS, STACK), BF16)

    def lift(head, which, slot, device):
        return remote(
            pieces.at[head, which], pieces.at[head, which],
            up_send.at[head, slot], up_recv.at[head, which], (device, me),
        )

    lifts = (
        (0, y < 3, 0, above),
        (1, y == 0, 0, below),
        (2, core == 0, 0, sibling),
        (3, (y == 1) | (y == 2), 1, above),
        (4, y >= 1, 1, sibling),
        (5, y >= 2, 2, sibling),
        (6, y == 3, 3, sibling),
    )

    def lift_copy(head, entry):
        slot, _, hops, device = entry
        return lift(head, jnp.maximum(level - 2 * hops, 0), slot, device)

    def start_lifts(head, chosen_slots):
        for entry in lifts:
            if entry[0] in chosen_slots:
                pl.when(entry[1])(lambda entry=entry: lift_copy(head, entry).start())

    def wait_lift(head, hops):
        which = jnp.maximum(level - 2 * hops, 0)
        wait_bytes(pieces.at[head, which], up_recv.at[head, which])

    @pl.loop(0, KV_HEADS)
    def _(head):
        wait_bytes(pieces.at[head, level], p1_recv.at[head])
        start_lifts(head, (0, 1, 2))

    @pl.loop(0, KV_HEADS + 1)
    def _(tick):
        @pl.when(tick < KV_HEADS)
        def _():
            @pl.when(y >= 1)
            def _():
                wait_lift(tick, 1)
                start_lifts(tick, (3, 4))

        @pl.when(tick > 0)
        def _():
            head = tick - 1

            @pl.loop(0, 4)
            def _(pair):
                other = 2 * pair + 1 - core

                @pl.when(other < level)
                def _():
                    wait_bytes(pieces.at[head, other], up_recv.at[head, other])

            @pl.loop(1, level + 1)
            def _(offset):
                found = jnp.dot(
                    pick[offset],
                    pieces[head, level - offset].reshape(SEGS * PIECE, HEAD_DIM),
                    preferred_element_type=F32,
                )
                chosen[head, :, offset - 1] = found.astype(BF16).reshape(SEGS, PIECE, HEAD_DIM)

            def send(count):
                def arrived():
                    return blocks.at[
                        head, pl.ds(1, count), me // PIECES_PER_PART,
                        rows_of(me % PIECES_PER_PART, PIECE), :,
                    ]

                @pl.loop(1, SEGS)
                def _(step):
                    peer = (me + step) % SEGS
                    remote(
                        chosen.at[head, peer, pl.ds(0, count)], arrived(),
                        p3_send.at[head], p3_recv.at[head], (level, peer),
                    ).start()

                pltpu.make_async_copy(
                    chosen.at[head, me, pl.ds(0, count)], arrived(), p3_recv.at[head]
                ).start()

            per_level(send)

        @pl.when(tick < KV_HEADS)
        def _():
            @pl.when(y >= 2)
            def _():
                wait_lift(tick, 2)
                start_lifts(tick, (5,))

            @pl.when(y == 3)
            def _():
                wait_lift(tick, 3)
                start_lifts(tick, (6,))

    def attend(head):
        for group in range(GROUP):
            span = pl.ds(group * ROWS, ROWS)
            q_stack[span, :] = queries[0, 0, :, lanes(head * GROUP + group)]
            g_stack[span, :] = grad_out[0, 0, :, lanes(head * GROUP + group)]
        keys = blocks[head, :, 0].reshape(LEVELS * ROWS, HEAD_DIM)
        values = blocks[head, :, 1].reshape(LEVELS * ROWS, HEAD_DIM)
        contract_last = (((1,), (1,)), ((), ()))
        logits[...] = lax.dot_general(
            keys, q_stack[...], contract_last, preferred_element_type=F32
        )
        grad_probs[...] = lax.dot_general(
            values, g_stack[...], contract_last, preferred_element_type=F32
        )

        @pl.loop(0, GROUP)
        def _(group):
            span = lanes(group)
            u_row = lax.broadcasted_iota(jnp.int32, (ROWS, ROWS), 0)
            t_row = lax.broadcasted_iota(jnp.int32, (ROWS, ROWS), 1)
            first = jnp.where(u_row <= t_row, logits[0:ROWS, span], NEG_FILL)
            logits[0:ROWS, span] = first

            def step_max(offset, best):
                tile = logits[rows_of(offset, ROWS), span]
                return jnp.maximum(best, fold(tile).max(0))

            best = lax.fori_loop(1, level + 1, step_max, fold(first).max(0))
            top = best.max(0, keepdims=True)

            def step_exp(offset, total):
                span_rows = rows_of(offset, ROWS)
                tile = jnp.exp2((logits[span_rows, span] - top) * EXP2_SCALE)
                logits[span_rows, span] = tile
                return total + fold(tile).sum(0)

            total = lax.fori_loop(0, level + 1, step_exp, jnp.zeros((8, HEAD_DIM), F32))
            inverse = 1.0 / total.sum(0, keepdims=True)

            def step_delta(offset, delta):
                span_rows = rows_of(offset, ROWS)
                exact = logits[span_rows, span] * inverse
                rounded = exact.astype(BF16)
                logits[span_rows, span] = exact
                probs[span_rows, span] = rounded
                return delta + fold(rounded.astype(F32) * grad_probs[span_rows, span]).sum(0)

            delta = lax.fori_loop(0, level + 1, step_delta, jnp.zeros((8, HEAD_DIM), F32))
            delta = delta.sum(0, keepdims=True)

            @pl.loop(0, level + 1)
            def _(offset):
                span_rows = rows_of(offset, ROWS)
                grad_logits[span_rows, span] = (
                    logits[span_rows, span] * (grad_probs[span_rows, span] - delta)
                ).astype(BF16)

        value_term = jnp.dot(probs[...], g_stack[...], preferred_element_type=F32)
        own[head, 1] = value_term[0:ROWS]
        terms[head, :, 1] = value_term.astype(BF16).reshape(LEVELS, ROWS, HEAD_DIM)
        key_term = SCALE * jnp.dot(grad_logits[...], q_stack[...], preferred_element_type=F32)
        own[head, 0] = key_term[0:ROWS]
        terms[head, :, 0] = key_term.astype(BF16).reshape(LEVELS, ROWS, HEAD_DIM)
        grad_query = lax.dot_general(
            keys, grad_logits[...], (((0,), (0,)), ((), ())), preferred_element_type=F32
        )
        for group in range(GROUP):
            tile = grad_query[:, group * ROWS:(group + 1) * ROWS]
            grad_queries[0, 0, :, lanes(head * GROUP + group)] = (SCALE * tile.T).astype(BF16)

    def send_terms(head, count):
        @pl.loop(1, SEGS)
        def _(step):
            peer = (me + step) % SEGS
            remote(
                terms.at[
                    head, pl.ds(1, count), peer // PIECES_PER_PART,
                    rows_of(peer % PIECES_PER_PART, PIECE), :,
                ],
                term_pieces.at[head, pl.ds(1, count), me],
                b1_send.at[head], b1_recv.at[head], (level, peer),
            ).start()

        pltpu.make_async_copy(
            terms.at[
                head, pl.ds(1, count), me // PIECES_PER_PART,
                rows_of(me % PIECES_PER_PART, PIECE), :,
            ],
            term_pieces.at[head, pl.ds(1, count), me], b1_recv.at[head],
        ).start()

    def summed(head, offset):
        return jnp.dot(
            spread[offset], term_pieces[head, offset].reshape(SEGS * PIECE, HEAD_DIM),
            preferred_element_type=F32,
        )

    def cross_copy(head, pair):
        return remote(
            cross_out.at[head, pair], cross_in.at[head, pair],
            x_send.at[head, pair], x_recv.at[head, pair], (sibling, me),
        )

    def chain_copy(head, slot, device):
        return remote(
            chain_out.at[head, slot], chain_in.at[head, slot],
            c_send.at[head, slot], c_recv.at[head, slot], (device, me),
        )

    def wait_chain(head, slot):
        wait_bytes(chain_in.at[head, slot], c_recv.at[head, slot])

    def sum_stage(head):
        per_level(
            lambda count: wait_bytes(term_pieces.at[head, pl.ds(1, count)], b1_recv.at[head])
        )

        @pl.loop(0, 4)
        def _(pair):
            offset = level - (2 * pair + 1 - core)

            @pl.when(offset >= 1)
            def _():
                cross_out[head, pair] = summed(head, offset).astype(BF16)
                cross_copy(head, pair).start()

        @pl.loop(0, y)
        def _(pair):
            kept[head, pair] = summed(head, 2 * (y - pair))

    def chain_first(head):
        @pl.loop(0, y - core + 1)
        def _(pair):
            wait_bytes(cross_in.at[head, pair], x_recv.at[head, pair])

        @pl.loop(0, y)
        def _(pair):
            kept[head, pair] += cross_in[head, pair].astype(F32)

        @pl.when(y == 3)
        def _():
            for slot, pair, device in ((0, 2, below), (1, 1, below), (2, 0, above)):
                chain_out[head, slot] = kept[head, pair].astype(BF16)
                chain_copy(head, slot, device).start()

        @pl.when(y == 2)
        def _():
            chain_out[head, 1] = kept[head, 0].astype(BF16)
            chain_copy(head, 1, below).start()

    def chain_second(head):
        @pl.when((y == 1) | (y == 2))
        def _():
            wait_chain(head, 1)
            chain_out[head, 0] = (kept[head, y - 1] + chain_in[head, 1].astype(F32)).astype(BF16)
            chain_copy(head, 0, below).start()

    def own_span(index):
        return index // PIECES_PER_PART, rows_of(index % PIECES_PER_PART, PIECE)

    def final_send(head):
        @pl.when(level < LEVELS - 1)
        def _():
            kept[head, 3] = jnp.zeros((SEGS * PIECE, HEAD_DIM), F32)

            @pl.when(y < 3)
            def _():
                wait_chain(head, 0)
                kept[head, 3] += chain_in[head, 0].astype(F32)

            @pl.when(y == 0)
            def _():
                wait_chain(head, 2)
                kept[head, 3] += chain_in[head, 2].astype(F32)

            @pl.when(core == 0)
            def _():
                kept[head, 3] += cross_in[head, y].astype(F32)

            final_out[head] = kept[head, 3].astype(BF16).reshape(SEGS, PIECE, HEAD_DIM)
            part, span = own_span(me)

            @pl.loop(1, SEGS)
            def _(step):
                peer = (me + step) % SEGS
                remote(
                    final_out.at[head, peer], final_in.at[head, part, span, :],
                    f_send.at[head], f_recv.at[head], (level, peer),
                ).start()

            pltpu.make_async_copy(
                final_out.at[head, me], final_in.at[head, part, span, :], f_recv.at[head]
            ).start()

    def final_store(head):
        @pl.when(level < LEVELS - 1)
        def _():
            wait_bytes(final_in.at[head], f_recv.at[head])
            own[head] = own[head] + final_in[head].astype(F32)

        grad_kv[0, 0, :, :, lanes(head)] = own[head].astype(BF16)

    @pl.loop(0, KV_HEADS + 5)
    def _(tick):
        @pl.when(tick < KV_HEADS)
        def _():
            per_level(
                lambda count: wait_bytes(blocks.at[tick, pl.ds(1, count)], p3_recv.at[tick])
            )
            attend(tick)
            per_level(lambda count: send_terms(tick, count))

        for lag, stage in enumerate(
            (sum_stage, chain_first, chain_second, final_send, final_store), 1
        ):
            @pl.when((tick >= lag) & (tick < KV_HEADS + lag))
            def _():
                stage(tick - lag)

    @pl.loop(0, KV_HEADS)
    def _(head):
        wait_bytes(final_out.at[head, pl.ds(1, SEGS - 1)], p1_send.at[head])
        for entry in lifts:
            pl.when(entry[1])(lambda entry=entry: lift_copy(head, entry).wait_send())

        def sent(count):
            wait_bytes(chosen.at[head, pl.ds(1, SEGS - 1), pl.ds(0, count)], p3_send.at[head])
            wait_bytes(
                term_pieces.at[head, pl.ds(1, count), pl.ds(1, SEGS - 1)], b1_send.at[head]
            )

        per_level(sent)

        @pl.loop(0, 4)
        def _(pair):
            @pl.when(level - (2 * pair + 1 - core) >= 1)
            def _():
                cross_copy(head, pair).wait_send()

        @pl.when(y == 3)
        def _():
            for slot, device in ((0, below), (1, below), (2, above)):
                chain_copy(head, slot, device).wait_send()

        @pl.when(y == 2)
        def _():
            chain_copy(head, 1, below).wait_send()

        @pl.when((y == 1) | (y == 2))
        def _():
            chain_copy(head, 0, below).wait_send()

        @pl.when(level < LEVELS - 1)
        def _():
            wait_bytes(final_out.at[head, pl.ds(1, SEGS - 1)], f_send.at[head])


def shards(queries, keys_values, grad_out, parents):
    vmem = pl.BlockSpec(memory_space=pltpu.VMEM)
    smem = pl.BlockSpec(memory_space=pltpu.SMEM)
    dma = pltpu.SemaphoreType.DMA
    tile = (SEGS, PIECE, HEAD_DIM)
    flat = (SEGS * PIECE, HEAD_DIM)
    keys_count = LEVELS * ROWS
    scratch = [
        pltpu.SMEM((LEVELS, SEGS), jnp.int32),
        pltpu.VMEM((LEVELS, SEGS * PIECE, SEGS * PIECE), BF16),
        pltpu.VMEM((LEVELS, SEGS * PIECE, SEGS * PIECE), BF16),
        pltpu.VMEM((KV_HEADS, LEVELS) + tile, BF16),
        pltpu.VMEM((KV_HEADS, SEGS, LEVELS - 1, PIECE, HEAD_DIM), BF16),
        pltpu.VMEM((KV_HEADS, LEVELS, 2, ROWS, HEAD_DIM), BF16),
        pltpu.VMEM((KV_HEADS, LEVELS, 2, ROWS, HEAD_DIM), BF16),
        pltpu.VMEM((KV_HEADS, LEVELS) + tile, BF16),
        pltpu.VMEM((KV_HEADS, 2, ROWS, HEAD_DIM), F32),
        pltpu.VMEM((STACK, HEAD_DIM), BF16),
        pltpu.VMEM((STACK, HEAD_DIM), BF16),
        pltpu.VMEM((keys_count, STACK), F32),
        pltpu.VMEM((keys_count, STACK), F32),
        pltpu.VMEM((keys_count, STACK), BF16),
        pltpu.VMEM((keys_count, STACK), BF16),
        pltpu.VMEM((KV_HEADS, 4) + flat, F32),
        pltpu.VMEM((KV_HEADS, 4) + flat, BF16),
        pltpu.VMEM((KV_HEADS, 4) + flat, BF16),
        pltpu.VMEM((KV_HEADS, 3) + flat, BF16),
        pltpu.VMEM((KV_HEADS, 3) + flat, BF16),
        pltpu.VMEM((KV_HEADS,) + tile, BF16),
        pltpu.VMEM((KV_HEADS, 2, ROWS, HEAD_DIM), BF16),
        dma((KV_HEADS,)), dma((KV_HEADS,)),
        dma((KV_HEADS, 7)), dma((KV_HEADS, LEVELS)),
        dma((KV_HEADS,)), dma((KV_HEADS,)),
        dma((KV_HEADS,)), dma((KV_HEADS,)),
        dma((KV_HEADS, 4)), dma((KV_HEADS, 4)),
        dma((KV_HEADS, 3)), dma((KV_HEADS, 3)),
        dma((KV_HEADS,)), dma((KV_HEADS,)),
    ]
    return pl.pallas_call(
        kernel,
        out_shape=(
            jax.ShapeDtypeStruct(queries.shape, BF16),
            jax.ShapeDtypeStruct(keys_values.shape, BF16),
        ),
        in_specs=[smem, vmem, vmem, vmem],
        out_specs=(vmem, vmem),
        scratch_shapes=scratch,
        compiler_params=pltpu.CompilerParams(
            collective_id=0, has_side_effects=True, vmem_limit_bytes=48 * 1024 * 1024
        ),
        cost_estimate=pl.CostEstimate(
            flops=5 * 2 * HEADS * LEVELS * ROWS * ROWS * HEAD_DIM,
            bytes_accessed=8 * 1024 * 1024,
            transcendentals=HEADS * LEVELS * ROWS * ROWS,
        ),
    )(parents.reshape(LEVELS - 1, SEGS), queries, keys_values, grad_out)


def solution(mesh):
    in_specs = (
        P("depth", "seg", None, None),
        P("depth", "seg", None, None, None),
        P("depth", "seg", None, None),
        P(),
    )
    out_specs = (P("depth", "seg", None, None), P("depth", "seg", None, None, None))
    return jax.shard_map(shards, mesh=mesh, in_specs=in_specs, out_specs=out_specs, check_vma=False)
```

```python
import functools

import jax
import jax.numpy as jnp
from jax import lax
from jax.experimental import pallas as pl
from jax.experimental.pallas import tpu as pltpu
from jax.sharding import PartitionSpec as P

HEADS = 20
KV_HEADS = 4
HEAD_DIM = 128
GROUP = HEADS // KV_HEADS
ROWS = 128
LEVELS = 8
SEGS = 16
PIECE = 16
PIECES_PER_PART = ROWS // PIECE
STACK = GROUP * ROWS
PAIR = 2 * ROWS
LAG = 2

NEG_FILL = -1e30
SCALE = HEAD_DIM ** -0.5
EXP2_SCALE = SCALE * 1.4426950408889634
MESH = pl.DeviceIdType.MESH
BF16 = jnp.bfloat16
F32 = jnp.float32

PLANE = ((0, 1, 2, 3), (3, 1, 2, 0))

LIFTS = (
    (0, 0, 0, 0, ("above", "below"), True),
    (0, 1, 0, 1, ("above",), True),
    (0, 2, 0, 2, ("above",), True),
    (0, 3, 0, 3, (), True),
    (0, 1, 1, 0, ("above",), True),
    (0, 2, 1, 1, ("above",), True),
    (0, 3, 1, 2, (), True),
    (0, 3, 1, 0, (), True),
    (0, 2, 2, 0, (), True),
    (0, 3, 2, 1, (), True),
    (1, 3, 0, 0, ("above", "below"), True),
    (1, 1, 0, 1, ("above", "below"), True),
    (1, 2, 0, 2, ("below",), True),
    (1, 0, 0, 3, (), True),
    (1, 2, 1, 0, ("below",), True),
    (1, 2, 1, 1, (), True),
    (1, 1, 1, 2, ("below",), False),
    (1, 0, 1, 0, (), True),
    (1, 0, 1, 1, (), True),
    (1, 1, 2, 0, (), True),
    (1, 0, 2, 2, (), True),
)

CHAIN = (
    (0, 3, 0, 2, None, 0, "below"),
    (0, 3, 0, 1, None, 1, "below"),
    (0, 3, 0, 0, None, 2, "above"),
    (0, 2, 0, 0, None, 1, "below"),
    (0, 2, 1, 1, 1, 0, "below"),
    (0, 1, 1, 0, 1, 0, "below"),
    (1, 0, 0, 0, None, 2, "below"),
    (1, 0, 0, 1, None, 0, "above"),
    (1, 0, 0, 2, None, 1, "above"),
    (1, 2, 0, 1, None, 2, "below"),
    (1, 1, 0, 0, None, 1, "above"),
    (1, 2, 1, 0, 1, 0, "above"),
    (1, 1, 1, None, 1, 0, "above"),
)

TOTALS = (
    (0, 0, (0, 2)), (0, 1, (0,)), (0, 2, (0,)),
    (1, 1, (0, 2)), (1, 2, (0,)), (1, 3, (0, 2)),
)


def lanes(index, count=1):
    width = count * HEAD_DIM
    return pl.ds(pl.multiple_of(index * width, width), width)


def rows_of(index, count):
    return pl.ds(pl.multiple_of(index * count, count), count)


def piece_of(index):
    return index // PIECES_PER_PART, rows_of(index % PIECES_PER_PART, PIECE)


def fold(tile):
    return tile.reshape(tile.shape[0] // 8, 8, tile.shape[1])


def kernel(
    parents, queries, keys_values, grad_out, grad_queries, grad_kv,
    anc, pick, spread, pieces, chosen, blocks, terms, term_pieces, own, own_out, own_in,
    stacks, staged, query_sum, stats, logits, grad_probs, probs, grad_logits,
    kept, total_sum, cross_out, cross_in, chain_out, chain_in, final_out, final_in,
    p1_send, p1_recv, up_send, up_recv, q_send, q_recv, k_send, k_recv, p3_send, p3_recv,
    b1_send, b1_recv, o_send, o_recv, d_send, d_recv, x_send, x_recv, c_send, c_recv,
    f_send, f_recv,
):
    level = lax.axis_index("depth")
    me = lax.axis_index("seg")
    y = level // 2
    core = level % 2
    places = {
        "sibling": 2 * y + 1 - core,
        "above": 2 * ((y + 1) % 4) + core,
        "below": 2 * ((y + 3) % 4) + core,
    }
    sibling = places["sibling"]
    outer = (y == 0) | (y == 3)
    partner = jnp.where(outer, 2 * (3 - y) + core, level)

    def host_of(head):
        return jnp.where(head % 2 == 1, partner, level)

    def remote(src, dst, send_sem, recv_sem, device):
        return pltpu.make_async_remote_copy(
            src_ref=src, dst_ref=dst, send_sem=send_sem, recv_sem=recv_sem,
            device_id=device, device_id_type=MESH,
        )

    def wait_bytes(ref, sem):
        pltpu.make_async_copy(ref, ref, sem).wait()

    def per_level(which, action):
        for count in range(1, LEVELS):
            pl.when(which == count)(functools.partial(action, count))

    def move(head, src, dst, send_sem, recv_sem):
        host = host_of(head)

        @pl.when(host != level)
        def _():
            remote(src, dst, send_sem, recv_sem, (host, me)).start()

        @pl.when(host == level)
        def _():
            pltpu.make_async_copy(src, dst, recv_sem).start()

    barrier = pltpu.get_barrier_semaphore()

    def greet(device):
        pl.semaphore_signal(barrier, inc=1, device_id=device, device_id_type=MESH)

    @pl.loop(1, SEGS)
    def _(step):
        greet((level, (me + step) % SEGS))

    for other in places.values():
        greet((other, me))

    @pl.when(outer)
    def _():
        @pl.loop(0, SEGS)
        def _(step):
            greet((partner, (me + step) % SEGS))

    pl.semaphore_wait(barrier, SEGS - 1 + 3 + jnp.where(outer, SEGS, 0))

    @pl.loop(0, KV_HEADS)
    def _(head):
        host = host_of(head)

        def source(peer):
            part, span = piece_of(peer)
            return keys_values.at[0, 0, part, span, lanes(head)]

        @pl.loop(1, SEGS)
        def _(step):
            peer = (me + step) % SEGS
            remote(
                source(peer), pieces.at[head, level, me],
                p1_send.at[head], p1_recv.at[head], (host, peer),
            ).start()

        @pl.when(host != level)
        def _():
            remote(
                source(me), pieces.at[head, level, me],
                p1_send.at[head], p1_recv.at[head], (host, me),
            ).start()

        @pl.when(host == level)
        def _():
            pltpu.make_async_copy(
                source(me), pieces.at[head, level, me], p1_recv.at[head]
            ).start()

    def move_inputs(head):
        move(
            head, keys_values.at[0, 0, :, :, lanes(head)], blocks.at[head, 0],
            k_send.at[head], k_recv.at[head],
        )

        @pl.loop(0, GROUP)
        def _(group):
            for index, array in enumerate((queries, grad_out)):
                move(
                    head, array.at[0, 0, :, lanes(head * GROUP + group)],
                    stacks.at[head, index, rows_of(group, ROWS), :],
                    q_send.at[head], q_recv.at[head],
                )

    @pl.loop(0, 2)
    def _(parity):
        target_level = host_of(parity)

        @pl.loop(0, SEGS)
        def _(column):
            current = column
            for offset in range(1, LEVELS):
                current = parents[jnp.maximum(target_level - offset, 0), 0, current]
                anc[parity, offset, column] = current

        @pl.loop(1, LEVELS)
        def _(offset):
            lane = lax.broadcasted_iota(jnp.int32, (PIECE, SEGS * PIECE), 1)
            row = lax.broadcasted_iota(jnp.int32, (PIECE, SEGS * PIECE), 0)
            target = lane % PIECE
            lane_column = lane // PIECE
            for column in range(SEGS):
                found = anc[parity, offset, column] * PIECE
                pick[parity, offset, rows_of(column, PIECE), :] = jnp.where(
                    lane == found + row, 1.0, 0.0
                ).astype(BF16)
                target = target + jnp.where(lane_column == column, found, 0)
            for column in range(SEGS):
                spread[parity, offset, rows_of(column, PIECE), :] = jnp.where(
                    target == row + column * PIECE, 1.0, 0.0
                ).astype(BF16)

    @pl.loop(0, KV_HEADS)
    def _(head):
        here = host_of(head)

        @pl.when(here % 2 == 0)
        def _():
            blocks[head, here + 1] = jnp.zeros((2, ROWS, HEAD_DIM), BF16)

    def lift_copies(head, entry):
        parity, row, stage, plane, targets, to_sibling = entry
        which = 2 * plane + core
        copies = []
        slots = {"above": 0, "below": 1} if stage == 0 else {"above": 2, "below": 2}
        for target in targets:
            copies.append((slots[target], None, places[target]))
        if to_sibling:
            copies.append((3 + plane, core == 0 if stage == 0 else None, sibling))
        return [
            (
                condition,
                remote(
                    pieces.at[head, which], pieces.at[head, which],
                    up_send.at[head, slot], up_recv.at[head, which], (device, me),
                ),
            )
            for slot, condition, device in copies
        ]

    def each_lift(head, stages, action):
        for entry in LIFTS:
            if entry[2] in stages:
                pl.when((head % 2 == entry[0]) & (y == entry[1]))(
                    functools.partial(action, entry)
                )

    def lift_stage(head, stage):
        def forward(entry):
            if stage > 0:
                which = 2 * entry[3] + core
                wait_bytes(pieces.at[head, which], up_recv.at[head, which])
            for condition, copy in lift_copies(head, entry):
                if condition is None:
                    copy.start()
                else:
                    pl.when(condition)(copy.start)

        each_lift(head, (stage,), forward)

    @pl.loop(0, KV_HEADS)
    def _(head):
        here = host_of(head)
        wait_bytes(pieces.at[head, here], p1_recv.at[head])
        lift_stage(head, 0)
        move_inputs(head)

    def select(head):
        here = host_of(head)
        parity = head % 2

        @pl.loop(0, 4)
        def _(plane):
            other = 2 * plane + 1 - core

            @pl.when(other < here)
            def _():
                wait_bytes(pieces.at[head, other], up_recv.at[head, other])

        def pick_up(last):
            for offset in range(1, last + 1):
                found = jnp.dot(
                    pick[parity, offset],
                    pieces[head, jnp.maximum(here - offset, 0)].reshape(SEGS * PIECE, HEAD_DIM),
                    preferred_element_type=F32,
                )
                chosen[head, :, offset - 1] = found.astype(BF16).reshape(SEGS, PIECE, HEAD_DIM)

        pl.when((here > 0) & (here < 4))(lambda: pick_up(3))
        pl.when(here >= 4)(lambda: pick_up(7))

        def send(count):
            part, span = piece_of(me)

            @pl.loop(1, SEGS)
            def _(step):
                peer = (me + step) % SEGS
                remote(
                    chosen.at[head, peer, pl.ds(0, count)],
                    blocks.at[head, pl.ds(1, count), part, span, :],
                    p3_send.at[head], p3_recv.at[head], (level, peer),
                ).start()

            pltpu.make_async_copy(
                chosen.at[head, me, pl.ds(0, count)],
                blocks.at[head, pl.ds(1, count), part, span, :], p3_recv.at[head],
            ).start()

        per_level(here, send)

    def attend(head):
        here = host_of(head)
        pairs = here // 2 + 1
        contract_last = (((1,), (1,)), ((), ()))
        span_all = [pl.ds(group * ROWS, ROWS) for group in range(GROUP)]

        def block_pair(pair, part):
            return blocks[head, pl.ds(2 * pair, 2), part].reshape(PAIR, HEAD_DIM)

        stats[0] = jnp.full((8, STACK), NEG_FILL, F32)

        @pl.loop(0, pairs)
        def _(pair):
            span_rows = rows_of(pair, PAIR)
            logits[span_rows, :] = lax.dot_general(
                block_pair(pair, 0), stacks[head, 0], contract_last, preferred_element_type=F32
            )
            grad_probs[span_rows, :] = lax.dot_general(
                block_pair(pair, 1), stacks[head, 1], contract_last, preferred_element_type=F32
            )

            @pl.when(pair == 0)
            def _():
                u_row = lax.broadcasted_iota(jnp.int32, (ROWS, ROWS), 0)
                t_row = lax.broadcasted_iota(jnp.int32, (ROWS, ROWS), 1)
                for span in span_all:
                    logits[0:ROWS, span] = jnp.where(
                        u_row <= t_row, logits[0:ROWS, span], NEG_FILL
                    )

            @pl.when((pair == pairs - 1) & (here % 2 == 0))
            def _():
                logits[rows_of(here + 1, ROWS), :] = jnp.full((ROWS, STACK), NEG_FILL, F32)

            for span in span_all:
                stats[0, :, span] = jnp.maximum(
                    stats[0, :, span], fold(logits[span_rows, span]).max(0)
                )

        stats[1] = jnp.zeros((8, STACK), F32)
        stats[2] = jnp.zeros((8, STACK), F32)
        stats[0] = jnp.broadcast_to(stats[0].max(0, keepdims=True), (8, STACK))

        @pl.loop(0, pairs)
        def _(pair):
            span_rows = rows_of(pair, PAIR)
            for span in span_all:
                top = stats[0, 0:1, span]
                tile = jnp.exp2((logits[span_rows, span] - top) * EXP2_SCALE)
                logits[span_rows, span] = tile
                stats[1, :, span] += fold(tile).sum(0)
                stats[2, :, span] += fold(tile * grad_probs[span_rows, span]).sum(0)

        inverse = 1.0 / stats[1].sum(0, keepdims=True)
        delta = stats[2].sum(0, keepdims=True) * inverse
        stats[1] = jnp.broadcast_to(inverse, (8, STACK))
        stats[2] = jnp.broadcast_to(delta, (8, STACK))
        query_sum[...] = jnp.zeros((HEAD_DIM, STACK), F32)

        @pl.loop(0, pairs)
        def _(pair):
            span_rows = rows_of(pair, PAIR)
            for span in span_all:
                exact = logits[span_rows, span] * stats[1, 0:1, span]
                probs[:, span] = exact.astype(BF16)
                grad_logits[:, span] = (
                    exact * (grad_probs[span_rows, span] - stats[2, 0:1, span])
                ).astype(BF16)
            value_term = jnp.dot(probs[...], stacks[head, 1], preferred_element_type=F32)
            key_term = SCALE * jnp.dot(
                grad_logits[...], stacks[head, 0], preferred_element_type=F32
            )
            for part, term in enumerate((key_term, value_term)):
                terms[head, pl.ds(2 * pair, 2), part] = term.astype(BF16).reshape(
                    2, ROWS, HEAD_DIM
                )

                @pl.when(pair == 0)
                def _():
                    own[head, part] = term[0:ROWS]

            query_sum[...] += lax.dot_general(
                block_pair(pair, 0), grad_logits[...], (((0,), (0,)), ((), ())),
                preferred_element_type=F32,
            )

        for group, span in enumerate(span_all):
            staged[head, :, span] = (SCALE * query_sum[:, span].T).astype(BF16)

    def staged_copy_target(head):
        return grad_queries.at[0, 0, :, lanes(head, GROUP)]

    def send_results(head):
        host = host_of(head)
        here = host

        def send(count):
            @pl.loop(1, SEGS)
            def _(step):
                peer = (me + step) % SEGS
                part, span = piece_of(peer)
                remote(
                    terms.at[head, pl.ds(1, count), part, span, :],
                    term_pieces.at[head, pl.ds(1, count), me],
                    b1_send.at[head], b1_recv.at[head], (level, peer),
                ).start()

            part, span = piece_of(me)
            pltpu.make_async_copy(
                terms.at[head, pl.ds(1, count), part, span, :],
                term_pieces.at[head, pl.ds(1, count), me], b1_recv.at[head],
            ).start()

        per_level(here, send)
        move(
            head, staged.at[head], staged_copy_target(head), d_send.at[head], d_recv.at[head]
        )

        @pl.when(host != level)
        def _():
            own_out[head] = own[head].astype(BF16)
            remote(
                own_out.at[head], own_in.at[head], o_send.at[head], o_recv.at[head], (host, me)
            ).start()

    def summed(head, offset):
        return jnp.dot(
            spread[head % 2, offset],
            term_pieces[head, offset].reshape(SEGS * PIECE, HEAD_DIM),
            preferred_element_type=F32,
        )

    def cross_copy(head, plane):
        return remote(
            cross_out.at[head, plane], cross_in.at[head, plane],
            x_send.at[head, plane], x_recv.at[head, plane], (sibling, me),
        )

    def sum_stage(head):
        here = host_of(head)
        per_level(
            here,
            lambda count: wait_bytes(term_pieces.at[head, pl.ds(1, count)], b1_recv.at[head]),
        )

        def sums(planes):
            for plane in range(planes):
                offset = jnp.maximum(here - (2 * plane + 1 - core), 1)
                cross_out[head, plane] = summed(head, offset).astype(BF16)
            for plane in range(planes - 1):
                offset = jnp.maximum(here - (2 * plane + core), 1)
                kept[head, plane] = summed(head, offset)

        pl.when((here > 0) & (here < 4))(lambda: sums(2))
        pl.when(here >= 4)(lambda: sums(4))

        @pl.loop(0, 4)
        def _(plane):
            @pl.when(here - (2 * plane + 1 - core) >= 1)
            def _():
                cross_copy(head, plane).start()

    def chain_copy(head, entry):
        added, slot, place = entry[4:]
        source = chain_in.at[head, added] if entry[3] is None else chain_out.at[head, slot]
        return remote(
            source, chain_in.at[head, slot], c_send.at[head, slot], c_recv.at[head, slot],
            (places[place], me),
        )

    def each_chain(head, stages, action):
        for entry in CHAIN:
            if entry[2] in stages:
                pl.when((head % 2 == entry[0]) & (y == entry[1]))(
                    functools.partial(action, entry)
                )

    def chain_stage(head, stage):
        def send(entry):
            plane, added, slot = entry[3:6]
            if added is not None:
                wait_bytes(chain_in.at[head, added], c_recv.at[head, added])
            if plane is not None:
                value = kept[head, plane]
                if added is not None:
                    value = value + chain_in[head, added].astype(F32)
                chain_out[head, slot] = value.astype(BF16)
            chain_copy(head, entry).start()

        each_chain(head, (stage,), send)

    def chain_first(head):
        plane_here = host_of(head) // 2

        @pl.loop(0, plane_here - core + 1)
        def _(plane):
            wait_bytes(cross_in.at[head, plane], x_recv.at[head, plane])

        @pl.loop(0, plane_here)
        def _(plane):
            kept[head, plane] += cross_in[head, plane].astype(F32)

        chain_stage(head, 0)

    def chain_second(head):
        chain_stage(head, 1)

    def final_send(head):
        host = host_of(head)

        @pl.when(host < LEVELS - 1)
        def _():
            total_sum[...] = jnp.zeros((SEGS * PIECE, HEAD_DIM), F32)

            def add(slots):
                for slot in slots:
                    wait_bytes(chain_in.at[head, slot], c_recv.at[head, slot])
                    total_sum[...] += chain_in[head, slot].astype(F32)

            for parity, row, slots in TOTALS:
                pl.when((head % 2 == parity) & (y == row))(functools.partial(add, slots))

            @pl.when(core == 0)
            def _():
                total_sum[...] += cross_in[head, host // 2].astype(F32)

            final_out[head] = total_sum[...].astype(BF16).reshape(SEGS, PIECE, HEAD_DIM)
            part, span = piece_of(me)

            @pl.loop(1, SEGS)
            def _(step):
                peer = (me + step) % SEGS
                remote(
                    final_out.at[head, peer], final_in.at[head, part, span, :],
                    f_send.at[head], f_recv.at[head], (host, peer),
                ).start()

            move(
                head, final_out.at[head, me], final_in.at[head, part, span, :],
                f_send.at[head], f_recv.at[head],
            )

    def final_store(head):
        away = host_of(head) != level

        @pl.when(away)
        def _():
            wait_bytes(own_in.at[head], o_recv.at[head])
            own[head] = own_in[head].astype(F32)

        @pl.when(level < LEVELS - 1)
        def _():
            wait_bytes(final_in.at[head], f_recv.at[head])
            own[head] = own[head] + final_in[head].astype(F32)

        grad_kv[0, 0, :, :, lanes(head)] = own[head].astype(BF16)

    stages = (sum_stage, chain_first, chain_second, final_send, final_store)

    @pl.loop(0, KV_HEADS + LAG + len(stages))
    def _(tick):
        @pl.when(tick < KV_HEADS)
        def _():
            lift_stage(tick, 1)

        @pl.when((tick >= 1) & (tick < KV_HEADS + 1))
        def _():
            select(tick - 1)

        @pl.when(tick < KV_HEADS)
        def _():
            lift_stage(tick, 2)

        @pl.when((tick >= LAG) & (tick < KV_HEADS + LAG))
        def _():
            head = tick - LAG
            per_level(
                host_of(head),
                lambda count: wait_bytes(blocks.at[head, pl.ds(1, count)], p3_recv.at[head]),
            )
            wait_bytes(blocks.at[head, 0], k_recv.at[head])
            wait_bytes(stacks.at[head], q_recv.at[head])
            attend(head)
            send_results(head)

        for lag, stage in enumerate(stages, LAG + 1):
            @pl.when((tick >= lag) & (tick < KV_HEADS + lag))
            def _():
                stage(tick - lag)

    @pl.loop(0, KV_HEADS)
    def _(head):
        host = host_of(head)
        away = host != level
        wait_bytes(staged_copy_target(head), d_recv.at[head])
        wait_bytes(final_out.at[head, pl.ds(1, SEGS - 1)], p1_send.at[head])

        @pl.when(away)
        def _():
            wait_bytes(final_out.at[head, 0], p1_send.at[head])
            wait_bytes(blocks.at[head, 0], k_send.at[head])
            wait_bytes(stacks.at[head], q_send.at[head])
            wait_bytes(staged.at[head], d_send.at[head])
            wait_bytes(own_out.at[head], o_send.at[head])

        def lifted(entry):
            for condition, copy in lift_copies(head, entry):
                if condition is None:
                    copy.wait_send()
                else:
                    pl.when(condition)(copy.wait_send)

        each_lift(head, (0, 1, 2), lifted)

        def sent(count):
            wait_bytes(chosen.at[head, pl.ds(1, SEGS - 1), pl.ds(0, count)], p3_send.at[head])
            wait_bytes(
                term_pieces.at[head, pl.ds(1, count), pl.ds(1, SEGS - 1)], b1_send.at[head]
            )

        per_level(host, sent)

        @pl.loop(0, 4)
        def _(plane):
            @pl.when(host - (2 * plane + 1 - core) >= 1)
            def _():
                cross_copy(head, plane).wait_send()

        each_chain(head, (0, 1), lambda entry: chain_copy(head, entry).wait_send())

        @pl.when(host < LEVELS - 1)
        def _():
            wait_bytes(final_out.at[head, pl.ds(1, SEGS - 1)], f_send.at[head])

            @pl.when(away)
            def _():
                wait_bytes(final_out.at[head, 0], f_send.at[head])


def shards(queries, keys_values, grad_out, parents):
    vmem = pl.BlockSpec(memory_space=pltpu.VMEM)
    smem = pl.BlockSpec(memory_space=pltpu.SMEM)
    anywhere = pl.BlockSpec(memory_space=pl.ANY)
    dma = pltpu.SemaphoreType.DMA
    tile = (SEGS, PIECE, HEAD_DIM)
    flat = (SEGS * PIECE, HEAD_DIM)
    keys_count = LEVELS * ROWS
    part_pair = (2, ROWS, HEAD_DIM)
    selectors = (2, LEVELS, SEGS * PIECE, SEGS * PIECE)
    scratch = [
        pltpu.SMEM((2, LEVELS, SEGS), jnp.int32),
        pltpu.VMEM(selectors, BF16),
        pltpu.VMEM(selectors, BF16),
        pltpu.VMEM((KV_HEADS, LEVELS) + tile, BF16),
        pltpu.VMEM((KV_HEADS, SEGS, LEVELS - 1, PIECE, HEAD_DIM), BF16),
        pltpu.VMEM((KV_HEADS, LEVELS) + part_pair, BF16),
        pltpu.VMEM((KV_HEADS, LEVELS) + part_pair, BF16),
        pltpu.VMEM((KV_HEADS, LEVELS) + tile, BF16),
        pltpu.VMEM((KV_HEADS,) + part_pair, F32),
        pltpu.VMEM((KV_HEADS,) + part_pair, BF16),
        pltpu.VMEM((KV_HEADS,) + part_pair, BF16),
        pltpu.VMEM((KV_HEADS, 2, STACK, HEAD_DIM), BF16),
        pltpu.VMEM((KV_HEADS, ROWS, STACK), BF16),
        pltpu.VMEM((HEAD_DIM, STACK), F32),
        pltpu.VMEM((3, 8, STACK), F32),
        pltpu.VMEM((keys_count, STACK), F32),
        pltpu.VMEM((keys_count, STACK), F32),
        pltpu.VMEM((PAIR, STACK), BF16),
        pltpu.VMEM((PAIR, STACK), BF16),
        pltpu.VMEM((KV_HEADS, 3) + flat, F32),
        pltpu.VMEM(flat, F32),
        pltpu.VMEM((KV_HEADS, 4) + flat, BF16),
        pltpu.VMEM((KV_HEADS, 4) + flat, BF16),
        pltpu.VMEM((KV_HEADS, 3) + flat, BF16),
        pltpu.VMEM((KV_HEADS, 3) + flat, BF16),
        pltpu.VMEM((KV_HEADS,) + tile, BF16),
        pltpu.VMEM((KV_HEADS,) + part_pair, BF16),
        dma((KV_HEADS,)), dma((KV_HEADS,)),
        dma((KV_HEADS, 7)), dma((KV_HEADS, LEVELS)),
        dma((KV_HEADS,)), dma((KV_HEADS,)),
        dma((KV_HEADS,)), dma((KV_HEADS,)),
        dma((KV_HEADS,)), dma((KV_HEADS,)),
        dma((KV_HEADS,)), dma((KV_HEADS,)),
        dma((KV_HEADS,)), dma((KV_HEADS,)),
        dma((KV_HEADS,)), dma((KV_HEADS,)),
        dma((KV_HEADS, 4)), dma((KV_HEADS, 4)),
        dma((KV_HEADS, 3)), dma((KV_HEADS, 3)),
        dma((KV_HEADS,)), dma((KV_HEADS,)),
    ]
    return pl.pallas_call(
        kernel,
        out_shape=(
            jax.ShapeDtypeStruct(queries.shape, BF16),
            jax.ShapeDtypeStruct(keys_values.shape, BF16),
        ),
        in_specs=[smem, anywhere, anywhere, anywhere],
        out_specs=(anywhere, vmem),
        scratch_shapes=scratch,
        compiler_params=pltpu.CompilerParams(
            collective_id=0, has_side_effects=True, vmem_limit_bytes=56 * 1024 * 1024
        ),
        cost_estimate=pl.CostEstimate(
            flops=5 * 2 * HEADS * LEVELS * ROWS * ROWS * HEAD_DIM,
            bytes_accessed=8 * 1024 * 1024,
            transcendentals=HEADS * LEVELS * ROWS * ROWS,
        ),
    )(parents.transpose(0, 2, 1), queries, keys_values, grad_out)


def solution(mesh):
    in_specs = (
        P("depth", "seg", None, None),
        P("depth", "seg", None, None, None),
        P("depth", "seg", None, None),
        P(),
    )
    out_specs = (P("depth", "seg", None, None), P("depth", "seg", None, None, None))
    return jax.shard_map(shards, mesh=mesh, in_specs=in_specs, out_specs=out_specs, check_vma=False)
```

```python
import functools

import jax
import jax.numpy as jnp
from jax import lax
from jax.experimental import pallas as pl
from jax.experimental.pallas import tpu as pltpu
from jax.sharding import PartitionSpec as P

HEADS = 20
KV_HEADS = 4
HEAD_DIM = 128
GROUP = HEADS // KV_HEADS
ROWS = 128
LEVELS = 8
SEGS = 16
PIECE = 16
PIECES_PER_PART = ROWS // PIECE
STACK = GROUP * ROWS
PAIR = 2 * ROWS
LAG = 2

NEG_FILL = -1e30
SCALE = HEAD_DIM ** -0.5
EXP2_SCALE = SCALE * 1.4426950408889634
MESH = pl.DeviceIdType.MESH
BF16 = jnp.bfloat16
F32 = jnp.float32


def half(value):
    return lax.div(value, 2)


def odd(value):
    return lax.rem(value, 2)


def name_of(head):
    return 2 * odd(head) + half(head)


def wrapped(index):
    return jnp.where(index >= SEGS, index - SEGS, index)


def lanes(index, count=1):
    width = count * HEAD_DIM
    return pl.ds(pl.multiple_of(index * width, width), width)


def rows_of(index, count):
    return pl.ds(pl.multiple_of(index * count, count), count)


def piece_of(index):
    part = jnp.where(index >= PIECES_PER_PART, 1, 0)
    return part, rows_of(index - part * PIECES_PER_PART, PIECE)


def fold(tile):
    return tile.reshape(tile.shape[0] // 8, 8, tile.shape[1])


def kernel(
    parents, queries, keys_values, grad_out, grad_queries, grad_kv,
    anc, pick, spread, pieces, chosen, blocks, terms, term_pieces, own, own_out, own_in,
    inputs, stacks, staged, query_sum, stats, logits, grad_probs, probs, grad_logits,
    kept, total_sum, cross_out, cross_in, climb_out, climb_in, final_out, final_in,
    p1_send, p1_recv, up_send, up_recv, q_send, q_recv, k_send, k_recv, p3_send, p3_recv,
    b1_send, b1_recv, o_send, o_recv, d_send, d_recv, x_send, x_recv, c_send, c_recv,
    f_send, f_recv,
):
    level = lax.axis_index("depth")
    me = lax.axis_index("seg")
    y = half(level)
    core = odd(level)
    sibling = 2 * y + 1 - core
    outer = (y == 0) | (y == 3)
    partner = jnp.where(outer, 2 * (3 - y) + core, level)

    def host_of(head):
        return jnp.where(odd(head) == 1, partner, level)

    def device_of(head, plane):
        swapped = (odd(head) == 1) & ((plane == 0) | (plane == 3))
        return 2 * jnp.where(swapped, 3 - plane, plane) + core

    def remote(src, dst, send_sem, recv_sem, device):
        return pltpu.make_async_remote_copy(
            src_ref=src, dst_ref=dst, send_sem=send_sem, recv_sem=recv_sem,
            device_id=device, device_id_type=MESH,
        )

    def wait_bytes(ref, sem):
        pltpu.make_async_copy(ref, ref, sem).wait()

    def per_plane(which, action):
        for plane in range(LEVELS // 2):
            pl.when((which > 0) & (half(which) == plane))(
                functools.partial(action, 2 * plane + 1)
            )

    def move(head, src, dst, send_sem, recv_sem):
        host = host_of(head)

        @pl.when(host != level)
        def _():
            remote(src, dst, send_sem, recv_sem, (host, me)).start()

        @pl.when(host == level)
        def _():
            pltpu.make_async_copy(src, dst, recv_sem).start()

    barrier = pltpu.get_barrier_semaphore()

    def greet(device):
        pl.semaphore_signal(barrier, inc=1, device_id=device, device_id_type=MESH)

    @pl.loop(1, SEGS)
    def _(step):
        greet((level, wrapped(me + step)))

    greet((sibling, me))
    for step in range(1, 4):
        greet((lax.rem(level + 2 * step, LEVELS), me))

    @pl.when(outer)
    def _():
        @pl.loop(0, SEGS)
        def _(step):
            greet((partner, wrapped(me + step)))

    pl.semaphore_wait(barrier, SEGS - 1 + 4 + jnp.where(outer, SEGS, 0))

    @pl.loop(0, 2)
    def _(group):
        host = host_of(group)

        def source(peer):
            part, span = piece_of(peer)
            return keys_values.at[0, 0, part, span, lanes(group, 2)]

        @pl.loop(1, SEGS)
        def _(step):
            peer = wrapped(me + step)
            remote(
                source(peer), pieces.at[group, level, me],
                p1_send.at[group], p1_recv.at[group], (host, peer),
            ).start()

        @pl.when(host != level)
        def _():
            remote(
                source(me), pieces.at[group, level, me],
                p1_send.at[group], p1_recv.at[group], (host, me),
            ).start()

        @pl.when(host == level)
        def _():
            pltpu.make_async_copy(
                source(me), pieces.at[group, level, me], p1_recv.at[group]
            ).start()

    def move_inputs(head):
        name = name_of(head)
        move(
            head, keys_values.at[0, 0, :, :, lanes(name)], blocks.at[head, 0],
            k_send.at[head], k_recv.at[head],
        )
        for index, array in enumerate((queries, grad_out)):
            move(
                head, array.at[0, 0, :, lanes(name, GROUP)], inputs.at[head, index],
                q_send.at[head], q_recv.at[head],
            )

    def unit(head, which):
        return pieces.at[odd(head), which, :, :, lanes(half(head))]

    def lift(head, which, slot, device):
        return remote(
            unit(head, which), unit(head, which),
            up_send.at[head, slot], up_recv.at[head, which], (device, me),
        )

    def own_lifts(head, action):
        here = host_of(head)
        plane = half(here)
        for step in range(1, 4):
            @pl.when(plane + step <= 3)
            def _():
                action(lift(head, here, step - 1, device_of(head, plane + step)))

        @pl.when(core == 0)
        def _():
            action(lift(head, here, 3, sibling))

    def passed_on(head, action):
        @pl.loop(0, half(host_of(head)))
        def _(plane):
            action(2 * plane + core, lift(head, 2 * plane + core, 4 + plane, sibling))

    for group in range(2):
        here = host_of(group)
        wait_bytes(pieces.at[group, here], p1_recv.at[group])
        own_lifts(group, lambda copy: copy.start())
        move_inputs(group)
        own_lifts(group + 2, lambda copy: copy.start())
        move_inputs(group + 2)

    @pl.loop(0, 2)
    def _(parity):
        target_level = host_of(parity)

        @pl.loop(0, SEGS)
        def _(column):
            current = column
            for offset in range(1, LEVELS):
                current = parents[jnp.maximum(target_level - offset, 0), 0, current]
                anc[parity, offset, column] = current

        @pl.loop(1, 2 * half(target_level) + 2)
        def _(offset):
            lane = lax.broadcasted_iota(jnp.int32, (PIECE, SEGS * PIECE), 1)
            row = lax.broadcasted_iota(jnp.int32, (PIECE, SEGS * PIECE), 0)
            target = lane % PIECE
            lane_column = lane // PIECE
            for column in range(SEGS):
                found = anc[parity, offset, column] * PIECE
                pick[parity, offset, rows_of(column, PIECE), :] = jnp.where(
                    lane == found + row, 1.0, 0.0
                ).astype(BF16)
                target = target + jnp.where(lane_column == column, found, 0)
            for column in range(SEGS):
                spread[parity, offset, rows_of(column, PIECE), :] = jnp.where(
                    target == row + column * PIECE, 1.0, 0.0
                ).astype(BF16)

    @pl.loop(0, KV_HEADS)
    def _(head):
        @pl.when(host_of(head) == 0)
        def _():
            blocks[head, 1] = jnp.zeros((2, ROWS, HEAD_DIM), BF16)

    def pass_on(head):
        def forward(which, copy):
            wait_bytes(unit(head, which), up_recv.at[head, which])
            copy.start()

        passed_on(head, forward)

    def select(head):
        here = host_of(head)
        parity = odd(head)

        @pl.loop(0, 4)
        def _(plane):
            other = 2 * plane + 1 - core

            @pl.when(other < here)
            def _():
                wait_bytes(unit(head, other), up_recv.at[head, other])

        def send(count):
            for offset in range(1, count + 1):
                found = jnp.dot(
                    pick[parity, offset],
                    pieces[
                        parity, jnp.maximum(here - offset, 0), :, :, lanes(half(head))
                    ].reshape(SEGS * PIECE, HEAD_DIM),
                    preferred_element_type=F32,
                )
                chosen[head, :, offset - 1] = found.astype(BF16).reshape(SEGS, PIECE, HEAD_DIM)
            part, span = piece_of(me)

            @pl.loop(1, SEGS)
            def _(step):
                peer = wrapped(me + step)
                remote(
                    chosen.at[head, peer, pl.ds(0, count)],
                    blocks.at[head, pl.ds(1, count), part, span, :],
                    p3_send.at[head], p3_recv.at[head], (level, peer),
                ).start()

            pltpu.make_async_copy(
                chosen.at[head, me, pl.ds(0, count)],
                blocks.at[head, pl.ds(1, count), part, span, :], p3_recv.at[head],
            ).start()

        per_plane(here, send)

    def attend(head):
        here = host_of(head)
        pairs = half(here) + 1
        contract_last = (((1,), (1,)), ((), ()))
        span_all = [pl.ds(group * ROWS, ROWS) for group in range(GROUP)]

        def block_pair(pair, part):
            return blocks[head, pl.ds(2 * pair, 2), part].reshape(PAIR, HEAD_DIM)

        stats[0] = jnp.full((8, STACK), NEG_FILL, F32)
        for index in range(2):
            for group, span in enumerate(span_all):
                stacks[index, span, :] = inputs[head, index, :, span]

        @pl.loop(0, pairs)
        def _(pair):
            span_rows = rows_of(pair, PAIR)
            logits[span_rows, :] = lax.dot_general(
                block_pair(pair, 0), stacks[0], contract_last, preferred_element_type=F32
            )
            grad_probs[span_rows, :] = lax.dot_general(
                block_pair(pair, 1), stacks[1], contract_last, preferred_element_type=F32
            )

            @pl.when(pair == 0)
            def _():
                u_row = lax.broadcasted_iota(jnp.int32, (ROWS, ROWS), 0)
                t_row = lax.broadcasted_iota(jnp.int32, (ROWS, ROWS), 1)
                for span in span_all:
                    logits[0:ROWS, span] = jnp.where(
                        u_row <= t_row, logits[0:ROWS, span], NEG_FILL
                    )

            @pl.when((pair == pairs - 1) & (odd(here) == 0))
            def _():
                logits[rows_of(here + 1, ROWS), :] = jnp.full((ROWS, STACK), NEG_FILL, F32)

            for span in span_all:
                stats[0, :, span] = jnp.maximum(
                    stats[0, :, span], fold(logits[span_rows, span]).max(0)
                )

        stats[1] = jnp.zeros((8, STACK), F32)
        stats[2] = jnp.zeros((8, STACK), F32)
        stats[0] = jnp.broadcast_to(stats[0].max(0, keepdims=True), (8, STACK))

        @pl.loop(0, pairs)
        def _(pair):
            span_rows = rows_of(pair, PAIR)
            for span in span_all:
                top = stats[0, 0:1, span]
                tile = jnp.exp2((logits[span_rows, span] - top) * EXP2_SCALE)
                logits[span_rows, span] = tile
                stats[1, :, span] += fold(tile).sum(0)
                stats[2, :, span] += fold(tile * grad_probs[span_rows, span]).sum(0)

        inverse = 1.0 / stats[1].sum(0, keepdims=True)
        delta = stats[2].sum(0, keepdims=True) * inverse
        stats[1] = jnp.broadcast_to(inverse, (8, STACK))
        stats[2] = jnp.broadcast_to(delta, (8, STACK))
        query_sum[...] = jnp.zeros((HEAD_DIM, STACK), F32)

        @pl.loop(0, pairs)
        def _(pair):
            span_rows = rows_of(pair, PAIR)
            for span in span_all:
                exact = logits[span_rows, span] * stats[1, 0:1, span]
                probs[:, span] = exact.astype(BF16)
                grad_logits[:, span] = (
                    exact * (grad_probs[span_rows, span] - stats[2, 0:1, span])
                ).astype(BF16)
            value_term = jnp.dot(probs[...], stacks[1], preferred_element_type=F32)
            key_term = SCALE * jnp.dot(
                grad_logits[...], stacks[0], preferred_element_type=F32
            )
            for part, term in enumerate((key_term, value_term)):
                terms[head, pl.ds(2 * pair, 2), part] = term.astype(BF16).reshape(
                    2, ROWS, HEAD_DIM
                )

                @pl.when(pair == 0)
                def _():
                    own[head, part] = term[0:ROWS]

            query_sum[...] += lax.dot_general(
                block_pair(pair, 0), grad_logits[...], (((0,), (0,)), ((), ())),
                preferred_element_type=F32,
            )

        for group, span in enumerate(span_all):
            staged[head, :, span] = (SCALE * query_sum[:, span].T).astype(BF16)

    def query_target(head):
        return grad_queries.at[0, 0, :, lanes(name_of(head), GROUP)]

    def send_results(head):
        host = host_of(head)
        here = host

        def send(count):
            @pl.loop(1, SEGS)
            def _(step):
                peer = wrapped(me + step)
                part, span = piece_of(peer)
                remote(
                    terms.at[head, pl.ds(1, count), part, span, :],
                    term_pieces.at[head, pl.ds(1, count), me],
                    b1_send.at[head], b1_recv.at[head], (level, peer),
                ).start()

            part, span = piece_of(me)
            pltpu.make_async_copy(
                terms.at[head, pl.ds(1, count), part, span, :],
                term_pieces.at[head, pl.ds(1, count), me], b1_recv.at[head],
            ).start()

        per_plane(here, send)
        move(
            head, staged.at[head], query_target(head), d_send.at[head], d_recv.at[head]
        )

        @pl.when(host != level)
        def _():
            own_out[head] = own[head].astype(BF16)
            remote(
                own_out.at[head], own_in.at[head], o_send.at[head], o_recv.at[head], (host, me)
            ).start()

    def summed(head, offset):
        return jnp.dot(
            spread[odd(head), offset],
            term_pieces[head, offset].reshape(SEGS * PIECE, HEAD_DIM),
            preferred_element_type=F32,
        )

    def cross_copy(head, plane):
        return remote(
            cross_out.at[head, plane], cross_in.at[head, plane],
            x_send.at[head, plane], x_recv.at[head, plane], (sibling, me),
        )

    def sum_stage(head):
        here = host_of(head)

        def sums(count):
            wait_bytes(term_pieces.at[head, pl.ds(1, count)], b1_recv.at[head])
            for plane in range((count + 1) // 2):
                offset = jnp.maximum(here - (2 * plane + 1 - core), 1)
                cross_out[head, plane] = summed(head, offset).astype(BF16)
            for plane in range((count - 1) // 2):
                offset = jnp.maximum(here - (2 * plane + core), 1)
                kept[head, plane] = summed(head, offset)

        per_plane(here, sums)

        @pl.loop(0, 4)
        def _(plane):
            @pl.when(here - (2 * plane + 1 - core) >= 1)
            def _():
                cross_copy(head, plane).start()

    def climb_copy(head, plane):
        slot = half(host_of(head)) - 1
        return remote(
            climb_out.at[head, plane], climb_in.at[head, slot],
            c_send.at[head, plane], c_recv.at[head, slot], (device_of(head, plane), me),
        )

    def climb(head):
        plane_here = half(host_of(head))

        @pl.loop(0, plane_here - core + 1)
        def _(plane):
            wait_bytes(cross_in.at[head, plane], x_recv.at[head, plane])

        @pl.loop(0, plane_here)
        def _(plane):
            climb_out[head, plane] = (
                kept[head, plane] + cross_in[head, plane].astype(F32)
            ).astype(BF16)
            climb_copy(head, plane).start()

    def final_send(head):
        host = host_of(head)

        @pl.when(host < LEVELS - 1)
        def _():
            total_sum[...] = jnp.zeros((SEGS * PIECE, HEAD_DIM), F32)

            @pl.loop(half(host), 3)
            def _(slot):
                wait_bytes(climb_in.at[head, slot], c_recv.at[head, slot])
                total_sum[...] += climb_in[head, slot].astype(F32)

            @pl.when(core == 0)
            def _():
                total_sum[...] += cross_in[head, half(host)].astype(F32)

            final_out[head] = total_sum[...].astype(BF16).reshape(SEGS, PIECE, HEAD_DIM)
            part, span = piece_of(me)

            @pl.loop(1, SEGS)
            def _(step):
                peer = wrapped(me + step)
                remote(
                    final_out.at[head, peer], final_in.at[head, part, span, :],
                    f_send.at[head], f_recv.at[head], (host, peer),
                ).start()

            move(
                head, final_out.at[head, me], final_in.at[head, part, span, :],
                f_send.at[head], f_recv.at[head],
            )

    def final_store(head):
        away = host_of(head) != level

        @pl.when(away)
        def _():
            wait_bytes(own_in.at[head], o_recv.at[head])
            own[head] = own_in[head].astype(F32)

        @pl.when(level < LEVELS - 1)
        def _():
            wait_bytes(final_in.at[head], f_recv.at[head])
            own[head] = own[head] + final_in[head].astype(F32)

        grad_kv[0, 0, :, :, lanes(name_of(head))] = own[head].astype(BF16)

    stages = (sum_stage, climb, final_send, final_store)

    @pl.loop(0, KV_HEADS + LAG + len(stages))
    def _(tick):
        @pl.when(tick < KV_HEADS)
        def _():
            pass_on(tick)

        @pl.when((tick >= 1) & (tick < KV_HEADS + 1))
        def _():
            select(tick - 1)

        @pl.when((tick >= LAG) & (tick < KV_HEADS + LAG))
        def _():
            head = tick - LAG
            per_plane(
                host_of(head),
                lambda count: wait_bytes(blocks.at[head, pl.ds(1, count)], p3_recv.at[head]),
            )
            wait_bytes(blocks.at[head, 0], k_recv.at[head])
            wait_bytes(inputs.at[head], q_recv.at[head])
            attend(head)
            send_results(head)

        for lag, stage in enumerate(stages, LAG + 1):
            @pl.when((tick >= lag) & (tick < KV_HEADS + lag))
            def _():
                stage(tick - lag)

    @pl.loop(0, 2)
    def _(group):
        wait_bytes(pieces.at[group, 0, pl.ds(1, SEGS - 1)], p1_send.at[group])

        @pl.when(host_of(group) != level)
        def _():
            wait_bytes(pieces.at[group, 0, 0], p1_send.at[group])

    @pl.loop(0, KV_HEADS)
    def _(head):
        host = host_of(head)
        away = host != level
        wait_bytes(query_target(head), d_recv.at[head])
        own_lifts(head, lambda copy: copy.wait_send())
        passed_on(head, lambda which, copy: copy.wait_send())

        @pl.when(away)
        def _():
            wait_bytes(blocks.at[head, 0], k_send.at[head])
            wait_bytes(inputs.at[head], q_send.at[head])
            wait_bytes(staged.at[head], d_send.at[head])
            wait_bytes(own_out.at[head], o_send.at[head])

        def sent(count):
            wait_bytes(chosen.at[head, pl.ds(1, SEGS - 1), pl.ds(0, count)], p3_send.at[head])
            wait_bytes(
                term_pieces.at[head, pl.ds(1, count), pl.ds(1, SEGS - 1)], b1_send.at[head]
            )

        per_plane(host, sent)

        @pl.loop(0, 4)
        def _(plane):
            @pl.when(host - (2 * plane + 1 - core) >= 1)
            def _():
                cross_copy(head, plane).wait_send()

        @pl.loop(0, half(host))
        def _(plane):
            climb_copy(head, plane).wait_send()

        @pl.when(host < LEVELS - 1)
        def _():
            wait_bytes(final_out.at[head, pl.ds(1, SEGS - 1)], f_send.at[head])

            @pl.when(away)
            def _():
                wait_bytes(final_out.at[head, 0], f_send.at[head])


def shards(queries, keys_values, grad_out, parents):
    vmem = pl.BlockSpec(memory_space=pltpu.VMEM)
    smem = pl.BlockSpec(memory_space=pltpu.SMEM)
    anywhere = pl.BlockSpec(memory_space=pl.ANY)
    dma = pltpu.SemaphoreType.DMA
    tile = (SEGS, PIECE, HEAD_DIM)
    flat = (SEGS * PIECE, HEAD_DIM)
    keys_count = LEVELS * ROWS
    part_pair = (2, ROWS, HEAD_DIM)
    selectors = (2, LEVELS, SEGS * PIECE, SEGS * PIECE)
    scratch = [
        pltpu.SMEM((2, LEVELS, SEGS), jnp.int32),
        pltpu.VMEM(selectors, BF16),
        pltpu.VMEM(selectors, BF16),
        pltpu.VMEM((2, LEVELS, SEGS, PIECE, 2 * HEAD_DIM), BF16),
        pltpu.VMEM((KV_HEADS, SEGS, LEVELS - 1, PIECE, HEAD_DIM), BF16),
        pltpu.VMEM((KV_HEADS, LEVELS) + part_pair, BF16),
        pltpu.VMEM((KV_HEADS, LEVELS) + part_pair, BF16),
        pltpu.VMEM((KV_HEADS, LEVELS) + tile, BF16),
        pltpu.VMEM((KV_HEADS,) + part_pair, F32),
        pltpu.VMEM((KV_HEADS,) + part_pair, BF16),
        pltpu.VMEM((KV_HEADS,) + part_pair, BF16),
        pltpu.VMEM((KV_HEADS, 2, ROWS, STACK), BF16),
        pltpu.VMEM((2, STACK, HEAD_DIM), BF16),
        pltpu.VMEM((KV_HEADS, ROWS, STACK), BF16),
        pltpu.VMEM((HEAD_DIM, STACK), F32),
        pltpu.VMEM((3, 8, STACK), F32),
        pltpu.VMEM((keys_count, STACK), F32),
        pltpu.VMEM((keys_count, STACK), F32),
        pltpu.VMEM((PAIR, STACK), BF16),
        pltpu.VMEM((PAIR, STACK), BF16),
        pltpu.VMEM((KV_HEADS, 3) + flat, F32),
        pltpu.VMEM(flat, F32),
        pltpu.VMEM((KV_HEADS, 4) + flat, BF16),
        pltpu.VMEM((KV_HEADS, 4) + flat, BF16),
        pltpu.VMEM((KV_HEADS, 3) + flat, BF16),
        pltpu.VMEM((KV_HEADS, 3) + flat, BF16),
        pltpu.VMEM((KV_HEADS,) + tile, BF16),
        pltpu.VMEM((KV_HEADS,) + part_pair, BF16),
        dma((2,)), dma((2,)),
        dma((KV_HEADS, 7)), dma((KV_HEADS, LEVELS)),
        dma((KV_HEADS,)), dma((KV_HEADS,)),
        dma((KV_HEADS,)), dma((KV_HEADS,)),
        dma((KV_HEADS,)), dma((KV_HEADS,)),
        dma((KV_HEADS,)), dma((KV_HEADS,)),
        dma((KV_HEADS,)), dma((KV_HEADS,)),
        dma((KV_HEADS,)), dma((KV_HEADS,)),
        dma((KV_HEADS, 4)), dma((KV_HEADS, 4)),
        dma((KV_HEADS, 3)), dma((KV_HEADS, 3)),
        dma((KV_HEADS,)), dma((KV_HEADS,)),
    ]
    return pl.pallas_call(
        kernel,
        out_shape=(
            jax.ShapeDtypeStruct(queries.shape, BF16),
            jax.ShapeDtypeStruct(keys_values.shape, BF16),
        ),
        in_specs=[smem, anywhere, anywhere, anywhere],
        out_specs=(vmem, vmem),
        scratch_shapes=scratch,
        compiler_params=pltpu.CompilerParams(
            collective_id=0, has_side_effects=True, vmem_limit_bytes=56 * 1024 * 1024
        ),
        cost_estimate=pl.CostEstimate(
            flops=5 * 2 * HEADS * LEVELS * ROWS * ROWS * HEAD_DIM,
            bytes_accessed=8 * 1024 * 1024,
            transcendentals=HEADS * LEVELS * ROWS * ROWS,
        ),
    )(parents.transpose(0, 2, 1), queries, keys_values, grad_out)


def solution(mesh):
    in_specs = (
        P("depth", "seg", None, None),
        P("depth", "seg", None, None, None),
        P("depth", "seg", None, None),
        P(),
    )
    out_specs = (P("depth", "seg", None, None), P("depth", "seg", None, None, None))
    return jax.shard_map(shards, mesh=mesh, in_specs=in_specs, out_specs=out_specs, check_vma=False)
```

```python
import functools

import jax
import jax.numpy as jnp
from jax import lax
from jax.experimental import pallas as pl
from jax.experimental.pallas import tpu as pltpu
from jax.sharding import PartitionSpec as P

HEADS = 20
KV_HEADS = 4
HEAD_DIM = 128
GROUP = HEADS // KV_HEADS
ROWS = 128
LEVELS = 8
SEGS = 16
PIECE = 16
PIECES_PER_PART = ROWS // PIECE
STACK = GROUP * ROWS
PAIR = 2 * ROWS
LAG = 2
SWAPPED = 1

NEG_FILL = -1e30
SCALE = HEAD_DIM ** -0.5
EXP2_SCALE = SCALE * 1.4426950408889634
MESH = pl.DeviceIdType.MESH
BF16 = jnp.bfloat16
F32 = jnp.float32


def half(value):
    return lax.div(value, 2)


def odd(value):
    return lax.rem(value, 2)


def is_swapped(head):
    return head == SWAPPED


def name_of(head):
    return jnp.where(is_swapped(head), KV_HEADS - 1, head - jnp.where(head > SWAPPED, 1, 0))


def group_of(head):
    return jnp.where(is_swapped(head), 1, 0)


def wrapped(index):
    return jnp.where(index >= SEGS, index - SEGS, index)


def lanes(index, count=1):
    width = count * HEAD_DIM
    return pl.ds(pl.multiple_of(index * width, width), width)


def rows_of(index, count):
    return pl.ds(pl.multiple_of(index * count, count), count)


def piece_of(index):
    part = jnp.where(index >= PIECES_PER_PART, 1, 0)
    return part, rows_of(index - part * PIECES_PER_PART, PIECE)


def fold(tile):
    return tile.reshape(tile.shape[0] // 8, 8, tile.shape[1])


def kernel(
    parents, queries, keys_values, grad_out, grad_queries, grad_kv,
    anc, pick, spread, pieces, chosen, blocks, terms, term_pieces, own, own_out, own_in,
    inputs, stacks, turned, staged, query_sum, stats, logits, grad_probs, probs, grad_logits,
    kept, total_sum, cross_out, cross_in, climb_out, climb_in, final_out, final_in,
    p1_send, p1_recv, up_send, up_recv, q_send, q_recv, k_send, k_recv, p3_send, p3_recv,
    b1_send, b1_recv, o_send, o_recv, d_send, d_recv, x_send, x_recv, c_send, c_recv,
    f_send, f_recv,
):
    level = lax.axis_index("depth")
    me = lax.axis_index("seg")
    y = half(level)
    core = odd(level)
    sibling = 2 * y + 1 - core
    outer = (y == 0) | (y == 3)
    partner = jnp.where(outer, 2 * (3 - y) + core, level)

    def host_of(head):
        return jnp.where(is_swapped(head), partner, level)

    def device_of(head, plane):
        swapped = is_swapped(head) & ((plane == 0) | (plane == 3))
        return 2 * jnp.where(swapped, 3 - plane, plane) + core

    def remote(src, dst, send_sem, recv_sem, device):
        return pltpu.make_async_remote_copy(
            src_ref=src, dst_ref=dst, send_sem=send_sem, recv_sem=recv_sem,
            device_id=device, device_id_type=MESH,
        )

    def wait_bytes(ref, sem):
        pltpu.make_async_copy(ref, ref, sem).wait()

    def per_plane(which, action):
        for plane in range(LEVELS // 2):
            pl.when((which > 0) & (half(which) == plane))(
                functools.partial(action, 2 * plane + 1)
            )

    def move(head, src, dst, send_sem, recv_sem):
        host = host_of(head)

        @pl.when(host != level)
        def _():
            remote(src, dst, send_sem, recv_sem, (host, me)).start()

        @pl.when(host == level)
        def _():
            pltpu.make_async_copy(src, dst, recv_sem).start()

    kept_width = (KV_HEADS - 1) * HEAD_DIM
    spread_groups = (
        (level, pl.ds(0, kept_width)),
        (partner, pl.ds(kept_width, HEAD_DIM)),
    )

    barrier = pltpu.get_barrier_semaphore()

    def greet(device):
        pl.semaphore_signal(barrier, inc=1, device_id=device, device_id_type=MESH)

    @pl.loop(1, SEGS)
    def _(step):
        greet((level, wrapped(me + step)))

    greet((sibling, me))
    for step in range(1, 4):
        greet((lax.rem(level + 2 * step, LEVELS), me))

    @pl.when(outer)
    def _():
        @pl.loop(0, SEGS)
        def _(step):
            greet((partner, wrapped(me + step)))

    pl.semaphore_wait(barrier, SEGS - 1 + 4 + jnp.where(outer, SEGS, 0))

    for group, (host, span_lanes) in enumerate(spread_groups):
        def source(peer):
            part, span = piece_of(peer)
            return keys_values.at[0, 0, part, span, span_lanes]

        def landing():
            return pieces.at[level, me, :, span_lanes]

        @pl.loop(1, SEGS)
        def _(step):
            peer = wrapped(me + step)
            remote(
                source(peer), landing(), p1_send.at[group], p1_recv.at[group], (host, peer)
            ).start()

        if group == 1:
            @pl.when(host != level)
            def _():
                remote(
                    source(me), landing(), p1_send.at[group], p1_recv.at[group], (host, me)
                ).start()

        @pl.when(host == level)
        def _():
            pltpu.make_async_copy(source(me), landing(), p1_recv.at[group]).start()

    def move_inputs(head):
        name = name_of(head)
        move(
            head, keys_values.at[0, 0, :, :, lanes(name)], blocks.at[head, 0],
            k_send.at[head], k_recv.at[head],
        )
        for index, array in enumerate((queries, grad_out)):
            move(
                head, array.at[0, 0, :, lanes(name, GROUP)], inputs.at[head, index],
                q_send.at[head], q_recv.at[head],
            )

    def unit(head, which):
        return pieces.at[which, :, :, lanes(name_of(head))]

    def lift(head, which, slot, device):
        return remote(
            unit(head, which), unit(head, which),
            up_send.at[head, slot], up_recv.at[head, which], (device, me),
        )

    def own_lifts(head, action):
        here = host_of(head)
        plane = half(here)
        for step in range(1, 4):
            @pl.when(plane + step <= 3)
            def _():
                action(lift(head, here, step - 1, device_of(head, plane + step)))

        @pl.when(core == 0)
        def _():
            action(lift(head, here, 3, sibling))

    def passed_on(head, action):
        @pl.loop(0, half(host_of(head)))
        def _(plane):
            action(2 * plane + core, lift(head, 2 * plane + core, 4 + plane, sibling))

    for group, (host, span_lanes) in enumerate(spread_groups):
        wait_bytes(pieces.at[host, :, :, span_lanes], p1_recv.at[group])

    @pl.loop(0, KV_HEADS)
    def _(head):
        own_lifts(head, lambda copy: copy.start())

    @pl.loop(0, KV_HEADS)
    def _(head):
        move_inputs(head)

    @pl.loop(0, 2)
    def _(parity):
        target_level = jnp.where(parity == 1, partner, level)

        @pl.loop(0, SEGS)
        def _(column):
            current = column
            for offset in range(1, LEVELS):
                current = parents[jnp.maximum(target_level - offset, 0), 0, current]
                anc[parity, offset, column] = current

        @pl.loop(1, 2 * half(target_level) + 2)
        def _(offset):
            lane = lax.broadcasted_iota(jnp.int32, (PIECE, SEGS * PIECE), 1)
            row = lax.broadcasted_iota(jnp.int32, (PIECE, SEGS * PIECE), 0)
            target = lane & (PIECE - 1)
            lane_column = lane >> 4
            for column in range(SEGS):
                found = anc[parity, offset, column] * PIECE
                pick[parity, offset, rows_of(column, PIECE), :] = jnp.where(
                    lane == found + row, 1.0, 0.0
                ).astype(BF16)
                target = target + jnp.where(lane_column == column, found, 0)
            for column in range(SEGS):
                spread[parity, offset, rows_of(column, PIECE), :] = jnp.where(
                    target == row + column * PIECE, 1.0, 0.0
                ).astype(BF16)

    @pl.loop(0, KV_HEADS)
    def _(head):
        @pl.when(host_of(head) == 0)
        def _():
            blocks[head, 1] = jnp.zeros((2, ROWS, HEAD_DIM), BF16)

    def pass_on(head):
        def forward(which, copy):
            wait_bytes(unit(head, which), up_recv.at[head, which])
            copy.start()

        passed_on(head, forward)

    def select(head):
        here = host_of(head)
        parity = group_of(head)

        @pl.loop(0, 4)
        def _(plane):
            other = 2 * plane + 1 - core

            @pl.when(other < here)
            def _():
                wait_bytes(unit(head, other), up_recv.at[head, other])

        def send(count):
            for offset in range(1, count + 1):
                found = jnp.dot(
                    pick[parity, offset],
                    pieces[
                        jnp.maximum(here - offset, 0), :, :, lanes(name_of(head))
                    ].reshape(SEGS * PIECE, HEAD_DIM),
                    preferred_element_type=F32,
                )
                chosen[head, :, offset - 1] = found.astype(BF16).reshape(SEGS, PIECE, HEAD_DIM)
            part, span = piece_of(me)

            @pl.loop(1, SEGS)
            def _(step):
                peer = wrapped(me + step)
                remote(
                    chosen.at[head, peer, pl.ds(0, count)],
                    blocks.at[head, pl.ds(1, count), part, span, :],
                    p3_send.at[head], p3_recv.at[head], (level, peer),
                ).start()

            pltpu.make_async_copy(
                chosen.at[head, me, pl.ds(0, count)],
                blocks.at[head, pl.ds(1, count), part, span, :], p3_recv.at[head],
            ).start()

        per_plane(here, send)

    def attend(head):
        here = host_of(head)
        pairs = half(here) + 1
        span_all = [pl.ds(group * ROWS, ROWS) for group in range(GROUP)]

        def block_pair(pair, part):
            return blocks[head, pl.ds(2 * pair, 2), part].reshape(PAIR, HEAD_DIM)

        stats[0] = jnp.full((8, STACK), NEG_FILL, F32)
        for index in range(2):
            for group, span in enumerate(span_all):
                tile = inputs[head, index, :, span]
                stacks[index, span, :] = tile
                turned[index, :, span] = tile.T

        @pl.loop(0, pairs)
        def _(pair):
            span_rows = rows_of(pair, PAIR)
            logits[span_rows, :] = jnp.dot(
                block_pair(pair, 0), turned[0], preferred_element_type=F32
            )
            grad_probs[span_rows, :] = jnp.dot(
                block_pair(pair, 1), turned[1], preferred_element_type=F32
            )

            @pl.when(pair == 0)
            def _():
                u_row = lax.broadcasted_iota(jnp.int32, (ROWS, ROWS), 0)
                t_row = lax.broadcasted_iota(jnp.int32, (ROWS, ROWS), 1)
                for span in span_all:
                    logits[0:ROWS, span] = jnp.where(
                        u_row <= t_row, logits[0:ROWS, span], NEG_FILL
                    )

            @pl.when((pair == pairs - 1) & (odd(here) == 0))
            def _():
                logits[rows_of(here + 1, ROWS), :] = jnp.full((ROWS, STACK), NEG_FILL, F32)

            for span in span_all:
                stats[0, :, span] = jnp.maximum(
                    stats[0, :, span], fold(logits[span_rows, span]).max(0)
                )

        stats[1] = jnp.zeros((8, STACK), F32)
        stats[2] = jnp.zeros((8, STACK), F32)
        stats[0] = jnp.broadcast_to(stats[0].max(0, keepdims=True), (8, STACK))

        @pl.loop(0, pairs)
        def _(pair):
            span_rows = rows_of(pair, PAIR)
            for span in span_all:
                top = stats[0, 0:1, span]
                tile = jnp.exp2((logits[span_rows, span] - top) * EXP2_SCALE)
                logits[span_rows, span] = tile
                stats[1, :, span] += fold(tile).sum(0)
                stats[2, :, span] += fold(tile * grad_probs[span_rows, span]).sum(0)

        inverse = 1.0 / stats[1].sum(0, keepdims=True)
        delta = stats[2].sum(0, keepdims=True) * inverse
        stats[1] = jnp.broadcast_to(inverse, (8, STACK))
        stats[2] = jnp.broadcast_to(delta, (8, STACK))
        query_sum[...] = jnp.zeros((HEAD_DIM, STACK), F32)

        @pl.loop(0, pairs)
        def _(pair):
            span_rows = rows_of(pair, PAIR)
            for span in span_all:
                exact = logits[span_rows, span] * stats[1, 0:1, span]
                probs[:, span] = exact.astype(BF16)
                grad_logits[:, span] = (
                    exact * (grad_probs[span_rows, span] - stats[2, 0:1, span])
                ).astype(BF16)
            value_term = jnp.dot(probs[...], stacks[1], preferred_element_type=F32)
            key_term = SCALE * jnp.dot(
                grad_logits[...], stacks[0], preferred_element_type=F32
            )
            for part, term in enumerate((key_term, value_term)):
                terms[head, pl.ds(2 * pair, 2), part] = term.astype(BF16).reshape(
                    2, ROWS, HEAD_DIM
                )

                @pl.when(pair == 0)
                def _():
                    own[head, part] = term[0:ROWS]

            query_sum[...] += lax.dot_general(
                block_pair(pair, 0), grad_logits[...], (((0,), (0,)), ((), ())),
                preferred_element_type=F32,
            )

        for group, span in enumerate(span_all):
            staged[head, :, span] = (SCALE * query_sum[:, span].T).astype(BF16)

    def query_target(head):
        return grad_queries.at[0, 0, :, lanes(name_of(head), GROUP)]

    def send_results(head):
        host = host_of(head)
        here = host

        def send(count):
            @pl.loop(1, SEGS)
            def _(step):
                peer = wrapped(me + step)
                part, span = piece_of(peer)
                remote(
                    terms.at[head, pl.ds(1, count), part, span, :],
                    term_pieces.at[head, pl.ds(1, count), me],
                    b1_send.at[head], b1_recv.at[head], (level, peer),
                ).start()

            part, span = piece_of(me)
            pltpu.make_async_copy(
                terms.at[head, pl.ds(1, count), part, span, :],
                term_pieces.at[head, pl.ds(1, count), me], b1_recv.at[head],
            ).start()

        per_plane(here, send)
        move(
            head, staged.at[head], query_target(head), d_send.at[head], d_recv.at[head]
        )

        @pl.when(host != level)
        def _():
            own_out[head] = own[head].astype(BF16)
            remote(
                own_out.at[head], own_in.at[head], o_send.at[head], o_recv.at[head], (host, me)
            ).start()

    def summed(head, offset):
        return jnp.dot(
            spread[group_of(head), offset],
            term_pieces[head, offset].reshape(SEGS * PIECE, HEAD_DIM),
            preferred_element_type=F32,
        )

    def cross_copy(head, plane):
        return remote(
            cross_out.at[head, plane], cross_in.at[head, plane],
            x_send.at[head, plane], x_recv.at[head, plane], (sibling, me),
        )

    def sum_stage(head):
        here = host_of(head)

        def sums(count):
            wait_bytes(term_pieces.at[head, pl.ds(1, count)], b1_recv.at[head])
            for plane in range((count + 1) // 2):
                offset = jnp.maximum(here - (2 * plane + 1 - core), 1)
                cross_out[head, plane] = summed(head, offset).astype(BF16)
            for plane in range((count - 1) // 2):
                offset = jnp.maximum(here - (2 * plane + core), 1)
                kept[head, plane] = summed(head, offset)

        per_plane(here, sums)

        @pl.loop(0, 4)
        def _(plane):
            @pl.when(here - (2 * plane + 1 - core) >= 1)
            def _():
                cross_copy(head, plane).start()

    def climb_copy(head, plane):
        slot = half(host_of(head)) - 1
        return remote(
            climb_out.at[head, plane], climb_in.at[head, slot],
            c_send.at[head, plane], c_recv.at[head, slot], (device_of(head, plane), me),
        )

    def climb(head):
        plane_here = half(host_of(head))

        @pl.loop(0, plane_here - core + 1)
        def _(plane):
            wait_bytes(cross_in.at[head, plane], x_recv.at[head, plane])

        @pl.loop(0, plane_here)
        def _(plane):
            climb_out[head, plane] = (
                kept[head, plane] + cross_in[head, plane].astype(F32)
            ).astype(BF16)
            climb_copy(head, plane).start()

    def final_send(head):
        host = host_of(head)

        @pl.when(host < LEVELS - 1)
        def _():
            total_sum[...] = jnp.zeros((SEGS * PIECE, HEAD_DIM), F32)

            @pl.loop(half(host), 3)
            def _(slot):
                wait_bytes(climb_in.at[head, slot], c_recv.at[head, slot])
                total_sum[...] += climb_in[head, slot].astype(F32)

            @pl.when(core == 0)
            def _():
                total_sum[...] += cross_in[head, half(host)].astype(F32)

            final_out[head] = total_sum[...].astype(BF16).reshape(SEGS, PIECE, HEAD_DIM)
            part, span = piece_of(me)

            @pl.loop(1, SEGS)
            def _(step):
                peer = wrapped(me + step)
                remote(
                    final_out.at[head, peer], final_in.at[head, part, span, :],
                    f_send.at[head], f_recv.at[head], (host, peer),
                ).start()

            move(
                head, final_out.at[head, me], final_in.at[head, part, span, :],
                f_send.at[head], f_recv.at[head],
            )

    def final_store(head):
        away = host_of(head) != level

        @pl.when(away)
        def _():
            wait_bytes(own_in.at[head], o_recv.at[head])
            own[head] = own_in[head].astype(F32)

        @pl.when(level < LEVELS - 1)
        def _():
            wait_bytes(final_in.at[head], f_recv.at[head])
            own[head] = own[head] + final_in[head].astype(F32)

        grad_kv[0, 0, :, :, lanes(name_of(head))] = own[head].astype(BF16)

    stages = (sum_stage, climb, final_send, final_store)

    @pl.loop(0, KV_HEADS + LAG + len(stages))
    def _(tick):
        @pl.when(tick < KV_HEADS)
        def _():
            pass_on(tick)

        @pl.when((tick >= 1) & (tick < KV_HEADS + 1))
        def _():
            select(tick - 1)

        @pl.when((tick >= LAG) & (tick < KV_HEADS + LAG))
        def _():
            head = tick - LAG
            per_plane(
                host_of(head),
                lambda count: wait_bytes(blocks.at[head, pl.ds(1, count)], p3_recv.at[head]),
            )
            wait_bytes(blocks.at[head, 0], k_recv.at[head])
            wait_bytes(inputs.at[head], q_recv.at[head])
            attend(head)
            send_results(head)

        for lag, stage in enumerate(stages, LAG + 1):
            @pl.when((tick >= lag) & (tick < KV_HEADS + lag))
            def _():
                stage(tick - lag)

    for group, (host, span_lanes) in enumerate(spread_groups):
        wait_bytes(pieces.at[0, pl.ds(1, SEGS - 1), :, span_lanes], p1_send.at[group])
        if group == 1:
            @pl.when(host != level)
            def _():
                wait_bytes(pieces.at[0, 0, :, span_lanes], p1_send.at[group])

    @pl.loop(0, KV_HEADS)
    def _(head):
        host = host_of(head)
        away = host != level
        wait_bytes(query_target(head), d_recv.at[head])
        own_lifts(head, lambda copy: copy.wait_send())
        passed_on(head, lambda which, copy: copy.wait_send())

        @pl.when(away)
        def _():
            wait_bytes(blocks.at[head, 0], k_send.at[head])
            wait_bytes(inputs.at[head], q_send.at[head])
            wait_bytes(staged.at[head], d_send.at[head])
            wait_bytes(own_out.at[head], o_send.at[head])

        def sent(count):
            wait_bytes(chosen.at[head, pl.ds(1, SEGS - 1), pl.ds(0, count)], p3_send.at[head])
            wait_bytes(
                term_pieces.at[head, pl.ds(1, count), pl.ds(1, SEGS - 1)], b1_send.at[head]
            )

        per_plane(host, sent)

        @pl.loop(0, 4)
        def _(plane):
            @pl.when(host - (2 * plane + 1 - core) >= 1)
            def _():
                cross_copy(head, plane).wait_send()

        @pl.loop(0, half(host))
        def _(plane):
            climb_copy(head, plane).wait_send()

        @pl.when(host < LEVELS - 1)
        def _():
            wait_bytes(final_out.at[head, pl.ds(1, SEGS - 1)], f_send.at[head])

            @pl.when(away)
            def _():
                wait_bytes(final_out.at[head, 0], f_send.at[head])


def shards(queries, keys_values, grad_out, parents):
    vmem = pl.BlockSpec(memory_space=pltpu.VMEM)
    smem = pl.BlockSpec(memory_space=pltpu.SMEM)
    anywhere = pl.BlockSpec(memory_space=pl.ANY)
    dma = pltpu.SemaphoreType.DMA
    tile = (SEGS, PIECE, HEAD_DIM)
    flat = (SEGS * PIECE, HEAD_DIM)
    keys_count = LEVELS * ROWS
    part_pair = (2, ROWS, HEAD_DIM)
    selectors = (2, LEVELS, SEGS * PIECE, SEGS * PIECE)
    scratch = [
        pltpu.SMEM((2, LEVELS, SEGS), jnp.int32),
        pltpu.VMEM(selectors, BF16),
        pltpu.VMEM(selectors, BF16),
        pltpu.VMEM((LEVELS, SEGS, PIECE, KV_HEADS * HEAD_DIM), BF16),
        pltpu.VMEM((KV_HEADS, SEGS, LEVELS - 1, PIECE, HEAD_DIM), BF16),
        pltpu.VMEM((KV_HEADS, LEVELS) + part_pair, BF16),
        pltpu.VMEM((KV_HEADS, LEVELS) + part_pair, BF16),
        pltpu.VMEM((KV_HEADS, LEVELS) + tile, BF16),
        pltpu.VMEM((KV_HEADS,) + part_pair, F32),
        pltpu.VMEM((KV_HEADS,) + part_pair, BF16),
        pltpu.VMEM((KV_HEADS,) + part_pair, BF16),
        pltpu.VMEM((KV_HEADS, 2, ROWS, STACK), BF16),
        pltpu.VMEM((2, STACK, HEAD_DIM), BF16),
        pltpu.VMEM((2, HEAD_DIM, STACK), BF16),
        pltpu.VMEM((KV_HEADS, ROWS, STACK), BF16),
        pltpu.VMEM((HEAD_DIM, STACK), F32),
        pltpu.VMEM((3, 8, STACK), F32),
        pltpu.VMEM((keys_count, STACK), F32),
        pltpu.VMEM((keys_count, STACK), F32),
        pltpu.VMEM((PAIR, STACK), BF16),
        pltpu.VMEM((PAIR, STACK), BF16),
        pltpu.VMEM((KV_HEADS, 3) + flat, F32),
        pltpu.VMEM(flat, F32),
        pltpu.VMEM((KV_HEADS, 4) + flat, BF16),
        pltpu.VMEM((KV_HEADS, 4) + flat, BF16),
        pltpu.VMEM((KV_HEADS, 3) + flat, BF16),
        pltpu.VMEM((KV_HEADS, 3) + flat, BF16),
        pltpu.VMEM((KV_HEADS,) + tile, BF16),
        pltpu.VMEM((KV_HEADS,) + part_pair, BF16),
        dma((2,)), dma((2,)),
        dma((KV_HEADS, 7)), dma((KV_HEADS, LEVELS)),
        dma((KV_HEADS,)), dma((KV_HEADS,)),
        dma((KV_HEADS,)), dma((KV_HEADS,)),
        dma((KV_HEADS,)), dma((KV_HEADS,)),
        dma((KV_HEADS,)), dma((KV_HEADS,)),
        dma((KV_HEADS,)), dma((KV_HEADS,)),
        dma((KV_HEADS,)), dma((KV_HEADS,)),
        dma((KV_HEADS, 4)), dma((KV_HEADS, 4)),
        dma((KV_HEADS, 3)), dma((KV_HEADS, 3)),
        dma((KV_HEADS,)), dma((KV_HEADS,)),
    ]
    return pl.pallas_call(
        kernel,
        out_shape=(
            jax.ShapeDtypeStruct(queries.shape, BF16),
            jax.ShapeDtypeStruct(keys_values.shape, BF16),
        ),
        in_specs=[smem, anywhere, anywhere, anywhere],
        out_specs=(vmem, vmem),
        scratch_shapes=scratch,
        compiler_params=pltpu.CompilerParams(
            collective_id=0, has_side_effects=True, vmem_limit_bytes=56 * 1024 * 1024
        ),
        cost_estimate=pl.CostEstimate(
            flops=5 * 2 * HEADS * LEVELS * ROWS * ROWS * HEAD_DIM,
            bytes_accessed=8 * 1024 * 1024,
            transcendentals=HEADS * LEVELS * ROWS * ROWS,
        ),
    )(parents.transpose(0, 2, 1), queries, keys_values, grad_out)


def solution(mesh):
    in_specs = (
        P("depth", "seg", None, None),
        P("depth", "seg", None, None, None),
        P("depth", "seg", None, None),
        P(),
    )
    out_specs = (P("depth", "seg", None, None), P("depth", "seg", None, None, None))
    return jax.shard_map(shards, mesh=mesh, in_specs=in_specs, out_specs=out_specs, check_vma=False)
```

```python
import functools

import jax
import jax.numpy as jnp
from jax import lax
from jax.experimental import pallas as pl
from jax.experimental.pallas import tpu as pltpu
from jax.sharding import PartitionSpec as P

HEADS = 20
KV_HEADS = 4
HEAD_DIM = 128
GROUP = HEADS // KV_HEADS
ROWS = 128
LEVELS = 8
SEGS = 16
PIECE = 16
PIECES_PER_PART = ROWS // PIECE
STACK = GROUP * ROWS
PAIR = 2 * ROWS

NEG_FILL = -1e30
SCALE = HEAD_DIM ** -0.5
EXP2_SCALE = SCALE * 1.4426950408889634
MESH = pl.DeviceIdType.MESH
BF16 = jnp.bfloat16
F32 = jnp.float32


def half(value):
    return lax.div(value, 2)


def odd(value):
    return lax.rem(value, 2)


def wrapped(index):
    return jnp.where(index >= SEGS, index - SEGS, index)


def lanes(index, count=1):
    width = count * HEAD_DIM
    return pl.ds(pl.multiple_of(index * width, width), width)


def rows_of(index, count):
    return pl.ds(pl.multiple_of(index * count, count), count)


def piece_of(index):
    part = jnp.where(index >= PIECES_PER_PART, 1, 0)
    return part, rows_of(index - part * PIECES_PER_PART, PIECE)


def fold(tile):
    return tile.reshape(tile.shape[0] // 8, 8, tile.shape[1])


def place():
    level = lax.axis_index("depth")
    return level, lax.axis_index("seg"), half(level), odd(level)


def host_of(head):
    return lax.axis_index("depth")


def device_of(head, plane):
    return 2 * plane + odd(lax.axis_index("depth"))


def remote(src, dst, send_sem, recv_sem, device):
    return pltpu.make_async_remote_copy(
        src_ref=src, dst_ref=dst, send_sem=send_sem, recv_sem=recv_sem,
        device_id=device, device_id_type=MESH,
    )


def wait_bytes(ref, sem):
    pltpu.make_async_copy(ref, ref, sem).wait()


def per_plane(which, action):
    for plane in range(LEVELS // 2):
        pl.when((which > 0) & (half(which) == plane))(
            functools.partial(action, 2 * plane + 1)
        )


def enter():
    level, me, y, core = place()
    barrier = pltpu.get_barrier_semaphore()

    def greet(device):
        pl.semaphore_signal(barrier, inc=1, device_id=device, device_id_type=MESH)

    @pl.loop(1, SEGS)
    def _(step):
        greet((level, wrapped(me + step)))

    greet((2 * y + 1 - core, me))
    for step in range(1, 4):
        greet((lax.rem(level + 2 * step, LEVELS), me))
    pl.semaphore_wait(barrier, SEGS - 1 + 4)


def find_ancestors(parents, anc, level):
    @pl.loop(0, SEGS)
    def _(column):
        current = column
        for offset in range(1, LEVELS):
            current = parents[jnp.maximum(level - offset, 0), 0, current]
            anc[offset, column] = current


def make_pick(pick, anc, level):
    @pl.loop(1, 2 * half(level) + 2)
    def _(offset):
        lane = lax.broadcasted_iota(jnp.int32, (PIECE, SEGS * PIECE), 1)
        row = lax.broadcasted_iota(jnp.int32, (PIECE, SEGS * PIECE), 0)
        for column in range(SEGS):
            pick[offset, rows_of(column, PIECE), :] = jnp.where(
                lane == anc[offset, column] * PIECE + row, 1.0, 0.0
            ).astype(BF16)


def make_spread(spread, anc, level):
    @pl.loop(1, 2 * half(level) + 2)
    def _(offset):
        lane = lax.broadcasted_iota(jnp.int32, (PIECE, SEGS * PIECE), 1)
        row = lax.broadcasted_iota(jnp.int32, (PIECE, SEGS * PIECE), 0)
        target = lane & (PIECE - 1)
        lane_column = lane >> 4
        for column in range(SEGS):
            target = target + jnp.where(lane_column == column, anc[offset, column] * PIECE, 0)
        for column in range(SEGS):
            spread[offset, rows_of(column, PIECE), :] = jnp.where(
                target == row + column * PIECE, 1.0, 0.0
            ).astype(BF16)


def gather_kernel(
    parents, keys_values, blocks,
    anc, pick, pieces, chosen,
    p1_send, p1_recv, up_send, up_recv, p3_send, p3_recv,
):
    level, me, y, core = place()
    sibling = 2 * y + 1 - core
    enter()

    def source(peer):
        part, span = piece_of(peer)
        return keys_values.at[0, 0, part, span, :]

    @pl.loop(1, SEGS)
    def _(step):
        peer = wrapped(me + step)
        remote(source(peer), pieces.at[level, me], p1_send, p1_recv, (level, peer)).start()

    pltpu.make_async_copy(source(me), pieces.at[level, me], p1_recv).start()

    def unit(head, which):
        return pieces.at[which, :, :, lanes(head)]

    def lift(head, which, slot, device):
        return remote(
            unit(head, which), unit(head, which),
            up_send.at[head, slot], up_recv.at[head, which], (device, me),
        )

    def own_lifts(head, action):
        here = host_of(head)
        plane = half(here)
        for step in range(1, 4):
            @pl.when(plane + step <= 3)
            def _():
                action(lift(head, here, step - 1, device_of(head, plane + step)))

        @pl.when(core == 0)
        def _():
            action(lift(head, here, 3, sibling))

    def passed_on(head, action):
        @pl.loop(0, half(host_of(head)))
        def _(plane):
            action(2 * plane + core, lift(head, 2 * plane + core, 4 + plane, sibling))

    find_ancestors(parents, anc, level)
    wait_bytes(pieces.at[level], p1_recv)

    @pl.loop(0, KV_HEADS)
    def _(head):
        own_lifts(head, lambda copy: copy.start())

    make_pick(pick, anc, level)

    @pl.loop(0, KV_HEADS)
    def _(head):
        blocks[head, 0] = keys_values[0, 0, :, :, lanes(head)]

        @pl.when(level == 0)
        def _():
            blocks[head, 1] = jnp.zeros((2, ROWS, HEAD_DIM), BF16)

    def pass_on(head):
        def forward(which, copy):
            wait_bytes(unit(head, which), up_recv.at[head, which])
            copy.start()

        passed_on(head, forward)

    def select(head):
        here = host_of(head)

        @pl.loop(0, 4)
        def _(plane):
            other = 2 * plane + 1 - core

            @pl.when(other < here)
            def _():
                wait_bytes(unit(head, other), up_recv.at[head, other])

        def send(count):
            for offset in range(1, count + 1):
                found = jnp.dot(
                    pick[offset],
                    pieces[
                        jnp.maximum(here - offset, 0), :, :, lanes(head)
                    ].reshape(SEGS * PIECE, HEAD_DIM),
                    preferred_element_type=F32,
                )
                chosen[head, :, offset - 1] = found.astype(BF16).reshape(SEGS, PIECE, HEAD_DIM)
            part, span = piece_of(me)

            @pl.loop(1, SEGS)
            def _(step):
                peer = wrapped(me + step)
                remote(
                    chosen.at[head, peer, pl.ds(0, count)],
                    blocks.at[head, pl.ds(1, count), part, span, :],
                    p3_send.at[head], p3_recv.at[head], (level, peer),
                ).start()

            pltpu.make_async_copy(
                chosen.at[head, me, pl.ds(0, count)],
                blocks.at[head, pl.ds(1, count), part, span, :], p3_recv.at[head],
            ).start()

        per_plane(here, send)

    @pl.loop(0, KV_HEADS)
    def _(head):
        pass_on(head)

    @pl.loop(0, KV_HEADS)
    def _(head):
        select(head)

    wait_bytes(pieces.at[0, pl.ds(1, SEGS - 1)], p1_send)

    @pl.loop(0, KV_HEADS)
    def _(head):
        own_lifts(head, lambda copy: copy.wait_send())
        passed_on(head, lambda which, copy: copy.wait_send())

        def settle(count):
            wait_bytes(blocks.at[head, pl.ds(1, count)], p3_recv.at[head])
            wait_bytes(chosen.at[head, pl.ds(1, SEGS - 1), pl.ds(0, count)], p3_send.at[head])

        per_plane(level, settle)


def attend_kernel(
    blocks, queries, grad_out, grad_queries, terms, own,
    stacks, turned, query_sum, stats, logits, grad_probs, probs, grad_logits,
):
    def attend(head):
        here = host_of(head)
        pairs = half(here) + 1
        span_all = [pl.ds(group * ROWS, ROWS) for group in range(GROUP)]

        def block_pair(pair, part):
            return blocks[head, pl.ds(2 * pair, 2), part].reshape(PAIR, HEAD_DIM)

        stats[0] = jnp.full((8, STACK), NEG_FILL, F32)
        for index in range(2):
            for group, span in enumerate(span_all):
                tile = (queries, grad_out)[index][0, 0, :, lanes(head * GROUP + group)]
                stacks[index, span, :] = tile
                turned[index, :, span] = tile.T

        @pl.loop(0, pairs)
        def _(pair):
            span_rows = rows_of(pair, PAIR)
            logits[span_rows, :] = jnp.dot(
                block_pair(pair, 0), turned[0], preferred_element_type=F32
            )
            grad_probs[span_rows, :] = jnp.dot(
                block_pair(pair, 1), turned[1], preferred_element_type=F32
            )

            @pl.when(pair == 0)
            def _():
                u_row = lax.broadcasted_iota(jnp.int32, (ROWS, ROWS), 0)
                t_row = lax.broadcasted_iota(jnp.int32, (ROWS, ROWS), 1)
                for span in span_all:
                    logits[0:ROWS, span] = jnp.where(
                        u_row <= t_row, logits[0:ROWS, span], NEG_FILL
                    )

            @pl.when((pair == pairs - 1) & (odd(here) == 0))
            def _():
                logits[rows_of(here + 1, ROWS), :] = jnp.full((ROWS, STACK), NEG_FILL, F32)

            for span in span_all:
                stats[0, :, span] = jnp.maximum(
                    stats[0, :, span], fold(logits[span_rows, span]).max(0)
                )

        stats[1] = jnp.zeros((8, STACK), F32)
        stats[2] = jnp.zeros((8, STACK), F32)
        stats[0] = jnp.broadcast_to(stats[0].max(0, keepdims=True), (8, STACK))

        @pl.loop(0, pairs)
        def _(pair):
            span_rows = rows_of(pair, PAIR)
            for span in span_all:
                top = stats[0, 0:1, span]
                tile = jnp.exp2((logits[span_rows, span] - top) * EXP2_SCALE)
                logits[span_rows, span] = tile
                stats[1, :, span] += fold(tile).sum(0)
                stats[2, :, span] += fold(tile * grad_probs[span_rows, span]).sum(0)

        inverse = 1.0 / stats[1].sum(0, keepdims=True)
        delta = stats[2].sum(0, keepdims=True) * inverse
        stats[1] = jnp.broadcast_to(inverse, (8, STACK))
        stats[2] = jnp.broadcast_to(delta, (8, STACK))
        query_sum[...] = jnp.zeros((HEAD_DIM, STACK), F32)

        @pl.loop(0, pairs)
        def _(pair):
            span_rows = rows_of(pair, PAIR)
            for span in span_all:
                exact = logits[span_rows, span] * stats[1, 0:1, span]
                probs[:, span] = exact.astype(BF16)
                grad_logits[:, span] = (
                    exact * (grad_probs[span_rows, span] - stats[2, 0:1, span])
                ).astype(BF16)
            value_term = jnp.dot(probs[...], stacks[1], preferred_element_type=F32)
            key_term = SCALE * jnp.dot(
                grad_logits[...], stacks[0], preferred_element_type=F32
            )
            for part, term in enumerate((key_term, value_term)):
                terms[head, pl.ds(2 * pair, 2), part] = term.astype(BF16).reshape(
                    2, ROWS, HEAD_DIM
                )

                @pl.when(pair == 0)
                def _():
                    own[head, part] = term[0:ROWS]

            query_sum[...] += lax.dot_general(
                block_pair(pair, 0), grad_logits[...], (((0,), (0,)), ((), ())),
                preferred_element_type=F32,
            )

        for group, span in enumerate(span_all):
            grad_queries[0, 0, :, lanes(head * GROUP + group)] = (SCALE * query_sum[:, span].T).astype(BF16)

    pl.loop(0, KV_HEADS)(attend)


def reduce_kernel(
    parents, terms, own, grad_kv,
    anc, spread, term_pieces,
    kept, total_sum, cross_out, cross_in, climb_out, climb_in, final_out, final_in,
    b1_send, b1_recv, x_send, x_recv, c_send, c_recv, f_send, f_recv,
):
    level, me, y, core = place()
    sibling = 2 * y + 1 - core
    enter()

    def send_terms(head):
        here = level

        def send(count):
            @pl.loop(1, SEGS)
            def _(step):
                peer = wrapped(me + step)
                part, span = piece_of(peer)
                remote(
                    terms.at[head, pl.ds(1, count), part, span, :],
                    term_pieces.at[head, pl.ds(1, count), me],
                    b1_send.at[head], b1_recv.at[head], (level, peer),
                ).start()

            part, span = piece_of(me)
            pltpu.make_async_copy(
                terms.at[head, pl.ds(1, count), part, span, :],
                term_pieces.at[head, pl.ds(1, count), me], b1_recv.at[head],
            ).start()

        per_plane(here, send)
    pl.loop(0, KV_HEADS)(send_terms)
    find_ancestors(parents, anc, level)
    make_spread(spread, anc, level)

    def summed(head, offset):
        return jnp.dot(
            spread[offset],
            term_pieces[head, offset].reshape(SEGS * PIECE, HEAD_DIM),
            preferred_element_type=F32,
        )

    def cross_copy(head, plane):
        return remote(
            cross_out.at[head, plane], cross_in.at[head, plane],
            x_send.at[head, plane], x_recv.at[head, plane], (sibling, me),
        )

    def sum_stage(head):
        here = host_of(head)

        def sums(count):
            wait_bytes(term_pieces.at[head, pl.ds(1, count)], b1_recv.at[head])
            for plane in range((count + 1) // 2):
                offset = jnp.maximum(here - (2 * plane + 1 - core), 1)
                cross_out[head, plane] = summed(head, offset).astype(BF16)
            for plane in range((count - 1) // 2):
                offset = jnp.maximum(here - (2 * plane + core), 1)
                kept[head, plane] = summed(head, offset)

        per_plane(here, sums)

        @pl.loop(0, 4)
        def _(plane):
            @pl.when(here - (2 * plane + 1 - core) >= 1)
            def _():
                cross_copy(head, plane).start()

    def climb_copy(head, plane):
        slot = half(host_of(head)) - 1
        return remote(
            climb_out.at[head, plane], climb_in.at[head, slot],
            c_send.at[head, plane], c_recv.at[head, slot], (device_of(head, plane), me),
        )

    def climb(head):
        plane_here = half(host_of(head))

        @pl.loop(0, plane_here - core + 1)
        def _(plane):
            wait_bytes(cross_in.at[head, plane], x_recv.at[head, plane])

        @pl.loop(0, plane_here)
        def _(plane):
            climb_out[head, plane] = (
                kept[head, plane] + cross_in[head, plane].astype(F32)
            ).astype(BF16)
            climb_copy(head, plane).start()

    def final_send(head):
        host = host_of(head)

        @pl.when(host < LEVELS - 1)
        def _():
            total_sum[...] = jnp.zeros((SEGS * PIECE, HEAD_DIM), F32)

            @pl.loop(half(host), 3)
            def _(slot):
                wait_bytes(climb_in.at[head, slot], c_recv.at[head, slot])
                total_sum[...] += climb_in[head, slot].astype(F32)

            @pl.when(core == 0)
            def _():
                total_sum[...] += cross_in[head, half(host)].astype(F32)

            final_out[head] = total_sum[...].astype(BF16).reshape(SEGS, PIECE, HEAD_DIM)
            part, span = piece_of(me)

            @pl.loop(1, SEGS)
            def _(step):
                peer = wrapped(me + step)
                remote(
                    final_out.at[head, peer], final_in.at[head, part, span, :],
                    f_send.at[head], f_recv.at[head], (host, peer),
                ).start()

            pltpu.make_async_copy(
                final_out.at[head, me], final_in.at[head, part, span, :], f_recv.at[head]
            ).start()

    def final_store(head):
        @pl.when(level < LEVELS - 1)
        def _():
            wait_bytes(final_in.at[head], f_recv.at[head])
            grad_kv[0, 0, :, :, lanes(head)] = (
                own[head] + final_in[head].astype(F32)
            ).astype(BF16)

        @pl.when(level == LEVELS - 1)
        def _():
            grad_kv[0, 0, :, :, lanes(head)] = own[head].astype(BF16)

    stages = (sum_stage, climb, final_send, final_store)

    @pl.loop(0, KV_HEADS + len(stages) - 1)
    def _(tick):
        for lag, stage in enumerate(stages):
            @pl.when((tick >= lag) & (tick < KV_HEADS + lag))
            def _():
                stage(tick - lag)

    @pl.loop(0, KV_HEADS)
    def _(head):
        per_plane(
            level,
            lambda count: wait_bytes(
                term_pieces.at[head, pl.ds(1, count), pl.ds(1, SEGS - 1)], b1_send.at[head]
            ),
        )

        @pl.loop(0, 4)
        def _(plane):
            @pl.when(level - (2 * plane + 1 - core) >= 1)
            def _():
                cross_copy(head, plane).wait_send()

        @pl.loop(0, half(level))
        def _(plane):
            climb_copy(head, plane).wait_send()

        @pl.when(level < LEVELS - 1)
        def _():
            wait_bytes(final_out.at[head, pl.ds(1, SEGS - 1)], f_send.at[head])


def shards(queries, keys_values, grad_out, parents):
    vmem = pl.BlockSpec(memory_space=pltpu.VMEM)
    smem = pl.BlockSpec(memory_space=pltpu.SMEM)
    dma = pltpu.SemaphoreType.DMA
    tile = (SEGS, PIECE, HEAD_DIM)
    flat = (SEGS * PIECE, HEAD_DIM)
    keys_count = LEVELS * ROWS
    part_pair = (2, ROWS, HEAD_DIM)
    selectors = (LEVELS, SEGS * PIECE, SEGS * PIECE)
    found = pltpu.SMEM((LEVELS, SEGS), jnp.int32)
    all_parts = jax.ShapeDtypeStruct((KV_HEADS, LEVELS) + part_pair, BF16)
    parent_rows = parents.transpose(0, 2, 1)

    def limits(**more):
        return pltpu.CompilerParams(vmem_limit_bytes=24 * 1024 * 1024, **more)

    blocks = pl.pallas_call(
        gather_kernel,
        out_shape=all_parts,
        in_specs=[smem, vmem],
        out_specs=vmem,
        scratch_shapes=[
            found,
            pltpu.VMEM(selectors, BF16),
            pltpu.VMEM((LEVELS, SEGS, PIECE, KV_HEADS * HEAD_DIM), BF16),
            pltpu.VMEM((KV_HEADS, SEGS, LEVELS - 1, PIECE, HEAD_DIM), BF16),
            dma, dma,
            dma((KV_HEADS, 7)), dma((KV_HEADS, LEVELS)),
            dma((KV_HEADS,)), dma((KV_HEADS,)),
        ],
        compiler_params=limits(collective_id=0, has_side_effects=True),
    )(parent_rows, keys_values)
    grad_queries, terms, own = pl.pallas_call(
        attend_kernel,
        out_shape=(
            jax.ShapeDtypeStruct(queries.shape, BF16),
            all_parts,
            jax.ShapeDtypeStruct((KV_HEADS,) + part_pair, F32),
        ),
        in_specs=[vmem, vmem, vmem],
        out_specs=(vmem, vmem, vmem),
        scratch_shapes=[
            pltpu.VMEM((2, STACK, HEAD_DIM), BF16),
            pltpu.VMEM((2, HEAD_DIM, STACK), BF16),
            pltpu.VMEM((HEAD_DIM, STACK), F32),
            pltpu.VMEM((3, 8, STACK), F32),
            pltpu.VMEM((keys_count, STACK), F32),
            pltpu.VMEM((keys_count, STACK), F32),
            pltpu.VMEM((PAIR, STACK), BF16),
            pltpu.VMEM((PAIR, STACK), BF16),
        ],
        compiler_params=limits(),
    )(blocks, queries, grad_out)
    grad_kv = pl.pallas_call(
        reduce_kernel,
        out_shape=jax.ShapeDtypeStruct(keys_values.shape, BF16),
        in_specs=[smem, vmem, vmem],
        out_specs=vmem,
        scratch_shapes=[
            found,
            pltpu.VMEM(selectors, BF16),
            pltpu.VMEM((KV_HEADS, LEVELS) + tile, BF16),
            pltpu.VMEM((KV_HEADS, 3) + flat, F32),
            pltpu.VMEM(flat, F32),
            pltpu.VMEM((KV_HEADS, 4) + flat, BF16),
            pltpu.VMEM((KV_HEADS, 4) + flat, BF16),
            pltpu.VMEM((KV_HEADS, 3) + flat, BF16),
            pltpu.VMEM((KV_HEADS, 3) + flat, BF16),
            pltpu.VMEM((KV_HEADS,) + tile, BF16),
            pltpu.VMEM((KV_HEADS,) + part_pair, BF16),
            dma((KV_HEADS,)), dma((KV_HEADS,)),
            dma((KV_HEADS, 4)), dma((KV_HEADS, 4)),
            dma((KV_HEADS, 3)), dma((KV_HEADS, 3)),
            dma((KV_HEADS,)), dma((KV_HEADS,)),
        ],
        compiler_params=limits(collective_id=1, has_side_effects=True),
    )(parent_rows, terms, own)
    return grad_queries, grad_kv


def solution(mesh):
    in_specs = (
        P("depth", "seg", None, None),
        P("depth", "seg", None, None, None),
        P("depth", "seg", None, None),
        P(),
    )
    out_specs = (P("depth", "seg", None, None), P("depth", "seg", None, None, None))
    return jax.shard_map(shards, mesh=mesh, in_specs=in_specs, out_specs=out_specs, check_vma=False)
```

```python
import functools

import jax
import jax.numpy as jnp
from jax import lax
from jax.experimental import pallas as pl
from jax.experimental.pallas import tpu as pltpu
from jax.sharding import PartitionSpec as P

HEADS = 20
KV_HEADS = 4
HEAD_DIM = 128
GROUP = HEADS // KV_HEADS
ROWS = 128
LEVELS = 8
SEGS = 16
PIECE = 16
PIECES_PER_PART = ROWS // PIECE
STACK = GROUP * ROWS
PAIR = 2 * ROWS
LAG = 3

NEG_FILL = -1e30
SCALE = HEAD_DIM ** -0.5
EXP2_SCALE = SCALE * 1.4426950408889634
MESH = pl.DeviceIdType.MESH
BF16 = jnp.bfloat16
F32 = jnp.float32


def half(value):
    return lax.div(value, 2)


def odd(value):
    return lax.rem(value, 2)


def name_of(head):
    return 2 * odd(head) + half(head)


def wrapped(index):
    return jnp.where(index >= SEGS, index - SEGS, index)


def lanes(index, count=1):
    width = count * HEAD_DIM
    return pl.ds(pl.multiple_of(index * width, width), width)


def rows_of(index, count):
    return pl.ds(pl.multiple_of(index * count, count), count)


def piece_of(index):
    part = jnp.where(index >= PIECES_PER_PART, 1, 0)
    return part, rows_of(index - part * PIECES_PER_PART, PIECE)


def fold(tile):
    return tile.reshape(tile.shape[0] // 8, 8, tile.shape[1])


def kernel(
    parents, queries, keys_values, grad_out, grad_queries, grad_kv,
    anc, pick, spread, pieces, chosen, blocks, terms, term_pieces, own, own_out, own_in,
    inputs, stacks, turned, staged, query_sum, stats, logits, grad_probs, probs, grad_logits,
    kept, total_sum, cross_out, cross_in, climb_out, climb_in, final_out, final_in,
    p1_send, p1_recv, up_send, up_recv, q_send, q_recv, k_send, k_recv, p3_send, p3_recv,
    b1_send, b1_recv, o_send, o_recv, d_send, d_recv, x_send, x_recv, c_send, c_recv,
    f_send, f_recv,
):
    level = lax.axis_index("depth")
    me = lax.axis_index("seg")
    y = half(level)
    core = odd(level)
    sibling = 2 * y + 1 - core
    partner = 2 * (3 - y) + core

    def host_of(head):
        return jnp.where(odd(head) == 1, partner, level)

    def device_of(head, plane):
        return 2 * jnp.where(odd(head) == 1, 3 - plane, plane) + core

    def remote(src, dst, send_sem, recv_sem, device):
        return pltpu.make_async_remote_copy(
            src_ref=src, dst_ref=dst, send_sem=send_sem, recv_sem=recv_sem,
            device_id=device, device_id_type=MESH,
        )

    def wait_bytes(ref, sem):
        pltpu.make_async_copy(ref, ref, sem).wait()

    def per_plane(which, action):
        for plane in range(LEVELS // 2):
            pl.when((which > 0) & (half(which) == plane))(
                functools.partial(action, 2 * plane + 1)
            )

    def move(head, src, dst, send_sem, recv_sem):
        host = host_of(head)

        @pl.when(host != level)
        def _():
            remote(src, dst, send_sem, recv_sem, (host, me)).start()

        @pl.when(host == level)
        def _():
            pltpu.make_async_copy(src, dst, recv_sem).start()

    barrier = pltpu.get_barrier_semaphore()

    def greet(device):
        pl.semaphore_signal(barrier, inc=1, device_id=device, device_id_type=MESH)

    @pl.loop(1, SEGS)
    def _(step):
        greet((level, wrapped(me + step)))

    greet((sibling, me))
    for step in range(1, 4):
        greet((lax.rem(level + 2 * step, LEVELS), me))

    @pl.loop(0, SEGS)
    def _(step):
        greet((partner, wrapped(me + step)))

    pl.semaphore_wait(barrier, 2 * SEGS + 3)

    def spread_out(head):
        host = host_of(head)
        span_lanes = lanes(name_of(head))

        def source(peer):
            part, span = piece_of(peer)
            return keys_values.at[0, 0, part, span, span_lanes]

        landing = pieces.at[level, me, :, span_lanes]

        @pl.loop(1, SEGS)
        def _(step):
            peer = wrapped(me + step)
            remote(
                source(peer), landing, p1_send.at[head], p1_recv.at[head], (host, peer)
            ).start()

        move(head, source(me), landing, p1_send.at[head], p1_recv.at[head])

    def move_inputs(head):
        name = name_of(head)
        move(
            head, keys_values.at[0, 0, :, :, lanes(name)], blocks.at[head, 0],
            k_send.at[head], k_recv.at[head],
        )
        for index, array in enumerate((queries, grad_out)):
            move(
                head, array.at[0, 0, :, lanes(name, GROUP)], inputs.at[head, index],
                q_send.at[head], q_recv.at[head],
            )

    def unit(head, which):
        return pieces.at[which, :, :, lanes(name_of(head))]

    def lift(head, which, slot, device):
        return remote(
            unit(head, which), unit(head, which),
            up_send.at[head, slot], up_recv.at[head, which], (device, me),
        )

    def own_lifts(head, action):
        here = host_of(head)
        plane = half(here)
        routes = (
            (plane <= 2, 0, plane + 1),
            (plane == 0, 1, 3),
            ((plane == 1) & (core == 1), 1, 0),
        )
        for condition, slot, target in routes:
            @pl.when(condition)
            def _():
                action(lift(head, here, slot, device_of(head, target)))

        @pl.when(core == 0)
        def _():
            action(lift(head, here, 2, sibling))

    relays = (
        (0, 1, 1, 3),
        (1, 0, 0, 2),
        (2, 1, 0, 3),
        (2, 0, None, None),
        (3, 0, 1, 2),
        (3, 2, None, None),
        (3, 1, None, None),
    )

    def passed_on(head, before, action):
        plane_here = half(host_of(head))
        for plane, owner, relay_core, target in relays:
            which = 2 * owner + core
            needed = plane_here == plane
            if plane < owner:
                needed = needed & (core == relay_core)

            @pl.when(needed)
            def _():
                before(which)
                if target is not None:
                    copy = lift(head, which, 3, device_of(head, target))
                    if plane < owner:
                        action(copy)
                    else:
                        pl.when(core == relay_core)(lambda: action(copy))
                if plane > owner:
                    action(lift(head, which, 4 + owner, sibling))

    def launch(head):
        wait_bytes(
            pieces.at[host_of(head), :, :, lanes(name_of(head))], p1_recv.at[head]
        )
        own_lifts(head, lambda copy: copy.start())
        move_inputs(head)

    pl.loop(0, 2)(spread_out)
    pl.loop(0, 2)(launch)
    pl.loop(2, KV_HEADS)(spread_out)

    def make_selectors(parity):
        target_level = host_of(parity)

        @pl.loop(0, SEGS)
        def _(column):
            current = column
            for offset in range(1, LEVELS):
                current = parents[jnp.maximum(target_level - offset, 0), 0, current]
                anc[parity, offset, column] = current

        @pl.loop(1, 2 * half(target_level) + 2)
        def _(offset):
            lane = lax.broadcasted_iota(jnp.int32, (PIECE, SEGS * PIECE), 1)
            row = lax.broadcasted_iota(jnp.int32, (PIECE, SEGS * PIECE), 0)
            target = lane & (PIECE - 1)
            lane_column = lane >> 4
            for column in range(SEGS):
                found = anc[parity, offset, column] * PIECE
                pick[parity, offset, rows_of(column, PIECE), :] = jnp.where(
                    lane == found + row, 1.0, 0.0
                ).astype(BF16)
                target = target + jnp.where(lane_column == column, found, 0)
            for column in range(SEGS):
                spread[parity, offset, rows_of(column, PIECE), :] = jnp.where(
                    target == row + column * PIECE, 1.0, 0.0
                ).astype(BF16)

    make_selectors(0)

    @pl.loop(0, KV_HEADS)
    def _(head):
        @pl.when(host_of(head) == 0)
        def _():
            blocks[head, 1] = jnp.zeros((2, ROWS, HEAD_DIM), BF16)

    def pass_on(head):
        passed_on(
            head,
            lambda which: wait_bytes(unit(head, which), up_recv.at[head, which]),
            lambda copy: copy.start(),
        )

    def select(head):
        here = host_of(head)
        parity = odd(head)

        @pl.loop(0, 4)
        def _(plane):
            other = 2 * plane + 1 - core

            @pl.when(other < here)
            def _():
                wait_bytes(unit(head, other), up_recv.at[head, other])

        def send(count):
            for offset in range(1, count + 1):
                found = jnp.dot(
                    pick[parity, offset],
                    pieces[
                        jnp.maximum(here - offset, 0), :, :, lanes(name_of(head))
                    ].reshape(SEGS * PIECE, HEAD_DIM),
                    preferred_element_type=F32,
                )
                chosen[head, :, offset - 1] = found.astype(BF16).reshape(SEGS, PIECE, HEAD_DIM)
            part, span = piece_of(me)

            @pl.loop(1, SEGS)
            def _(step):
                peer = wrapped(me + step)
                remote(
                    chosen.at[head, peer, pl.ds(0, count)],
                    blocks.at[head, pl.ds(1, count), part, span, :],
                    p3_send.at[head], p3_recv.at[head], (level, peer),
                ).start()

            pltpu.make_async_copy(
                chosen.at[head, me, pl.ds(0, count)],
                blocks.at[head, pl.ds(1, count), part, span, :], p3_recv.at[head],
            ).start()

        per_plane(here, send)

    def attend(head):
        here = host_of(head)
        pairs = half(here) + 1
        span_all = [pl.ds(group * ROWS, ROWS) for group in range(GROUP)]

        def block_pair(pair, part):
            return blocks[head, pl.ds(2 * pair, 2), part].reshape(PAIR, HEAD_DIM)

        stats[0] = jnp.full((8, STACK), NEG_FILL, F32)
        for index in range(2):
            for group, span in enumerate(span_all):
                tile = inputs[head, index, :, span]
                stacks[index, span, :] = tile
                turned[index, :, span] = tile.T

        @pl.loop(0, pairs)
        def _(pair):
            span_rows = rows_of(pair, PAIR)
            logits[span_rows, :] = jnp.dot(
                block_pair(pair, 0), turned[0], preferred_element_type=F32
            )
            grad_probs[span_rows, :] = jnp.dot(
                block_pair(pair, 1), turned[1], preferred_element_type=F32
            )

            @pl.when(pair == 0)
            def _():
                u_row = lax.broadcasted_iota(jnp.int32, (ROWS, ROWS), 0)
                t_row = lax.broadcasted_iota(jnp.int32, (ROWS, ROWS), 1)
                for span in span_all:
                    logits[0:ROWS, span] = jnp.where(
                        u_row <= t_row, logits[0:ROWS, span], NEG_FILL
                    )

            @pl.when((pair == pairs - 1) & (odd(here) == 0))
            def _():
                logits[rows_of(here + 1, ROWS), :] = jnp.full((ROWS, STACK), NEG_FILL, F32)

            for span in span_all:
                stats[0, :, span] = jnp.maximum(
                    stats[0, :, span], fold(logits[span_rows, span]).max(0)
                )

        stats[1] = jnp.zeros((8, STACK), F32)
        stats[2] = jnp.zeros((8, STACK), F32)
        stats[0] = jnp.broadcast_to(stats[0].max(0, keepdims=True), (8, STACK))

        @pl.loop(0, pairs)
        def _(pair):
            span_rows = rows_of(pair, PAIR)
            for span in span_all:
                top = stats[0, 0:1, span]
                tile = jnp.exp2((logits[span_rows, span] - top) * EXP2_SCALE)
                logits[span_rows, span] = tile
                stats[1, :, span] += fold(tile).sum(0)
                stats[2, :, span] += fold(tile * grad_probs[span_rows, span]).sum(0)

        inverse = 1.0 / stats[1].sum(0, keepdims=True)
        delta = stats[2].sum(0, keepdims=True) * inverse
        stats[1] = jnp.broadcast_to(inverse, (8, STACK))
        stats[2] = jnp.broadcast_to(delta, (8, STACK))
        query_sum[...] = jnp.zeros((HEAD_DIM, STACK), F32)

        @pl.loop(0, pairs)
        def _(pair):
            span_rows = rows_of(pair, PAIR)
            for span in span_all:
                exact = logits[span_rows, span] * stats[1, 0:1, span]
                probs[:, span] = exact.astype(BF16)
                grad_logits[:, span] = (
                    exact * (grad_probs[span_rows, span] - stats[2, 0:1, span])
                ).astype(BF16)
            value_term = jnp.dot(probs[...], stacks[1], preferred_element_type=F32)
            key_term = SCALE * jnp.dot(
                grad_logits[...], stacks[0], preferred_element_type=F32
            )
            for part, term in enumerate((key_term, value_term)):
                terms[head, pl.ds(2 * pair, 2), part] = term.astype(BF16).reshape(
                    2, ROWS, HEAD_DIM
                )

                @pl.when(pair == 0)
                def _():
                    own[head, part] = term[0:ROWS]

            query_sum[...] += lax.dot_general(
                block_pair(pair, 0), grad_logits[...], (((0,), (0,)), ((), ())),
                preferred_element_type=F32,
            )

        for group, span in enumerate(span_all):
            staged[head, :, span] = (SCALE * query_sum[:, span].T).astype(BF16)

    def query_target(head):
        return grad_queries.at[0, 0, :, lanes(name_of(head), GROUP)]

    def send_results(head):
        host = host_of(head)
        here = host

        def send(count):
            @pl.loop(1, SEGS)
            def _(step):
                peer = wrapped(me + step)
                part, span = piece_of(peer)
                remote(
                    terms.at[head, pl.ds(1, count), part, span, :],
                    term_pieces.at[head, pl.ds(1, count), me],
                    b1_send.at[head], b1_recv.at[head], (level, peer),
                ).start()

            part, span = piece_of(me)
            pltpu.make_async_copy(
                terms.at[head, pl.ds(1, count), part, span, :],
                term_pieces.at[head, pl.ds(1, count), me], b1_recv.at[head],
            ).start()

        per_plane(here, send)
        move(
            head, staged.at[head], query_target(head), d_send.at[head], d_recv.at[head]
        )

        @pl.when(host != level)
        def _():
            own_out[head] = own[head].astype(BF16)
            remote(
                own_out.at[head], own_in.at[head], o_send.at[head], o_recv.at[head], (host, me)
            ).start()

    def summed(head, offset):
        return jnp.dot(
            spread[odd(head), offset],
            term_pieces[head, offset].reshape(SEGS * PIECE, HEAD_DIM),
            preferred_element_type=F32,
        )

    def cross_copy(head, plane):
        return remote(
            cross_out.at[head, plane], cross_in.at[head, plane],
            x_send.at[head, plane], x_recv.at[head, plane], (sibling, me),
        )

    def sum_stage(head):
        here = host_of(head)

        def sums(count):
            wait_bytes(term_pieces.at[head, pl.ds(1, count)], b1_recv.at[head])
            for plane in range((count + 1) // 2):
                offset = jnp.maximum(here - (2 * plane + 1 - core), 1)
                cross_out[head, plane] = summed(head, offset).astype(BF16)
            for plane in range((count - 1) // 2):
                offset = jnp.maximum(here - (2 * plane + core), 1)
                kept[head, plane] = summed(head, offset)

        per_plane(here, sums)

        @pl.loop(0, 4)
        def _(plane):
            @pl.when(here - (2 * plane + 1 - core) >= 1)
            def _():
                cross_copy(head, plane).start()

    def climb_copy(head, plane):
        slot = half(host_of(head)) - 1
        return remote(
            climb_out.at[head, plane], climb_in.at[head, slot],
            c_send.at[head, plane], c_recv.at[head, slot], (device_of(head, plane), me),
        )

    def climb(head):
        plane_here = half(host_of(head))

        @pl.loop(0, plane_here - core + 1)
        def _(plane):
            wait_bytes(cross_in.at[head, plane], x_recv.at[head, plane])

        @pl.loop(0, plane_here)
        def _(plane):
            climb_out[head, plane] = (
                kept[head, plane] + cross_in[head, plane].astype(F32)
            ).astype(BF16)
            climb_copy(head, plane).start()

    def final_send(head):
        host = host_of(head)

        @pl.when(host < LEVELS - 1)
        def _():
            total_sum[...] = jnp.zeros((SEGS * PIECE, HEAD_DIM), F32)

            @pl.loop(half(host), 3)
            def _(slot):
                wait_bytes(climb_in.at[head, slot], c_recv.at[head, slot])
                total_sum[...] += climb_in[head, slot].astype(F32)

            @pl.when(core == 0)
            def _():
                total_sum[...] += cross_in[head, half(host)].astype(F32)

            final_out[head] = total_sum[...].astype(BF16).reshape(SEGS, PIECE, HEAD_DIM)
            part, span = piece_of(me)

            @pl.loop(1, SEGS)
            def _(step):
                peer = wrapped(me + step)
                remote(
                    final_out.at[head, peer], final_in.at[head, part, span, :],
                    f_send.at[head], f_recv.at[head], (host, peer),
                ).start()

            move(
                head, final_out.at[head, me], final_in.at[head, part, span, :],
                f_send.at[head], f_recv.at[head],
            )

    def final_store(head):
        away = host_of(head) != level

        @pl.when(away)
        def _():
            wait_bytes(own_in.at[head], o_recv.at[head])
            own[head] = own_in[head].astype(F32)

        @pl.when(level < LEVELS - 1)
        def _():
            wait_bytes(final_in.at[head], f_recv.at[head])
            own[head] = own[head] + final_in[head].astype(F32)

        grad_kv[0, 0, :, :, lanes(name_of(head))] = own[head].astype(BF16)

    stages = (sum_stage, climb, final_send, final_store)

    @pl.loop(0, KV_HEADS + LAG + len(stages))
    def _(tick):
        @pl.when((tick >= 1) & (tick < KV_HEADS + 1))
        def _():
            select(tick - 1)

        @pl.when(tick < KV_HEADS)
        def _():
            pass_on(tick)

        @pl.when(tick < KV_HEADS - 2)
        def _():
            launch(tick + 2)

        @pl.when(tick == 0)
        def _():
            make_selectors(1)

        @pl.when((tick >= LAG) & (tick < KV_HEADS + LAG))
        def _():
            head = tick - LAG
            per_plane(
                host_of(head),
                lambda count: wait_bytes(blocks.at[head, pl.ds(1, count)], p3_recv.at[head]),
            )
            wait_bytes(blocks.at[head, 0], k_recv.at[head])
            wait_bytes(inputs.at[head], q_recv.at[head])
            attend(head)
            send_results(head)

        for lag, stage in enumerate(stages, LAG + 1):
            @pl.when((tick >= lag) & (tick < KV_HEADS + lag))
            def _():
                stage(tick - lag)

    @pl.loop(0, KV_HEADS)
    def _(head):
        host = host_of(head)
        away = host != level
        wait_bytes(query_target(head), d_recv.at[head])
        wait_bytes(final_out.at[head, pl.ds(1, SEGS - 1)], p1_send.at[head])
        own_lifts(head, lambda copy: copy.wait_send())
        passed_on(head, lambda which: None, lambda copy: copy.wait_send())

        @pl.when(away)
        def _():
            wait_bytes(final_out.at[head, 0], p1_send.at[head])
            wait_bytes(blocks.at[head, 0], k_send.at[head])
            wait_bytes(inputs.at[head], q_send.at[head])
            wait_bytes(staged.at[head], d_send.at[head])
            wait_bytes(own_out.at[head], o_send.at[head])

        def sent(count):
            wait_bytes(chosen.at[head, pl.ds(1, SEGS - 1), pl.ds(0, count)], p3_send.at[head])
            wait_bytes(
                term_pieces.at[head, pl.ds(1, count), pl.ds(1, SEGS - 1)], b1_send.at[head]
            )

        per_plane(host, sent)

        @pl.loop(0, 4)
        def _(plane):
            @pl.when(host - (2 * plane + 1 - core) >= 1)
            def _():
                cross_copy(head, plane).wait_send()

        @pl.loop(0, half(host))
        def _(plane):
            climb_copy(head, plane).wait_send()

        @pl.when(host < LEVELS - 1)
        def _():
            wait_bytes(final_out.at[head, pl.ds(1, SEGS - 1)], f_send.at[head])

            @pl.when(away)
            def _():
                wait_bytes(final_out.at[head, 0], f_send.at[head])


def shards(queries, keys_values, grad_out, parents):
    vmem = pl.BlockSpec(memory_space=pltpu.VMEM)
    smem = pl.BlockSpec(memory_space=pltpu.SMEM)
    anywhere = pl.BlockSpec(memory_space=pl.ANY)
    dma = pltpu.SemaphoreType.DMA
    tile = (SEGS, PIECE, HEAD_DIM)
    flat = (SEGS * PIECE, HEAD_DIM)
    keys_count = LEVELS * ROWS
    part_pair = (2, ROWS, HEAD_DIM)
    selectors = (2, LEVELS, SEGS * PIECE, SEGS * PIECE)
    scratch = [
        pltpu.SMEM((2, LEVELS, SEGS), jnp.int32),
        pltpu.VMEM(selectors, BF16),
        pltpu.VMEM(selectors, BF16),
        pltpu.VMEM((LEVELS, SEGS, PIECE, KV_HEADS * HEAD_DIM), BF16),
        pltpu.VMEM((KV_HEADS, SEGS, LEVELS - 1, PIECE, HEAD_DIM), BF16),
        pltpu.VMEM((KV_HEADS, LEVELS) + part_pair, BF16),
        pltpu.VMEM((KV_HEADS, LEVELS) + part_pair, BF16),
        pltpu.VMEM((KV_HEADS, LEVELS) + tile, BF16),
        pltpu.VMEM((KV_HEADS,) + part_pair, F32),
        pltpu.VMEM((KV_HEADS,) + part_pair, BF16),
        pltpu.VMEM((KV_HEADS,) + part_pair, BF16),
        pltpu.VMEM((KV_HEADS, 2, ROWS, STACK), BF16),
        pltpu.VMEM((2, STACK, HEAD_DIM), BF16),
        pltpu.VMEM((2, HEAD_DIM, STACK), BF16),
        pltpu.VMEM((KV_HEADS, ROWS, STACK), BF16),
        pltpu.VMEM((HEAD_DIM, STACK), F32),
        pltpu.VMEM((3, 8, STACK), F32),
        pltpu.VMEM((keys_count, STACK), F32),
        pltpu.VMEM((keys_count, STACK), F32),
        pltpu.VMEM((PAIR, STACK), BF16),
        pltpu.VMEM((PAIR, STACK), BF16),
        pltpu.VMEM((KV_HEADS, 3) + flat, F32),
        pltpu.VMEM(flat, F32),
        pltpu.VMEM((KV_HEADS, 4) + flat, BF16),
        pltpu.VMEM((KV_HEADS, 4) + flat, BF16),
        pltpu.VMEM((KV_HEADS, 3) + flat, BF16),
        pltpu.VMEM((KV_HEADS, 3) + flat, BF16),
        pltpu.VMEM((KV_HEADS,) + tile, BF16),
        pltpu.VMEM((KV_HEADS,) + part_pair, BF16),
        dma((KV_HEADS,)), dma((KV_HEADS,)),
        dma((KV_HEADS, 7)), dma((KV_HEADS, LEVELS)),
        dma((KV_HEADS,)), dma((KV_HEADS,)),
        dma((KV_HEADS,)), dma((KV_HEADS,)),
        dma((KV_HEADS,)), dma((KV_HEADS,)),
        dma((KV_HEADS,)), dma((KV_HEADS,)),
        dma((KV_HEADS,)), dma((KV_HEADS,)),
        dma((KV_HEADS,)), dma((KV_HEADS,)),
        dma((KV_HEADS, 4)), dma((KV_HEADS, 4)),
        dma((KV_HEADS, 3)), dma((KV_HEADS, 3)),
        dma((KV_HEADS,)), dma((KV_HEADS,)),
    ]
    return pl.pallas_call(
        kernel,
        out_shape=(
            jax.ShapeDtypeStruct(queries.shape, BF16),
            jax.ShapeDtypeStruct(keys_values.shape, BF16),
        ),
        in_specs=[smem, anywhere, anywhere, anywhere],
        out_specs=(vmem, vmem),
        scratch_shapes=scratch,
        compiler_params=pltpu.CompilerParams(
            collective_id=0, has_side_effects=True, vmem_limit_bytes=56 * 1024 * 1024
        ),
        cost_estimate=pl.CostEstimate(
            flops=5 * 2 * HEADS * LEVELS * ROWS * ROWS * HEAD_DIM,
            bytes_accessed=8 * 1024 * 1024,
            transcendentals=HEADS * LEVELS * ROWS * ROWS,
        ),
    )(parents.transpose(0, 2, 1), queries, keys_values, grad_out)


def solution(mesh):
    in_specs = (
        P("depth", "seg", None, None),
        P("depth", "seg", None, None, None),
        P("depth", "seg", None, None),
        P(),
    )
    out_specs = (P("depth", "seg", None, None), P("depth", "seg", None, None, None))
    return jax.shard_map(shards, mesh=mesh, in_specs=in_specs, out_specs=out_specs, check_vma=False)
```

```python
import functools

import jax
import jax.numpy as jnp
from jax import lax
from jax.experimental import pallas as pl
from jax.experimental.pallas import tpu as pltpu
from jax.sharding import PartitionSpec as P

HEADS = 20
KV_HEADS = 4
HEAD_DIM = 128
GROUP = HEADS // KV_HEADS
ROWS = 128
LEVELS = 8
SEGS = 16
PIECE = 16
PIECES_PER_PART = ROWS // PIECE
STACK = GROUP * ROWS
PAIR = 2 * ROWS
LAG = 3

NEG_FILL = -1e30
SCALE = HEAD_DIM ** -0.5
EXP2_SCALE = SCALE * 1.4426950408889634
MESH = pl.DeviceIdType.MESH
BF16 = jnp.bfloat16
F32 = jnp.float32


def half(value):
    return lax.div(value, 2)


def odd(value):
    return lax.rem(value, 2)


def name_of(head):
    return 2 * odd(head) + half(head)


def wrapped(index):
    return jnp.where(index >= SEGS, index - SEGS, index)


def lanes(index, count=1):
    width = count * HEAD_DIM
    return pl.ds(pl.multiple_of(index * width, width), width)


def rows_of(index, count):
    return pl.ds(pl.multiple_of(index * count, count), count)


def piece_of(index):
    part = jnp.where(index >= PIECES_PER_PART, 1, 0)
    return part, rows_of(index - part * PIECES_PER_PART, PIECE)


def fold(tile):
    return tile.reshape(tile.shape[0] // 8, 8, tile.shape[1])


def kernel(
    parents, queries, keys_values, grad_out, grad_queries, grad_kv,
    anc, pick, spread, pieces, chosen, blocks, terms, term_pieces, own, own_out, own_in,
    inputs, stacks, turned, staged, query_sum, stats, logits, grad_probs, probs, grad_logits,
    kept, total_sum, cross_out, cross_in, climb_out, climb_in, final_out, final_in,
    p1_send, p1_recv, up_send, up_recv, q_send, q_recv, k_send, k_recv, p3_send, p3_recv,
    b1_send, b1_recv, o_send, o_recv, d_send, d_recv, x_send, x_recv, c_send, c_recv,
    f_send, f_recv,
):
    level = lax.axis_index("depth")
    me = lax.axis_index("seg")
    y = half(level)
    core = odd(level)
    sibling = 2 * y + 1 - core
    outer = (y == 0) | (y == 3)
    partner = jnp.where(outer, 2 * (3 - y) + core, level)

    def host_of(head):
        return jnp.where(odd(head) == 1, partner, level)

    def device_of(head, plane):
        swapped = (odd(head) == 1) & ((plane == 0) | (plane == 3))
        return 2 * jnp.where(swapped, 3 - plane, plane) + core

    def remote(src, dst, send_sem, recv_sem, device):
        return pltpu.make_async_remote_copy(
            src_ref=src, dst_ref=dst, send_sem=send_sem, recv_sem=recv_sem,
            device_id=device, device_id_type=MESH,
        )

    def wait_bytes(ref, sem):
        pltpu.make_async_copy(ref, ref, sem).wait()

    def per_plane(which, action):
        for plane in range(LEVELS // 2):
            pl.when((which > 0) & (half(which) == plane))(
                functools.partial(action, 2 * plane + 1)
            )

    def move(head, src, dst, send_sem, recv_sem):
        host = host_of(head)

        @pl.when(host != level)
        def _():
            remote(src, dst, send_sem, recv_sem, (host, me)).start()

        @pl.when(host == level)
        def _():
            pltpu.make_async_copy(src, dst, recv_sem).start()

    barrier = pltpu.get_barrier_semaphore()

    def greet(device):
        pl.semaphore_signal(barrier, inc=1, device_id=device, device_id_type=MESH)

    @pl.loop(1, SEGS)
    def _(step):
        greet((level, wrapped(me + step)))

    greet((sibling, me))
    for step in range(1, 4):
        greet((lax.rem(level + 2 * step, LEVELS), me))

    @pl.when(outer)
    def _():
        @pl.loop(0, SEGS)
        def _(step):
            greet((partner, wrapped(me + step)))

    pl.semaphore_wait(barrier, SEGS + 3 + jnp.where(outer, SEGS, 0))

    def spread_out(head):
        host = host_of(head)
        span_lanes = lanes(name_of(head))

        def source(peer):
            part, span = piece_of(peer)
            return keys_values.at[0, 0, part, span, span_lanes]

        landing = pieces.at[level, me, :, span_lanes]

        @pl.loop(1, SEGS)
        def _(step):
            peer = wrapped(me + step)
            remote(
                source(peer), landing, p1_send.at[head], p1_recv.at[head], (host, peer)
            ).start()

        move(head, source(me), landing, p1_send.at[head], p1_recv.at[head])

    def move_inputs(head):
        name = name_of(head)
        move(
            head, keys_values.at[0, 0, :, :, lanes(name)], blocks.at[head, 0],
            k_send.at[head], k_recv.at[head],
        )
        for index, array in enumerate((queries, grad_out)):
            move(
                head, array.at[0, 0, :, lanes(name, GROUP)], inputs.at[head, index],
                q_send.at[head], q_recv.at[head],
            )

    def unit(head, which):
        return pieces.at[which, :, :, lanes(name_of(head))]

    def lift(head, which, slot, device):
        return remote(
            unit(head, which), unit(head, which),
            up_send.at[head, slot], up_recv.at[head, which], (device, me),
        )

    def own_lifts(head, action):
        here = host_of(head)
        plane = half(here)
        plain = odd(head) == 0
        routes = (
            (plain & (plane <= 2), 0, plane + 1),
            (plain & (plane == 0), 1, 3),
            (plain & (plane == 1) & (core == 1), 1, 0),
            ((~plain) & (plane <= 1), 0, 2),
            ((~plain) & (plane <= 1), 1, 3),
            ((~plain) & (plane == 2), 0, 1 - core),
        )
        for condition, slot, target in routes:
            @pl.when(condition)
            def _():
                action(lift(head, here, slot, device_of(head, target)))

        @pl.when(core == 0)
        def _():
            action(lift(head, here, 2, sibling))

    relays = (
        (0, 0, 1, 1, 3),
        (0, 1, 0, 0, 2),
        (0, 2, 1, 0, 3),
        (0, 2, 0, None, None),
        (0, 3, 0, 1, 2),
        (0, 3, 2, None, None),
        (0, 3, 1, None, None),
        (1, 0, 2, 1, 3),
        (1, 1, 2, 0, 3),
        (1, 1, 0, None, None),
        (1, 2, 0, 0, 1),
        (1, 2, 1, None, None),
        (1, 3, 0, 1, 1),
        (1, 3, 1, None, None),
        (1, 3, 2, None, None),
    )

    def passed_on(head, before, action):
        plane_here = half(host_of(head))
        for parity, plane, owner, relay_core, target in relays:
            which = 2 * owner + core
            needed = (plane_here == plane) & (odd(head) == parity)
            if plane < owner:
                needed = needed & (core == relay_core)

            @pl.when(needed)
            def _():
                before(which)
                if target is not None:
                    copy = lift(head, which, 3, device_of(head, target))
                    if plane < owner:
                        action(copy)
                    else:
                        pl.when(core == relay_core)(lambda: action(copy))
                if plane > owner:
                    action(lift(head, which, 4 + owner, sibling))

    def launch(head):
        wait_bytes(
            pieces.at[host_of(head), :, :, lanes(name_of(head))], p1_recv.at[head]
        )
        own_lifts(head, lambda copy: copy.start())

    pl.loop(0, 2)(spread_out)
    pl.loop(0, 2)(launch)
    pl.loop(2, KV_HEADS)(spread_out)

    def make_selectors(parity):
        target_level = host_of(parity)

        @pl.loop(0, SEGS)
        def _(column):
            current = column
            for offset in range(1, LEVELS):
                current = parents[jnp.maximum(target_level - offset, 0), 0, current]
                anc[parity, offset, column] = current

        @pl.loop(1, 2 * half(target_level) + 2)
        def _(offset):
            lane = lax.broadcasted_iota(jnp.int32, (PIECE, SEGS * PIECE), 1)
            row = lax.broadcasted_iota(jnp.int32, (PIECE, SEGS * PIECE), 0)
            target = lane & (PIECE - 1)
            lane_column = lane >> 4
            for column in range(SEGS):
                found = anc[parity, offset, column] * PIECE
                pick[parity, offset, rows_of(column, PIECE), :] = jnp.where(
                    lane == found + row, 1.0, 0.0
                ).astype(BF16)
                target = target + jnp.where(lane_column == column, found, 0)
            for column in range(SEGS):
                spread[parity, offset, rows_of(column, PIECE), :] = jnp.where(
                    target == row + column * PIECE, 1.0, 0.0
                ).astype(BF16)

    make_selectors(0)

    @pl.loop(0, KV_HEADS)
    def _(head):
        @pl.when(host_of(head) == 0)
        def _():
            blocks[head, 1] = jnp.zeros((2, ROWS, HEAD_DIM), BF16)

    def pass_on(head):
        passed_on(
            head,
            lambda which: wait_bytes(unit(head, which), up_recv.at[head, which]),
            lambda copy: copy.start(),
        )

    def select(head):
        here = host_of(head)
        parity = odd(head)

        @pl.loop(0, 4)
        def _(plane):
            other = 2 * plane + 1 - core

            @pl.when(other < here)
            def _():
                wait_bytes(unit(head, other), up_recv.at[head, other])

        def send(count):
            for offset in range(1, count + 1):
                found = jnp.dot(
                    pick[parity, offset],
                    pieces[
                        jnp.maximum(here - offset, 0), :, :, lanes(name_of(head))
                    ].reshape(SEGS * PIECE, HEAD_DIM),
                    preferred_element_type=F32,
                )
                chosen[head, :, offset - 1] = found.astype(BF16).reshape(SEGS, PIECE, HEAD_DIM)
            part, span = piece_of(me)

            @pl.loop(1, SEGS)
            def _(step):
                peer = wrapped(me + step)
                remote(
                    chosen.at[head, peer, pl.ds(0, count)],
                    blocks.at[head, pl.ds(1, count), part, span, :],
                    p3_send.at[head], p3_recv.at[head], (level, peer),
                ).start()

            pltpu.make_async_copy(
                chosen.at[head, me, pl.ds(0, count)],
                blocks.at[head, pl.ds(1, count), part, span, :], p3_recv.at[head],
            ).start()

        per_plane(here, send)

    def attend(head):
        here = host_of(head)
        pairs = half(here) + 1
        span_all = [pl.ds(group * ROWS, ROWS) for group in range(GROUP)]

        def block_pair(pair, part):
            return blocks[head, pl.ds(2 * pair, 2), part].reshape(PAIR, HEAD_DIM)

        stats[0] = jnp.full((8, STACK), NEG_FILL, F32)
        for index in range(2):
            for group, span in enumerate(span_all):
                tile = inputs[head, index, :, span]
                stacks[index, span, :] = tile
                turned[index, :, span] = tile.T

        @pl.loop(0, pairs)
        def _(pair):
            span_rows = rows_of(pair, PAIR)
            logits[span_rows, :] = jnp.dot(
                block_pair(pair, 0), turned[0], preferred_element_type=F32
            )
            grad_probs[span_rows, :] = jnp.dot(
                block_pair(pair, 1), turned[1], preferred_element_type=F32
            )

            @pl.when(pair == 0)
            def _():
                u_row = lax.broadcasted_iota(jnp.int32, (ROWS, ROWS), 0)
                t_row = lax.broadcasted_iota(jnp.int32, (ROWS, ROWS), 1)
                for span in span_all:
                    logits[0:ROWS, span] = jnp.where(
                        u_row <= t_row, logits[0:ROWS, span], NEG_FILL
                    )

            @pl.when((pair == pairs - 1) & (odd(here) == 0))
            def _():
                logits[rows_of(here + 1, ROWS), :] = jnp.full((ROWS, STACK), NEG_FILL, F32)

            for span in span_all:
                stats[0, :, span] = jnp.maximum(
                    stats[0, :, span], fold(logits[span_rows, span]).max(0)
                )

        stats[1] = jnp.zeros((8, STACK), F32)
        stats[2] = jnp.zeros((8, STACK), F32)
        stats[0] = jnp.broadcast_to(stats[0].max(0, keepdims=True), (8, STACK))

        @pl.loop(0, pairs)
        def _(pair):
            span_rows = rows_of(pair, PAIR)
            for span in span_all:
                top = stats[0, 0:1, span]
                tile = jnp.exp2((logits[span_rows, span] - top) * EXP2_SCALE)
                logits[span_rows, span] = tile
                stats[1, :, span] += fold(tile).sum(0)
                stats[2, :, span] += fold(tile * grad_probs[span_rows, span]).sum(0)

        inverse = 1.0 / stats[1].sum(0, keepdims=True)
        delta = stats[2].sum(0, keepdims=True) * inverse
        stats[1] = jnp.broadcast_to(inverse, (8, STACK))
        stats[2] = jnp.broadcast_to(delta, (8, STACK))
        query_sum[...] = jnp.zeros((HEAD_DIM, STACK), F32)

        @pl.loop(0, pairs)
        def _(pair):
            span_rows = rows_of(pair, PAIR)
            for span in span_all:
                exact = logits[span_rows, span] * stats[1, 0:1, span]
                probs[:, span] = exact.astype(BF16)
                grad_logits[:, span] = (
                    exact * (grad_probs[span_rows, span] - stats[2, 0:1, span])
                ).astype(BF16)
            value_term = jnp.dot(probs[...], stacks[1], preferred_element_type=F32)
            key_term = SCALE * jnp.dot(
                grad_logits[...], stacks[0], preferred_element_type=F32
            )
            for part, term in enumerate((key_term, value_term)):
                terms[head, pl.ds(2 * pair, 2), part] = term.astype(BF16).reshape(
                    2, ROWS, HEAD_DIM
                )

                @pl.when(pair == 0)
                def _():
                    own[head, part] = term[0:ROWS]

            query_sum[...] += lax.dot_general(
                block_pair(pair, 0), grad_logits[...], (((0,), (0,)), ((), ())),
                preferred_element_type=F32,
            )

        for group, span in enumerate(span_all):
            staged[head, :, span] = (SCALE * query_sum[:, span].T).astype(BF16)

    def query_target(head):
        return grad_queries.at[0, 0, :, lanes(name_of(head), GROUP)]

    def send_results(head):
        host = host_of(head)
        here = host

        def send(count):
            @pl.loop(1, SEGS)
            def _(step):
                peer = wrapped(me + step)
                part, span = piece_of(peer)
                remote(
                    terms.at[head, pl.ds(1, count), part, span, :],
                    term_pieces.at[head, pl.ds(1, count), me],
                    b1_send.at[head], b1_recv.at[head], (level, peer),
                ).start()

            part, span = piece_of(me)
            pltpu.make_async_copy(
                terms.at[head, pl.ds(1, count), part, span, :],
                term_pieces.at[head, pl.ds(1, count), me], b1_recv.at[head],
            ).start()

        per_plane(here, send)
        move(
            head, staged.at[head], query_target(head), d_send.at[head], d_recv.at[head]
        )

        @pl.when(host != level)
        def _():
            own_out[head] = own[head].astype(BF16)
            remote(
                own_out.at[head], own_in.at[head], o_send.at[head], o_recv.at[head], (host, me)
            ).start()

    def summed(head, offset):
        return jnp.dot(
            spread[odd(head), offset],
            term_pieces[head, offset].reshape(SEGS * PIECE, HEAD_DIM),
            preferred_element_type=F32,
        )

    def cross_copy(head, plane):
        return remote(
            cross_out.at[head, plane], cross_in.at[head, plane],
            x_send.at[head, plane], x_recv.at[head, plane], (sibling, me),
        )

    def sum_stage(head):
        here = host_of(head)

        def sums(count):
            wait_bytes(term_pieces.at[head, pl.ds(1, count)], b1_recv.at[head])
            for plane in range((count + 1) // 2):
                offset = jnp.maximum(here - (2 * plane + 1 - core), 1)
                cross_out[head, plane] = summed(head, offset).astype(BF16)
            for plane in range((count - 1) // 2):
                offset = jnp.maximum(here - (2 * plane + core), 1)
                kept[head, plane] = summed(head, offset)

        per_plane(here, sums)

        @pl.loop(0, 4)
        def _(plane):
            @pl.when(here - (2 * plane + 1 - core) >= 1)
            def _():
                cross_copy(head, plane).start()

    def climb_copy(head, plane):
        slot = half(host_of(head)) - 1
        return remote(
            climb_out.at[head, plane], climb_in.at[head, slot],
            c_send.at[head, plane], c_recv.at[head, slot], (device_of(head, plane), me),
        )

    def climb(head):
        plane_here = half(host_of(head))

        @pl.loop(0, plane_here - core + 1)
        def _(plane):
            wait_bytes(cross_in.at[head, plane], x_recv.at[head, plane])

        @pl.loop(0, plane_here)
        def _(plane):
            climb_out[head, plane] = (
                kept[head, plane] + cross_in[head, plane].astype(F32)
            ).astype(BF16)
            climb_copy(head, plane).start()

    def final_send(head):
        host = host_of(head)

        @pl.when(host < LEVELS - 1)
        def _():
            total_sum[...] = jnp.zeros((SEGS * PIECE, HEAD_DIM), F32)

            @pl.loop(half(host), 3)
            def _(slot):
                wait_bytes(climb_in.at[head, slot], c_recv.at[head, slot])
                total_sum[...] += climb_in[head, slot].astype(F32)

            @pl.when(core == 0)
            def _():
                total_sum[...] += cross_in[head, half(host)].astype(F32)

            final_out[head] = total_sum[...].astype(BF16).reshape(SEGS, PIECE, HEAD_DIM)
            part, span = piece_of(me)

            @pl.loop(1, SEGS)
            def _(step):
                peer = wrapped(me + step)
                remote(
                    final_out.at[head, peer], final_in.at[head, part, span, :],
                    f_send.at[head], f_recv.at[head], (host, peer),
                ).start()

            move(
                head, final_out.at[head, me], final_in.at[head, part, span, :],
                f_send.at[head], f_recv.at[head],
            )

    def final_store(head):
        away = host_of(head) != level

        @pl.when(away)
        def _():
            wait_bytes(own_in.at[head], o_recv.at[head])
            own[head] = own_in[head].astype(F32)

        @pl.when(level < LEVELS - 1)
        def _():
            wait_bytes(final_in.at[head], f_recv.at[head])
            own[head] = own[head] + final_in[head].astype(F32)

        grad_kv[0, 0, :, :, lanes(name_of(head))] = own[head].astype(BF16)

    stages = (sum_stage, climb, final_send, final_store)

    @pl.loop(0, KV_HEADS + LAG + len(stages))
    def _(tick):
        @pl.when((tick >= 1) & (tick < KV_HEADS + 1))
        def _():
            select(tick - 1)

        @pl.when(tick < KV_HEADS)
        def _():
            pass_on(tick)

        @pl.when(tick < KV_HEADS - 2)
        def _():
            launch(tick + 2)

        @pl.when(tick == 0)
        def _():
            make_selectors(1)
            move_inputs(0)
            move_inputs(2)

        @pl.when(tick == KV_HEADS - 1)
        def _():
            move_inputs(1)
            move_inputs(3)

        @pl.when((tick >= LAG) & (tick < KV_HEADS + LAG))
        def _():
            head = tick - LAG
            per_plane(
                host_of(head),
                lambda count: wait_bytes(blocks.at[head, pl.ds(1, count)], p3_recv.at[head]),
            )
            wait_bytes(blocks.at[head, 0], k_recv.at[head])
            wait_bytes(inputs.at[head], q_recv.at[head])
            attend(head)
            send_results(head)

        for lag, stage in enumerate(stages, LAG + 1):
            @pl.when((tick >= lag) & (tick < KV_HEADS + lag))
            def _():
                stage(tick - lag)

    @pl.loop(0, KV_HEADS)
    def _(head):
        host = host_of(head)
        away = host != level
        wait_bytes(query_target(head), d_recv.at[head])
        wait_bytes(final_out.at[head, pl.ds(1, SEGS - 1)], p1_send.at[head])
        own_lifts(head, lambda copy: copy.wait_send())
        passed_on(head, lambda which: None, lambda copy: copy.wait_send())

        @pl.when(away)
        def _():
            wait_bytes(final_out.at[head, 0], p1_send.at[head])
            wait_bytes(blocks.at[head, 0], k_send.at[head])
            wait_bytes(inputs.at[head], q_send.at[head])
            wait_bytes(staged.at[head], d_send.at[head])
            wait_bytes(own_out.at[head], o_send.at[head])

        def sent(count):
            wait_bytes(chosen.at[head, pl.ds(1, SEGS - 1), pl.ds(0, count)], p3_send.at[head])
            wait_bytes(
                term_pieces.at[head, pl.ds(1, count), pl.ds(1, SEGS - 1)], b1_send.at[head]
            )

        per_plane(host, sent)

        @pl.loop(0, 4)
        def _(plane):
            @pl.when(host - (2 * plane + 1 - core) >= 1)
            def _():
                cross_copy(head, plane).wait_send()

        @pl.loop(0, half(host))
        def _(plane):
            climb_copy(head, plane).wait_send()

        @pl.when(host < LEVELS - 1)
        def _():
            wait_bytes(final_out.at[head, pl.ds(1, SEGS - 1)], f_send.at[head])

            @pl.when(away)
            def _():
                wait_bytes(final_out.at[head, 0], f_send.at[head])


def shards(queries, keys_values, grad_out, parents):
    vmem = pl.BlockSpec(memory_space=pltpu.VMEM)
    smem = pl.BlockSpec(memory_space=pltpu.SMEM)
    anywhere = pl.BlockSpec(memory_space=pl.ANY)
    dma = pltpu.SemaphoreType.DMA
    tile = (SEGS, PIECE, HEAD_DIM)
    flat = (SEGS * PIECE, HEAD_DIM)
    keys_count = LEVELS * ROWS
    part_pair = (2, ROWS, HEAD_DIM)
    selectors = (2, LEVELS, SEGS * PIECE, SEGS * PIECE)
    scratch = [
        pltpu.SMEM((2, LEVELS, SEGS), jnp.int32),
        pltpu.VMEM(selectors, BF16),
        pltpu.VMEM(selectors, BF16),
        pltpu.VMEM((LEVELS, SEGS, PIECE, KV_HEADS * HEAD_DIM), BF16),
        pltpu.VMEM((KV_HEADS, SEGS, LEVELS - 1, PIECE, HEAD_DIM), BF16),
        pltpu.VMEM((KV_HEADS, LEVELS) + part_pair, BF16),
        pltpu.VMEM((KV_HEADS, LEVELS) + part_pair, BF16),
        pltpu.VMEM((KV_HEADS, LEVELS) + tile, BF16),
        pltpu.VMEM((KV_HEADS,) + part_pair, F32),
        pltpu.VMEM((KV_HEADS,) + part_pair, BF16),
        pltpu.VMEM((KV_HEADS,) + part_pair, BF16),
        pltpu.VMEM((KV_HEADS, 2, ROWS, STACK), BF16),
        pltpu.VMEM((2, STACK, HEAD_DIM), BF16),
        pltpu.VMEM((2, HEAD_DIM, STACK), BF16),
        pltpu.VMEM((KV_HEADS, ROWS, STACK), BF16),
        pltpu.VMEM((HEAD_DIM, STACK), F32),
        pltpu.VMEM((3, 8, STACK), F32),
        pltpu.VMEM((keys_count, STACK), F32),
        pltpu.VMEM((keys_count, STACK), F32),
        pltpu.VMEM((PAIR, STACK), BF16),
        pltpu.VMEM((PAIR, STACK), BF16),
        pltpu.VMEM((KV_HEADS, 3) + flat, F32),
        pltpu.VMEM(flat, F32),
        pltpu.VMEM((KV_HEADS, 4) + flat, BF16),
        pltpu.VMEM((KV_HEADS, 4) + flat, BF16),
        pltpu.VMEM((KV_HEADS, 3) + flat, BF16),
        pltpu.VMEM((KV_HEADS, 3) + flat, BF16),
        pltpu.VMEM((KV_HEADS,) + tile, BF16),
        pltpu.VMEM((KV_HEADS,) + part_pair, BF16),
        dma((KV_HEADS,)), dma((KV_HEADS,)),
        dma((KV_HEADS, 7)), dma((KV_HEADS, LEVELS)),
        dma((KV_HEADS,)), dma((KV_HEADS,)),
        dma((KV_HEADS,)), dma((KV_HEADS,)),
        dma((KV_HEADS,)), dma((KV_HEADS,)),
        dma((KV_HEADS,)), dma((KV_HEADS,)),
        dma((KV_HEADS,)), dma((KV_HEADS,)),
        dma((KV_HEADS,)), dma((KV_HEADS,)),
        dma((KV_HEADS, 4)), dma((KV_HEADS, 4)),
        dma((KV_HEADS, 3)), dma((KV_HEADS, 3)),
        dma((KV_HEADS,)), dma((KV_HEADS,)),
    ]
    return pl.pallas_call(
        kernel,
        out_shape=(
            jax.ShapeDtypeStruct(queries.shape, BF16),
            jax.ShapeDtypeStruct(keys_values.shape, BF16),
        ),
        in_specs=[smem, anywhere, anywhere, anywhere],
        out_specs=(vmem, vmem),
        scratch_shapes=scratch,
        compiler_params=pltpu.CompilerParams(
            collective_id=0, has_side_effects=True, vmem_limit_bytes=56 * 1024 * 1024
        ),
        cost_estimate=pl.CostEstimate(
            flops=5 * 2 * HEADS * LEVELS * ROWS * ROWS * HEAD_DIM,
            bytes_accessed=8 * 1024 * 1024,
            transcendentals=HEADS * LEVELS * ROWS * ROWS,
        ),
    )(parents.transpose(0, 2, 1), queries, keys_values, grad_out)


def solution(mesh):
    in_specs = (
        P("depth", "seg", None, None),
        P("depth", "seg", None, None, None),
        P("depth", "seg", None, None),
        P(),
    )
    out_specs = (P("depth", "seg", None, None), P("depth", "seg", None, None, None))
    return jax.shard_map(shards, mesh=mesh, in_specs=in_specs, out_specs=out_specs, check_vma=False)
```

```python
import functools

import jax
import jax.numpy as jnp
from jax import lax
from jax.experimental import pallas as pl
from jax.experimental.pallas import tpu as pltpu
from jax.sharding import PartitionSpec as P

HEADS = 20
KV_HEADS = 4
HEAD_DIM = 128
GROUP = HEADS // KV_HEADS
ROWS = 128
LEVELS = 8
SEGS = 16
PIECE = 16
PIECES_PER_PART = ROWS // PIECE
STACK = GROUP * ROWS
PAIR = 2 * ROWS
LAG = 3

NEG_FILL = -1e30
SCALE = HEAD_DIM ** -0.5
EXP2_SCALE = SCALE * 1.4426950408889634
MESH = pl.DeviceIdType.MESH
BF16 = jnp.bfloat16
F32 = jnp.float32


def half(value):
    return lax.div(value, 2)


def odd(value):
    return lax.rem(value, 2)


def name_of(head):
    return 2 * odd(head) + half(head)


def wrapped(index):
    return jnp.where(index >= SEGS, index - SEGS, index)


def lanes(index, count=1):
    width = count * HEAD_DIM
    return pl.ds(pl.multiple_of(index * width, width), width)


def rows_of(index, count):
    return pl.ds(pl.multiple_of(index * count, count), count)


def piece_of(index):
    part = jnp.where(index >= PIECES_PER_PART, 1, 0)
    return part, rows_of(index - part * PIECES_PER_PART, PIECE)


def fold(tile):
    return tile.reshape(tile.shape[0] // 8, 8, tile.shape[1])


def kernel(
    parents, queries, keys_values, grad_out, grad_queries, grad_kv,
    anc, pick, spread, pieces, chosen, blocks, terms, term_pieces, own, own_out, own_in,
    inputs, stacks, staged, query_sum, stats, logits, grad_probs, probs, grad_logits,
    kept, total_sum, cross_out, cross_in, climb_out, climb_in, final_out, final_in,
    p1_send, p1_recv, up_send, up_recv, q_send, q_recv, k_send, k_recv, p3_send, p3_recv,
    b1_send, b1_recv, o_send, o_recv, d_send, d_recv, x_send, x_recv, c_send, c_recv,
    f_send, f_recv,
):
    level = lax.axis_index("depth")
    me = lax.axis_index("seg")
    y = half(level)
    core = odd(level)
    sibling = 2 * y + 1 - core
    outer = (y == 0) | (y == 3)
    partner = jnp.where(outer, 2 * (3 - y) + core, level)

    def host_of(head):
        return jnp.where(odd(head) == 1, partner, level)

    def device_of(head, plane):
        swapped = (odd(head) == 1) & ((plane == 0) | (plane == 3))
        return 2 * jnp.where(swapped, 3 - plane, plane) + core

    def remote(src, dst, send_sem, recv_sem, device):
        return pltpu.make_async_remote_copy(
            src_ref=src, dst_ref=dst, send_sem=send_sem, recv_sem=recv_sem,
            device_id=device, device_id_type=MESH,
        )

    def wait_bytes(ref, sem):
        pltpu.make_async_copy(ref, ref, sem).wait()

    def per_plane(which, action):
        for plane in range(LEVELS // 2):
            pl.when((which > 0) & (half(which) == plane))(
                functools.partial(action, 2 * plane + 1)
            )

    def move(head, src, dst, send_sem, recv_sem):
        host = host_of(head)

        @pl.when(host != level)
        def _():
            remote(src, dst, send_sem, recv_sem, (host, me)).start()

        @pl.when(host == level)
        def _():
            pltpu.make_async_copy(src, dst, recv_sem).start()

    def find_ancestors(parity):
        target_level = host_of(parity)

        @pl.loop(0, SEGS)
        def _(column):
            current = column
            for offset in range(1, LEVELS):
                current = parents[jnp.maximum(target_level - offset, 0), 0, current]
                anc[parity, offset, column] = current

    def make_pick(parity):
        @pl.loop(1, 2 * half(host_of(parity)) + 2)
        def _(offset):
            lane = lax.broadcasted_iota(jnp.int32, (PIECE, SEGS * PIECE), 1)
            row = lax.broadcasted_iota(jnp.int32, (PIECE, SEGS * PIECE), 0)
            ahead = lane - row
            for column in range(SEGS):
                pick[parity, offset, rows_of(column, PIECE), :] = jnp.where(
                    ahead == anc[parity, offset, column] * PIECE, 1.0, 0.0
                ).astype(BF16)

    def make_spread(parity):
        @pl.loop(1, 2 * half(host_of(parity)) + 2)
        def _(offset):
            lane = lax.broadcasted_iota(jnp.int32, (PIECE, SEGS * PIECE), 1)
            row = lax.broadcasted_iota(jnp.int32, (PIECE, SEGS * PIECE), 0)
            lane_column = lane >> 4
            target = (lane & (PIECE - 1)) - row
            for column in range(SEGS):
                target = jnp.where(
                    lane_column == column, target + anc[parity, offset, column] * PIECE, target
                )
            for column in range(SEGS):
                spread[parity, offset, rows_of(column, PIECE), :] = jnp.where(
                    target == column * PIECE, 1.0, 0.0
                ).astype(BF16)

    barrier = pltpu.get_barrier_semaphore()

    def greet(device):
        pl.semaphore_signal(barrier, inc=1, device_id=device, device_id_type=MESH)

    @pl.loop(1, SEGS)
    def _(step):
        greet((level, wrapped(me + step)))

    greet((sibling, me))
    for step in range(1, 4):
        greet((lax.rem(level + 2 * step, LEVELS), me))

    @pl.when(outer)
    def _():
        @pl.loop(0, SEGS)
        def _(step):
            greet((partner, wrapped(me + step)))

    find_ancestors(0)
    pl.semaphore_wait(barrier, SEGS - 1 + 4 + jnp.where(outer, SEGS, 0))

    @pl.loop(0, 2)
    def _(group):
        host = host_of(group)

        def source(peer):
            part, span = piece_of(peer)
            return keys_values.at[0, 0, part, span, lanes(group, 2)]

        @pl.loop(1, SEGS)
        def _(step):
            peer = wrapped(me + step)
            remote(
                source(peer), pieces.at[group, level, me],
                p1_send.at[group], p1_recv.at[group], (host, peer),
            ).start()

        @pl.when(host != level)
        def _():
            remote(
                source(me), pieces.at[group, level, me],
                p1_send.at[group], p1_recv.at[group], (host, me),
            ).start()

        @pl.when(host == level)
        def _():
            pltpu.make_async_copy(
                source(me), pieces.at[group, level, me], p1_recv.at[group]
            ).start()

    def move_inputs(head):
        name = name_of(head)
        move(
            head, keys_values.at[0, 0, :, :, lanes(name)], blocks.at[head, 0],
            k_send.at[head], k_recv.at[head],
        )
        for index, array in enumerate((queries, grad_out)):
            move(
                head, array.at[0, 0, :, lanes(name, GROUP)], inputs.at[head, index],
                q_send.at[head], q_recv.at[head],
            )

    def unit(head, which):
        return pieces.at[odd(head), which, :, :, lanes(half(head))]

    def lift(head, which, slot, device):
        return remote(
            unit(head, which), unit(head, which),
            up_send.at[head, slot], up_recv.at[head, which], (device, me),
        )

    def own_lifts(head, action):
        here = host_of(head)
        plane = half(here)
        for step in range(1, 4):
            @pl.when(plane + step <= 3)
            def _():
                action(lift(head, here, step - 1, device_of(head, plane + step)))

        @pl.when(core == 0)
        def _():
            action(lift(head, here, 3, sibling))

    def passed_on(head, action):
        @pl.loop(0, half(host_of(head)))
        def _(plane):
            action(2 * plane + core, lift(head, 2 * plane + core, 4 + plane, sibling))

    def launch(head):
        @pl.when(head < 2)
        def _():
            wait_bytes(pieces.at[head, host_of(head)], p1_recv.at[head])

        own_lifts(head, lambda copy: copy.start())

    make_pick(0)
    launch(0)

    @pl.loop(0, KV_HEADS)
    def _(head):
        @pl.when(host_of(head) == 0)
        def _():
            blocks[head, 1] = jnp.zeros((2, ROWS, HEAD_DIM), BF16)

    def pass_on(head):
        def forward(which, copy):
            wait_bytes(unit(head, which), up_recv.at[head, which])
            copy.start()

        passed_on(head, forward)

    def select(head):
        here = host_of(head)
        parity = odd(head)

        @pl.loop(0, 4)
        def _(plane):
            other = 2 * plane + 1 - core

            @pl.when(other < here)
            def _():
                wait_bytes(unit(head, other), up_recv.at[head, other])

        def send(count):
            for offset in range(1, count + 1):
                found = jnp.dot(
                    pick[parity, offset],
                    pieces[
                        parity, jnp.maximum(here - offset, 0), :, :, lanes(half(head))
                    ].reshape(SEGS * PIECE, HEAD_DIM),
                    preferred_element_type=F32,
                )
                chosen[head, :, offset - 1] = found.astype(BF16).reshape(SEGS, PIECE, HEAD_DIM)
            part, span = piece_of(me)

            @pl.loop(1, SEGS)
            def _(step):
                peer = wrapped(me + step)
                remote(
                    chosen.at[head, peer, pl.ds(0, count)],
                    blocks.at[head, pl.ds(1, count), part, span, :],
                    p3_send.at[head], p3_recv.at[head], (level, peer),
                ).start()

            pltpu.make_async_copy(
                chosen.at[head, me, pl.ds(0, count)],
                blocks.at[head, pl.ds(1, count), part, span, :], p3_recv.at[head],
            ).start()

        per_plane(here, send)

    def attend(head):
        here = host_of(head)
        pairs = half(here) + 1
        contract_last = (((1,), (1,)), ((), ()))
        span_all = [pl.ds(group * ROWS, ROWS) for group in range(GROUP)]

        def block_pair(pair, part):
            return blocks[head, pl.ds(2 * pair, 2), part].reshape(PAIR, HEAD_DIM)

        stats[0] = jnp.full((8, STACK), NEG_FILL, F32)
        for index in range(2):
            for group, span in enumerate(span_all):
                stacks[index, span, :] = inputs[head, index, :, span]

        @pl.loop(0, pairs)
        def _(pair):
            span_rows = rows_of(pair, PAIR)
            logits[span_rows, :] = lax.dot_general(
                block_pair(pair, 0), stacks[0], contract_last, preferred_element_type=F32
            )
            grad_probs[span_rows, :] = lax.dot_general(
                block_pair(pair, 1), stacks[1], contract_last, preferred_element_type=F32
            )

            @pl.when(pair == 0)
            def _():
                u_row = lax.broadcasted_iota(jnp.int32, (ROWS, ROWS), 0)
                t_row = lax.broadcasted_iota(jnp.int32, (ROWS, ROWS), 1)
                for span in span_all:
                    logits[0:ROWS, span] = jnp.where(
                        u_row <= t_row, logits[0:ROWS, span], NEG_FILL
                    )

            @pl.when((pair == pairs - 1) & (odd(here) == 0))
            def _():
                logits[rows_of(here + 1, ROWS), :] = jnp.full((ROWS, STACK), NEG_FILL, F32)

            for span in span_all:
                stats[0, :, span] = jnp.maximum(
                    stats[0, :, span], fold(logits[span_rows, span]).max(0)
                )

        stats[1] = jnp.zeros((8, STACK), F32)
        stats[2] = jnp.zeros((8, STACK), F32)
        stats[0] = jnp.broadcast_to(stats[0].max(0, keepdims=True), (8, STACK))

        @pl.loop(0, pairs)
        def _(pair):
            span_rows = rows_of(pair, PAIR)
            for span in span_all:
                top = stats[0, 0:1, span]
                tile = jnp.exp2((logits[span_rows, span] - top) * EXP2_SCALE)
                logits[span_rows, span] = tile
                stats[1, :, span] += fold(tile).sum(0)
                stats[2, :, span] += fold(tile * grad_probs[span_rows, span]).sum(0)

        inverse = 1.0 / stats[1].sum(0, keepdims=True)
        delta = stats[2].sum(0, keepdims=True) * inverse
        stats[1] = jnp.broadcast_to(inverse, (8, STACK))
        stats[2] = jnp.broadcast_to(delta, (8, STACK))
        query_sum[...] = jnp.zeros((HEAD_DIM, STACK), F32)

        @pl.loop(0, pairs)
        def _(pair):
            span_rows = rows_of(pair, PAIR)
            for span in span_all:
                exact = logits[span_rows, span] * stats[1, 0:1, span]
                probs[:, span] = exact.astype(BF16)
                grad_logits[:, span] = (
                    exact * (grad_probs[span_rows, span] - stats[2, 0:1, span])
                ).astype(BF16)
            value_term = jnp.dot(probs[...], stacks[1], preferred_element_type=F32)
            key_term = SCALE * jnp.dot(
                grad_logits[...], stacks[0], preferred_element_type=F32
            )
            for part, term in enumerate((key_term, value_term)):
                terms[head, pl.ds(2 * pair, 2), part] = term.astype(BF16).reshape(
                    2, ROWS, HEAD_DIM
                )

                @pl.when(pair == 0)
                def _():
                    own[head, part] = term[0:ROWS]

            query_sum[...] += lax.dot_general(
                block_pair(pair, 0), grad_logits[...], (((0,), (0,)), ((), ())),
                preferred_element_type=F32,
            )

        for group, span in enumerate(span_all):
            staged[head, :, span] = (SCALE * query_sum[:, span].T).astype(BF16)

    def query_target(head):
        return grad_queries.at[0, 0, :, lanes(name_of(head), GROUP)]

    def send_results(head):
        host = host_of(head)
        here = host

        def send(count):
            @pl.loop(1, SEGS)
            def _(step):
                peer = wrapped(me + step)
                part, span = piece_of(peer)
                remote(
                    terms.at[head, pl.ds(1, count), part, span, :],
                    term_pieces.at[head, pl.ds(1, count), me],
                    b1_send.at[head], b1_recv.at[head], (level, peer),
                ).start()

            part, span = piece_of(me)
            pltpu.make_async_copy(
                terms.at[head, pl.ds(1, count), part, span, :],
                term_pieces.at[head, pl.ds(1, count), me], b1_recv.at[head],
            ).start()

        per_plane(here, send)
        move(
            head, staged.at[head], query_target(head), d_send.at[head], d_recv.at[head]
        )

        @pl.when(host != level)
        def _():
            own_out[head] = own[head].astype(BF16)
            remote(
                own_out.at[head], own_in.at[head], o_send.at[head], o_recv.at[head], (host, me)
            ).start()

    def summed(head, offset):
        return jnp.dot(
            spread[odd(head), offset],
            term_pieces[head, offset].reshape(SEGS * PIECE, HEAD_DIM),
            preferred_element_type=F32,
        )

    def cross_copy(head, plane):
        return remote(
            cross_out.at[head, plane], cross_in.at[head, plane],
            x_send.at[head, plane], x_recv.at[head, plane], (sibling, me),
        )

    def sum_stage(head):
        here = host_of(head)

        def sums(count):
            wait_bytes(term_pieces.at[head, pl.ds(1, count)], b1_recv.at[head])
            for plane in range((count + 1) // 2):
                offset = jnp.maximum(here - (2 * plane + 1 - core), 1)
                cross_out[head, plane] = summed(head, offset).astype(BF16)
            for plane in range((count - 1) // 2):
                offset = jnp.maximum(here - (2 * plane + core), 1)
                kept[head, plane] = summed(head, offset)

        per_plane(here, sums)

        @pl.loop(0, 4)
        def _(plane):
            @pl.when(here - (2 * plane + 1 - core) >= 1)
            def _():
                cross_copy(head, plane).start()

    def climb_copy(head, plane):
        slot = half(host_of(head)) - 1
        return remote(
            climb_out.at[head, plane], climb_in.at[head, slot],
            c_send.at[head, plane], c_recv.at[head, slot], (device_of(head, plane), me),
        )

    def climb(head):
        plane_here = half(host_of(head))

        @pl.loop(0, plane_here - core + 1)
        def _(plane):
            wait_bytes(cross_in.at[head, plane], x_recv.at[head, plane])

        @pl.loop(0, plane_here)
        def _(plane):
            climb_out[head, plane] = (
                kept[head, plane] + cross_in[head, plane].astype(F32)
            ).astype(BF16)
            climb_copy(head, plane).start()

    def final_send(head):
        host = host_of(head)

        @pl.when(host < LEVELS - 1)
        def _():
            total_sum[...] = jnp.zeros((SEGS * PIECE, HEAD_DIM), F32)

            @pl.loop(half(host), 3)
            def _(slot):
                wait_bytes(climb_in.at[head, slot], c_recv.at[head, slot])
                total_sum[...] += climb_in[head, slot].astype(F32)

            @pl.when(core == 0)
            def _():
                total_sum[...] += cross_in[head, half(host)].astype(F32)

            final_out[head] = total_sum[...].astype(BF16).reshape(SEGS, PIECE, HEAD_DIM)
            part, span = piece_of(me)

            @pl.loop(1, SEGS)
            def _(step):
                peer = wrapped(me + step)
                remote(
                    final_out.at[head, peer], final_in.at[head, part, span, :],
                    f_send.at[head], f_recv.at[head], (host, peer),
                ).start()

            move(
                head, final_out.at[head, me], final_in.at[head, part, span, :],
                f_send.at[head], f_recv.at[head],
            )

    def final_store(head):
        away = host_of(head) != level

        @pl.when(away)
        def _():
            wait_bytes(own_in.at[head], o_recv.at[head])
            own[head] = own_in[head].astype(F32)

        @pl.when(level < LEVELS - 1)
        def _():
            wait_bytes(final_in.at[head], f_recv.at[head])
            own[head] = own[head] + final_in[head].astype(F32)

        grad_kv[0, 0, :, :, lanes(name_of(head))] = own[head].astype(BF16)

    stages = (sum_stage, climb, final_send, final_store)

    @pl.loop(0, KV_HEADS + LAG + len(stages))
    def _(tick):
        @pl.when((tick >= 1) & (tick < KV_HEADS + 1))
        def _():
            select(tick - 1)

        @pl.when(tick < KV_HEADS - 1)
        def _():
            launch(tick + 1)

        @pl.when(tick < KV_HEADS)
        def _():
            pass_on(tick)

        @pl.when(tick == 0)
        def _():
            find_ancestors(1)
            make_pick(1)

        @pl.when(tick == 2)
        def _():
            move_inputs(0)
            move_inputs(2)
            make_spread(0)
            make_spread(1)

        @pl.when(tick == 3)
        def _():
            move_inputs(1)
            move_inputs(3)

        for lag, stage in reversed(list(enumerate(stages[1:], LAG + 2))):
            @pl.when((tick >= lag) & (tick < KV_HEADS + lag))
            def _():
                stage(tick - lag)

        @pl.when((tick >= LAG) & (tick < KV_HEADS + LAG))
        def _():
            head = tick - LAG
            per_plane(
                host_of(head),
                lambda count: wait_bytes(blocks.at[head, pl.ds(1, count)], p3_recv.at[head]),
            )
            wait_bytes(blocks.at[head, 0], k_recv.at[head])
            wait_bytes(inputs.at[head], q_recv.at[head])
            attend(head)
            send_results(head)

        @pl.when((tick >= LAG + 1) & (tick < KV_HEADS + LAG + 1))
        def _():
            sum_stage(tick - LAG - 1)

    @pl.loop(0, 2)
    def _(group):
        wait_bytes(pieces.at[group, 0, pl.ds(1, SEGS - 1)], p1_send.at[group])

        @pl.when(host_of(group) != level)
        def _():
            wait_bytes(pieces.at[group, 0, 0], p1_send.at[group])

    @pl.loop(0, KV_HEADS)
    def _(head):
        host = host_of(head)
        away = host != level
        wait_bytes(query_target(head), d_recv.at[head])
        own_lifts(head, lambda copy: copy.wait_send())
        passed_on(head, lambda which, copy: copy.wait_send())

        @pl.when(away)
        def _():
            wait_bytes(blocks.at[head, 0], k_send.at[head])
            wait_bytes(inputs.at[head], q_send.at[head])
            wait_bytes(staged.at[head], d_send.at[head])
            wait_bytes(own_out.at[head], o_send.at[head])

        def sent(count):
            wait_bytes(chosen.at[head, pl.ds(1, SEGS - 1), pl.ds(0, count)], p3_send.at[head])
            wait_bytes(
                term_pieces.at[head, pl.ds(1, count), pl.ds(1, SEGS - 1)], b1_send.at[head]
            )

        per_plane(host, sent)

        @pl.loop(0, 4)
        def _(plane):
            @pl.when(host - (2 * plane + 1 - core) >= 1)
            def _():
                cross_copy(head, plane).wait_send()

        @pl.loop(0, half(host))
        def _(plane):
            climb_copy(head, plane).wait_send()

        @pl.when(host < LEVELS - 1)
        def _():
            wait_bytes(final_out.at[head, pl.ds(1, SEGS - 1)], f_send.at[head])

            @pl.when(away)
            def _():
                wait_bytes(final_out.at[head, 0], f_send.at[head])


def shards(queries, keys_values, grad_out, parents):
    vmem = pl.BlockSpec(memory_space=pltpu.VMEM)
    smem = pl.BlockSpec(memory_space=pltpu.SMEM)
    anywhere = pl.BlockSpec(memory_space=pl.ANY)
    dma = pltpu.SemaphoreType.DMA
    tile = (SEGS, PIECE, HEAD_DIM)
    flat = (SEGS * PIECE, HEAD_DIM)
    keys_count = LEVELS * ROWS
    part_pair = (2, ROWS, HEAD_DIM)
    selectors = (2, LEVELS, SEGS * PIECE, SEGS * PIECE)
    scratch = [
        pltpu.SMEM((2, LEVELS, SEGS), jnp.int32),
        pltpu.VMEM(selectors, BF16),
        pltpu.VMEM(selectors, BF16),
        pltpu.VMEM((2, LEVELS, SEGS, PIECE, 2 * HEAD_DIM), BF16),
        pltpu.VMEM((KV_HEADS, SEGS, LEVELS - 1, PIECE, HEAD_DIM), BF16),
        pltpu.VMEM((KV_HEADS, LEVELS) + part_pair, BF16),
        pltpu.VMEM((KV_HEADS, LEVELS) + part_pair, BF16),
        pltpu.VMEM((KV_HEADS, LEVELS) + tile, BF16),
        pltpu.VMEM((KV_HEADS,) + part_pair, F32),
        pltpu.VMEM((KV_HEADS,) + part_pair, BF16),
        pltpu.VMEM((KV_HEADS,) + part_pair, BF16),
        pltpu.VMEM((KV_HEADS, 2, ROWS, STACK), BF16),
        pltpu.VMEM((2, STACK, HEAD_DIM), BF16),
        pltpu.VMEM((KV_HEADS, ROWS, STACK), BF16),
        pltpu.VMEM((HEAD_DIM, STACK), F32),
        pltpu.VMEM((3, 8, STACK), F32),
        pltpu.VMEM((keys_count, STACK), F32),
        pltpu.VMEM((keys_count, STACK), F32),
        pltpu.VMEM((PAIR, STACK), BF16),
        pltpu.VMEM((PAIR, STACK), BF16),
        pltpu.VMEM((KV_HEADS, 3) + flat, F32),
        pltpu.VMEM(flat, F32),
        pltpu.VMEM((KV_HEADS, 4) + flat, BF16),
        pltpu.VMEM((KV_HEADS, 4) + flat, BF16),
        pltpu.VMEM((KV_HEADS, 3) + flat, BF16),
        pltpu.VMEM((KV_HEADS, 3) + flat, BF16),
        pltpu.VMEM((KV_HEADS,) + tile, BF16),
        pltpu.VMEM((KV_HEADS,) + part_pair, BF16),
        dma((2,)), dma((2,)),
        dma((KV_HEADS, 7)), dma((KV_HEADS, LEVELS)),
        dma((KV_HEADS,)), dma((KV_HEADS,)),
        dma((KV_HEADS,)), dma((KV_HEADS,)),
        dma((KV_HEADS,)), dma((KV_HEADS,)),
        dma((KV_HEADS,)), dma((KV_HEADS,)),
        dma((KV_HEADS,)), dma((KV_HEADS,)),
        dma((KV_HEADS,)), dma((KV_HEADS,)),
        dma((KV_HEADS, 4)), dma((KV_HEADS, 4)),
        dma((KV_HEADS, 3)), dma((KV_HEADS, 3)),
        dma((KV_HEADS,)), dma((KV_HEADS,)),
    ]
    return pl.pallas_call(
        kernel,
        out_shape=(
            jax.ShapeDtypeStruct(queries.shape, BF16),
            jax.ShapeDtypeStruct(keys_values.shape, BF16),
        ),
        in_specs=[smem, anywhere, anywhere, anywhere],
        out_specs=(vmem, vmem),
        scratch_shapes=scratch,
        compiler_params=pltpu.CompilerParams(
            collective_id=0, has_side_effects=True, vmem_limit_bytes=56 * 1024 * 1024
        ),
        cost_estimate=pl.CostEstimate(
            flops=5 * 2 * HEADS * LEVELS * ROWS * ROWS * HEAD_DIM,
            bytes_accessed=8 * 1024 * 1024,
            transcendentals=HEADS * LEVELS * ROWS * ROWS,
        ),
    )(parents.transpose(0, 2, 1), queries, keys_values, grad_out)


def solution(mesh):
    in_specs = (
        P("depth", "seg", None, None),
        P("depth", "seg", None, None, None),
        P("depth", "seg", None, None),
        P(),
    )
    out_specs = (P("depth", "seg", None, None), P("depth", "seg", None, None, None))
    return jax.shard_map(shards, mesh=mesh, in_specs=in_specs, out_specs=out_specs, check_vma=False)
```

```python
import functools

import jax
import jax.numpy as jnp
from jax import lax
from jax.experimental import pallas as pl
from jax.experimental.pallas import tpu as pltpu
from jax.sharding import PartitionSpec as P

HEADS = 20
KV_HEADS = 4
HEAD_DIM = 128
GROUP = HEADS // KV_HEADS
ROWS = 128
LEVELS = 8
SEGS = 16
PIECE = 16
PIECES_PER_PART = ROWS // PIECE
STACK = GROUP * ROWS
PAIR = 2 * ROWS
LAG = 2

NEG_FILL = -1e30
SCALE = HEAD_DIM ** -0.5
EXP2_SCALE = SCALE * 1.4426950408889634
MESH = pl.DeviceIdType.MESH
BF16 = jnp.bfloat16
F32 = jnp.float32


def half(value):
    return lax.div(value, 2)


def odd(value):
    return lax.rem(value, 2)


def name_of(head):
    return 2 * odd(head) + half(head)


def wrapped(index):
    return jnp.where(index >= SEGS, index - SEGS, index)


def lanes(index, count=1):
    width = count * HEAD_DIM
    return pl.ds(pl.multiple_of(index * width, width), width)


def rows_of(index, count):
    return pl.ds(pl.multiple_of(index * count, count), count)


def piece_of(index):
    part = jnp.where(index >= PIECES_PER_PART, 1, 0)
    return part, rows_of(index - part * PIECES_PER_PART, PIECE)


def fold(tile):
    return tile.reshape(tile.shape[0] // 8, 8, tile.shape[1])


def kernel(
    parents, queries, keys_values, grad_out, grad_queries, grad_kv,
    anc, pick, spread, pieces, chosen, blocks, terms, term_pieces, own, own_out, own_in,
    inputs, stacks, staged, query_sum, stats, logits, grad_probs, probs, grad_logits,
    kept, total_sum, cross_out, cross_in, climb_out, climb_in, final_out, final_in,
    p1_send, p1_recv, up_send, up_recv, q_send, q_recv, k_send, k_recv, p3_send, p3_recv,
    b1_send, b1_recv, o_send, o_recv, d_send, d_recv, x_send, x_recv, c_send, c_recv,
    f_send, f_recv,
):
    level = lax.axis_index("depth")
    me = lax.axis_index("seg")
    y = half(level)
    core = odd(level)
    sibling = 2 * y + 1 - core
    outer = (y == 0) | (y == 3)
    partner = jnp.where(outer, 2 * (3 - y) + core, level)

    def host_of(head):
        return jnp.where(odd(head) == 1, partner, level)

    def device_of(head, plane):
        swapped = (odd(head) == 1) & ((plane == 0) | (plane == 3))
        return 2 * jnp.where(swapped, 3 - plane, plane) + core

    def remote(src, dst, send_sem, recv_sem, device):
        return pltpu.make_async_remote_copy(
            src_ref=src, dst_ref=dst, send_sem=send_sem, recv_sem=recv_sem,
            device_id=device, device_id_type=MESH,
        )

    def wait_bytes(ref, sem):
        pltpu.make_async_copy(ref, ref, sem).wait()

    def per_plane(which, action):
        for plane in range(LEVELS // 2):
            pl.when((which > 0) & (half(which) == plane))(
                functools.partial(action, 2 * plane + 1)
            )

    def move(head, src, dst, send_sem, recv_sem):
        host = host_of(head)

        @pl.when(host != level)
        def _():
            remote(src, dst, send_sem, recv_sem, (host, me)).start()

        @pl.when(host == level)
        def _():
            pltpu.make_async_copy(src, dst, recv_sem).start()

    def find_ancestors(parity):
        target_level = host_of(parity)

        @pl.loop(0, SEGS)
        def _(column):
            current = column
            for offset in range(1, LEVELS):
                current = parents[jnp.maximum(target_level - offset, 0), 0, current]
                anc[parity, offset, column] = current

    def make_pick(parity):
        @pl.loop(1, 2 * half(host_of(parity)) + 2)
        def _(offset):
            lane = lax.broadcasted_iota(jnp.int32, (PIECE, SEGS * PIECE), 1)
            row = lax.broadcasted_iota(jnp.int32, (PIECE, SEGS * PIECE), 0)
            ahead = lane - row
            for column in range(SEGS):
                pick[parity, offset, rows_of(column, PIECE), :] = jnp.where(
                    ahead == anc[parity, offset, column] * PIECE, 1.0, 0.0
                ).astype(BF16)

    def make_spread(parity):
        @pl.loop(1, 2 * half(host_of(parity)) + 2)
        def _(offset):
            lane = lax.broadcasted_iota(jnp.int32, (PIECE, SEGS * PIECE), 1)
            row = lax.broadcasted_iota(jnp.int32, (PIECE, SEGS * PIECE), 0)
            lane_column = lane >> 4
            target = (lane & (PIECE - 1)) - row
            for column in range(SEGS):
                target = jnp.where(
                    lane_column == column, target + anc[parity, offset, column] * PIECE, target
                )
            for column in range(SEGS):
                spread[parity, offset, rows_of(column, PIECE), :] = jnp.where(
                    target == column * PIECE, 1.0, 0.0
                ).astype(BF16)

    barrier = pltpu.get_barrier_semaphore()

    def greet(device):
        pl.semaphore_signal(barrier, inc=1, device_id=device, device_id_type=MESH)

    @pl.loop(1, SEGS)
    def _(step):
        greet((level, wrapped(me + step)))

    greet((sibling, me))
    for step in range(1, 4):
        greet((lax.rem(level + 2 * step, LEVELS), me))

    @pl.when(outer)
    def _():
        @pl.loop(0, SEGS)
        def _(step):
            greet((partner, wrapped(me + step)))

    find_ancestors(0)
    pl.semaphore_wait(barrier, SEGS - 1 + 4 + jnp.where(outer, SEGS, 0))

    @pl.loop(0, 2)
    def _(group):
        host = host_of(group)

        def source(peer):
            part, span = piece_of(peer)
            return keys_values.at[0, 0, part, span, lanes(group, 2)]

        @pl.loop(1, SEGS)
        def _(step):
            peer = wrapped(me + step)
            remote(
                source(peer), pieces.at[group, level, me],
                p1_send.at[group], p1_recv.at[group], (host, peer),
            ).start()

        @pl.when(host != level)
        def _():
            remote(
                source(me), pieces.at[group, level, me],
                p1_send.at[group], p1_recv.at[group], (host, me),
            ).start()

        @pl.when(host == level)
        def _():
            pltpu.make_async_copy(
                source(me), pieces.at[group, level, me], p1_recv.at[group]
            ).start()

    def move_inputs(head):
        name = name_of(head)
        move(
            head, keys_values.at[0, 0, :, :, lanes(name)], blocks.at[head, 0],
            k_send.at[head], k_recv.at[head],
        )
        for index, array in enumerate((queries, grad_out)):
            move(
                head, array.at[0, 0, :, lanes(name, GROUP)], inputs.at[head, index],
                q_send.at[head], q_recv.at[head],
            )

    def unit(head, which):
        return pieces.at[odd(head), which, :, :, lanes(half(head))]

    def lift(head, which, slot, device):
        return remote(
            unit(head, which), unit(head, which),
            up_send.at[head, slot], up_recv.at[head, which], (device, me),
        )

    def own_lifts(head, action):
        here = host_of(head)
        plane = half(here)
        for step in range(1, 4):
            @pl.when(plane + step <= 3)
            def _():
                action(lift(head, here, step - 1, device_of(head, plane + step)))

        @pl.when(core == 0)
        def _():
            action(lift(head, here, 3, sibling))

    def passed_on(head, action):
        @pl.loop(0, half(host_of(head)))
        def _(plane):
            action(2 * plane + core, lift(head, 2 * plane + core, 4 + plane, sibling))

    def launch(head):
        @pl.when(head < 2)
        def _():
            wait_bytes(pieces.at[head, host_of(head)], p1_recv.at[head])

        own_lifts(head, lambda copy: copy.start())
        move_inputs(head)

    make_pick(0)
    launch(0)

    @pl.loop(0, KV_HEADS)
    def _(head):
        @pl.when(host_of(head) == 0)
        def _():
            blocks[head, 1] = jnp.zeros((2, ROWS, HEAD_DIM), BF16)

    def pass_on(head):
        def forward(which, copy):
            wait_bytes(unit(head, which), up_recv.at[head, which])
            copy.start()

        passed_on(head, forward)

    def select(head):
        here = host_of(head)
        parity = odd(head)

        @pl.loop(0, 4)
        def _(plane):
            other = 2 * plane + 1 - core

            @pl.when(other < here)
            def _():
                wait_bytes(unit(head, other), up_recv.at[head, other])

        def send(count):
            for offset in range(1, count + 1):
                found = jnp.dot(
                    pick[parity, offset],
                    pieces[
                        parity, jnp.maximum(here - offset, 0), :, :, lanes(half(head))
                    ].reshape(SEGS * PIECE, HEAD_DIM),
                    preferred_element_type=F32,
                )
                chosen[head, :, offset - 1] = found.astype(BF16).reshape(SEGS, PIECE, HEAD_DIM)
            part, span = piece_of(me)

            @pl.loop(1, SEGS)
            def _(step):
                peer = wrapped(me + step)
                remote(
                    chosen.at[head, peer, pl.ds(0, count)],
                    blocks.at[head, pl.ds(1, count), part, span, :],
                    p3_send.at[head], p3_recv.at[head], (level, peer),
                ).start()

            pltpu.make_async_copy(
                chosen.at[head, me, pl.ds(0, count)],
                blocks.at[head, pl.ds(1, count), part, span, :], p3_recv.at[head],
            ).start()

        per_plane(here, send)

    def attend(head):
        here = host_of(head)
        pairs = half(here) + 1
        contract_last = (((1,), (1,)), ((), ()))
        span_all = [pl.ds(group * ROWS, ROWS) for group in range(GROUP)]

        def block_pair(pair, part):
            return blocks[head, pl.ds(2 * pair, 2), part].reshape(PAIR, HEAD_DIM)

        stats[0] = jnp.full((8, STACK), NEG_FILL, F32)
        for index in range(2):
            for group, span in enumerate(span_all):
                stacks[index, span, :] = inputs[head, index, :, span]

        @pl.loop(0, pairs)
        def _(pair):
            span_rows = rows_of(pair, PAIR)
            logits[span_rows, :] = lax.dot_general(
                block_pair(pair, 0), stacks[0], contract_last, preferred_element_type=F32
            )
            grad_probs[span_rows, :] = lax.dot_general(
                block_pair(pair, 1), stacks[1], contract_last, preferred_element_type=F32
            )

            @pl.when(pair == 0)
            def _():
                u_row = lax.broadcasted_iota(jnp.int32, (ROWS, ROWS), 0)
                t_row = lax.broadcasted_iota(jnp.int32, (ROWS, ROWS), 1)
                for span in span_all:
                    logits[0:ROWS, span] = jnp.where(
                        u_row <= t_row, logits[0:ROWS, span], NEG_FILL
                    )

            @pl.when((pair == pairs - 1) & (odd(here) == 0))
            def _():
                logits[rows_of(here + 1, ROWS), :] = jnp.full((ROWS, STACK), NEG_FILL, F32)

            for span in span_all:
                stats[0, :, span] = jnp.maximum(
                    stats[0, :, span], fold(logits[span_rows, span]).max(0)
                )

        stats[1] = jnp.zeros((8, STACK), F32)
        stats[2] = jnp.zeros((8, STACK), F32)
        stats[0] = jnp.broadcast_to(stats[0].max(0, keepdims=True), (8, STACK))

        @pl.loop(0, pairs)
        def _(pair):
            span_rows = rows_of(pair, PAIR)
            for span in span_all:
                top = stats[0, 0:1, span]
                tile = jnp.exp2((logits[span_rows, span] - top) * EXP2_SCALE)
                logits[span_rows, span] = tile
                stats[1, :, span] += fold(tile).sum(0)
                stats[2, :, span] += fold(tile * grad_probs[span_rows, span]).sum(0)

        inverse = 1.0 / stats[1].sum(0, keepdims=True)
        delta = stats[2].sum(0, keepdims=True) * inverse
        stats[1] = jnp.broadcast_to(inverse, (8, STACK))
        stats[2] = jnp.broadcast_to(delta, (8, STACK))
        query_sum[...] = jnp.zeros((HEAD_DIM, STACK), F32)

        @pl.loop(0, pairs)
        def _(pair):
            span_rows = rows_of(pair, PAIR)
            for span in span_all:
                exact = logits[span_rows, span] * stats[1, 0:1, span]
                probs[:, span] = exact.astype(BF16)
                grad_logits[:, span] = (
                    exact * (grad_probs[span_rows, span] - stats[2, 0:1, span])
                ).astype(BF16)
            value_term = jnp.dot(probs[...], stacks[1], preferred_element_type=F32)
            key_term = SCALE * jnp.dot(
                grad_logits[...], stacks[0], preferred_element_type=F32
            )
            for part, term in enumerate((key_term, value_term)):
                terms[head, pl.ds(2 * pair, 2), part] = term.astype(BF16).reshape(
                    2, ROWS, HEAD_DIM
                )

                @pl.when(pair == 0)
                def _():
                    own[head, part] = term[0:ROWS]

            query_sum[...] += lax.dot_general(
                block_pair(pair, 0), grad_logits[...], (((0,), (0,)), ((), ())),
                preferred_element_type=F32,
            )

        for group, span in enumerate(span_all):
            staged[head, :, span] = (SCALE * query_sum[:, span].T).astype(BF16)

    def query_target(head):
        return grad_queries.at[0, 0, :, lanes(name_of(head), GROUP)]

    def send_results(head):
        host = host_of(head)
        here = host

        def send(count):
            @pl.loop(1, SEGS)
            def _(step):
                peer = wrapped(me + step)
                part, span = piece_of(peer)
                remote(
                    terms.at[head, pl.ds(1, count), part, span, :],
                    term_pieces.at[head, pl.ds(1, count), me],
                    b1_send.at[head], b1_recv.at[head], (level, peer),
                ).start()

            part, span = piece_of(me)
            pltpu.make_async_copy(
                terms.at[head, pl.ds(1, count), part, span, :],
                term_pieces.at[head, pl.ds(1, count), me], b1_recv.at[head],
            ).start()

        per_plane(here, send)
        move(
            head, staged.at[head], query_target(head), d_send.at[head], d_recv.at[head]
        )

        @pl.when(host != level)
        def _():
            own_out[head] = own[head].astype(BF16)
            remote(
                own_out.at[head], own_in.at[head], o_send.at[head], o_recv.at[head], (host, me)
            ).start()

    def summed(head, offset):
        return jnp.dot(
            spread[odd(head), offset],
            term_pieces[head, offset].reshape(SEGS * PIECE, HEAD_DIM),
            preferred_element_type=F32,
        )

    def cross_copy(head, plane):
        return remote(
            cross_out.at[head, plane], cross_in.at[head, plane],
            x_send.at[head, plane], x_recv.at[head, plane], (sibling, me),
        )

    def sum_stage(head):
        here = host_of(head)

        def sums(count):
            wait_bytes(term_pieces.at[head, pl.ds(1, count)], b1_recv.at[head])
            for plane in range((count + 1) // 2):
                offset = jnp.maximum(here - (2 * plane + 1 - core), 1)
                cross_out[head, plane] = summed(head, offset).astype(BF16)
            for plane in range((count - 1) // 2):
                offset = jnp.maximum(here - (2 * plane + core), 1)
                kept[head, plane] = summed(head, offset)

        per_plane(here, sums)

        @pl.loop(0, 4)
        def _(plane):
            @pl.when(here - (2 * plane + 1 - core) >= 1)
            def _():
                cross_copy(head, plane).start()

    def climb_copy(head, plane):
        slot = half(host_of(head)) - 1
        return remote(
            climb_out.at[head, plane], climb_in.at[head, slot],
            c_send.at[head, plane], c_recv.at[head, slot], (device_of(head, plane), me),
        )

    def climb(head):
        plane_here = half(host_of(head))

        @pl.loop(0, plane_here - core + 1)
        def _(plane):
            wait_bytes(cross_in.at[head, plane], x_recv.at[head, plane])

        @pl.loop(0, plane_here)
        def _(plane):
            climb_out[head, plane] = (
                kept[head, plane] + cross_in[head, plane].astype(F32)
            ).astype(BF16)
            climb_copy(head, plane).start()

    def final_send(head):
        host = host_of(head)

        @pl.when(host < LEVELS - 1)
        def _():
            total_sum[...] = jnp.zeros((SEGS * PIECE, HEAD_DIM), F32)

            @pl.loop(half(host), 3)
            def _(slot):
                wait_bytes(climb_in.at[head, slot], c_recv.at[head, slot])
                total_sum[...] += climb_in[head, slot].astype(F32)

            @pl.when(core == 0)
            def _():
                total_sum[...] += cross_in[head, half(host)].astype(F32)

            final_out[head] = total_sum[...].astype(BF16).reshape(SEGS, PIECE, HEAD_DIM)
            part, span = piece_of(me)

            @pl.loop(1, SEGS)
            def _(step):
                peer = wrapped(me + step)
                remote(
                    final_out.at[head, peer], final_in.at[head, part, span, :],
                    f_send.at[head], f_recv.at[head], (host, peer),
                ).start()

            move(
                head, final_out.at[head, me], final_in.at[head, part, span, :],
                f_send.at[head], f_recv.at[head],
            )

    def final_store(head):
        away = host_of(head) != level

        @pl.when(away)
        def _():
            wait_bytes(own_in.at[head], o_recv.at[head])
            own[head] = own_in[head].astype(F32)

        @pl.when(level < LEVELS - 1)
        def _():
            wait_bytes(final_in.at[head], f_recv.at[head])
            own[head] = own[head] + final_in[head].astype(F32)

        grad_kv[0, 0, :, :, lanes(name_of(head))] = own[head].astype(BF16)

    stages = (sum_stage, climb, final_send, final_store)

    @pl.loop(0, KV_HEADS + LAG + len(stages))
    def _(tick):
        @pl.when((tick >= 1) & (tick < KV_HEADS + 1))
        def _():
            select(tick - 1)

        @pl.when(tick < KV_HEADS - 1)
        def _():
            launch(tick + 1)

        @pl.when(tick < KV_HEADS)
        def _():
            pass_on(tick)

        @pl.when(tick == 0)
        def _():
            find_ancestors(1)
            make_pick(1)

        @pl.when(tick == 2)
        def _():
            make_spread(0)
            make_spread(1)

        for lag, stage in reversed(list(enumerate(stages[1:], LAG + 2))):
            @pl.when((tick >= lag) & (tick < KV_HEADS + lag))
            def _():
                stage(tick - lag)

        @pl.when((tick >= LAG) & (tick < KV_HEADS + LAG))
        def _():
            head = tick - LAG
            per_plane(
                host_of(head),
                lambda count: wait_bytes(blocks.at[head, pl.ds(1, count)], p3_recv.at[head]),
            )
            wait_bytes(blocks.at[head, 0], k_recv.at[head])
            wait_bytes(inputs.at[head], q_recv.at[head])
            attend(head)
            send_results(head)

        @pl.when((tick >= LAG + 1) & (tick < KV_HEADS + LAG + 1))
        def _():
            sum_stage(tick - LAG - 1)

    @pl.loop(0, 2)
    def _(group):
        wait_bytes(pieces.at[group, 0, pl.ds(1, SEGS - 1)], p1_send.at[group])

        @pl.when(host_of(group) != level)
        def _():
            wait_bytes(pieces.at[group, 0, 0], p1_send.at[group])

    @pl.loop(0, KV_HEADS)
    def _(head):
        host = host_of(head)
        away = host != level
        wait_bytes(query_target(head), d_recv.at[head])
        own_lifts(head, lambda copy: copy.wait_send())
        passed_on(head, lambda which, copy: copy.wait_send())

        @pl.when(away)
        def _():
            wait_bytes(blocks.at[head, 0], k_send.at[head])
            wait_bytes(inputs.at[head], q_send.at[head])
            wait_bytes(staged.at[head], d_send.at[head])
            wait_bytes(own_out.at[head], o_send.at[head])

        def sent(count):
            wait_bytes(chosen.at[head, pl.ds(1, SEGS - 1), pl.ds(0, count)], p3_send.at[head])
            wait_bytes(
                term_pieces.at[head, pl.ds(1, count), pl.ds(1, SEGS - 1)], b1_send.at[head]
            )

        per_plane(host, sent)

        @pl.loop(0, 4)
        def _(plane):
            @pl.when(host - (2 * plane + 1 - core) >= 1)
            def _():
                cross_copy(head, plane).wait_send()

        @pl.loop(0, half(host))
        def _(plane):
            climb_copy(head, plane).wait_send()

        @pl.when(host < LEVELS - 1)
        def _():
            wait_bytes(final_out.at[head, pl.ds(1, SEGS - 1)], f_send.at[head])

            @pl.when(away)
            def _():
                wait_bytes(final_out.at[head, 0], f_send.at[head])


def shards(queries, keys_values, grad_out, parents):
    vmem = pl.BlockSpec(memory_space=pltpu.VMEM)
    smem = pl.BlockSpec(memory_space=pltpu.SMEM)
    anywhere = pl.BlockSpec(memory_space=pl.ANY)
    dma = pltpu.SemaphoreType.DMA
    tile = (SEGS, PIECE, HEAD_DIM)
    flat = (SEGS * PIECE, HEAD_DIM)
    keys_count = LEVELS * ROWS
    part_pair = (2, ROWS, HEAD_DIM)
    selectors = (2, LEVELS, SEGS * PIECE, SEGS * PIECE)
    scratch = [
        pltpu.SMEM((2, LEVELS, SEGS), jnp.int32),
        pltpu.VMEM(selectors, BF16),
        pltpu.VMEM(selectors, BF16),
        pltpu.VMEM((2, LEVELS, SEGS, PIECE, 2 * HEAD_DIM), BF16),
        pltpu.VMEM((KV_HEADS, SEGS, LEVELS - 1, PIECE, HEAD_DIM), BF16),
        pltpu.VMEM((KV_HEADS, LEVELS) + part_pair, BF16),
        pltpu.VMEM((KV_HEADS, LEVELS) + part_pair, BF16),
        pltpu.VMEM((KV_HEADS, LEVELS) + tile, BF16),
        pltpu.VMEM((KV_HEADS,) + part_pair, F32),
        pltpu.VMEM((KV_HEADS,) + part_pair, BF16),
        pltpu.VMEM((KV_HEADS,) + part_pair, BF16),
        pltpu.VMEM((KV_HEADS, 2, ROWS, STACK), BF16),
        pltpu.VMEM((2, STACK, HEAD_DIM), BF16),
        pltpu.VMEM((KV_HEADS, ROWS, STACK), BF16),
        pltpu.VMEM((HEAD_DIM, STACK), F32),
        pltpu.VMEM((3, 8, STACK), F32),
        pltpu.VMEM((keys_count, STACK), F32),
        pltpu.VMEM((keys_count, STACK), F32),
        pltpu.VMEM((PAIR, STACK), BF16),
        pltpu.VMEM((PAIR, STACK), BF16),
        pltpu.VMEM((KV_HEADS, 3) + flat, F32),
        pltpu.VMEM(flat, F32),
        pltpu.VMEM((KV_HEADS, 4) + flat, BF16),
        pltpu.VMEM((KV_HEADS, 4) + flat, BF16),
        pltpu.VMEM((KV_HEADS, 3) + flat, BF16),
        pltpu.VMEM((KV_HEADS, 3) + flat, BF16),
        pltpu.VMEM((KV_HEADS,) + tile, BF16),
        pltpu.VMEM((KV_HEADS,) + part_pair, BF16),
        dma((2,)), dma((2,)),
        dma((KV_HEADS, 7)), dma((KV_HEADS, LEVELS)),
        dma((KV_HEADS,)), dma((KV_HEADS,)),
        dma((KV_HEADS,)), dma((KV_HEADS,)),
        dma((KV_HEADS,)), dma((KV_HEADS,)),
        dma((KV_HEADS,)), dma((KV_HEADS,)),
        dma((KV_HEADS,)), dma((KV_HEADS,)),
        dma((KV_HEADS,)), dma((KV_HEADS,)),
        dma((KV_HEADS, 4)), dma((KV_HEADS, 4)),
        dma((KV_HEADS, 3)), dma((KV_HEADS, 3)),
        dma((KV_HEADS,)), dma((KV_HEADS,)),
    ]
    return pl.pallas_call(
        kernel,
        out_shape=(
            jax.ShapeDtypeStruct(queries.shape, BF16),
            jax.ShapeDtypeStruct(keys_values.shape, BF16),
        ),
        in_specs=[smem, anywhere, anywhere, anywhere],
        out_specs=(vmem, vmem),
        scratch_shapes=scratch,
        compiler_params=pltpu.CompilerParams(
            collective_id=0, has_side_effects=True, vmem_limit_bytes=56 * 1024 * 1024
        ),
        cost_estimate=pl.CostEstimate(
            flops=5 * 2 * HEADS * LEVELS * ROWS * ROWS * HEAD_DIM,
            bytes_accessed=8 * 1024 * 1024,
            transcendentals=HEADS * LEVELS * ROWS * ROWS,
        ),
    )(parents.transpose(0, 2, 1), queries, keys_values, grad_out)


def solution(mesh):
    in_specs = (
        P("depth", "seg", None, None),
        P("depth", "seg", None, None, None),
        P("depth", "seg", None, None),
        P(),
    )
    out_specs = (P("depth", "seg", None, None), P("depth", "seg", None, None, None))
    return jax.shard_map(shards, mesh=mesh, in_specs=in_specs, out_specs=out_specs, check_vma=False)
```

```python
import functools

import jax
import jax.numpy as jnp
from jax import lax
from jax.experimental import pallas as pl
from jax.experimental.pallas import tpu as pltpu
from jax.sharding import PartitionSpec as P

HEADS = 20
KV_HEADS = 4
HEAD_DIM = 128
GROUP = HEADS // KV_HEADS
ROWS = 128
LEVELS = 8
SEGS = 16
PIECE = 16
PIECES_PER_PART = ROWS // PIECE
STACK = GROUP * ROWS
PAIR = 2 * ROWS
LAG = 2

NEG_FILL = -1e30
SCALE = HEAD_DIM ** -0.5
EXP2_SCALE = SCALE * 1.4426950408889634
MESH = pl.DeviceIdType.MESH
BF16 = jnp.bfloat16
F32 = jnp.float32


def half(value):
    return lax.div(value, 2)


def odd(value):
    return lax.rem(value, 2)


def name_of(head):
    return 2 * odd(head) + half(head)


def wrapped(index):
    return jnp.where(index >= SEGS, index - SEGS, index)


def lanes(index, count=1):
    width = count * HEAD_DIM
    return pl.ds(pl.multiple_of(index * width, width), width)


def rows_of(index, count):
    return pl.ds(pl.multiple_of(index * count, count), count)


def piece_of(index):
    part = jnp.where(index >= PIECES_PER_PART, 1, 0)
    return part, rows_of(index - part * PIECES_PER_PART, PIECE)


def fold(tile):
    return tile.reshape(tile.shape[0] // 8, 8, tile.shape[1])


def kernel(
    parents, queries, keys_values, grad_out, grad_queries, grad_kv,
    anc, pick, spread, kv_in, kv_stage, pieces, chosen, blocks, own_blocks, whole,
    terms, term_pieces, own, own_out, own_in,
    inputs, stacks, staged, query_sum, stats, logits, grad_probs, probs, grad_logits,
    kept, total_sum, cross_out, cross_in, climb_out, climb_in, final_out, final_in,
    kv_sem, p1_send, p1_recv, up_send, up_recv, q_send, q_recv, k_send, k_recv, p3_send, p3_recv,
    b1_send, b1_recv, o_send, o_recv, d_send, d_recv, x_send, x_recv, c_send, c_recv,
    f_send, f_recv,
):
    level = lax.axis_index("depth")
    me = lax.axis_index("seg")
    y = half(level)
    core = odd(level)
    sibling = 2 * y + 1 - core
    outer = (y == 0) | (y == 3)
    partner = jnp.where(outer, 2 * (3 - y) + core, level)

    def host_of(head):
        return jnp.where(odd(head) == 1, partner, level)

    def device_of(head, plane):
        swapped = (odd(head) == 1) & ((plane == 0) | (plane == 3))
        return 2 * jnp.where(swapped, 3 - plane, plane) + core

    def remote(src, dst, send_sem, recv_sem, device):
        return pltpu.make_async_remote_copy(
            src_ref=src, dst_ref=dst, send_sem=send_sem, recv_sem=recv_sem,
            device_id=device, device_id_type=MESH,
        )

    def wait_bytes(ref, sem):
        pltpu.make_async_copy(ref, ref, sem).wait()

    def per_plane(which, action):
        for plane in range(LEVELS // 2):
            pl.when((which > 0) & (half(which) == plane))(
                functools.partial(action, 2 * plane + 1)
            )

    def move(head, src, dst, send_sem, recv_sem):
        host = host_of(head)

        @pl.when(host != level)
        def _():
            remote(src, dst, send_sem, recv_sem, (host, me)).start()

        @pl.when(host == level)
        def _():
            pltpu.make_async_copy(src, dst, recv_sem).start()

    def find_ancestors(parity):
        target_level = host_of(parity)

        @pl.loop(0, SEGS)
        def _(column):
            current = column
            for offset in range(1, LEVELS):
                current = parents[jnp.maximum(target_level - offset, 0), 0, current]
                anc[parity, offset, column] = current

    def make_pick(parity):
        @pl.loop(1, 2 * half(host_of(parity)) + 2)
        def _(offset):
            lane = lax.broadcasted_iota(jnp.int32, (PIECE, SEGS * PIECE), 1)
            row = lax.broadcasted_iota(jnp.int32, (PIECE, SEGS * PIECE), 0)
            ahead = lane - row
            for column in range(SEGS):
                pick[parity, offset, rows_of(column, PIECE), :] = jnp.where(
                    ahead == anc[parity, offset, column] * PIECE, 1.0, 0.0
                ).astype(BF16)

    def make_spread(parity):
        @pl.loop(1, 2 * half(host_of(parity)) + 2)
        def _(offset):
            lane = lax.broadcasted_iota(jnp.int32, (PIECE, SEGS * PIECE), 1)
            row = lax.broadcasted_iota(jnp.int32, (PIECE, SEGS * PIECE), 0)
            lane_column = lane >> 4
            target = (lane & (PIECE - 1)) - row
            for column in range(SEGS):
                target = jnp.where(
                    lane_column == column, target + anc[parity, offset, column] * PIECE, target
                )
            for column in range(SEGS):
                spread[parity, offset, rows_of(column, PIECE), :] = jnp.where(
                    target == column * PIECE, 1.0, 0.0
                ).astype(BF16)

    barrier = pltpu.get_barrier_semaphore()

    def greet(device):
        pl.semaphore_signal(barrier, inc=1, device_id=device, device_id_type=MESH)

    load = pltpu.make_async_copy(keys_values, kv_in, kv_sem)
    load.start()

    @pl.loop(1, SEGS)
    def _(step):
        greet((level, wrapped(me + step)))

    greet((sibling, me))
    for step in range(1, 4):
        greet((lax.rem(level + 2 * step, LEVELS), me))

    @pl.when(outer)
    def _():
        @pl.loop(0, SEGS)
        def _(step):
            greet((partner, wrapped(me + step)))

    find_ancestors(0)
    load.wait()
    for name in range(KV_HEADS):
        for part in range(2):
            kv_stage[name, pl.ds(part * PIECES_PER_PART, PIECES_PER_PART)] = kv_in[
                0, 0, part, :, name * HEAD_DIM:(name + 1) * HEAD_DIM
            ].reshape(PIECES_PER_PART, PIECE, HEAD_DIM)
    pl.semaphore_wait(barrier, SEGS - 1 + 4 + jnp.where(outer, SEGS, 0))

    @pl.loop(0, 2)
    def _(group):
        host = host_of(group)

        names = pl.ds(2 * group, 2)
        landing = pieces.at[names, level, me]

        @pl.loop(1, SEGS)
        def _(step):
            peer = wrapped(me + step)
            remote(
                kv_stage.at[names, peer], landing,
                p1_send.at[group], p1_recv.at[group], (host, peer),
            ).start()

        move(group, kv_stage.at[names, me], landing, p1_send.at[group], p1_recv.at[group])

    def move_inputs(head):
        name = name_of(head)
        move(
            head, kv_stage.at[name], own_blocks.at[head],
            k_send.at[head], k_recv.at[head],
        )
        for index, array in enumerate((queries, grad_out)):
            move(
                head, array.at[0, 0, :, lanes(name, GROUP)], inputs.at[head, index],
                q_send.at[head], q_recv.at[head],
            )

    def unit(head, which):
        return pieces.at[name_of(head), which]

    def lift(head, which, slot, device):
        return remote(
            unit(head, which), unit(head, which),
            up_send.at[head, slot], up_recv.at[head, which], (device, me),
        )

    def own_lifts(head, action):
        here = host_of(head)
        plane = half(here)
        for step in range(1, 4):
            @pl.when(plane + step <= 3)
            def _():
                action(lift(head, here, step - 1, device_of(head, plane + step)))

        @pl.when(core == 0)
        def _():
            action(lift(head, here, 3, sibling))

    def passed_on(head, action):
        @pl.loop(0, half(host_of(head)))
        def _(plane):
            action(2 * plane + core, lift(head, 2 * plane + core, 4 + plane, sibling))

    def launch(head):
        @pl.when(head < 2)
        def _():
            wait_bytes(pieces.at[pl.ds(2 * head, 2), host_of(head)], p1_recv.at[head])

        own_lifts(head, lambda copy: copy.start())
        move_inputs(head)

    make_pick(0)
    launch(0)

    def pass_on(head):
        def forward(which, copy):
            wait_bytes(unit(head, which), up_recv.at[head, which])
            copy.start()

        passed_on(head, forward)

    def select(head):
        here = host_of(head)
        parity = odd(head)

        @pl.loop(0, 4)
        def _(plane):
            other = 2 * plane + 1 - core

            @pl.when(other < here)
            def _():
                wait_bytes(unit(head, other), up_recv.at[head, other])

        def send(count):
            for offset in range(1, count + 1):
                found = jnp.dot(
                    pick[parity, offset],
                    pieces[name_of(head), jnp.maximum(here - offset, 0)].reshape(
                        SEGS * PIECE, HEAD_DIM
                    ),
                    preferred_element_type=F32,
                )
                chosen[head, :, offset - 1] = found.astype(BF16).reshape(SEGS, PIECE, HEAD_DIM)
            @pl.loop(1, SEGS)
            def _(step):
                peer = wrapped(me + step)
                remote(
                    chosen.at[head, peer, pl.ds(0, count)],
                    blocks.at[head, me, pl.ds(0, count)],
                    p3_send.at[head], p3_recv.at[head], (level, peer),
                ).start()

            pltpu.make_async_copy(
                chosen.at[head, me, pl.ds(0, count)],
                blocks.at[head, me, pl.ds(0, count)], p3_recv.at[head],
            ).start()

        per_plane(here, send)

    def attend(head):
        here = host_of(head)
        pairs = half(here) + 1
        contract_last = (((1,), (1,)), ((), ()))
        span_all = [pl.ds(group * ROWS, ROWS) for group in range(GROUP)]

        def block_pair(pair, part):
            return whole[part, rows_of(pair, PAIR), :]

        halves = [pl.ds(part * PIECES_PER_PART, PIECES_PER_PART) for part in range(2)]
        for part, span in enumerate(halves):
            whole[part, 0:ROWS, :] = own_blocks[head, span].reshape(ROWS, HEAD_DIM)

        @pl.when(here == 0)
        def _():
            whole[:, ROWS:PAIR, :] = jnp.zeros((2, ROWS, HEAD_DIM), BF16)

        @pl.when(here > 0)
        def _():
            @pl.loop(1, 2 * pairs)
            def _(offset):
                for part, span in enumerate(halves):
                    whole[part, rows_of(offset, ROWS), :] = blocks[
                        head, span, offset - 1
                    ].reshape(ROWS, HEAD_DIM)

        stats[0] = jnp.full((8, STACK), NEG_FILL, F32)
        for index in range(2):
            for group, span in enumerate(span_all):
                stacks[index, span, :] = inputs[head, index, :, span]

        @pl.loop(0, pairs)
        def _(pair):
            span_rows = rows_of(pair, PAIR)
            logits[span_rows, :] = lax.dot_general(
                block_pair(pair, 0), stacks[0], contract_last, preferred_element_type=F32
            )
            grad_probs[span_rows, :] = lax.dot_general(
                block_pair(pair, 1), stacks[1], contract_last, preferred_element_type=F32
            )

            @pl.when(pair == 0)
            def _():
                u_row = lax.broadcasted_iota(jnp.int32, (ROWS, ROWS), 0)
                t_row = lax.broadcasted_iota(jnp.int32, (ROWS, ROWS), 1)
                for span in span_all:
                    logits[0:ROWS, span] = jnp.where(
                        u_row <= t_row, logits[0:ROWS, span], NEG_FILL
                    )

            @pl.when((pair == pairs - 1) & (odd(here) == 0))
            def _():
                logits[rows_of(here + 1, ROWS), :] = jnp.full((ROWS, STACK), NEG_FILL, F32)

            for span in span_all:
                stats[0, :, span] = jnp.maximum(
                    stats[0, :, span], fold(logits[span_rows, span]).max(0)
                )

        stats[1] = jnp.zeros((8, STACK), F32)
        stats[2] = jnp.zeros((8, STACK), F32)
        stats[0] = jnp.broadcast_to(stats[0].max(0, keepdims=True), (8, STACK))

        @pl.loop(0, pairs)
        def _(pair):
            span_rows = rows_of(pair, PAIR)
            for span in span_all:
                top = stats[0, 0:1, span]
                tile = jnp.exp2((logits[span_rows, span] - top) * EXP2_SCALE)
                logits[span_rows, span] = tile
                stats[1, :, span] += fold(tile).sum(0)
                stats[2, :, span] += fold(tile * grad_probs[span_rows, span]).sum(0)

        inverse = 1.0 / stats[1].sum(0, keepdims=True)
        delta = stats[2].sum(0, keepdims=True) * inverse
        stats[1] = jnp.broadcast_to(inverse, (8, STACK))
        stats[2] = jnp.broadcast_to(delta, (8, STACK))
        query_sum[...] = jnp.zeros((HEAD_DIM, STACK), F32)

        @pl.loop(0, pairs)
        def _(pair):
            span_rows = rows_of(pair, PAIR)
            for span in span_all:
                exact = logits[span_rows, span] * stats[1, 0:1, span]
                probs[:, span] = exact.astype(BF16)
                grad_logits[:, span] = (
                    exact * (grad_probs[span_rows, span] - stats[2, 0:1, span])
                ).astype(BF16)
            value_term = jnp.dot(probs[...], stacks[1], preferred_element_type=F32)
            key_term = SCALE * jnp.dot(
                grad_logits[...], stacks[0], preferred_element_type=F32
            )
            for part, term in enumerate((key_term, value_term)):
                cut = term.astype(BF16).reshape(2, PIECES_PER_PART, PIECE, HEAD_DIM)
                for index in range(2):
                    terms[head, halves[part], 2 * pair + index] = cut[index]

                @pl.when(pair == 0)
                def _():
                    own[head, part] = term[0:ROWS]

            query_sum[...] += lax.dot_general(
                block_pair(pair, 0), grad_logits[...], (((0,), (0,)), ((), ())),
                preferred_element_type=F32,
            )

        for group, span in enumerate(span_all):
            staged[head, :, span] = (SCALE * query_sum[:, span].T).astype(BF16)

    def query_target(head):
        return grad_queries.at[0, 0, :, lanes(name_of(head), GROUP)]

    def send_results(head):
        host = host_of(head)
        here = host

        def send(count):
            @pl.loop(1, SEGS)
            def _(step):
                peer = wrapped(me + step)
                remote(
                    terms.at[head, peer, pl.ds(1, count)],
                    term_pieces.at[head, me, pl.ds(0, count)],
                    b1_send.at[head], b1_recv.at[head], (level, peer),
                ).start()

            pltpu.make_async_copy(
                terms.at[head, me, pl.ds(1, count)],
                term_pieces.at[head, me, pl.ds(0, count)], b1_recv.at[head],
            ).start()

        per_plane(here, send)
        move(
            head, staged.at[head], query_target(head), d_send.at[head], d_recv.at[head]
        )

        @pl.when(host != level)
        def _():
            own_out[head] = own[head].astype(BF16)
            remote(
                own_out.at[head], own_in.at[head], o_send.at[head], o_recv.at[head], (host, me)
            ).start()

    def summed(head, offset):
        return jnp.dot(
            spread[odd(head), offset],
            term_pieces[head, :, offset - 1].reshape(SEGS * PIECE, HEAD_DIM),
            preferred_element_type=F32,
        )

    def cross_copy(head, plane):
        return remote(
            cross_out.at[head, plane], cross_in.at[head, plane],
            x_send.at[head, plane], x_recv.at[head, plane], (sibling, me),
        )

    def sum_stage(head):
        here = host_of(head)

        def sums(count):
            wait_bytes(term_pieces.at[head, :, pl.ds(0, count)], b1_recv.at[head])
            for plane in range((count + 1) // 2):
                offset = jnp.maximum(here - (2 * plane + 1 - core), 1)
                cross_out[head, plane] = summed(head, offset).astype(BF16)
            for plane in range((count - 1) // 2):
                offset = jnp.maximum(here - (2 * plane + core), 1)
                kept[head, plane] = summed(head, offset)

        per_plane(here, sums)

        @pl.loop(0, 4)
        def _(plane):
            @pl.when(here - (2 * plane + 1 - core) >= 1)
            def _():
                cross_copy(head, plane).start()

    def climb_copy(head, plane):
        slot = half(host_of(head)) - 1
        return remote(
            climb_out.at[head, plane], climb_in.at[head, slot],
            c_send.at[head, plane], c_recv.at[head, slot], (device_of(head, plane), me),
        )

    def climb(head):
        plane_here = half(host_of(head))

        @pl.loop(0, plane_here - core + 1)
        def _(plane):
            wait_bytes(cross_in.at[head, plane], x_recv.at[head, plane])

        @pl.loop(0, plane_here)
        def _(plane):
            climb_out[head, plane] = (
                kept[head, plane] + cross_in[head, plane].astype(F32)
            ).astype(BF16)
            climb_copy(head, plane).start()

    def final_send(head):
        host = host_of(head)

        @pl.when(host < LEVELS - 1)
        def _():
            total_sum[...] = jnp.zeros((SEGS * PIECE, HEAD_DIM), F32)

            @pl.loop(half(host), 3)
            def _(slot):
                wait_bytes(climb_in.at[head, slot], c_recv.at[head, slot])
                total_sum[...] += climb_in[head, slot].astype(F32)

            @pl.when(core == 0)
            def _():
                total_sum[...] += cross_in[head, half(host)].astype(F32)

            final_out[head] = total_sum[...].astype(BF16).reshape(SEGS, PIECE, HEAD_DIM)
            part, span = piece_of(me)

            @pl.loop(1, SEGS)
            def _(step):
                peer = wrapped(me + step)
                remote(
                    final_out.at[head, peer], final_in.at[head, part, span, :],
                    f_send.at[head], f_recv.at[head], (host, peer),
                ).start()

            move(
                head, final_out.at[head, me], final_in.at[head, part, span, :],
                f_send.at[head], f_recv.at[head],
            )

    def final_store(head):
        away = host_of(head) != level

        @pl.when(away)
        def _():
            wait_bytes(own_in.at[head], o_recv.at[head])
            own[head] = own_in[head].astype(F32)

        @pl.when(level < LEVELS - 1)
        def _():
            wait_bytes(final_in.at[head], f_recv.at[head])
            own[head] = own[head] + final_in[head].astype(F32)

        grad_kv[0, 0, :, :, lanes(name_of(head))] = own[head].astype(BF16)

    stages = (sum_stage, climb, final_send, final_store)

    @pl.loop(0, KV_HEADS + LAG + len(stages))
    def _(tick):
        @pl.when((tick >= 1) & (tick < KV_HEADS + 1))
        def _():
            select(tick - 1)

        @pl.when(tick < KV_HEADS - 1)
        def _():
            launch(tick + 1)

        @pl.when(tick < KV_HEADS)
        def _():
            pass_on(tick)

        @pl.when(tick == 0)
        def _():
            find_ancestors(1)
            make_pick(1)

        @pl.when(tick == 2)
        def _():
            make_spread(0)
            make_spread(1)

        for lag, stage in reversed(list(enumerate(stages[1:], LAG + 2))):
            @pl.when((tick >= lag) & (tick < KV_HEADS + lag))
            def _():
                stage(tick - lag)

        @pl.when((tick >= LAG) & (tick < KV_HEADS + LAG))
        def _():
            head = tick - LAG
            per_plane(
                host_of(head),
                lambda count: wait_bytes(blocks.at[head, :, pl.ds(0, count)], p3_recv.at[head]),
            )
            wait_bytes(own_blocks.at[head], k_recv.at[head])
            wait_bytes(inputs.at[head], q_recv.at[head])
            attend(head)
            send_results(head)

        @pl.when((tick >= LAG + 1) & (tick < KV_HEADS + LAG + 1))
        def _():
            sum_stage(tick - LAG - 1)

    @pl.loop(0, 2)
    def _(group):
        names = pl.ds(2 * group, 2)
        wait_bytes(pieces.at[names, 0, pl.ds(1, SEGS - 1)], p1_send.at[group])

        @pl.when(host_of(group) != level)
        def _():
            wait_bytes(pieces.at[names, 0, 0], p1_send.at[group])

    @pl.loop(0, KV_HEADS)
    def _(head):
        host = host_of(head)
        away = host != level
        wait_bytes(query_target(head), d_recv.at[head])
        own_lifts(head, lambda copy: copy.wait_send())
        passed_on(head, lambda which, copy: copy.wait_send())

        @pl.when(away)
        def _():
            wait_bytes(own_blocks.at[head], k_send.at[head])
            wait_bytes(inputs.at[head], q_send.at[head])
            wait_bytes(staged.at[head], d_send.at[head])
            wait_bytes(own_out.at[head], o_send.at[head])

        def sent(count):
            wait_bytes(chosen.at[head, pl.ds(1, SEGS - 1), pl.ds(0, count)], p3_send.at[head])
            wait_bytes(
                term_pieces.at[head, pl.ds(1, SEGS - 1), pl.ds(0, count)], b1_send.at[head]
            )

        per_plane(host, sent)

        @pl.loop(0, 4)
        def _(plane):
            @pl.when(host - (2 * plane + 1 - core) >= 1)
            def _():
                cross_copy(head, plane).wait_send()

        @pl.loop(0, half(host))
        def _(plane):
            climb_copy(head, plane).wait_send()

        @pl.when(host < LEVELS - 1)
        def _():
            wait_bytes(final_out.at[head, pl.ds(1, SEGS - 1)], f_send.at[head])

            @pl.when(away)
            def _():
                wait_bytes(final_out.at[head, 0], f_send.at[head])


def shards(queries, keys_values, grad_out, parents):
    vmem = pl.BlockSpec(memory_space=pltpu.VMEM)
    smem = pl.BlockSpec(memory_space=pltpu.SMEM)
    anywhere = pl.BlockSpec(memory_space=pl.ANY)
    dma = pltpu.SemaphoreType.DMA
    tile = (SEGS, PIECE, HEAD_DIM)
    flat = (SEGS * PIECE, HEAD_DIM)
    keys_count = LEVELS * ROWS
    part_pair = (2, ROWS, HEAD_DIM)
    selectors = (2, LEVELS, SEGS * PIECE, SEGS * PIECE)
    scratch = [
        pltpu.SMEM((2, LEVELS, SEGS), jnp.int32),
        pltpu.VMEM(selectors, BF16),
        pltpu.VMEM(selectors, BF16),
        pltpu.VMEM(keys_values.shape, BF16),
        pltpu.VMEM((KV_HEADS,) + tile, BF16),
        pltpu.VMEM((KV_HEADS, LEVELS) + tile, BF16),
        pltpu.VMEM((KV_HEADS, SEGS, LEVELS - 1, PIECE, HEAD_DIM), BF16),
        pltpu.VMEM((KV_HEADS, SEGS, LEVELS - 1, PIECE, HEAD_DIM), BF16),
        pltpu.VMEM((KV_HEADS,) + tile, BF16),
        pltpu.VMEM((2, keys_count, HEAD_DIM), BF16),
        pltpu.VMEM((KV_HEADS, SEGS, LEVELS, PIECE, HEAD_DIM), BF16),
        pltpu.VMEM((KV_HEADS, SEGS, LEVELS - 1, PIECE, HEAD_DIM), BF16),
        pltpu.VMEM((KV_HEADS,) + part_pair, F32),
        pltpu.VMEM((KV_HEADS,) + part_pair, BF16),
        pltpu.VMEM((KV_HEADS,) + part_pair, BF16),
        pltpu.VMEM((KV_HEADS, 2, ROWS, STACK), BF16),
        pltpu.VMEM((2, STACK, HEAD_DIM), BF16),
        pltpu.VMEM((KV_HEADS, ROWS, STACK), BF16),
        pltpu.VMEM((HEAD_DIM, STACK), F32),
        pltpu.VMEM((3, 8, STACK), F32),
        pltpu.VMEM((keys_count, STACK), F32),
        pltpu.VMEM((keys_count, STACK), F32),
        pltpu.VMEM((PAIR, STACK), BF16),
        pltpu.VMEM((PAIR, STACK), BF16),
        pltpu.VMEM((KV_HEADS, 3) + flat, F32),
        pltpu.VMEM(flat, F32),
        pltpu.VMEM((KV_HEADS, 4) + flat, BF16),
        pltpu.VMEM((KV_HEADS, 4) + flat, BF16),
        pltpu.VMEM((KV_HEADS, 3) + flat, BF16),
        pltpu.VMEM((KV_HEADS, 3) + flat, BF16),
        pltpu.VMEM((KV_HEADS,) + tile, BF16),
        pltpu.VMEM((KV_HEADS,) + part_pair, BF16),
        dma,
        dma((2,)), dma((2,)),
        dma((KV_HEADS, 7)), dma((KV_HEADS, LEVELS)),
        dma((KV_HEADS,)), dma((KV_HEADS,)),
        dma((KV_HEADS,)), dma((KV_HEADS,)),
        dma((KV_HEADS,)), dma((KV_HEADS,)),
        dma((KV_HEADS,)), dma((KV_HEADS,)),
        dma((KV_HEADS,)), dma((KV_HEADS,)),
        dma((KV_HEADS,)), dma((KV_HEADS,)),
        dma((KV_HEADS, 4)), dma((KV_HEADS, 4)),
        dma((KV_HEADS, 3)), dma((KV_HEADS, 3)),
        dma((KV_HEADS,)), dma((KV_HEADS,)),
    ]
    return pl.pallas_call(
        kernel,
        out_shape=(
            jax.ShapeDtypeStruct(queries.shape, BF16),
            jax.ShapeDtypeStruct(keys_values.shape, BF16),
        ),
        in_specs=[smem, anywhere, anywhere, anywhere],
        out_specs=(vmem, vmem),
        scratch_shapes=scratch,
        compiler_params=pltpu.CompilerParams(
            collective_id=0, has_side_effects=True, vmem_limit_bytes=56 * 1024 * 1024
        ),
        cost_estimate=pl.CostEstimate(
            flops=5 * 2 * HEADS * LEVELS * ROWS * ROWS * HEAD_DIM,
            bytes_accessed=8 * 1024 * 1024,
            transcendentals=HEADS * LEVELS * ROWS * ROWS,
        ),
    )(parents.transpose(0, 2, 1), queries, keys_values, grad_out)


def solution(mesh):
    in_specs = (
        P("depth", "seg", None, None),
        P("depth", "seg", None, None, None),
        P("depth", "seg", None, None),
        P(),
    )
    out_specs = (P("depth", "seg", None, None), P("depth", "seg", None, None, None))
    return jax.shard_map(shards, mesh=mesh, in_specs=in_specs, out_specs=out_specs, check_vma=False)
```

```python
import functools

import jax
import jax.numpy as jnp
from jax import lax
from jax.experimental import pallas as pl
from jax.experimental.pallas import tpu as pltpu
from jax.sharding import PartitionSpec as P

HEADS = 20
KV_HEADS = 4
HEAD_DIM = 128
GROUP = HEADS // KV_HEADS
ROWS = 128
LEVELS = 8
SEGS = 16
PIECE = 16
PIECES_PER_PART = ROWS // PIECE
STACK = GROUP * ROWS
PAIR = 2 * ROWS
TILE = SEGS * PIECE

NEG_FILL = -1e30
SCALE = HEAD_DIM ** -0.5
EXP2_SCALE = SCALE * 1.4426950408889634
MESH = pl.DeviceIdType.MESH
BF16 = jnp.bfloat16
F32 = jnp.float32


def half(value):
    return lax.div(value, 2)


def odd(value):
    return lax.rem(value, 2)


def wrapped(index):
    return jnp.where(index >= SEGS, index - SEGS, index)


def lanes(index, count=1):
    width = count * HEAD_DIM
    return pl.ds(pl.multiple_of(index * width, width), width)


def rows_of(index, count):
    return pl.ds(pl.multiple_of(index * count, count), count)


def fold(tile):
    return tile.reshape(tile.shape[0] // 8, 8, tile.shape[1])


def kernel(
    parents, queries, keys_values, grad_out, grad_queries, grad_kv,
    anc, pick, spread, kv_in, q_in, g_in, kv_stage, pieces, chosen, blocks,
    terms, term_pieces, own, stacks, turned, query_sum, stats, logits, grad_probs,
    probs, grad_logits, total_sum, final_out, final_in,
    kv_sem, q_sem, g_sem, ready, p1_send, p1_recv, p3_send, p3_recv, b1_send, b1_recv,
    f_send, f_recv,
):
    level = lax.axis_index("depth")
    me = lax.axis_index("seg")
    below = LEVELS - 1 - level

    def remote(src, dst, send_sem, recv_sem, device):
        return pltpu.make_async_remote_copy(
            src_ref=src, dst_ref=dst, send_sem=send_sem, recv_sem=recv_sem,
            device_id=device, device_id_type=MESH,
        )

    def wait_bytes(ref, sem):
        pltpu.make_async_copy(ref, ref, sem).wait()

    def per_count(which, action):
        for count in range(1, LEVELS):
            pl.when(which == count)(functools.partial(action, count))

    load_kv = pltpu.make_async_copy(keys_values, kv_in, kv_sem)
    load_q = pltpu.make_async_copy(queries, q_in, q_sem)
    load_g = pltpu.make_async_copy(grad_out, g_in, g_sem)
    load_kv.start()
    load_q.start()
    load_g.start()

    barrier = pltpu.get_barrier_semaphore()

    def in_line(step):
        other = level + step
        return (jnp.where(other >= LEVELS, other - LEVELS, other), me)

    @pl.loop(1, SEGS)
    def _(step):
        pl.semaphore_signal(
            barrier, inc=1, device_id=(level, wrapped(me + step)), device_id_type=MESH
        )

    @pl.loop(1, LEVELS)
    def _(step):
        pl.semaphore_signal(barrier, inc=1, device_id=in_line(step), device_id_type=MESH)

    @pl.loop(0, SEGS)
    def _(column):
        anc[0, column] = column

    @pl.loop(1, below + 1)
    def _(offset):
        @pl.loop(0, SEGS)
        def _(column):
            anc[offset, column] = anc[offset - 1, parents[level + offset - 1, 0, column]]

    load_kv.wait()
    for head in range(KV_HEADS):
        for part in range(2):
            kv_stage[head, pl.ds(part * PIECES_PER_PART, PIECES_PER_PART)] = kv_in[
                0, 0, part, :, head * HEAD_DIM:(head + 1) * HEAD_DIM
            ].reshape(PIECES_PER_PART, PIECE, HEAD_DIM)
    pl.semaphore_wait(barrier, SEGS - 1 + LEVELS - 1)

    def spread_out(group, heads):
        @pl.loop(1, SEGS)
        def _(step):
            peer = wrapped(me + step)
            remote(
                kv_stage.at[heads, peer], pieces.at[heads, me],
                p1_send.at[group], p1_recv.at[group], (level, peer),
            ).start()

        pltpu.make_async_copy(
            kv_stage.at[heads, me], pieces.at[heads, me], p1_recv.at[group]
        ).start()

    groups = (pl.ds(0, 1), pl.ds(1, KV_HEADS - 1))
    for group, heads in enumerate(groups):
        spread_out(group, heads)

    @pl.loop(1, LEVELS)
    def _(step):
        pl.semaphore_signal(ready, inc=1, device_id=in_line(step), device_id_type=MESH)

    @pl.loop(1, below + 1)
    def _(offset):
        lane = lax.broadcasted_iota(jnp.int32, (PIECE, TILE), 1)
        row = lax.broadcasted_iota(jnp.int32, (PIECE, TILE), 0)
        ahead = lane - row
        for column in range(SEGS):
            pick[offset, rows_of(column, PIECE), :] = jnp.where(
                ahead == anc[offset, column] * PIECE, 1.0, 0.0
            ).astype(BF16)

    def pick_and_send(head):
        @pl.loop(1, below + 1)
        def _(offset):
            found = jnp.dot(
                pick[offset], pieces[head].reshape(TILE, HEAD_DIM), preferred_element_type=F32
            )
            chosen[head, offset - 1] = found.astype(BF16).reshape(SEGS, PIECE, HEAD_DIM)

        @pl.loop(0, SEGS)
        def _(step):
            column = wrapped(me + step)

            @pl.loop(1, below + 1)
            def _(offset):
                remote(
                    chosen.at[head, offset - 1, column], blocks.at[head, offset, me],
                    p3_send.at[head], p3_recv.at[head], (level + offset, column),
                ).start()

    wait_bytes(pieces.at[groups[0]], p1_recv.at[0])
    pl.semaphore_wait(ready, LEVELS - 1)

    @pl.loop(0, KV_HEADS)
    def _(head):
        @pl.when(head == 1)
        def _():
            wait_bytes(pieces.at[groups[1]], p1_recv.at[1])

        pick_and_send(head)

    @pl.loop(0, KV_HEADS)
    def _(head):
        blocks[head, 0] = kv_stage[head]

        @pl.when(odd(level) == 0)
        def _():
            blocks[head, level + 1] = jnp.zeros((SEGS, PIECE, HEAD_DIM), BF16)

    @pl.loop(1, below + 1)
    def _(offset):
        lane = lax.broadcasted_iota(jnp.int32, (PIECE, TILE), 1)
        row = lax.broadcasted_iota(jnp.int32, (PIECE, TILE), 0)
        lane_column = lane >> 4
        target = (lane & (PIECE - 1)) - row
        for column in range(SEGS):
            target = jnp.where(
                lane_column == column, target + anc[offset, column] * PIECE, target
            )
        for column in range(SEGS):
            spread[offset, rows_of(column, PIECE), :] = jnp.where(
                target == column * PIECE, 1.0, 0.0
            ).astype(BF16)

    load_q.wait()
    load_g.wait()
    halves = [pl.ds(part * PIECES_PER_PART, PIECES_PER_PART) for part in range(2)]

    def attend(head):
        pairs = half(level) + 1
        span_all = [pl.ds(group * ROWS, ROWS) for group in range(GROUP)]

        def block_pair(pair, part):
            return blocks[head, pl.ds(2 * pair, 2), halves[part]].reshape(PAIR, HEAD_DIM)

        stats[0] = jnp.full((8, STACK), NEG_FILL, F32)
        for index in range(2):
            for group, span in enumerate(span_all):
                tile = (q_in, g_in)[index][0, 0, :, lanes(head * GROUP + group)]
                stacks[index, span, :] = tile
                turned[index, :, span] = tile.T

        @pl.loop(0, pairs)
        def _(pair):
            span_rows = rows_of(pair, PAIR)
            logits[span_rows, :] = jnp.dot(
                block_pair(pair, 0), turned[0], preferred_element_type=F32
            )
            grad_probs[span_rows, :] = jnp.dot(
                block_pair(pair, 1), turned[1], preferred_element_type=F32
            )

            @pl.when(pair == 0)
            def _():
                u_row = lax.broadcasted_iota(jnp.int32, (ROWS, ROWS), 0)
                t_row = lax.broadcasted_iota(jnp.int32, (ROWS, ROWS), 1)
                for span in span_all:
                    logits[0:ROWS, span] = jnp.where(
                        u_row <= t_row, logits[0:ROWS, span], NEG_FILL
                    )

            @pl.when((pair == pairs - 1) & (odd(level) == 0))
            def _():
                logits[rows_of(level + 1, ROWS), :] = jnp.full((ROWS, STACK), NEG_FILL, F32)

            for span in span_all:
                stats[0, :, span] = jnp.maximum(
                    stats[0, :, span], fold(logits[span_rows, span]).max(0)
                )

        stats[1] = jnp.zeros((8, STACK), F32)
        stats[2] = jnp.zeros((8, STACK), F32)
        stats[0] = jnp.broadcast_to(stats[0].max(0, keepdims=True), (8, STACK))

        @pl.loop(0, pairs)
        def _(pair):
            span_rows = rows_of(pair, PAIR)
            for span in span_all:
                top = stats[0, 0:1, span]
                tile = jnp.exp2((logits[span_rows, span] - top) * EXP2_SCALE)
                logits[span_rows, span] = tile
                stats[1, :, span] += fold(tile).sum(0)
                stats[2, :, span] += fold(tile * grad_probs[span_rows, span]).sum(0)

        inverse = 1.0 / stats[1].sum(0, keepdims=True)
        delta = stats[2].sum(0, keepdims=True) * inverse
        stats[1] = jnp.broadcast_to(inverse, (8, STACK))
        stats[2] = jnp.broadcast_to(delta, (8, STACK))
        query_sum[...] = jnp.zeros((HEAD_DIM, STACK), F32)

        @pl.loop(0, pairs)
        def _(pair):
            span_rows = rows_of(pair, PAIR)
            for span in span_all:
                exact = logits[span_rows, span] * stats[1, 0:1, span]
                probs[:, span] = exact.astype(BF16)
                grad_logits[:, span] = (
                    exact * (grad_probs[span_rows, span] - stats[2, 0:1, span])
                ).astype(BF16)
            value_term = jnp.dot(probs[...], stacks[1], preferred_element_type=F32)
            key_term = SCALE * jnp.dot(
                grad_logits[...], stacks[0], preferred_element_type=F32
            )
            for part, term in enumerate((key_term, value_term)):
                cut = term.astype(BF16).reshape(2, PIECES_PER_PART, PIECE, HEAD_DIM)
                terms[head, pl.ds(2 * pair, 2), halves[part]] = cut

                @pl.when(pair == 0)
                def _():
                    own[head, part] = term[0:ROWS]

            query_sum[...] += lax.dot_general(
                block_pair(pair, 0), grad_logits[...], (((0,), (0,)), ((), ())),
                preferred_element_type=F32,
            )

        for group, span in enumerate(span_all):
            grad_queries[0, 0, :, lanes(head * GROUP + group)] = (
                SCALE * query_sum[:, span].T
            ).astype(BF16)

    def send_terms(head):
        @pl.loop(0, SEGS)
        def _(step):
            peer = wrapped(me + step)

            @pl.loop(1, level + 1)
            def _(offset):
                remote(
                    terms.at[head, offset, peer], term_pieces.at[head, offset - 1, me],
                    b1_send.at[head], b1_recv.at[head], (level - offset, peer),
                ).start()

    def sum_and_return(head):
        @pl.when(level < LEVELS - 1)
        def _():
            per_count(
                below,
                lambda count: wait_bytes(
                    term_pieces.at[head, pl.ds(0, count)], b1_recv.at[head]
                ),
            )
            total_sum[...] = jnp.zeros((TILE, HEAD_DIM), F32)

            @pl.loop(1, below + 1)
            def _(offset):
                total_sum[...] += jnp.dot(
                    spread[offset], term_pieces[head, offset - 1].reshape(TILE, HEAD_DIM),
                    preferred_element_type=F32,
                )

            final_out[head] = total_sum[...].astype(BF16).reshape(SEGS, PIECE, HEAD_DIM)

            @pl.loop(1, SEGS)
            def _(step):
                peer = wrapped(me + step)
                remote(
                    final_out.at[head, peer], final_in.at[head, me],
                    f_send.at[head], f_recv.at[head], (level, peer),
                ).start()

            pltpu.make_async_copy(
                final_out.at[head, me], final_in.at[head, me], f_recv.at[head]
            ).start()

    def store(head):
        @pl.when(level < LEVELS - 1)
        def _():
            wait_bytes(final_in.at[head], f_recv.at[head])
            for part in range(2):
                own[head, part] += final_in[head, halves[part]].reshape(
                    ROWS, HEAD_DIM
                ).astype(F32)

        grad_kv[0, 0, :, :, lanes(head)] = own[head].astype(BF16)

    @pl.loop(0, KV_HEADS + 2)
    def _(tick):
        @pl.when(tick < KV_HEADS)
        def _():
            per_count(
                level,
                lambda count: wait_bytes(blocks.at[tick, pl.ds(1, count)], p3_recv.at[tick]),
            )
            attend(tick)
            send_terms(tick)

        @pl.when((tick >= 1) & (tick < KV_HEADS + 1))
        def _():
            sum_and_return(tick - 1)

        @pl.when(tick >= 2)
        def _():
            store(tick - 2)

    for group, heads in enumerate(groups):
        wait_bytes(pieces.at[heads, pl.ds(1, SEGS - 1)], p1_send.at[group])

    @pl.loop(0, KV_HEADS)
    def _(head):
        per_count(
            below, lambda count: wait_bytes(chosen.at[head, pl.ds(0, count)], p3_send.at[head])
        )
        per_count(
            level, lambda count: wait_bytes(terms.at[head, pl.ds(1, count)], b1_send.at[head])
        )

        @pl.when(level < LEVELS - 1)
        def _():
            wait_bytes(final_out.at[head, pl.ds(1, SEGS - 1)], f_send.at[head])


def shards(queries, keys_values, grad_out, parents):
    vmem = pl.BlockSpec(memory_space=pltpu.VMEM)
    smem = pl.BlockSpec(memory_space=pltpu.SMEM)
    anywhere = pl.BlockSpec(memory_space=pl.ANY)
    dma = pltpu.SemaphoreType.DMA
    tile = (SEGS, PIECE, HEAD_DIM)
    keys_count = LEVELS * ROWS
    scratch = [
        pltpu.SMEM((LEVELS, SEGS), jnp.int32),
        pltpu.VMEM((LEVELS, TILE, TILE), BF16),
        pltpu.VMEM((LEVELS, TILE, TILE), BF16),
        pltpu.VMEM(keys_values.shape, BF16),
        pltpu.VMEM(queries.shape, BF16),
        pltpu.VMEM(queries.shape, BF16),
        pltpu.VMEM((KV_HEADS,) + tile, BF16),
        pltpu.VMEM((KV_HEADS,) + tile, BF16),
        pltpu.VMEM((KV_HEADS, LEVELS - 1) + tile, BF16),
        pltpu.VMEM((KV_HEADS, LEVELS) + tile, BF16),
        pltpu.VMEM((KV_HEADS, LEVELS) + tile, BF16),
        pltpu.VMEM((KV_HEADS, LEVELS - 1) + tile, BF16),
        pltpu.VMEM((KV_HEADS, 2, ROWS, HEAD_DIM), F32),
        pltpu.VMEM((2, STACK, HEAD_DIM), BF16),
        pltpu.VMEM((2, HEAD_DIM, STACK), BF16),
        pltpu.VMEM((HEAD_DIM, STACK), F32),
        pltpu.VMEM((3, 8, STACK), F32),
        pltpu.VMEM((keys_count, STACK), F32),
        pltpu.VMEM((keys_count, STACK), F32),
        pltpu.VMEM((PAIR, STACK), BF16),
        pltpu.VMEM((PAIR, STACK), BF16),
        pltpu.VMEM((TILE, HEAD_DIM), F32),
        pltpu.VMEM((KV_HEADS,) + tile, BF16),
        pltpu.VMEM((KV_HEADS,) + tile, BF16),
        dma, dma, dma,
        pltpu.SemaphoreType.REGULAR,
        dma((2,)), dma((2,)),
        dma((KV_HEADS,)), dma((KV_HEADS,)),
        dma((KV_HEADS,)), dma((KV_HEADS,)),
        dma((KV_HEADS,)), dma((KV_HEADS,)),
    ]
    return pl.pallas_call(
        kernel,
        out_shape=(
            jax.ShapeDtypeStruct(queries.shape, BF16),
            jax.ShapeDtypeStruct(keys_values.shape, BF16),
        ),
        in_specs=[smem, anywhere, anywhere, anywhere],
        out_specs=(vmem, vmem),
        scratch_shapes=scratch,
        compiler_params=pltpu.CompilerParams(
            collective_id=0, has_side_effects=True, vmem_limit_bytes=56 * 1024 * 1024
        ),
        cost_estimate=pl.CostEstimate(
            flops=5 * 2 * HEADS * LEVELS * ROWS * ROWS * HEAD_DIM,
            bytes_accessed=8 * 1024 * 1024,
            transcendentals=HEADS * LEVELS * ROWS * ROWS,
        ),
    )(parents.transpose(0, 2, 1), queries, keys_values, grad_out)


def solution(mesh):
    in_specs = (
        P("depth", "seg", None, None),
        P("depth", "seg", None, None, None),
        P("depth", "seg", None, None),
        P(),
    )
    out_specs = (P("depth", "seg", None, None), P("depth", "seg", None, None, None))
    return jax.shard_map(shards, mesh=mesh, in_specs=in_specs, out_specs=out_specs, check_vma=False)
```

```python
import functools

import jax
import jax.numpy as jnp
from jax import lax
from jax.experimental import pallas as pl
from jax.experimental.pallas import tpu as pltpu
from jax.sharding import PartitionSpec as P

HEADS = 20
KV_HEADS = 4
HEAD_DIM = 128
GROUP = HEADS // KV_HEADS
ROWS = 128
LEVELS = 8
SEGS = 16
PIECE = 16
PIECES_PER_PART = ROWS // PIECE
STACK = GROUP * ROWS
PAIR = 2 * ROWS
TILE = SEGS * PIECE

NEG_FILL = -1e30
SCALE = HEAD_DIM ** -0.5
EXP2_SCALE = SCALE * 1.4426950408889634
MESH = pl.DeviceIdType.MESH
BF16 = jnp.bfloat16
F32 = jnp.float32


def half(value):
    return lax.div(value, 2)


def odd(value):
    return lax.rem(value, 2)


def wrapped(index):
    return jnp.where(index >= SEGS, index - SEGS, index)


def lanes(index, count=1):
    width = count * HEAD_DIM
    return pl.ds(pl.multiple_of(index * width, width), width)


def rows_of(index, count):
    return pl.ds(pl.multiple_of(index * count, count), count)


def fold(tile):
    return tile.reshape(tile.shape[0] // 8, 8, tile.shape[1])


def kernel(
    parents, queries, keys_values, grad_out, grad_queries, grad_kv,
    anc, pick, spread, kv_in, q_in, g_in, kv_stage, pieces, chosen, blocks,
    terms, term_pieces, own, stacks, turned, query_sum, stats, logits, grad_probs,
    probs, grad_logits, final_out, final_in,
    kv_sem, q_sem, g_sem, ready, p1_send, p1_recv, p3_send, p3_recv, b1_send, b1_recv,
    f_send, f_recv,
):
    level = lax.axis_index("depth")
    me = lax.axis_index("seg")
    below = LEVELS - 1 - level

    def remote(src, dst, send_sem, recv_sem, device):
        return pltpu.make_async_remote_copy(
            src_ref=src, dst_ref=dst, send_sem=send_sem, recv_sem=recv_sem,
            device_id=device, device_id_type=MESH,
        )

    def wait_bytes(ref, sem):
        pltpu.make_async_copy(ref, ref, sem).wait()

    def per_count(which, action):
        for count in range(1, LEVELS):
            pl.when(which == count)(functools.partial(action, count))

    load_kv = pltpu.make_async_copy(keys_values, kv_in, kv_sem)
    load_q = pltpu.make_async_copy(queries, q_in, q_sem)
    load_g = pltpu.make_async_copy(grad_out, g_in, g_sem)
    load_kv.start()
    load_q.start()
    load_g.start()

    barrier = pltpu.get_barrier_semaphore()

    def in_line(step):
        other = level + step
        return (jnp.where(other >= LEVELS, other - LEVELS, other), me)

    @pl.loop(1, SEGS)
    def _(step):
        pl.semaphore_signal(
            barrier, inc=1, device_id=(level, wrapped(me + step)), device_id_type=MESH
        )

    @pl.loop(1, LEVELS)
    def _(step):
        pl.semaphore_signal(barrier, inc=1, device_id=in_line(step), device_id_type=MESH)

    @pl.loop(0, SEGS)
    def _(column):
        anc[0, column] = column

    @pl.loop(1, below + 1)
    def _(offset):
        @pl.loop(0, SEGS)
        def _(column):
            anc[offset, column] = anc[offset - 1, parents[level + offset - 1, 0, column]]

    load_kv.wait()
    for head in range(KV_HEADS):
        for part in range(2):
            kv_stage[head, pl.ds(part * PIECES_PER_PART, PIECES_PER_PART)] = kv_in[
                0, 0, part, :, head * HEAD_DIM:(head + 1) * HEAD_DIM
            ].reshape(PIECES_PER_PART, PIECE, HEAD_DIM)
    pl.semaphore_wait(barrier, SEGS - 1 + LEVELS - 1)

    def spread_out(group, heads):
        @pl.loop(1, SEGS)
        def _(step):
            peer = wrapped(me + step)
            remote(
                kv_stage.at[heads, peer], pieces.at[heads, me],
                p1_send.at[group], p1_recv.at[group], (level, peer),
            ).start()

        pltpu.make_async_copy(
            kv_stage.at[heads, me], pieces.at[heads, me], p1_recv.at[group]
        ).start()

    groups = (pl.ds(0, 1), pl.ds(1, KV_HEADS - 1))
    for group, heads in enumerate(groups):
        spread_out(group, heads)

    @pl.loop(1, LEVELS)
    def _(step):
        pl.semaphore_signal(ready, inc=1, device_id=in_line(step), device_id_type=MESH)

    @pl.loop(1, below + 1)
    def _(offset):
        lane = lax.broadcasted_iota(jnp.int32, (PIECE, TILE), 1)
        row = lax.broadcasted_iota(jnp.int32, (PIECE, TILE), 0)
        ahead = lane - row
        for column in range(SEGS):
            pick[offset - 1, rows_of(column, PIECE), :] = jnp.where(
                ahead == anc[offset, column] * PIECE, 1.0, 0.0
            ).astype(BF16)

    def pick_and_send(head):
        found = jnp.dot(
            pick[...].reshape((LEVELS - 1) * TILE, TILE),
            pieces[head].reshape(TILE, HEAD_DIM), preferred_element_type=F32,
        )
        chosen[head] = found.astype(BF16).reshape(LEVELS - 1, SEGS, PIECE, HEAD_DIM)

        @pl.loop(0, below)
        def _(step):
            offset = below - step
            for turn in range(SEGS):
                column = wrapped(me + turn)
                remote(
                    chosen.at[head, offset - 1, column], blocks.at[head, offset, me],
                    p3_send.at[head], p3_recv.at[head], (level + offset, column),
                ).start()

    wait_bytes(pieces.at[groups[0]], p1_recv.at[0])
    pl.semaphore_wait(ready, LEVELS - 1)

    @pl.loop(0, KV_HEADS)
    def _(head):
        @pl.when(head == 1)
        def _():
            wait_bytes(pieces.at[groups[1]], p1_recv.at[1])

        pick_and_send(head)

    @pl.loop(0, KV_HEADS)
    def _(head):
        blocks[head, 0] = kv_stage[head]

        @pl.when(odd(level) == 0)
        def _():
            blocks[head, level + 1] = jnp.zeros((SEGS, PIECE, HEAD_DIM), BF16)

    @pl.loop(1, below + 1)
    def _(offset):
        lane = lax.broadcasted_iota(jnp.int32, (PIECE, TILE), 1)
        row = lax.broadcasted_iota(jnp.int32, (PIECE, TILE), 0)
        lane_column = lane >> 4
        span = pl.ds(pl.multiple_of((offset - 1) * TILE, TILE), TILE)
        target = (lane & (PIECE - 1)) - row
        for column in range(SEGS):
            target = jnp.where(
                lane_column == column, target + anc[offset, column] * PIECE, target
            )
        for column in range(SEGS):
            spread[rows_of(column, PIECE), span] = jnp.where(
                target == column * PIECE, 1.0, 0.0
            ).astype(BF16)

    @pl.loop(below, LEVELS - 1)
    def _(index):
        spread[:, pl.ds(pl.multiple_of(index * TILE, TILE), TILE)] = jnp.zeros(
            (TILE, TILE), BF16
        )
        for head in range(KV_HEADS):
            term_pieces[head, index] = jnp.zeros((SEGS, PIECE, HEAD_DIM), BF16)

    load_q.wait()
    load_g.wait()
    halves = [pl.ds(part * PIECES_PER_PART, PIECES_PER_PART) for part in range(2)]

    def attend(head):
        pairs = half(level) + 1
        span_all = [pl.ds(group * ROWS, ROWS) for group in range(GROUP)]

        def block_pair(pair, part):
            return blocks[head, pl.ds(2 * pair, 2), halves[part]].reshape(PAIR, HEAD_DIM)

        stats[0] = jnp.full((8, STACK), NEG_FILL, F32)
        for index in range(2):
            for group, span in enumerate(span_all):
                tile = (q_in, g_in)[index][0, 0, :, lanes(head * GROUP + group)]
                stacks[index, span, :] = tile
                turned[index, :, span] = tile.T

        @pl.loop(0, pairs)
        def _(pair):
            span_rows = rows_of(pair, PAIR)
            logits[span_rows, :] = jnp.dot(
                block_pair(pair, 0), turned[0], preferred_element_type=F32
            )
            grad_probs[span_rows, :] = jnp.dot(
                block_pair(pair, 1), turned[1], preferred_element_type=F32
            )

            @pl.when(pair == 0)
            def _():
                u_row = lax.broadcasted_iota(jnp.int32, (ROWS, ROWS), 0)
                t_row = lax.broadcasted_iota(jnp.int32, (ROWS, ROWS), 1)
                for span in span_all:
                    logits[0:ROWS, span] = jnp.where(
                        u_row <= t_row, logits[0:ROWS, span], NEG_FILL
                    )

            @pl.when((pair == pairs - 1) & (odd(level) == 0))
            def _():
                logits[rows_of(level + 1, ROWS), :] = jnp.full((ROWS, STACK), NEG_FILL, F32)

            for span in span_all:
                stats[0, :, span] = jnp.maximum(
                    stats[0, :, span], fold(logits[span_rows, span]).max(0)
                )

        stats[1] = jnp.zeros((8, STACK), F32)
        stats[2] = jnp.zeros((8, STACK), F32)
        stats[0] = jnp.broadcast_to(stats[0].max(0, keepdims=True), (8, STACK))

        @pl.loop(0, pairs)
        def _(pair):
            span_rows = rows_of(pair, PAIR)
            for span in span_all:
                top = stats[0, 0:1, span]
                tile = jnp.exp2((logits[span_rows, span] - top) * EXP2_SCALE)
                logits[span_rows, span] = tile
                stats[1, :, span] += fold(tile).sum(0)
                stats[2, :, span] += fold(tile * grad_probs[span_rows, span]).sum(0)

        inverse = 1.0 / stats[1].sum(0, keepdims=True)
        delta = stats[2].sum(0, keepdims=True) * inverse
        stats[1] = jnp.broadcast_to(inverse, (8, STACK))
        stats[2] = jnp.broadcast_to(delta, (8, STACK))
        query_sum[...] = jnp.zeros((HEAD_DIM, STACK), F32)

        @pl.loop(0, pairs)
        def _(pair):
            span_rows = rows_of(pair, PAIR)
            for span in span_all:
                exact = logits[span_rows, span] * stats[1, 0:1, span]
                probs[:, span] = exact.astype(BF16)
                grad_logits[:, span] = (
                    exact * (grad_probs[span_rows, span] - stats[2, 0:1, span])
                ).astype(BF16)
            value_term = jnp.dot(probs[...], stacks[1], preferred_element_type=F32)
            key_term = SCALE * jnp.dot(
                grad_logits[...], stacks[0], preferred_element_type=F32
            )
            for part, term in enumerate((key_term, value_term)):
                cut = term.astype(BF16).reshape(2, PIECES_PER_PART, PIECE, HEAD_DIM)
                terms[head, pl.ds(2 * pair, 2), halves[part]] = cut

                @pl.when(pair == 0)
                def _():
                    own[head, part] = term[0:ROWS]

            query_sum[...] += lax.dot_general(
                block_pair(pair, 0), grad_logits[...], (((0,), (0,)), ((), ())),
                preferred_element_type=F32,
            )

        for group, span in enumerate(span_all):
            grad_queries[0, 0, :, lanes(head * GROUP + group)] = (
                SCALE * query_sum[:, span].T
            ).astype(BF16)

    def send_terms(head):
        @pl.loop(0, level)
        def _(step):
            offset = level - step
            for turn in range(SEGS):
                peer = wrapped(me + turn)
                remote(
                    terms.at[head, offset, peer], term_pieces.at[head, offset - 1, me],
                    b1_send.at[head], b1_recv.at[head], (level - offset, peer),
                ).start()

    def sum_and_return(head):
        @pl.when(level < LEVELS - 1)
        def _():
            per_count(
                below,
                lambda count: wait_bytes(
                    term_pieces.at[head, pl.ds(0, count)], b1_recv.at[head]
                ),
            )
            total = jnp.dot(
                spread[...], term_pieces[head].reshape((LEVELS - 1) * TILE, HEAD_DIM),
                preferred_element_type=F32,
            )
            final_out[head] = total.astype(BF16).reshape(SEGS, PIECE, HEAD_DIM)

            @pl.loop(1, SEGS)
            def _(step):
                peer = wrapped(me + step)
                remote(
                    final_out.at[head, peer], final_in.at[head, me],
                    f_send.at[head], f_recv.at[head], (level, peer),
                ).start()

            pltpu.make_async_copy(
                final_out.at[head, me], final_in.at[head, me], f_recv.at[head]
            ).start()

    def store(head):
        @pl.when(level < LEVELS - 1)
        def _():
            wait_bytes(final_in.at[head], f_recv.at[head])
            for part in range(2):
                own[head, part] += final_in[head, halves[part]].reshape(
                    ROWS, HEAD_DIM
                ).astype(F32)

        grad_kv[0, 0, :, :, lanes(head)] = own[head].astype(BF16)

    @pl.loop(0, KV_HEADS + 2)
    def _(tick):
        @pl.when(tick < KV_HEADS)
        def _():
            per_count(
                level,
                lambda count: wait_bytes(blocks.at[tick, pl.ds(1, count)], p3_recv.at[tick]),
            )
            attend(tick)
            send_terms(tick)

        @pl.when((tick >= 1) & (tick < KV_HEADS + 1))
        def _():
            sum_and_return(tick - 1)

        @pl.when(tick >= 2)
        def _():
            store(tick - 2)

    for group, heads in enumerate(groups):
        wait_bytes(pieces.at[heads, pl.ds(1, SEGS - 1)], p1_send.at[group])

    @pl.loop(0, KV_HEADS)
    def _(head):
        per_count(
            below, lambda count: wait_bytes(chosen.at[head, pl.ds(0, count)], p3_send.at[head])
        )
        per_count(
            level, lambda count: wait_bytes(terms.at[head, pl.ds(1, count)], b1_send.at[head])
        )

        @pl.when(level < LEVELS - 1)
        def _():
            wait_bytes(final_out.at[head, pl.ds(1, SEGS - 1)], f_send.at[head])


def shards(queries, keys_values, grad_out, parents):
    vmem = pl.BlockSpec(memory_space=pltpu.VMEM)
    smem = pl.BlockSpec(memory_space=pltpu.SMEM)
    hbm = pl.BlockSpec(memory_space=pltpu.HBM)
    dma = pltpu.SemaphoreType.DMA
    tile = (SEGS, PIECE, HEAD_DIM)
    keys_count = LEVELS * ROWS
    scratch = [
        pltpu.SMEM((LEVELS, SEGS), jnp.int32),
        pltpu.VMEM((LEVELS - 1, TILE, TILE), BF16),
        pltpu.VMEM((TILE, (LEVELS - 1) * TILE), BF16),
        pltpu.VMEM(keys_values.shape, BF16),
        pltpu.VMEM(queries.shape, BF16),
        pltpu.VMEM(queries.shape, BF16),
        pltpu.VMEM((KV_HEADS,) + tile, BF16),
        pltpu.VMEM((KV_HEADS,) + tile, BF16),
        pltpu.VMEM((KV_HEADS, LEVELS - 1) + tile, BF16),
        pltpu.VMEM((KV_HEADS, LEVELS) + tile, BF16),
        pltpu.VMEM((KV_HEADS, LEVELS) + tile, BF16),
        pltpu.VMEM((KV_HEADS, LEVELS - 1) + tile, BF16),
        pltpu.VMEM((KV_HEADS, 2, ROWS, HEAD_DIM), F32),
        pltpu.VMEM((2, STACK, HEAD_DIM), BF16),
        pltpu.VMEM((2, HEAD_DIM, STACK), BF16),
        pltpu.VMEM((HEAD_DIM, STACK), F32),
        pltpu.VMEM((3, 8, STACK), F32),
        pltpu.VMEM((keys_count, STACK), F32),
        pltpu.VMEM((keys_count, STACK), F32),
        pltpu.VMEM((PAIR, STACK), BF16),
        pltpu.VMEM((PAIR, STACK), BF16),
        pltpu.VMEM((KV_HEADS,) + tile, BF16),
        pltpu.VMEM((KV_HEADS,) + tile, BF16),
        dma, dma, dma,
        pltpu.SemaphoreType.REGULAR,
        dma((2,)), dma((2,)),
        dma((KV_HEADS,)), dma((KV_HEADS,)),
        dma((KV_HEADS,)), dma((KV_HEADS,)),
        dma((KV_HEADS,)), dma((KV_HEADS,)),
    ]
    return pl.pallas_call(
        kernel,
        out_shape=(
            jax.ShapeDtypeStruct(queries.shape, BF16),
            jax.ShapeDtypeStruct(keys_values.shape, BF16),
        ),
        in_specs=[smem, hbm, hbm, hbm],
        out_specs=(vmem, vmem),
        scratch_shapes=scratch,
        compiler_params=pltpu.CompilerParams(
            collective_id=0, has_side_effects=True, vmem_limit_bytes=32 * 1024 * 1024
        ),
        cost_estimate=pl.CostEstimate(
            flops=5 * 2 * HEADS * LEVELS * ROWS * ROWS * HEAD_DIM,
            bytes_accessed=8 * 1024 * 1024,
            transcendentals=HEADS * LEVELS * ROWS * ROWS,
        ),
    )(parents.transpose(0, 2, 1), queries, keys_values, grad_out)


def solution(mesh):
    in_specs = (
        P("depth", "seg", None, None),
        P("depth", "seg", None, None, None),
        P("depth", "seg", None, None),
        P(),
    )
    out_specs = (P("depth", "seg", None, None), P("depth", "seg", None, None, None))
    return jax.shard_map(shards, mesh=mesh, in_specs=in_specs, out_specs=out_specs, check_vma=False)
```

```python
import functools

import jax
import jax.numpy as jnp
from jax import lax
from jax.experimental import pallas as pl
from jax.experimental.pallas import tpu as pltpu
from jax.sharding import PartitionSpec as P

HEADS = 20
KV_HEADS = 4
HEAD_DIM = 128
GROUP = HEADS // KV_HEADS
ROWS = 128
LEVELS = 8
SEGS = 16
PIECE = 16
PIECES_PER_PART = ROWS // PIECE
STACK = GROUP * ROWS
PAIR = 2 * ROWS
TILE = SEGS * PIECE
OWNERS = SEGS // 2

NEG_FILL = -1e30
SCALE = HEAD_DIM ** -0.5
EXP2_SCALE = SCALE * 1.4426950408889634
MESH = pl.DeviceIdType.MESH
BF16 = jnp.bfloat16
F32 = jnp.float32


def half(value):
    return lax.div(value, 2)


def odd(value):
    return lax.rem(value, 2)


def wrapped(index):
    return jnp.where(index >= SEGS, index - SEGS, index)


def lanes(index, count=1):
    width = count * HEAD_DIM
    return pl.ds(pl.multiple_of(index * width, width), width)


def rows_of(index, count):
    return pl.ds(pl.multiple_of(index * count, count), count)


def owner_column(owner, parity):
    z = half(owner)
    return 4 * z + 2 * odd(owner) + odd(z + parity)


def fold(tile):
    return tile.reshape(tile.shape[0] // 8, 8, tile.shape[1])


def kernel(
    parents, queries, keys_values, grad_out, grad_queries, grad_kv,
    anc, pick, spread, kv_in, q_in, g_in, kv_stage, pieces, chosen, blocks,
    terms, term_pieces, own, stacks, turned, query_sum, logits, grad_probs,
    probs, grad_logits, final_out, final_in,
    kv_sem, q_sem, g_sem, ready, p1_send, p1_recv, p3_send, p3_recv, b1_send, b1_recv,
    f_send, f_recv,
):
    level = lax.axis_index("depth")
    me = lax.axis_index("seg")
    below = LEVELS - 1 - level
    my_z, my_x = lax.div(me, 4), lax.rem(me, 4)
    my_parity = odd(my_z + my_x)
    my_owner = 2 * my_z + half(my_x)

    def remote(src, dst, send_sem, recv_sem, device):
        return pltpu.make_async_remote_copy(
            src_ref=src, dst_ref=dst, send_sem=send_sem, recv_sem=recv_sem,
            device_id=device, device_id_type=MESH,
        )

    def wait_bytes(ref, sem):
        pltpu.make_async_copy(ref, ref, sem).wait()

    def per_count(which, action):
        for count in range(1, LEVELS):
            pl.when(which == count)(functools.partial(action, count))

    load_kv = pltpu.make_async_copy(keys_values, kv_in, kv_sem)
    load_q = pltpu.make_async_copy(queries, q_in, q_sem)
    load_g = pltpu.make_async_copy(grad_out, g_in, g_sem)
    load_kv.start()
    load_q.start()
    load_g.start()

    barrier = pltpu.get_barrier_semaphore()

    def in_line(step):
        other = level + step
        return (jnp.where(other >= LEVELS, other - LEVELS, other), me)

    @pl.loop(1, SEGS)
    def _(step):
        pl.semaphore_signal(
            barrier, inc=1, device_id=(level, wrapped(me + step)), device_id_type=MESH
        )

    @pl.loop(1, LEVELS)
    def _(step):
        pl.semaphore_signal(barrier, inc=1, device_id=in_line(step), device_id_type=MESH)

    @pl.loop(0, SEGS)
    def _(column):
        anc[0, column] = column

    @pl.loop(1, below + 1)
    def _(offset):
        @pl.loop(0, SEGS)
        def _(column):
            anc[offset, column] = anc[offset - 1, parents[level + offset - 1, 0, column]]

    load_kv.wait()
    for head in range(KV_HEADS):
        for part in range(2):
            kv_stage[head, pl.ds(part * PIECES_PER_PART, PIECES_PER_PART)] = kv_in[
                0, 0, part, :, head * HEAD_DIM:(head + 1) * HEAD_DIM
            ].reshape(PIECES_PER_PART, PIECE, HEAD_DIM)
    pl.semaphore_wait(barrier, SEGS - 1 + LEVELS - 1)

    def spread_out(group, heads):
        @pl.loop(1, SEGS)
        def _(step):
            peer = wrapped(me + step)
            remote(
                kv_stage.at[heads, peer], pieces.at[heads, me],
                p1_send.at[group], p1_recv.at[group], (level, peer),
            ).start()

        pltpu.make_async_copy(
            kv_stage.at[heads, me], pieces.at[heads, me], p1_recv.at[group]
        ).start()

    groups = (pl.ds(0, 1), pl.ds(1, KV_HEADS - 1))
    for group, heads in enumerate(groups):
        spread_out(group, heads)

    @pl.loop(1, LEVELS)
    def _(step):
        pl.semaphore_signal(ready, inc=1, device_id=in_line(step), device_id_type=MESH)

    @pl.loop(1, below + 1)
    def _(offset):
        lane = lax.broadcasted_iota(jnp.int32, (PIECE, TILE), 1)
        row = lax.broadcasted_iota(jnp.int32, (PIECE, TILE), 0)
        ahead = lane - row
        for column in range(SEGS):
            pick[offset - 1, rows_of(column, PIECE), :] = jnp.where(
                ahead == anc[offset, column] * PIECE, 1.0, 0.0
            ).astype(BF16)

    def pick_and_send(head):
        def pick_up(count):
            found = jnp.dot(
                pick[0:count].reshape(count * TILE, TILE),
                pieces[head].reshape(TILE, HEAD_DIM), preferred_element_type=F32,
            )
            chosen[head, 0:count] = found.astype(BF16).reshape(count, SEGS, PIECE, HEAD_DIM)

        pl.when((below > 0) & (below <= 2))(lambda: pick_up(2))
        pl.when((below > 2) & (below <= 4))(lambda: pick_up(4))
        pl.when(below > 4)(lambda: pick_up(LEVELS - 1))

        @pl.loop(0, below)
        def _(step):
            offset = below - step
            for turn in range(SEGS):
                column = wrapped(me + turn)
                remote(
                    chosen.at[head, offset - 1, column], blocks.at[head, offset, me],
                    p3_send.at[head], p3_recv.at[head], (level + offset, column),
                ).start()

    wait_bytes(pieces.at[groups[0]], p1_recv.at[0])
    pl.semaphore_wait(ready, LEVELS - 1)

    @pl.loop(0, KV_HEADS)
    def _(head):
        @pl.when(head == 1)
        def _():
            wait_bytes(pieces.at[groups[1]], p1_recv.at[1])

        pick_and_send(head)

    @pl.loop(0, KV_HEADS)
    def _(head):
        blocks[head, 0] = kv_stage[head]

        @pl.when(odd(level) == 0)
        def _():
            blocks[head, level + 1] = jnp.zeros((SEGS, PIECE, HEAD_DIM), BF16)

    @pl.loop(1, below + 1)
    def _(offset):
        lane = lax.broadcasted_iota(jnp.int32, (PIECE, TILE), 1)
        row = lax.broadcasted_iota(jnp.int32, (PIECE, TILE), 0)
        lane_column = lane >> 4
        span = pl.ds(pl.multiple_of((offset - 1) * TILE, TILE), TILE)
        target = (lane & (PIECE - 1)) - row
        for column in range(SEGS):
            target = jnp.where(
                lane_column == column, target + anc[offset, column] * PIECE, target
            )
        for column in range(SEGS):
            spread[rows_of(column, PIECE), span] = jnp.where(
                target == column * PIECE, 1.0, 0.0
            ).astype(BF16)

    @pl.loop(below, LEVELS - 1)
    def _(index):
        spread[:, pl.ds(pl.multiple_of(index * TILE, TILE), TILE)] = jnp.zeros(
            (TILE, TILE), BF16
        )
        for slot in range(2):
            term_pieces[slot, index] = jnp.zeros((SEGS, 2, PIECE, HEAD_DIM), BF16)

    load_q.wait()
    load_g.wait()
    halves = [pl.ds(part * PIECES_PER_PART, PIECES_PER_PART) for part in range(2)]

    def attend(head, pairs):
        span_all = [pl.ds(group * ROWS, ROWS) for group in range(GROUP)]

        def block_pair(pair, part):
            return blocks[head, 2 * pair:2 * pair + 2, halves[part]].reshape(PAIR, HEAD_DIM)

        for index in range(2):
            for group, span in enumerate(span_all):
                tile = (q_in, g_in)[index][0, 0, :, lanes(head * GROUP + group)]
                stacks[index, span, :] = tile
                turned[index, :, span] = tile.T
        u_row = lax.broadcasted_iota(jnp.int32, (ROWS, ROWS), 0)
        t_row = lax.broadcasted_iota(jnp.int32, (ROWS, ROWS), 1)
        last_seen = odd(level) == 1
        best = [jnp.full((8, ROWS), NEG_FILL, F32) for group in range(GROUP)]
        for pair in range(pairs):
            raw = jnp.dot(block_pair(pair, 0), turned[0], preferred_element_type=F32)
            for group, span in enumerate(span_all):
                first = raw[0:ROWS, group * ROWS:(group + 1) * ROWS]
                second = raw[ROWS:PAIR, group * ROWS:(group + 1) * ROWS]
                if pair == 0:
                    first = jnp.where(u_row <= t_row, first, NEG_FILL)
                if pair == pairs - 1:
                    second = jnp.where(last_seen, second, NEG_FILL)
                logits[pair * PAIR:pair * PAIR + ROWS, span] = first
                logits[pair * PAIR + ROWS:(pair + 1) * PAIR, span] = second
                best[group] = jnp.maximum(
                    best[group], jnp.maximum(fold(first).max(0), fold(second).max(0))
                )
        top = [value.max(0, keepdims=True) for value in best]
        total = [jnp.zeros((8, ROWS), F32) for group in range(GROUP)]
        delta = [jnp.zeros((8, ROWS), F32) for group in range(GROUP)]
        for pair in range(pairs):
            rows = slice(pair * PAIR, (pair + 1) * PAIR)
            raw = jnp.dot(block_pair(pair, 1), turned[1], preferred_element_type=F32)
            for group, span in enumerate(span_all):
                tile = jnp.exp2((logits[rows, span] - top[group]) * EXP2_SCALE)
                part = raw[:, group * ROWS:(group + 1) * ROWS]
                logits[rows, span] = tile
                grad_probs[rows, span] = part
                total[group] += fold(tile).sum(0)
                delta[group] += fold(tile * part).sum(0)
        inverse = [1.0 / value.sum(0, keepdims=True) for value in total]
        delta = [value.sum(0, keepdims=True) * by for value, by in zip(delta, inverse)]
        for pair in range(pairs):
            rows = slice(pair * PAIR, (pair + 1) * PAIR)
            for group, span in enumerate(span_all):
                exact = logits[rows, span] * inverse[group]
                probs[rows, span] = exact.astype(BF16)
                grad_logits[rows, span] = (
                    exact * (grad_probs[rows, span] - delta[group])
                ).astype(BF16)
            value_term = jnp.dot(probs[rows, :], stacks[1], preferred_element_type=F32)
            key_term = SCALE * jnp.dot(
                grad_logits[rows, :], stacks[0], preferred_element_type=F32
            )
            for part, term in enumerate((key_term, value_term)):
                terms[head, 2 * pair:2 * pair + 2, halves[part]] = term.astype(BF16).reshape(
                    2, PIECES_PER_PART, PIECE, HEAD_DIM
                )
                if pair == 0:
                    own[head, part] = term[0:ROWS]
            moved = lax.dot_general(
                block_pair(pair, 0), grad_logits[rows, :], (((0,), (0,)), ((), ())),
                preferred_element_type=F32,
            )
            if pair == 0:
                query_sum[...] = moved
            else:
                query_sum[...] += moved
        for group, span in enumerate(span_all):
            grad_queries[0, 0, :, lanes(head * GROUP + group)] = (
                SCALE * query_sum[:, span].T
            ).astype(BF16)

    def send_terms(head):
        targets = []
        for turn in range(OWNERS):
            owner = my_owner + turn
            owner = jnp.where(owner >= OWNERS, owner - OWNERS, owner)
            targets.append((owner, owner_column(owner, odd(head))))

        @pl.loop(0, level)
        def _(step):
            offset = level - step
            for owner, column in targets:
                remote(
                    terms.at[head, offset, pl.ds(2 * owner, 2)],
                    term_pieces.at[half(head), offset - 1, me],
                    b1_send.at[head], b1_recv.at[half(head)], (level - offset, column),
                ).start()

    def sum_and_return(head):
        slot = half(head)

        @pl.when((level < LEVELS - 1) & (odd(head) == my_parity))
        def _():
            per_count(
                below,
                lambda count: wait_bytes(
                    term_pieces.at[slot, pl.ds(0, count)], b1_recv.at[slot]
                ),
            )

            def add_up(count):
                received = term_pieces[slot, 0:count]
                total = jnp.dot(
                    spread[:, 0:count * TILE],
                    jnp.concatenate(
                        [
                            received[:, :, index].reshape(count * TILE, HEAD_DIM)
                            for index in range(2)
                        ],
                        axis=1,
                    ),
                    preferred_element_type=F32,
                )
                for index in range(2):
                    final_out[slot, :, index] = total[
                        :, index * HEAD_DIM:(index + 1) * HEAD_DIM
                    ].astype(BF16).reshape(SEGS, PIECE, HEAD_DIM)

            pl.when(below <= 2)(lambda: add_up(2))
            pl.when((below > 2) & (below <= 4))(lambda: add_up(4))
            pl.when(below > 4)(lambda: add_up(LEVELS - 1))
            landing = final_in.at[head, pl.ds(2 * my_owner, 2)]
            for turn in range(1, SEGS):
                peer = wrapped(me + turn)
                remote(
                    final_out.at[slot, peer], landing,
                    f_send.at[slot], f_recv.at[head], (level, peer),
                ).start()
            pltpu.make_async_copy(final_out.at[slot, me], landing, f_recv.at[head]).start()

    def store(head):
        @pl.when(level < LEVELS - 1)
        def _():
            wait_bytes(final_in.at[head], f_recv.at[head])
            for part in range(2):
                own[head, part] += final_in[head, halves[part]].reshape(
                    ROWS, HEAD_DIM
                ).astype(F32)

        grad_kv[0, 0, :, :, lanes(head)] = own[head].astype(BF16)

    @pl.loop(0, KV_HEADS + 2)
    def _(tick):
        @pl.when(tick < KV_HEADS)
        def _():
            per_count(
                level,
                lambda count: wait_bytes(blocks.at[tick, pl.ds(1, count)], p3_recv.at[tick]),
            )
            for pairs in range(1, LEVELS // 2 + 1):
                pl.when(half(level) == pairs - 1)(functools.partial(attend, tick, pairs))
            send_terms(tick)

        @pl.when((tick >= 1) & (tick < KV_HEADS + 1))
        def _():
            sum_and_return(tick - 1)

        @pl.when(tick >= 2)
        def _():
            store(tick - 2)

    for group, heads in enumerate(groups):
        wait_bytes(pieces.at[heads, pl.ds(1, SEGS - 1)], p1_send.at[group])

    @pl.loop(0, KV_HEADS)
    def _(head):
        per_count(
            below, lambda count: wait_bytes(chosen.at[head, pl.ds(0, count)], p3_send.at[head])
        )
        per_count(
            level, lambda count: wait_bytes(terms.at[head, pl.ds(1, count)], b1_send.at[head])
        )

    @pl.when(level < LEVELS - 1)
    def _():
        for slot in range(2):
            wait_bytes(final_out.at[slot, pl.ds(1, SEGS - 1)], f_send.at[slot])


def shards(queries, keys_values, grad_out, parents):
    vmem = pl.BlockSpec(memory_space=pltpu.VMEM)
    smem = pl.BlockSpec(memory_space=pltpu.SMEM)
    hbm = pl.BlockSpec(memory_space=pltpu.HBM)
    dma = pltpu.SemaphoreType.DMA
    tile = (SEGS, PIECE, HEAD_DIM)
    keys_count = LEVELS * ROWS
    scratch = [
        pltpu.SMEM((LEVELS, SEGS), jnp.int32),
        pltpu.VMEM((LEVELS - 1, TILE, TILE), BF16),
        pltpu.VMEM((TILE, (LEVELS - 1) * TILE), BF16),
        pltpu.VMEM(keys_values.shape, BF16),
        pltpu.VMEM(queries.shape, BF16),
        pltpu.VMEM(queries.shape, BF16),
        pltpu.VMEM((KV_HEADS,) + tile, BF16),
        pltpu.VMEM((KV_HEADS,) + tile, BF16),
        pltpu.VMEM((KV_HEADS, LEVELS - 1) + tile, BF16),
        pltpu.VMEM((KV_HEADS, LEVELS) + tile, BF16),
        pltpu.VMEM((KV_HEADS, LEVELS) + tile, BF16),
        pltpu.VMEM((2, LEVELS - 1, SEGS, 2, PIECE, HEAD_DIM), BF16),
        pltpu.VMEM((KV_HEADS, 2, ROWS, HEAD_DIM), F32),
        pltpu.VMEM((2, STACK, HEAD_DIM), BF16),
        pltpu.VMEM((2, HEAD_DIM, STACK), BF16),
        pltpu.VMEM((HEAD_DIM, STACK), F32),
        pltpu.VMEM((keys_count, STACK), F32),
        pltpu.VMEM((keys_count, STACK), F32),
        pltpu.VMEM((keys_count, STACK), BF16),
        pltpu.VMEM((keys_count, STACK), BF16),
        pltpu.VMEM((2, SEGS, 2, PIECE, HEAD_DIM), BF16),
        pltpu.VMEM((KV_HEADS,) + tile, BF16),
        dma, dma, dma,
        pltpu.SemaphoreType.REGULAR,
        dma((2,)), dma((2,)),
        dma((KV_HEADS,)), dma((KV_HEADS,)),
        dma((KV_HEADS,)), dma((2,)),
        dma((2,)), dma((KV_HEADS,)),
    ]
    return pl.pallas_call(
        kernel,
        out_shape=(
            jax.ShapeDtypeStruct(queries.shape, BF16),
            jax.ShapeDtypeStruct(keys_values.shape, BF16),
        ),
        in_specs=[smem, hbm, hbm, hbm],
        out_specs=(vmem, vmem),
        scratch_shapes=scratch,
        compiler_params=pltpu.CompilerParams(
            collective_id=0, has_side_effects=True, vmem_limit_bytes=56 * 1024 * 1024
        ),
        cost_estimate=pl.CostEstimate(
            flops=5 * 2 * HEADS * LEVELS * ROWS * ROWS * HEAD_DIM,
            bytes_accessed=8 * 1024 * 1024,
            transcendentals=HEADS * LEVELS * ROWS * ROWS,
        ),
    )(parents.transpose(0, 2, 1), queries, keys_values, grad_out)


def solution(mesh):
    in_specs = (
        P("depth", "seg", None, None),
        P("depth", "seg", None, None, None),
        P("depth", "seg", None, None),
        P(),
    )
    out_specs = (P("depth", "seg", None, None), P("depth", "seg", None, None, None))
    return jax.shard_map(shards, mesh=mesh, in_specs=in_specs, out_specs=out_specs, check_vma=False)
```

```python
import functools

import jax
import jax.numpy as jnp
from jax import lax
from jax.experimental import pallas as pl
from jax.experimental.pallas import tpu as pltpu
from jax.sharding import PartitionSpec as P

HEADS = 20
KV_HEADS = 4
HEAD_DIM = 128
GROUP = HEADS // KV_HEADS
ROWS = 128
LEVELS = 8
SEGS = 16
PIECE = 16
PIECES_PER_PART = ROWS // PIECE
STACK = GROUP * ROWS
PAIR = 2 * ROWS
TILE = SEGS * PIECE
OWNERS = SEGS // 2

NEG_FILL = -1e30
SCALE = HEAD_DIM ** -0.5
EXP2_SCALE = SCALE * 1.4426950408889634
MESH = pl.DeviceIdType.MESH
BF16 = jnp.bfloat16
F32 = jnp.float32


def half(value):
    return lax.div(value, 2)


def odd(value):
    return lax.rem(value, 2)


def wrapped(index):
    return jnp.where(index >= SEGS, index - SEGS, index)


def lanes(index, count=1):
    width = count * HEAD_DIM
    return pl.ds(pl.multiple_of(index * width, width), width)


def rows_of(index, count):
    return pl.ds(pl.multiple_of(index * count, count), count)


def owner_column(owner, parity):
    z = half(owner)
    return 4 * z + 2 * odd(owner) + odd(z + parity)


def fold(tile):
    return tile.reshape(tile.shape[0] // 8, 8, tile.shape[1])


def kernel(
    parents, queries, keys_values, grad_out, grad_queries, grad_kv,
    anc, pick, spread, kv_in, q_in, g_in, kv_stage, pieces, chosen, blocks,
    terms, term_pieces, own, stacks, turned, query_sum, logits, grad_probs,
    probs, grad_logits, final_out, final_in,
    kv_sem, q_sem, g_sem, ready, p1_send, p1_recv, p3_send, p3_recv, b1_send, b1_recv,
    f_send, f_recv,
):
    level = lax.axis_index("depth")
    me = lax.axis_index("seg")
    below = LEVELS - 1 - level
    my_z, my_x = lax.div(me, 4), lax.rem(me, 4)
    my_parity = odd(my_z + my_x)
    my_owner = 2 * my_z + half(my_x)

    def remote(src, dst, send_sem, recv_sem, device):
        return pltpu.make_async_remote_copy(
            src_ref=src, dst_ref=dst, send_sem=send_sem, recv_sem=recv_sem,
            device_id=device, device_id_type=MESH,
        )

    def wait_bytes(ref, sem):
        pltpu.make_async_copy(ref, ref, sem).wait()

    def per_count(which, action):
        for count in range(1, LEVELS):
            pl.when(which == count)(functools.partial(action, count))

    load_kv = pltpu.make_async_copy(keys_values, kv_in, kv_sem)
    load_q = pltpu.make_async_copy(queries, q_in, q_sem)
    load_g = pltpu.make_async_copy(grad_out, g_in, g_sem)
    load_kv.start()
    load_q.start()
    load_g.start()

    barrier = pltpu.get_barrier_semaphore()

    def in_line(step):
        other = level + step
        return (jnp.where(other >= LEVELS, other - LEVELS, other), me)

    @pl.loop(1, SEGS)
    def _(step):
        pl.semaphore_signal(
            barrier, inc=1, device_id=(level, wrapped(me + step)), device_id_type=MESH
        )

    @pl.loop(1, LEVELS)
    def _(step):
        pl.semaphore_signal(barrier, inc=1, device_id=in_line(step), device_id_type=MESH)

    @pl.loop(0, SEGS)
    def _(column):
        anc[0, column] = column

    @pl.loop(1, below + 1)
    def _(offset):
        @pl.loop(0, SEGS)
        def _(column):
            anc[offset, column] = anc[offset - 1, parents[level + offset - 1, 0, column]]

    load_kv.wait()
    for head in range(KV_HEADS):
        for part in range(2):
            kv_stage[head, pl.ds(part * PIECES_PER_PART, PIECES_PER_PART)] = kv_in[
                0, 0, part, :, head * HEAD_DIM:(head + 1) * HEAD_DIM
            ].reshape(PIECES_PER_PART, PIECE, HEAD_DIM)
    pl.semaphore_wait(barrier, SEGS - 1 + LEVELS - 1)

    def owner_after(turn):
        owner = my_owner + turn
        return jnp.where(owner >= OWNERS, owner - OWNERS, owner)

    for slot in range(2):
        for turn in range(OWNERS):
            for parity in range(2):
                owner = owner_after(turn)
                source = kv_stage.at[2 * slot + parity, pl.ds(2 * owner, 2)]
                copy = remote(
                    source, pieces.at[slot, me], p1_send.at[slot], p1_recv.at[slot],
                    (level, owner_column(owner, parity)),
                )
                if turn > 0:
                    copy.start()
                else:
                    pl.when(my_parity != parity)(copy.start)
                    pl.when(my_parity == parity)(
                        pltpu.make_async_copy(source, pieces.at[slot, me], p1_recv.at[slot]).start
                    )

    @pl.loop(1, LEVELS)
    def _(step):
        pl.semaphore_signal(ready, inc=1, device_id=in_line(step), device_id_type=MESH)

    @pl.loop(1, below + 1)
    def _(offset):
        lane = lax.broadcasted_iota(jnp.int32, (PIECE, TILE), 1)
        row = lax.broadcasted_iota(jnp.int32, (PIECE, TILE), 0)
        ahead = lane - row
        for column in range(SEGS):
            pick[offset - 1, rows_of(column, PIECE), :] = jnp.where(
                ahead == anc[offset, column] * PIECE, 1.0, 0.0
            ).astype(BF16)

    def pick_and_send(slot):
        wait_bytes(pieces.at[slot], p1_recv.at[slot])
        head = 2 * slot + my_parity

        def pick_up(count):
            found = jnp.dot(
                pick[0:count].reshape(count * TILE, TILE),
                jnp.concatenate(
                    [pieces[slot, :, index].reshape(TILE, HEAD_DIM) for index in range(2)], axis=1
                ),
                preferred_element_type=F32,
            ).astype(BF16)
            for index in range(2):
                chosen[slot, 0:count, :, index] = found[
                    :, index * HEAD_DIM:(index + 1) * HEAD_DIM
                ].reshape(count, SEGS, PIECE, HEAD_DIM)

        pl.when((below > 0) & (below <= 2))(lambda: pick_up(2))
        pl.when((below > 2) & (below <= 4))(lambda: pick_up(4))
        pl.when(below > 4)(lambda: pick_up(LEVELS - 1))

        @pl.loop(0, below)
        def _(step):
            offset = below - step
            for turn in range(SEGS):
                column = wrapped(me + turn)
                remote(
                    chosen.at[slot, offset - 1, column],
                    blocks.at[head, offset, pl.ds(2 * my_owner, 2)],
                    p3_send.at[slot], p3_recv.at[head], (level + offset, column),
                ).start()

    pl.semaphore_wait(ready, LEVELS - 1)
    pl.loop(0, 2)(pick_and_send)

    @pl.loop(0, KV_HEADS)
    def _(head):
        blocks[head, 0] = kv_stage[head]

        @pl.when(odd(level) == 0)
        def _():
            blocks[head, level + 1] = jnp.zeros((SEGS, PIECE, HEAD_DIM), BF16)

    @pl.loop(1, below + 1)
    def _(offset):
        lane = lax.broadcasted_iota(jnp.int32, (PIECE, TILE), 1)
        row = lax.broadcasted_iota(jnp.int32, (PIECE, TILE), 0)
        lane_column = lane >> 4
        span = pl.ds(pl.multiple_of((offset - 1) * TILE, TILE), TILE)
        target = (lane & (PIECE - 1)) - row
        for column in range(SEGS):
            target = jnp.where(
                lane_column == column, target + anc[offset, column] * PIECE, target
            )
        for column in range(SEGS):
            spread[rows_of(column, PIECE), span] = jnp.where(
                target == column * PIECE, 1.0, 0.0
            ).astype(BF16)

    @pl.loop(below, LEVELS - 1)
    def _(index):
        spread[:, pl.ds(pl.multiple_of(index * TILE, TILE), TILE)] = jnp.zeros(
            (TILE, TILE), BF16
        )
        for slot in range(2):
            term_pieces[slot, index] = jnp.zeros((SEGS, 2, PIECE, HEAD_DIM), BF16)

    load_q.wait()
    load_g.wait()
    halves = [pl.ds(part * PIECES_PER_PART, PIECES_PER_PART) for part in range(2)]

    def attend(head, pairs):
        span_all = [pl.ds(group * ROWS, ROWS) for group in range(GROUP)]

        def block_pair(pair, part):
            return blocks[head, 2 * pair:2 * pair + 2, halves[part]].reshape(PAIR, HEAD_DIM)

        for index in range(2):
            for group, span in enumerate(span_all):
                tile = (q_in, g_in)[index][0, 0, :, lanes(head * GROUP + group)]
                stacks[index, span, :] = tile
                turned[index, :, span] = tile.T
        u_row = lax.broadcasted_iota(jnp.int32, (ROWS, ROWS), 0)
        t_row = lax.broadcasted_iota(jnp.int32, (ROWS, ROWS), 1)
        last_seen = odd(level) == 1
        best = [jnp.full((8, ROWS), NEG_FILL, F32) for group in range(GROUP)]
        for pair in range(pairs):
            raw = jnp.dot(block_pair(pair, 0), turned[0], preferred_element_type=F32)
            for group, span in enumerate(span_all):
                first = raw[0:ROWS, group * ROWS:(group + 1) * ROWS]
                second = raw[ROWS:PAIR, group * ROWS:(group + 1) * ROWS]
                if pair == 0:
                    first = jnp.where(u_row <= t_row, first, NEG_FILL)
                if pair == pairs - 1:
                    second = jnp.where(last_seen, second, NEG_FILL)
                logits[pair * PAIR:pair * PAIR + ROWS, span] = first
                logits[pair * PAIR + ROWS:(pair + 1) * PAIR, span] = second
                best[group] = jnp.maximum(
                    best[group], jnp.maximum(fold(first).max(0), fold(second).max(0))
                )
        top = [value.max(0, keepdims=True) for value in best]
        total = [jnp.zeros((8, ROWS), F32) for group in range(GROUP)]
        delta = [jnp.zeros((8, ROWS), F32) for group in range(GROUP)]
        for pair in range(pairs):
            rows = slice(pair * PAIR, (pair + 1) * PAIR)
            raw = jnp.dot(block_pair(pair, 1), turned[1], preferred_element_type=F32)
            for group, span in enumerate(span_all):
                tile = jnp.exp2((logits[rows, span] - top[group]) * EXP2_SCALE)
                part = raw[:, group * ROWS:(group + 1) * ROWS]
                logits[rows, span] = tile
                grad_probs[rows, span] = part
                total[group] += fold(tile).sum(0)
                delta[group] += fold(tile * part).sum(0)
        inverse = [1.0 / value.sum(0, keepdims=True) for value in total]
        delta = [value.sum(0, keepdims=True) * by for value, by in zip(delta, inverse)]
        for pair in range(pairs):
            rows = slice(pair * PAIR, (pair + 1) * PAIR)
            for group, span in enumerate(span_all):
                exact = logits[rows, span] * inverse[group]
                probs[rows, span] = exact.astype(BF16)
                grad_logits[rows, span] = (
                    exact * (grad_probs[rows, span] - delta[group])
                ).astype(BF16)
            value_term = jnp.dot(probs[rows, :], stacks[1], preferred_element_type=F32)
            key_term = SCALE * jnp.dot(
                grad_logits[rows, :], stacks[0], preferred_element_type=F32
            )
            for part, term in enumerate((key_term, value_term)):
                terms[head, 2 * pair:2 * pair + 2, halves[part]] = term.astype(BF16).reshape(
                    2, PIECES_PER_PART, PIECE, HEAD_DIM
                )
                if pair == 0:
                    own[head, part] = term[0:ROWS]
            moved = lax.dot_general(
                block_pair(pair, 0), grad_logits[rows, :], (((0,), (0,)), ((), ())),
                preferred_element_type=F32,
            )
            if pair == 0:
                query_sum[...] = moved
            else:
                query_sum[...] += moved
        for group, span in enumerate(span_all):
            grad_queries[0, 0, :, lanes(head * GROUP + group)] = (
                SCALE * query_sum[:, span].T
            ).astype(BF16)

    def send_terms(head):
        targets = []
        for turn in range(OWNERS):
            owner = owner_after(turn)
            targets.append((owner, owner_column(owner, odd(head))))

        @pl.loop(0, level)
        def _(step):
            offset = level - step
            for owner, column in targets:
                remote(
                    terms.at[head, offset, pl.ds(2 * owner, 2)],
                    term_pieces.at[half(head), offset - 1, me],
                    b1_send.at[head], b1_recv.at[half(head)], (level - offset, column),
                ).start()

    def sum_and_return(head):
        slot = half(head)

        @pl.when((level < LEVELS - 1) & (odd(head) == my_parity))
        def _():
            per_count(
                below,
                lambda count: wait_bytes(
                    term_pieces.at[slot, pl.ds(0, count)], b1_recv.at[slot]
                ),
            )

            def add_up(count):
                received = term_pieces[slot, 0:count]
                total = jnp.dot(
                    spread[:, 0:count * TILE],
                    jnp.concatenate(
                        [
                            received[:, :, index].reshape(count * TILE, HEAD_DIM)
                            for index in range(2)
                        ],
                        axis=1,
                    ),
                    preferred_element_type=F32,
                )
                for index in range(2):
                    final_out[slot, :, index] = total[
                        :, index * HEAD_DIM:(index + 1) * HEAD_DIM
                    ].astype(BF16).reshape(SEGS, PIECE, HEAD_DIM)

            pl.when(below <= 2)(lambda: add_up(2))
            pl.when((below > 2) & (below <= 4))(lambda: add_up(4))
            pl.when(below > 4)(lambda: add_up(LEVELS - 1))
            landing = final_in.at[head, pl.ds(2 * my_owner, 2)]
            for turn in range(1, SEGS):
                peer = wrapped(me + turn)
                remote(
                    final_out.at[slot, peer], landing,
                    f_send.at[slot], f_recv.at[head], (level, peer),
                ).start()
            pltpu.make_async_copy(final_out.at[slot, me], landing, f_recv.at[head]).start()

    def store(head):
        @pl.when(level < LEVELS - 1)
        def _():
            wait_bytes(final_in.at[head], f_recv.at[head])
            for part in range(2):
                own[head, part] += final_in[head, halves[part]].reshape(
                    ROWS, HEAD_DIM
                ).astype(F32)

        grad_kv[0, 0, :, :, lanes(head)] = own[head].astype(BF16)

    @pl.loop(0, KV_HEADS + 2)
    def _(tick):
        @pl.when(tick < KV_HEADS)
        def _():
            per_count(
                level,
                lambda count: wait_bytes(blocks.at[tick, pl.ds(1, count)], p3_recv.at[tick]),
            )
            for pairs in range(1, LEVELS // 2 + 1):
                pl.when(half(level) == pairs - 1)(functools.partial(attend, tick, pairs))
            send_terms(tick)

        @pl.when((tick >= 1) & (tick < KV_HEADS + 1))
        def _():
            sum_and_return(tick - 1)

        @pl.when(tick >= 2)
        def _():
            store(tick - 2)

    for slot in range(2):
        wait_bytes(pieces.at[slot, pl.ds(1, SEGS - 1)], p1_send.at[slot])
        per_count(
            below,
            lambda count, slot=slot: wait_bytes(
                chosen.at[slot, pl.ds(0, count)], p3_send.at[slot]
            ),
        )

    @pl.loop(0, KV_HEADS)
    def _(head):
        per_count(
            level, lambda count: wait_bytes(terms.at[head, pl.ds(1, count)], b1_send.at[head])
        )

    @pl.when(level < LEVELS - 1)
    def _():
        for slot in range(2):
            wait_bytes(final_out.at[slot, pl.ds(1, SEGS - 1)], f_send.at[slot])


def shards(queries, keys_values, grad_out, parents):
    vmem = pl.BlockSpec(memory_space=pltpu.VMEM)
    smem = pl.BlockSpec(memory_space=pltpu.SMEM)
    hbm = pl.BlockSpec(memory_space=pltpu.HBM)
    dma = pltpu.SemaphoreType.DMA
    tile = (SEGS, PIECE, HEAD_DIM)
    keys_count = LEVELS * ROWS
    scratch = [
        pltpu.SMEM((LEVELS, SEGS), jnp.int32),
        pltpu.VMEM((LEVELS - 1, TILE, TILE), BF16),
        pltpu.VMEM((TILE, (LEVELS - 1) * TILE), BF16),
        pltpu.VMEM(keys_values.shape, BF16),
        pltpu.VMEM(queries.shape, BF16),
        pltpu.VMEM(queries.shape, BF16),
        pltpu.VMEM((KV_HEADS,) + tile, BF16),
        pltpu.VMEM((2, SEGS, 2, PIECE, HEAD_DIM), BF16),
        pltpu.VMEM((2, LEVELS - 1, SEGS, 2, PIECE, HEAD_DIM), BF16),
        pltpu.VMEM((KV_HEADS, LEVELS) + tile, BF16),
        pltpu.VMEM((KV_HEADS, LEVELS) + tile, BF16),
        pltpu.VMEM((2, LEVELS - 1, SEGS, 2, PIECE, HEAD_DIM), BF16),
        pltpu.VMEM((KV_HEADS, 2, ROWS, HEAD_DIM), F32),
        pltpu.VMEM((2, STACK, HEAD_DIM), BF16),
        pltpu.VMEM((2, HEAD_DIM, STACK), BF16),
        pltpu.VMEM((HEAD_DIM, STACK), F32),
        pltpu.VMEM((keys_count, STACK), F32),
        pltpu.VMEM((keys_count, STACK), F32),
        pltpu.VMEM((keys_count, STACK), BF16),
        pltpu.VMEM((keys_count, STACK), BF16),
        pltpu.VMEM((2, SEGS, 2, PIECE, HEAD_DIM), BF16),
        pltpu.VMEM((KV_HEADS,) + tile, BF16),
        dma, dma, dma,
        pltpu.SemaphoreType.REGULAR,
        dma((2,)), dma((2,)),
        dma((2,)), dma((KV_HEADS,)),
        dma((KV_HEADS,)), dma((2,)),
        dma((2,)), dma((KV_HEADS,)),
    ]
    return pl.pallas_call(
        kernel,
        out_shape=(
            jax.ShapeDtypeStruct(queries.shape, BF16),
            jax.ShapeDtypeStruct(keys_values.shape, BF16),
        ),
        in_specs=[smem, hbm, hbm, hbm],
        out_specs=(vmem, vmem),
        scratch_shapes=scratch,
        compiler_params=pltpu.CompilerParams(
            collective_id=0, has_side_effects=True, vmem_limit_bytes=56 * 1024 * 1024
        ),
        cost_estimate=pl.CostEstimate(
            flops=5 * 2 * HEADS * LEVELS * ROWS * ROWS * HEAD_DIM,
            bytes_accessed=8 * 1024 * 1024,
            transcendentals=HEADS * LEVELS * ROWS * ROWS,
        ),
    )(parents.transpose(0, 2, 1), queries, keys_values, grad_out)


def solution(mesh):
    in_specs = (
        P("depth", "seg", None, None),
        P("depth", "seg", None, None, None),
        P("depth", "seg", None, None),
        P(),
    )
    out_specs = (P("depth", "seg", None, None), P("depth", "seg", None, None, None))
    return jax.shard_map(shards, mesh=mesh, in_specs=in_specs, out_specs=out_specs, check_vma=False)
```

```python
import functools

import jax
import jax.numpy as jnp
from jax import lax
from jax.experimental import pallas as pl
from jax.experimental.pallas import tpu as pltpu
from jax.sharding import PartitionSpec as P

HEADS = 20
KV_HEADS = 4
HEAD_DIM = 128
GROUP = HEADS // KV_HEADS
ROWS = 128
LEVELS = 8
SEGS = 16
PIECE = 16
PIECES_PER_PART = ROWS // PIECE
STACK = GROUP * ROWS
PAIR = 2 * ROWS
TILE = SEGS * PIECE
OWNERS = SEGS // 2

NEG_FILL = -1e30
SCALE = HEAD_DIM ** -0.5
EXP2_SCALE = SCALE * 1.4426950408889634
MESH = pl.DeviceIdType.MESH
BF16 = jnp.bfloat16
F32 = jnp.float32


def half(value):
    return lax.div(value, 2)


def odd(value):
    return lax.rem(value, 2)


def wrapped(index):
    return jnp.where(index >= SEGS, index - SEGS, index)


def lanes(index, count=1):
    width = count * HEAD_DIM
    return pl.ds(pl.multiple_of(index * width, width), width)


def rows_of(index, count):
    return pl.ds(pl.multiple_of(index * count, count), count)


def owner_column(owner, parity):
    z = half(owner)
    return 4 * z + 2 * odd(owner) + odd(z + parity)


def fold(tile):
    return tile.reshape(tile.shape[0] // 8, 8, tile.shape[1])


def remote(src, dst, send_sem, recv_sem, device):
    return pltpu.make_async_remote_copy(
        src_ref=src, dst_ref=dst, send_sem=send_sem, recv_sem=recv_sem,
        device_id=device, device_id_type=MESH,
    )


def wait_bytes(ref, sem):
    pltpu.make_async_copy(ref, ref, sem).wait()


def per_count(which, action):
    for count in range(1, LEVELS):
        pl.when(which == count)(functools.partial(action, count))


def in_line(level, me, step):
    other = level + step
    return (jnp.where(other >= LEVELS, other - LEVELS, other), me)


def owner_after(mine, turn):
    owner = mine + turn
    return jnp.where(owner >= OWNERS, owner - OWNERS, owner)


def greet(level, me):
    barrier = pltpu.get_barrier_semaphore()

    @pl.loop(1, SEGS)
    def _(step):
        pl.semaphore_signal(
            barrier, inc=1, device_id=(level, wrapped(me + step)), device_id_type=MESH
        )

    @pl.loop(1, LEVELS)
    def _(step):
        pl.semaphore_signal(
            barrier, inc=1, device_id=in_line(level, me, step), device_id_type=MESH
        )


def greeted():
    pl.semaphore_wait(pltpu.get_barrier_semaphore(), SEGS - 1 + LEVELS - 1)


def pass_word(ready, level, me):
    @pl.loop(1, LEVELS)
    def _(step):
        pl.semaphore_signal(
            ready, inc=1, device_id=in_line(level, me, step), device_id_type=MESH
        )


def find_columns(parents, anc, level, below):
    @pl.loop(0, SEGS)
    def _(column):
        anc[0, column] = column

    @pl.loop(1, below + 1)
    def _(offset):
        @pl.loop(0, SEGS)
        def _(column):
            anc[offset, column] = anc[offset - 1, parents[level + offset - 1, 0, column]]


def gather_kernel(
    parents, keys_values, blocks,
    anc, pick, kv_stage, pieces, chosen,
    ready, p1_send, p1_recv, p3_send, p3_recv,
):
    level = lax.axis_index("depth")
    me = lax.axis_index("seg")
    below = LEVELS - 1 - level
    my_z, my_x = lax.div(me, 4), lax.rem(me, 4)
    my_parity = odd(my_z + my_x)
    my_owner = 2 * my_z + half(my_x)
    greet(level, me)
    find_columns(parents, anc, level, below)
    for head in range(KV_HEADS):
        for part in range(2):
            kv_stage[head, pl.ds(part * PIECES_PER_PART, PIECES_PER_PART)] = keys_values[
                0, 0, part, :, head * HEAD_DIM:(head + 1) * HEAD_DIM
            ].reshape(PIECES_PER_PART, PIECE, HEAD_DIM)
    greeted()

    for slot in range(2):
        for turn in range(OWNERS):
            for parity in range(2):
                owner = owner_after(my_owner, turn)
                source = kv_stage.at[2 * slot + parity, pl.ds(2 * owner, 2)]
                copy = remote(
                    source, pieces.at[slot, me], p1_send.at[slot], p1_recv.at[slot],
                    (level, owner_column(owner, parity)),
                )
                if turn > 0:
                    copy.start()
                else:
                    pl.when(my_parity != parity)(copy.start)
                    pl.when(my_parity == parity)(
                        pltpu.make_async_copy(source, pieces.at[slot, me], p1_recv.at[slot]).start
                    )

    pass_word(ready, level, me)

    @pl.loop(1, below + 1)
    def _(offset):
        lane = lax.broadcasted_iota(jnp.int32, (PIECE, TILE), 1)
        row = lax.broadcasted_iota(jnp.int32, (PIECE, TILE), 0)
        ahead = lane - row
        for column in range(SEGS):
            pick[offset - 1, rows_of(column, PIECE), :] = jnp.where(
                ahead == anc[offset, column] * PIECE, 1.0, 0.0
            ).astype(BF16)

    def pick_and_send(slot):
        wait_bytes(pieces.at[slot], p1_recv.at[slot])
        head = 2 * slot + my_parity

        def pick_up(count):
            found = jnp.dot(
                pick[0:count].reshape(count * TILE, TILE),
                jnp.concatenate(
                    [pieces[slot, :, index].reshape(TILE, HEAD_DIM) for index in range(2)], axis=1
                ),
                preferred_element_type=F32,
            ).astype(BF16)
            for index in range(2):
                chosen[slot, 0:count, :, index] = found[
                    :, index * HEAD_DIM:(index + 1) * HEAD_DIM
                ].reshape(count, SEGS, PIECE, HEAD_DIM)

        pl.when((below > 0) & (below <= 2))(lambda: pick_up(2))
        pl.when((below > 2) & (below <= 4))(lambda: pick_up(4))
        pl.when(below > 4)(lambda: pick_up(LEVELS - 1))

        @pl.loop(0, below)
        def _(step):
            offset = below - step
            for turn in range(SEGS):
                column = wrapped(me + turn)
                remote(
                    chosen.at[slot, offset - 1, column],
                    blocks.at[head, offset, pl.ds(2 * my_owner, 2)],
                    p3_send.at[slot], p3_recv.at[head], (level + offset, column),
                ).start()

    pl.semaphore_wait(ready, LEVELS - 1)
    pl.loop(0, 2)(pick_and_send)

    @pl.loop(0, KV_HEADS)
    def _(head):
        blocks[head, 0] = kv_stage[head]

        @pl.when(odd(level) == 0)
        def _():
            blocks[head, level + 1] = jnp.zeros((SEGS, PIECE, HEAD_DIM), BF16)

    for slot in range(2):
        wait_bytes(pieces.at[slot, pl.ds(1, SEGS - 1)], p1_send.at[slot])
        per_count(
            below,
            lambda count, slot=slot: wait_bytes(
                chosen.at[slot, pl.ds(0, count)], p3_send.at[slot]
            ),
        )

    @pl.loop(0, KV_HEADS)
    def _(head):
        per_count(
            level,
            lambda count: wait_bytes(blocks.at[head, pl.ds(1, count)], p3_recv.at[head]),
        )


def attend_kernel(
    blocks, queries, grad_out, grad_queries, terms, own,
    stacks, turned, query_sum, logits, grad_probs, probs, grad_logits,
):
    level = lax.axis_index("depth")
    halves = [pl.ds(part * PIECES_PER_PART, PIECES_PER_PART) for part in range(2)]

    def attend(head, pairs):
        span_all = [pl.ds(group * ROWS, ROWS) for group in range(GROUP)]

        def block_pair(pair, part):
            return blocks[head, 2 * pair:2 * pair + 2, halves[part]].reshape(PAIR, HEAD_DIM)

        for index in range(2):
            for group, span in enumerate(span_all):
                tile = (queries, grad_out)[index][0, 0, :, lanes(head * GROUP + group)]
                stacks[index, span, :] = tile
                turned[index, :, span] = tile.T
        u_row = lax.broadcasted_iota(jnp.int32, (ROWS, ROWS), 0)
        t_row = lax.broadcasted_iota(jnp.int32, (ROWS, ROWS), 1)
        last_seen = odd(level) == 1
        best = [jnp.full((8, ROWS), NEG_FILL, F32) for group in range(GROUP)]
        for pair in range(pairs):
            raw = jnp.dot(block_pair(pair, 0), turned[0], preferred_element_type=F32)
            for group, span in enumerate(span_all):
                first = raw[0:ROWS, group * ROWS:(group + 1) * ROWS]
                second = raw[ROWS:PAIR, group * ROWS:(group + 1) * ROWS]
                if pair == 0:
                    first = jnp.where(u_row <= t_row, first, NEG_FILL)
                if pair == pairs - 1:
                    second = jnp.where(last_seen, second, NEG_FILL)
                logits[pair * PAIR:pair * PAIR + ROWS, span] = first
                logits[pair * PAIR + ROWS:(pair + 1) * PAIR, span] = second
                best[group] = jnp.maximum(
                    best[group], jnp.maximum(fold(first).max(0), fold(second).max(0))
                )
        top = [value.max(0, keepdims=True) for value in best]
        total = [jnp.zeros((8, ROWS), F32) for group in range(GROUP)]
        delta = [jnp.zeros((8, ROWS), F32) for group in range(GROUP)]
        for pair in range(pairs):
            rows = slice(pair * PAIR, (pair + 1) * PAIR)
            raw = jnp.dot(block_pair(pair, 1), turned[1], preferred_element_type=F32)
            for group, span in enumerate(span_all):
                tile = jnp.exp2((logits[rows, span] - top[group]) * EXP2_SCALE)
                part = raw[:, group * ROWS:(group + 1) * ROWS]
                logits[rows, span] = tile
                grad_probs[rows, span] = part
                total[group] += fold(tile).sum(0)
                delta[group] += fold(tile * part).sum(0)
        inverse = [1.0 / value.sum(0, keepdims=True) for value in total]
        delta = [value.sum(0, keepdims=True) * by for value, by in zip(delta, inverse)]
        for pair in range(pairs):
            rows = slice(pair * PAIR, (pair + 1) * PAIR)
            for group, span in enumerate(span_all):
                exact = logits[rows, span] * inverse[group]
                probs[rows, span] = exact.astype(BF16)
                grad_logits[rows, span] = (
                    exact * (grad_probs[rows, span] - delta[group])
                ).astype(BF16)
            value_term = jnp.dot(probs[rows, :], stacks[1], preferred_element_type=F32)
            key_term = SCALE * jnp.dot(
                grad_logits[rows, :], stacks[0], preferred_element_type=F32
            )
            for part, term in enumerate((key_term, value_term)):
                terms[head, 2 * pair:2 * pair + 2, halves[part]] = term.astype(BF16).reshape(
                    2, PIECES_PER_PART, PIECE, HEAD_DIM
                )
                if pair == 0:
                    own[head, part] = term[0:ROWS]
            moved = lax.dot_general(
                block_pair(pair, 0), grad_logits[rows, :], (((0,), (0,)), ((), ())),
                preferred_element_type=F32,
            )
            if pair == 0:
                query_sum[...] = moved
            else:
                query_sum[...] += moved
        for group, span in enumerate(span_all):
            grad_queries[0, 0, :, lanes(head * GROUP + group)] = (
                SCALE * query_sum[:, span].T
            ).astype(BF16)

    for pairs in range(1, LEVELS // 2 + 1):
        @pl.when(half(level) == pairs - 1)
        def _():
            pl.loop(0, KV_HEADS)(lambda head: attend(head, pairs))


def reduce_kernel(
    parents, terms, own, grad_kv,
    anc, spread, term_pieces, final_out, final_in,
    ready, b1_send, b1_recv, f_send, f_recv,
):
    level = lax.axis_index("depth")
    me = lax.axis_index("seg")
    below = LEVELS - 1 - level
    my_z, my_x = lax.div(me, 4), lax.rem(me, 4)
    my_parity = odd(my_z + my_x)
    my_owner = 2 * my_z + half(my_x)
    halves = [pl.ds(part * PIECES_PER_PART, PIECES_PER_PART) for part in range(2)]
    greet(level, me)
    find_columns(parents, anc, level, below)
    greeted()
    pass_word(ready, level, me)
    @pl.loop(1, below + 1)
    def _(offset):
        lane = lax.broadcasted_iota(jnp.int32, (PIECE, TILE), 1)
        row = lax.broadcasted_iota(jnp.int32, (PIECE, TILE), 0)
        lane_column = lane >> 4
        span = pl.ds(pl.multiple_of((offset - 1) * TILE, TILE), TILE)
        target = (lane & (PIECE - 1)) - row
        for column in range(SEGS):
            target = jnp.where(
                lane_column == column, target + anc[offset, column] * PIECE, target
            )
        for column in range(SEGS):
            spread[rows_of(column, PIECE), span] = jnp.where(
                target == column * PIECE, 1.0, 0.0
            ).astype(BF16)

    @pl.loop(below, LEVELS - 1)
    def _(index):
        spread[:, pl.ds(pl.multiple_of(index * TILE, TILE), TILE)] = jnp.zeros(
            (TILE, TILE), BF16
        )
        for slot in range(2):
            term_pieces[slot, index] = jnp.zeros((SEGS, 2, PIECE, HEAD_DIM), BF16)

    pl.semaphore_wait(ready, LEVELS - 1)

    def send_terms(head):
        targets = []
        for turn in range(OWNERS):
            owner = owner_after(my_owner, turn)
            targets.append((owner, owner_column(owner, odd(head))))

        @pl.loop(0, level)
        def _(step):
            offset = level - step
            for owner, column in targets:
                remote(
                    terms.at[head, offset, pl.ds(2 * owner, 2)],
                    term_pieces.at[half(head), offset - 1, me],
                    b1_send.at[head], b1_recv.at[half(head)], (level - offset, column),
                ).start()

    def sum_and_return(head):
        slot = half(head)

        @pl.when((level < LEVELS - 1) & (odd(head) == my_parity))
        def _():
            per_count(
                below,
                lambda count: wait_bytes(
                    term_pieces.at[slot, pl.ds(0, count)], b1_recv.at[slot]
                ),
            )

            def add_up(count):
                received = term_pieces[slot, 0:count]
                total = jnp.dot(
                    spread[:, 0:count * TILE],
                    jnp.concatenate(
                        [
                            received[:, :, index].reshape(count * TILE, HEAD_DIM)
                            for index in range(2)
                        ],
                        axis=1,
                    ),
                    preferred_element_type=F32,
                )
                for index in range(2):
                    final_out[slot, :, index] = total[
                        :, index * HEAD_DIM:(index + 1) * HEAD_DIM
                    ].astype(BF16).reshape(SEGS, PIECE, HEAD_DIM)

            pl.when(below <= 2)(lambda: add_up(2))
            pl.when((below > 2) & (below <= 4))(lambda: add_up(4))
            pl.when(below > 4)(lambda: add_up(LEVELS - 1))
            landing = final_in.at[head, pl.ds(2 * my_owner, 2)]
            for turn in range(1, SEGS):
                peer = wrapped(me + turn)
                remote(
                    final_out.at[slot, peer], landing,
                    f_send.at[slot], f_recv.at[head], (level, peer),
                ).start()
            pltpu.make_async_copy(final_out.at[slot, me], landing, f_recv.at[head]).start()

    def store(head):
        @pl.when(level < LEVELS - 1)
        def _():
            wait_bytes(final_in.at[head], f_recv.at[head])
            for part in range(2):
                grad_kv[0, 0, part, :, lanes(head)] = (
                    own[head, part]
                    + final_in[head, halves[part]].reshape(ROWS, HEAD_DIM).astype(F32)
                ).astype(BF16)

        @pl.when(level == LEVELS - 1)
        def _():
            grad_kv[0, 0, :, :, lanes(head)] = own[head].astype(BF16)

    pl.loop(0, KV_HEADS)(send_terms)
    pl.loop(0, KV_HEADS)(sum_and_return)
    pl.loop(0, KV_HEADS)(store)

    @pl.loop(0, KV_HEADS)
    def _(head):
        per_count(
            level, lambda count: wait_bytes(terms.at[head, pl.ds(1, count)], b1_send.at[head])
        )

    @pl.when(level < LEVELS - 1)
    def _():
        for slot in range(2):
            wait_bytes(final_out.at[slot, pl.ds(1, SEGS - 1)], f_send.at[slot])


def shards(queries, keys_values, grad_out, parents):
    vmem = pl.BlockSpec(memory_space=pltpu.VMEM)
    smem = pl.BlockSpec(memory_space=pltpu.SMEM)
    dma = pltpu.SemaphoreType.DMA
    regular = pltpu.SemaphoreType.REGULAR
    tile = (SEGS, PIECE, HEAD_DIM)
    double = (SEGS, 2, PIECE, HEAD_DIM)
    keys_count = LEVELS * ROWS
    found = pltpu.SMEM((LEVELS, SEGS), jnp.int32)
    all_blocks = jax.ShapeDtypeStruct((KV_HEADS, LEVELS) + tile, BF16)
    parent_rows = parents.transpose(0, 2, 1)

    def limits(**more):
        return pltpu.CompilerParams(vmem_limit_bytes=24 * 1024 * 1024, **more)

    blocks = pl.pallas_call(
        gather_kernel,
        out_shape=all_blocks,
        in_specs=[smem, vmem],
        out_specs=vmem,
        scratch_shapes=[
            found,
            pltpu.VMEM((LEVELS - 1, TILE, TILE), BF16),
            pltpu.VMEM((KV_HEADS,) + tile, BF16),
            pltpu.VMEM((2,) + double, BF16),
            pltpu.VMEM((2, LEVELS - 1) + double, BF16),
            regular, dma((2,)), dma((2,)), dma((2,)), dma((KV_HEADS,)),
        ],
        compiler_params=limits(collective_id=0, has_side_effects=True),
    )(parent_rows, keys_values)
    grad_queries, terms, own = pl.pallas_call(
        attend_kernel,
        out_shape=(
            jax.ShapeDtypeStruct(queries.shape, BF16),
            all_blocks,
            jax.ShapeDtypeStruct((KV_HEADS, 2, ROWS, HEAD_DIM), F32),
        ),
        in_specs=[vmem, vmem, vmem],
        out_specs=(vmem, vmem, vmem),
        scratch_shapes=[
            pltpu.VMEM((2, STACK, HEAD_DIM), BF16),
            pltpu.VMEM((2, HEAD_DIM, STACK), BF16),
            pltpu.VMEM((HEAD_DIM, STACK), F32),
            pltpu.VMEM((keys_count, STACK), F32),
            pltpu.VMEM((keys_count, STACK), F32),
            pltpu.VMEM((keys_count, STACK), BF16),
            pltpu.VMEM((keys_count, STACK), BF16),
        ],
        compiler_params=limits(),
    )(blocks, queries, grad_out)
    grad_kv = pl.pallas_call(
        reduce_kernel,
        out_shape=jax.ShapeDtypeStruct(keys_values.shape, BF16),
        in_specs=[smem, vmem, vmem],
        out_specs=vmem,
        scratch_shapes=[
            found,
            pltpu.VMEM((TILE, (LEVELS - 1) * TILE), BF16),
            pltpu.VMEM((2, LEVELS - 1) + double, BF16),
            pltpu.VMEM((2,) + double, BF16),
            pltpu.VMEM((KV_HEADS,) + tile, BF16),
            regular, dma((KV_HEADS,)), dma((2,)), dma((2,)), dma((KV_HEADS,)),
        ],
        compiler_params=limits(collective_id=1, has_side_effects=True),
    )(parent_rows, terms, own)
    return grad_queries, grad_kv


def solution(mesh):
    in_specs = (
        P("depth", "seg", None, None),
        P("depth", "seg", None, None, None),
        P("depth", "seg", None, None),
        P(),
    )
    out_specs = (P("depth", "seg", None, None), P("depth", "seg", None, None, None))
    return jax.shard_map(shards, mesh=mesh, in_specs=in_specs, out_specs=out_specs, check_vma=False)
```

```python
import functools

import jax
import jax.numpy as jnp
from jax import lax
from jax.experimental import pallas as pl
from jax.experimental.pallas import tpu as pltpu
from jax.sharding import PartitionSpec as P

HEADS = 20
KV_HEADS = 4
HEAD_DIM = 128
GROUP = HEADS // KV_HEADS
ROWS = 128
LEVELS = 8
SEGS = 16
PIECE = 16
PIECES_PER_PART = ROWS // PIECE
STACK = GROUP * ROWS
PAIR = 2 * ROWS
TILE = SEGS * PIECE
OWNERS = SEGS // 2

NEG_FILL = -1e30
SCALE = HEAD_DIM ** -0.5
EXP2_SCALE = SCALE * 1.4426950408889634
MESH = pl.DeviceIdType.MESH
BF16 = jnp.bfloat16
F32 = jnp.float32


def half(value):
    return lax.div(value, 2)


def odd(value):
    return lax.rem(value, 2)


def wrapped(index):
    return jnp.where(index >= SEGS, index - SEGS, index)


def lanes(index, count=1):
    width = count * HEAD_DIM
    return pl.ds(pl.multiple_of(index * width, width), width)


def rows_of(index, count):
    return pl.ds(pl.multiple_of(index * count, count), count)


def owner_column(owner, parity):
    z = half(owner)
    return 4 * z + 2 * odd(owner) + odd(z + parity)


def fold(tile):
    return tile.reshape(tile.shape[0] // 8, 8, tile.shape[1])


def kernel(
    parents, queries, keys_values, grad_out, grad_queries, grad_kv,
    anc, pick, spread, kv_in, q_in, g_in, kv_stage, pieces, chosen, blocks,
    terms, term_pieces, own, stacks, turned, query_sum, logits, grad_probs,
    probs, grad_logits, final_out, final_in,
    kv_sem, q_sem, g_sem, ready, p1_send, p1_recv, p3_send, p3_recv, b1_send, b1_recv,
    f_send, f_recv,
):
    level = lax.axis_index("depth")
    me = lax.axis_index("seg")
    below = LEVELS - 1 - level
    my_z, my_x = lax.div(me, 4), lax.rem(me, 4)
    my_parity = odd(my_z + my_x)
    my_owner = 2 * my_z + half(my_x)

    def remote(src, dst, send_sem, recv_sem, device):
        return pltpu.make_async_remote_copy(
            src_ref=src, dst_ref=dst, send_sem=send_sem, recv_sem=recv_sem,
            device_id=device, device_id_type=MESH,
        )

    def wait_bytes(ref, sem):
        pltpu.make_async_copy(ref, ref, sem).wait()

    def per_count(which, action):
        for count in range(1, LEVELS):
            pl.when(which == count)(functools.partial(action, count))

    load_kv = pltpu.make_async_copy(keys_values, kv_in, kv_sem)
    load_q = pltpu.make_async_copy(queries, q_in, q_sem)
    load_g = pltpu.make_async_copy(grad_out, g_in, g_sem)
    load_kv.start()
    load_q.start()
    load_g.start()

    barrier = pltpu.get_barrier_semaphore()

    def in_line(step):
        other = level + step
        return (jnp.where(other >= LEVELS, other - LEVELS, other), me)

    @pl.loop(1, SEGS)
    def _(step):
        pl.semaphore_signal(
            barrier, inc=1, device_id=(level, wrapped(me + step)), device_id_type=MESH
        )

    @pl.loop(1, LEVELS)
    def _(step):
        pl.semaphore_signal(barrier, inc=1, device_id=in_line(step), device_id_type=MESH)

    @pl.loop(0, SEGS)
    def _(column):
        anc[0, column] = column

    @pl.loop(1, below + 1)
    def _(offset):
        @pl.loop(0, SEGS)
        def _(column):
            anc[offset, column] = anc[offset - 1, parents[level + offset - 1, 0, column]]

    load_kv.wait()
    for head in range(KV_HEADS):
        for part in range(2):
            kv_stage[head, pl.ds(part * PIECES_PER_PART, PIECES_PER_PART)] = kv_in[
                0, 0, part, :, head * HEAD_DIM:(head + 1) * HEAD_DIM
            ].reshape(PIECES_PER_PART, PIECE, HEAD_DIM)
    pl.semaphore_wait(barrier, SEGS - 1 + LEVELS - 1)

    def owner_after(turn):
        owner = my_owner + turn
        return jnp.where(owner >= OWNERS, owner - OWNERS, owner)

    def spread_out(slot):
        for turn in range(OWNERS):
            for parity in range(2):
                owner = owner_after(turn)
                source = kv_stage.at[2 * slot + parity, pl.ds(2 * owner, 2)]
                copy = remote(
                    source, pieces.at[slot, me], p1_send.at[slot], p1_recv.at[slot],
                    (level, owner_column(owner, parity)),
                )
                if turn > 0:
                    copy.start()
                else:
                    pl.when(my_parity != parity)(copy.start)
                    pl.when(my_parity == parity)(
                        pltpu.make_async_copy(source, pieces.at[slot, me], p1_recv.at[slot]).start
                    )

    spread_out(0)

    @pl.loop(1, LEVELS)
    def _(step):
        pl.semaphore_signal(ready, inc=1, device_id=in_line(step), device_id_type=MESH)

    @pl.loop(1, below + 1)
    def _(offset):
        lane = lax.broadcasted_iota(jnp.int32, (PIECE, TILE), 1)
        row = lax.broadcasted_iota(jnp.int32, (PIECE, TILE), 0)
        ahead = lane - row
        for column in range(SEGS):
            pick[offset - 1, rows_of(column, PIECE), :] = jnp.where(
                ahead == anc[offset, column] * PIECE, 1.0, 0.0
            ).astype(BF16)

    def batch_left(slot, offset):
        wait_bytes(chosen.at[slot, offset - 1], p3_send.at[slot, offset - 1])

    def last_batches_left(slot):
        @pl.loop(1, jnp.minimum(below, 2) + 1)
        def _(offset):
            batch_left(slot, offset)

    def pick_and_send(slot):
        wait_bytes(pieces.at[slot], p1_recv.at[slot])
        pl.when(slot == 0)(lambda: spread_out(1))
        head = 2 * slot + my_parity

        def pick_up(count):
            found = jnp.dot(
                pick[0:count].reshape(count * TILE, TILE),
                jnp.concatenate(
                    [pieces[slot, :, index].reshape(TILE, HEAD_DIM) for index in range(2)], axis=1
                ),
                preferred_element_type=F32,
            ).astype(BF16)
            for index in range(2):
                chosen[slot, 0:count, :, index] = found[
                    :, index * HEAD_DIM:(index + 1) * HEAD_DIM
                ].reshape(count, SEGS, PIECE, HEAD_DIM)

        pl.when((below > 0) & (below <= 2))(lambda: pick_up(2))
        pl.when((below > 2) & (below <= 4))(lambda: pick_up(4))
        pl.when(below > 4)(lambda: pick_up(LEVELS - 1))

        pl.when(slot == 1)(lambda: last_batches_left(0))

        @pl.loop(0, below)
        def _(step):
            offset = below - step
            pl.when(step >= 2)(lambda: batch_left(slot, offset + 2))
            for turn in range(SEGS):
                column = wrapped(me + turn)
                remote(
                    chosen.at[slot, offset - 1, column],
                    blocks.at[head, offset, pl.ds(2 * my_owner, 2)],
                    p3_send.at[slot, offset - 1], p3_recv.at[head],
                    (level + offset, column),
                ).start()

    pl.semaphore_wait(ready, LEVELS - 1)
    pl.loop(0, 2)(pick_and_send)

    @pl.loop(0, KV_HEADS)
    def _(head):
        blocks[head, 0] = kv_stage[head]

        @pl.when(odd(level) == 0)
        def _():
            blocks[head, level + 1] = jnp.zeros((SEGS, PIECE, HEAD_DIM), BF16)

    @pl.loop(1, below + 1)
    def _(offset):
        lane = lax.broadcasted_iota(jnp.int32, (PIECE, TILE), 1)
        row = lax.broadcasted_iota(jnp.int32, (PIECE, TILE), 0)
        lane_column = lane >> 4
        span = pl.ds(pl.multiple_of((offset - 1) * TILE, TILE), TILE)
        target = (lane & (PIECE - 1)) - row
        for column in range(SEGS):
            target = jnp.where(
                lane_column == column, target + anc[offset, column] * PIECE, target
            )
        for column in range(SEGS):
            spread[rows_of(column, PIECE), span] = jnp.where(
                target == column * PIECE, 1.0, 0.0
            ).astype(BF16)

    @pl.loop(below, LEVELS - 1)
    def _(index):
        spread[:, pl.ds(pl.multiple_of(index * TILE, TILE), TILE)] = jnp.zeros(
            (TILE, TILE), BF16
        )
        for slot in range(2):
            term_pieces[slot, index] = jnp.zeros((SEGS, 2, PIECE, HEAD_DIM), BF16)

    load_q.wait()
    load_g.wait()
    halves = [pl.ds(part * PIECES_PER_PART, PIECES_PER_PART) for part in range(2)]

    def attend(head, pairs):
        span_all = [pl.ds(group * ROWS, ROWS) for group in range(GROUP)]

        def block_pair(pair, part):
            return blocks[head, 2 * pair:2 * pair + 2, halves[part]].reshape(PAIR, HEAD_DIM)

        for index in range(2):
            for group, span in enumerate(span_all):
                tile = (q_in, g_in)[index][0, 0, :, lanes(head * GROUP + group)]
                stacks[index, span, :] = tile
                turned[index, :, span] = tile.T
        u_row = lax.broadcasted_iota(jnp.int32, (ROWS, ROWS), 0)
        t_row = lax.broadcasted_iota(jnp.int32, (ROWS, ROWS), 1)
        last_seen = odd(level) == 1
        best = [jnp.full((8, ROWS), NEG_FILL, F32) for group in range(GROUP)]
        for pair in range(pairs):
            raw = jnp.dot(block_pair(pair, 0), turned[0], preferred_element_type=F32)
            for group, span in enumerate(span_all):
                first = raw[0:ROWS, group * ROWS:(group + 1) * ROWS]
                second = raw[ROWS:PAIR, group * ROWS:(group + 1) * ROWS]
                if pair == 0:
                    first = jnp.where(u_row <= t_row, first, NEG_FILL)
                if pair == pairs - 1:
                    second = jnp.where(last_seen, second, NEG_FILL)
                logits[pair * PAIR:pair * PAIR + ROWS, span] = first
                logits[pair * PAIR + ROWS:(pair + 1) * PAIR, span] = second
                best[group] = jnp.maximum(
                    best[group], jnp.maximum(fold(first).max(0), fold(second).max(0))
                )
        top = [value.max(0, keepdims=True) for value in best]
        total = [jnp.zeros((8, ROWS), F32) for group in range(GROUP)]
        delta = [jnp.zeros((8, ROWS), F32) for group in range(GROUP)]
        for pair in range(pairs):
            rows = slice(pair * PAIR, (pair + 1) * PAIR)
            raw = jnp.dot(block_pair(pair, 1), turned[1], preferred_element_type=F32)
            for group, span in enumerate(span_all):
                tile = jnp.exp2((logits[rows, span] - top[group]) * EXP2_SCALE)
                part = raw[:, group * ROWS:(group + 1) * ROWS]
                logits[rows, span] = tile
                grad_probs[rows, span] = part
                total[group] += fold(tile).sum(0)
                delta[group] += fold(tile * part).sum(0)
        inverse = [1.0 / value.sum(0, keepdims=True) for value in total]
        delta = [value.sum(0, keepdims=True) * by for value, by in zip(delta, inverse)]
        for pair in range(pairs):
            rows = slice(pair * PAIR, (pair + 1) * PAIR)
            for group, span in enumerate(span_all):
                exact = logits[rows, span] * inverse[group]
                probs[rows, span] = exact.astype(BF16)
                grad_logits[rows, span] = (
                    exact * (grad_probs[rows, span] - delta[group])
                ).astype(BF16)
            value_term = jnp.dot(probs[rows, :], stacks[1], preferred_element_type=F32)
            key_term = SCALE * jnp.dot(
                grad_logits[rows, :], stacks[0], preferred_element_type=F32
            )
            for part, term in enumerate((key_term, value_term)):
                terms[head, 2 * pair:2 * pair + 2, halves[part]] = term.astype(BF16).reshape(
                    2, PIECES_PER_PART, PIECE, HEAD_DIM
                )
                if pair == 0:
                    own[head, part] = term[0:ROWS]
            moved = lax.dot_general(
                block_pair(pair, 0), grad_logits[rows, :], (((0,), (0,)), ((), ())),
                preferred_element_type=F32,
            )
            if pair == 0:
                query_sum[...] = moved
            else:
                query_sum[...] += moved
        for group, span in enumerate(span_all):
            grad_queries[0, 0, :, lanes(head * GROUP + group)] = (
                SCALE * query_sum[:, span].T
            ).astype(BF16)

    def terms_left(head):
        per_count(
            level, lambda count: wait_bytes(terms.at[head, pl.ds(1, count)], b1_send.at[head])
        )

    def send_terms(head):
        pl.when(head > 0)(lambda: terms_left(head - 1))
        targets = []
        for turn in range(OWNERS):
            owner = owner_after(turn)
            targets.append((owner, owner_column(owner, odd(head))))

        @pl.loop(0, level)
        def _(step):
            offset = level - step
            for owner, column in targets:
                remote(
                    terms.at[head, offset, pl.ds(2 * owner, 2)],
                    term_pieces.at[half(head), offset - 1, me],
                    b1_send.at[head], b1_recv.at[half(head)], (level - offset, column),
                ).start()

    def sum_and_return(head):
        slot = half(head)

        @pl.when((level < LEVELS - 1) & (odd(head) == my_parity))
        def _():
            per_count(
                below,
                lambda count: wait_bytes(
                    term_pieces.at[slot, pl.ds(0, count)], b1_recv.at[slot]
                ),
            )

            def add_up(count):
                received = term_pieces[slot, 0:count]
                total = jnp.dot(
                    spread[:, 0:count * TILE],
                    jnp.concatenate(
                        [
                            received[:, :, index].reshape(count * TILE, HEAD_DIM)
                            for index in range(2)
                        ],
                        axis=1,
                    ),
                    preferred_element_type=F32,
                )
                for index in range(2):
                    final_out[slot, :, index] = total[
                        :, index * HEAD_DIM:(index + 1) * HEAD_DIM
                    ].astype(BF16).reshape(SEGS, PIECE, HEAD_DIM)

            pl.when(below <= 2)(lambda: add_up(2))
            pl.when((below > 2) & (below <= 4))(lambda: add_up(4))
            pl.when(below > 4)(lambda: add_up(LEVELS - 1))
            landing = final_in.at[head, pl.ds(2 * my_owner, 2)]
            for turn in range(1, SEGS):
                peer = wrapped(me + turn)
                remote(
                    final_out.at[slot, peer], landing,
                    f_send.at[slot], f_recv.at[head], (level, peer),
                ).start()
            pltpu.make_async_copy(final_out.at[slot, me], landing, f_recv.at[head]).start()

    def store(head):
        @pl.when(level < LEVELS - 1)
        def _():
            wait_bytes(final_in.at[head], f_recv.at[head])
            for part in range(2):
                own[head, part] += final_in[head, halves[part]].reshape(
                    ROWS, HEAD_DIM
                ).astype(F32)

        grad_kv[0, 0, :, :, lanes(head)] = own[head].astype(BF16)

    @pl.loop(0, KV_HEADS + 2)
    def _(tick):
        @pl.when(tick < KV_HEADS)
        def _():
            per_count(
                level,
                lambda count: wait_bytes(blocks.at[tick, pl.ds(1, count)], p3_recv.at[tick]),
            )
            for pairs in range(1, LEVELS // 2 + 1):
                pl.when(half(level) == pairs - 1)(functools.partial(attend, tick, pairs))
            send_terms(tick)

        @pl.when((tick >= 1) & (tick < KV_HEADS + 1))
        def _():
            sum_and_return(tick - 1)

        @pl.when(tick >= 2)
        def _():
            store(tick - 2)

    last_batches_left(1)
    terms_left(KV_HEADS - 1)
    for slot in range(2):
        wait_bytes(pieces.at[slot, pl.ds(1, SEGS - 1)], p1_send.at[slot])

    @pl.when(level < LEVELS - 1)
    def _():
        for slot in range(2):
            wait_bytes(final_out.at[slot, pl.ds(1, SEGS - 1)], f_send.at[slot])


def shards(queries, keys_values, grad_out, parents):
    vmem = pl.BlockSpec(memory_space=pltpu.VMEM)
    smem = pl.BlockSpec(memory_space=pltpu.SMEM)
    hbm = pl.BlockSpec(memory_space=pltpu.HBM)
    dma = pltpu.SemaphoreType.DMA
    tile = (SEGS, PIECE, HEAD_DIM)
    keys_count = LEVELS * ROWS
    scratch = [
        pltpu.SMEM((LEVELS, SEGS), jnp.int32),
        pltpu.VMEM((LEVELS - 1, TILE, TILE), BF16),
        pltpu.VMEM((TILE, (LEVELS - 1) * TILE), BF16),
        pltpu.VMEM(keys_values.shape, BF16),
        pltpu.VMEM(queries.shape, BF16),
        pltpu.VMEM(queries.shape, BF16),
        pltpu.VMEM((KV_HEADS,) + tile, BF16),
        pltpu.VMEM((2, SEGS, 2, PIECE, HEAD_DIM), BF16),
        pltpu.VMEM((2, LEVELS - 1, SEGS, 2, PIECE, HEAD_DIM), BF16),
        pltpu.VMEM((KV_HEADS, LEVELS) + tile, BF16),
        pltpu.VMEM((KV_HEADS, LEVELS) + tile, BF16),
        pltpu.VMEM((2, LEVELS - 1, SEGS, 2, PIECE, HEAD_DIM), BF16),
        pltpu.VMEM((KV_HEADS, 2, ROWS, HEAD_DIM), F32),
        pltpu.VMEM((2, STACK, HEAD_DIM), BF16),
        pltpu.VMEM((2, HEAD_DIM, STACK), BF16),
        pltpu.VMEM((HEAD_DIM, STACK), F32),
        pltpu.VMEM((keys_count, STACK), F32),
        pltpu.VMEM((keys_count, STACK), F32),
        pltpu.VMEM((keys_count, STACK), BF16),
        pltpu.VMEM((keys_count, STACK), BF16),
        pltpu.VMEM((2, SEGS, 2, PIECE, HEAD_DIM), BF16),
        pltpu.VMEM((KV_HEADS,) + tile, BF16),
        dma, dma, dma,
        pltpu.SemaphoreType.REGULAR,
        dma((2,)), dma((2,)),
        dma((2, LEVELS - 1)), dma((KV_HEADS,)),
        dma((KV_HEADS,)), dma((2,)),
        dma((2,)), dma((KV_HEADS,)),
    ]
    return pl.pallas_call(
        kernel,
        out_shape=(
            jax.ShapeDtypeStruct(queries.shape, BF16),
            jax.ShapeDtypeStruct(keys_values.shape, BF16),
        ),
        in_specs=[smem, hbm, hbm, hbm],
        out_specs=(vmem, vmem),
        scratch_shapes=scratch,
        compiler_params=pltpu.CompilerParams(
            collective_id=0, has_side_effects=True, vmem_limit_bytes=56 * 1024 * 1024
        ),
        cost_estimate=pl.CostEstimate(
            flops=5 * 2 * HEADS * LEVELS * ROWS * ROWS * HEAD_DIM,
            bytes_accessed=8 * 1024 * 1024,
            transcendentals=HEADS * LEVELS * ROWS * ROWS,
        ),
    )(parents.transpose(0, 2, 1), queries, keys_values, grad_out)


def solution(mesh):
    in_specs = (
        P("depth", "seg", None, None),
        P("depth", "seg", None, None, None),
        P("depth", "seg", None, None),
        P(),
    )
    out_specs = (P("depth", "seg", None, None), P("depth", "seg", None, None, None))
    return jax.shard_map(shards, mesh=mesh, in_specs=in_specs, out_specs=out_specs, check_vma=False)
```

```python
import functools

import jax
import jax.numpy as jnp
from jax import lax
from jax.experimental import pallas as pl
from jax.experimental.pallas import tpu as pltpu
from jax.sharding import PartitionSpec as P

HEADS = 20
KV_HEADS = 4
HEAD_DIM = 128
GROUP = HEADS // KV_HEADS
ROWS = 128
LEVELS = 8
SEGS = 16
PIECE = 16
PIECES_PER_PART = ROWS // PIECE
STACK = GROUP * ROWS
PAIR = 2 * ROWS
TILE = SEGS * PIECE
OWNERS = SEGS // 2

NEG_FILL = -1e30
SCALE = HEAD_DIM ** -0.5
EXP2_SCALE = SCALE * 1.4426950408889634
MESH = pl.DeviceIdType.MESH
BF16 = jnp.bfloat16
F32 = jnp.float32


def half(value):
    return lax.div(value, 2)


def odd(value):
    return lax.rem(value, 2)


def wrapped(index):
    return jnp.where(index >= SEGS, index - SEGS, index)


def lanes(index, count=1):
    width = count * HEAD_DIM
    return pl.ds(pl.multiple_of(index * width, width), width)


def rows_of(index, count):
    return pl.ds(pl.multiple_of(index * count, count), count)


def owner_column(owner, parity):
    z = half(owner)
    return 4 * z + 2 * odd(owner) + odd(z + parity)


def fold(tile):
    return tile.reshape(tile.shape[0] // 8, 8, tile.shape[1])


def kernel(
    parents, queries, keys_values, grad_out, grad_queries, grad_kv,
    anc, pick, spread, kv_in, q_in, g_in, kv_stage, pieces, chosen, blocks,
    terms, term_pieces, own, stacks, turned, query_sum, logits, grad_probs,
    probs, grad_logits, final_out, final_in,
    kv_sem, q_sem, g_sem, ready, p1_send, p1_recv, p3_send, p3_recv, b1_send, b1_recv,
    f_send, f_recv,
):
    level = lax.axis_index("depth")
    me = lax.axis_index("seg")
    below = LEVELS - 1 - level
    my_z, my_x = lax.div(me, 4), lax.rem(me, 4)
    my_parity = odd(my_z + my_x)
    my_owner = 2 * my_z + half(my_x)

    def remote(src, dst, send_sem, recv_sem, device):
        return pltpu.make_async_remote_copy(
            src_ref=src, dst_ref=dst, send_sem=send_sem, recv_sem=recv_sem,
            device_id=device, device_id_type=MESH,
        )

    def wait_bytes(ref, sem):
        pltpu.make_async_copy(ref, ref, sem).wait()

    def per_count(which, action):
        for count in range(1, LEVELS):
            pl.when(which == count)(functools.partial(action, count))

    load_kv = pltpu.make_async_copy(keys_values, kv_in, kv_sem)
    load_q = pltpu.make_async_copy(queries, q_in, q_sem)
    load_g = pltpu.make_async_copy(grad_out, g_in, g_sem)
    load_kv.start()
    load_q.start()
    load_g.start()

    barrier = pltpu.get_barrier_semaphore()

    def in_line(step):
        other = level + step
        return (jnp.where(other >= LEVELS, other - LEVELS, other), me)

    @pl.loop(1, SEGS)
    def _(step):
        pl.semaphore_signal(
            barrier, inc=1, device_id=(level, wrapped(me + step)), device_id_type=MESH
        )

    @pl.loop(1, LEVELS)
    def _(step):
        pl.semaphore_signal(barrier, inc=1, device_id=in_line(step), device_id_type=MESH)

    @pl.loop(0, SEGS)
    def _(column):
        anc[0, column] = column

    @pl.loop(1, below + 1)
    def _(offset):
        @pl.loop(0, SEGS)
        def _(column):
            anc[offset, column] = anc[offset - 1, parents[level + offset - 1, 0, column]]

    load_kv.wait()
    for head in range(KV_HEADS):
        for part in range(2):
            kv_stage[head, pl.ds(part * PIECES_PER_PART, PIECES_PER_PART)] = kv_in[
                0, 0, part, :, head * HEAD_DIM:(head + 1) * HEAD_DIM
            ].reshape(PIECES_PER_PART, PIECE, HEAD_DIM)
    pl.semaphore_wait(barrier, SEGS - 1 + LEVELS - 1)

    def spread_out(group, heads):
        @pl.loop(1, SEGS)
        def _(step):
            peer = wrapped(me + step)
            remote(
                kv_stage.at[heads, peer], pieces.at[heads, me],
                p1_send.at[group], p1_recv.at[group], (level, peer),
            ).start()

        pltpu.make_async_copy(
            kv_stage.at[heads, me], pieces.at[heads, me], p1_recv.at[group]
        ).start()

    groups = (pl.ds(0, 1), pl.ds(1, KV_HEADS - 1))
    for group, heads in enumerate(groups):
        spread_out(group, heads)

    @pl.loop(1, LEVELS)
    def _(step):
        pl.semaphore_signal(ready, inc=1, device_id=in_line(step), device_id_type=MESH)

    @pl.loop(1, below + 1)
    def _(offset):
        lane = lax.broadcasted_iota(jnp.int32, (PIECE, TILE), 1)
        row = lax.broadcasted_iota(jnp.int32, (PIECE, TILE), 0)
        ahead = lane - row
        for column in range(SEGS):
            pick[offset - 1, rows_of(column, PIECE), :] = jnp.where(
                ahead == anc[offset, column] * PIECE, 1.0, 0.0
            ).astype(BF16)

    def batch_left(head, offset):
        wait_bytes(chosen.at[head, offset - 1], p3_send.at[odd(head), offset - 1])

    def pick_and_send(head):
        pl.when(head == 0)(lambda: wait_bytes(pieces.at[groups[0]], p1_recv.at[0]))
        pl.when(head == 1)(lambda: wait_bytes(pieces.at[groups[1]], p1_recv.at[1]))

        def pick_up(count):
            found = jnp.dot(
                pick[0:count].reshape(count * TILE, TILE),
                pieces[head].reshape(TILE, HEAD_DIM), preferred_element_type=F32,
            )
            chosen[head, 0:count] = found.astype(BF16).reshape(count, SEGS, PIECE, HEAD_DIM)

        pl.when((below > 0) & (below <= 2))(lambda: pick_up(2))
        pl.when((below > 2) & (below <= 4))(lambda: pick_up(4))
        pl.when(below > 4)(lambda: pick_up(LEVELS - 1))

        @pl.loop(1, below + 1)
        def _(offset):
            pl.when(head > 0)(lambda: batch_left(head - 1, offset))
            for turn in range(SEGS):
                column = wrapped(me + turn)
                remote(
                    chosen.at[head, offset - 1, column], blocks.at[head, offset, me],
                    p3_send.at[odd(head), offset - 1], p3_recv.at[head],
                    (level + offset, column),
                ).start()

    pl.semaphore_wait(ready, LEVELS - 1)

    @pl.loop(0, KV_HEADS)
    def _(head):
        blocks[head, 0] = kv_stage[head]

        @pl.when(odd(level) == 0)
        def _():
            blocks[head, level + 1] = jnp.zeros((SEGS, PIECE, HEAD_DIM), BF16)

    def make_spread():
        @pl.loop(1, below + 1)
        def _(offset):
            lane = lax.broadcasted_iota(jnp.int32, (PIECE, TILE), 1)
            row = lax.broadcasted_iota(jnp.int32, (PIECE, TILE), 0)
            lane_column = lane >> 4
            span = pl.ds(pl.multiple_of((offset - 1) * TILE, TILE), TILE)
            target = (lane & (PIECE - 1)) - row
            for column in range(SEGS):
                target = jnp.where(
                    lane_column == column, target + anc[offset, column] * PIECE, target
                )
            for column in range(SEGS):
                spread[rows_of(column, PIECE), span] = jnp.where(
                    target == column * PIECE, 1.0, 0.0
                ).astype(BF16)

        @pl.loop(below, LEVELS - 1)
        def _(index):
            spread[:, pl.ds(pl.multiple_of(index * TILE, TILE), TILE)] = jnp.zeros(
                (TILE, TILE), BF16
            )
            for slot in range(2):
                term_pieces[slot, index] = jnp.zeros((SEGS, 2, PIECE, HEAD_DIM), BF16)

    halves = [pl.ds(part * PIECES_PER_PART, PIECES_PER_PART) for part in range(2)]

    def attend(head, pairs):
        span_all = [pl.ds(group * ROWS, ROWS) for group in range(GROUP)]

        def block_pair(pair, part):
            return blocks[head, 2 * pair:2 * pair + 2, halves[part]].reshape(PAIR, HEAD_DIM)

        for index in range(2):
            for group, span in enumerate(span_all):
                tile = (q_in, g_in)[index][0, 0, :, lanes(head * GROUP + group)]
                stacks[index, span, :] = tile
                turned[index, :, span] = tile.T
        u_row = lax.broadcasted_iota(jnp.int32, (ROWS, ROWS), 0)
        t_row = lax.broadcasted_iota(jnp.int32, (ROWS, ROWS), 1)
        last_seen = odd(level) == 1
        best = [jnp.full((8, ROWS), NEG_FILL, F32) for group in range(GROUP)]
        for pair in range(pairs):
            raw = jnp.dot(block_pair(pair, 0), turned[0], preferred_element_type=F32)
            for group, span in enumerate(span_all):
                first = raw[0:ROWS, group * ROWS:(group + 1) * ROWS]
                second = raw[ROWS:PAIR, group * ROWS:(group + 1) * ROWS]
                if pair == 0:
                    first = jnp.where(u_row <= t_row, first, NEG_FILL)
                if pair == pairs - 1:
                    second = jnp.where(last_seen, second, NEG_FILL)
                logits[pair * PAIR:pair * PAIR + ROWS, span] = first
                logits[pair * PAIR + ROWS:(pair + 1) * PAIR, span] = second
                best[group] = jnp.maximum(
                    best[group], jnp.maximum(fold(first).max(0), fold(second).max(0))
                )
        top = [value.max(0, keepdims=True) for value in best]
        total = [jnp.zeros((8, ROWS), F32) for group in range(GROUP)]
        delta = [jnp.zeros((8, ROWS), F32) for group in range(GROUP)]
        for pair in range(pairs):
            rows = slice(pair * PAIR, (pair + 1) * PAIR)
            raw = jnp.dot(block_pair(pair, 1), turned[1], preferred_element_type=F32)
            for group, span in enumerate(span_all):
                tile = jnp.exp2((logits[rows, span] - top[group]) * EXP2_SCALE)
                part = raw[:, group * ROWS:(group + 1) * ROWS]
                logits[rows, span] = tile
                grad_probs[rows, span] = part
                total[group] += fold(tile).sum(0)
                delta[group] += fold(tile * part).sum(0)
        inverse = [1.0 / value.sum(0, keepdims=True) for value in total]
        delta = [value.sum(0, keepdims=True) * by for value, by in zip(delta, inverse)]
        for pair in range(pairs):
            rows = slice(pair * PAIR, (pair + 1) * PAIR)
            for group, span in enumerate(span_all):
                exact = logits[rows, span] * inverse[group]
                probs[rows, span] = exact.astype(BF16)
                grad_logits[rows, span] = (
                    exact * (grad_probs[rows, span] - delta[group])
                ).astype(BF16)
            value_term = jnp.dot(probs[rows, :], stacks[1], preferred_element_type=F32)
            key_term = SCALE * jnp.dot(
                grad_logits[rows, :], stacks[0], preferred_element_type=F32
            )
            for part, term in enumerate((key_term, value_term)):
                terms[head, 2 * pair:2 * pair + 2, halves[part]] = term.astype(BF16).reshape(
                    2, PIECES_PER_PART, PIECE, HEAD_DIM
                )
                if pair == 0:
                    own[head, part] = term[0:ROWS]
            moved = lax.dot_general(
                block_pair(pair, 0), grad_logits[rows, :], (((0,), (0,)), ((), ())),
                preferred_element_type=F32,
            )
            if pair == 0:
                query_sum[...] = moved
            else:
                query_sum[...] += moved
        for group, span in enumerate(span_all):
            grad_queries[0, 0, :, lanes(head * GROUP + group)] = (
                SCALE * query_sum[:, span].T
            ).astype(BF16)

    def terms_left(head, offset):
        wait_bytes(terms.at[head, offset], b1_send.at[odd(head), offset - 1])

    def send_terms(head):
        targets = []
        for turn in range(OWNERS):
            owner = my_owner + turn
            owner = jnp.where(owner >= OWNERS, owner - OWNERS, owner)
            targets.append((owner, owner_column(owner, odd(head))))

        @pl.loop(1, level + 1)
        def _(offset):
            pl.when(head > 0)(lambda: terms_left(head - 1, offset))
            for owner, column in targets:
                remote(
                    terms.at[head, offset, pl.ds(2 * owner, 2)],
                    term_pieces.at[half(head), offset - 1, me],
                    b1_send.at[odd(head), offset - 1], b1_recv.at[half(head)],
                    (level - offset, column),
                ).start()

    def sum_and_return(head):
        slot = half(head)

        @pl.when((level < LEVELS - 1) & (odd(head) == my_parity))
        def _():
            per_count(
                below,
                lambda count: wait_bytes(
                    term_pieces.at[slot, pl.ds(0, count)], b1_recv.at[slot]
                ),
            )

            def add_up(count):
                received = term_pieces[slot, 0:count]
                total = jnp.dot(
                    spread[:, 0:count * TILE],
                    jnp.concatenate(
                        [
                            received[:, :, index].reshape(count * TILE, HEAD_DIM)
                            for index in range(2)
                        ],
                        axis=1,
                    ),
                    preferred_element_type=F32,
                )
                for index in range(2):
                    final_out[slot, :, index] = total[
                        :, index * HEAD_DIM:(index + 1) * HEAD_DIM
                    ].astype(BF16).reshape(SEGS, PIECE, HEAD_DIM)

            pl.when(below <= 2)(lambda: add_up(2))
            pl.when((below > 2) & (below <= 4))(lambda: add_up(4))
            pl.when(below > 4)(lambda: add_up(LEVELS - 1))
            landing = final_in.at[head, pl.ds(2 * my_owner, 2)]
            for turn in range(1, SEGS):
                peer = wrapped(me + turn)
                remote(
                    final_out.at[slot, peer], landing,
                    f_send.at[slot], f_recv.at[head], (level, peer),
                ).start()
            pltpu.make_async_copy(final_out.at[slot, me], landing, f_recv.at[head]).start()

    def store(head):
        @pl.when(level < LEVELS - 1)
        def _():
            wait_bytes(final_in.at[head], f_recv.at[head])
            for part in range(2):
                own[head, part] += final_in[head, halves[part]].reshape(
                    ROWS, HEAD_DIM
                ).astype(F32)

        grad_kv[0, 0, :, :, lanes(head)] = own[head].astype(BF16)

    @pl.loop(0, KV_HEADS + 4)
    def _(tick):
        @pl.when(tick < KV_HEADS)
        def _():
            pick_and_send(tick)

        @pl.when(tick == 0)
        def _():
            make_spread()
            load_q.wait()
            load_g.wait()

        @pl.when((tick >= 1) & (tick < KV_HEADS + 1))
        def _():
            head = tick - 1
            per_count(
                level,
                lambda count: wait_bytes(blocks.at[head, pl.ds(1, count)], p3_recv.at[head]),
            )
            for pairs in range(1, LEVELS // 2 + 1):
                pl.when(half(level) == pairs - 1)(functools.partial(attend, head, pairs))
            send_terms(head)

        @pl.when((tick >= 3) & (tick < KV_HEADS + 3))
        def _():
            sum_and_return(tick - 3)

        @pl.when(tick >= 4)
        def _():
            store(tick - 4)

    for group, heads in enumerate(groups):
        wait_bytes(pieces.at[heads, pl.ds(1, SEGS - 1)], p1_send.at[group])

    @pl.loop(1, below + 1)
    def _(offset):
        batch_left(KV_HEADS - 1, offset)

    @pl.loop(1, level + 1)
    def _(offset):
        terms_left(KV_HEADS - 1, offset)

    @pl.when(level < LEVELS - 1)
    def _():
        for slot in range(2):
            wait_bytes(final_out.at[slot, pl.ds(1, SEGS - 1)], f_send.at[slot])


def shards(queries, keys_values, grad_out, parents):
    vmem = pl.BlockSpec(memory_space=pltpu.VMEM)
    smem = pl.BlockSpec(memory_space=pltpu.SMEM)
    hbm = pl.BlockSpec(memory_space=pltpu.HBM)
    dma = pltpu.SemaphoreType.DMA
    tile = (SEGS, PIECE, HEAD_DIM)
    keys_count = LEVELS * ROWS
    scratch = [
        pltpu.SMEM((LEVELS, SEGS), jnp.int32),
        pltpu.VMEM((LEVELS - 1, TILE, TILE), BF16),
        pltpu.VMEM((TILE, (LEVELS - 1) * TILE), BF16),
        pltpu.VMEM(keys_values.shape, BF16),
        pltpu.VMEM(queries.shape, BF16),
        pltpu.VMEM(queries.shape, BF16),
        pltpu.VMEM((KV_HEADS,) + tile, BF16),
        pltpu.VMEM((KV_HEADS,) + tile, BF16),
        pltpu.VMEM((KV_HEADS, LEVELS - 1) + tile, BF16),
        pltpu.VMEM((KV_HEADS, LEVELS) + tile, BF16),
        pltpu.VMEM((KV_HEADS, LEVELS) + tile, BF16),
        pltpu.VMEM((2, LEVELS - 1, SEGS, 2, PIECE, HEAD_DIM), BF16),
        pltpu.VMEM((KV_HEADS, 2, ROWS, HEAD_DIM), F32),
        pltpu.VMEM((2, STACK, HEAD_DIM), BF16),
        pltpu.VMEM((2, HEAD_DIM, STACK), BF16),
        pltpu.VMEM((HEAD_DIM, STACK), F32),
        pltpu.VMEM((keys_count, STACK), F32),
        pltpu.VMEM((keys_count, STACK), F32),
        pltpu.VMEM((keys_count, STACK), BF16),
        pltpu.VMEM((keys_count, STACK), BF16),
        pltpu.VMEM((2, SEGS, 2, PIECE, HEAD_DIM), BF16),
        pltpu.VMEM((KV_HEADS,) + tile, BF16),
        dma, dma, dma,
        pltpu.SemaphoreType.REGULAR,
        dma((2,)), dma((2,)),
        dma((2, LEVELS - 1)), dma((KV_HEADS,)),
        dma((2, LEVELS - 1)), dma((2,)),
        dma((2,)), dma((KV_HEADS,)),
    ]
    return pl.pallas_call(
        kernel,
        out_shape=(
            jax.ShapeDtypeStruct(queries.shape, BF16),
            jax.ShapeDtypeStruct(keys_values.shape, BF16),
        ),
        in_specs=[smem, hbm, hbm, hbm],
        out_specs=(vmem, vmem),
        scratch_shapes=scratch,
        compiler_params=pltpu.CompilerParams(
            collective_id=0, has_side_effects=True, vmem_limit_bytes=56 * 1024 * 1024
        ),
        cost_estimate=pl.CostEstimate(
            flops=5 * 2 * HEADS * LEVELS * ROWS * ROWS * HEAD_DIM,
            bytes_accessed=8 * 1024 * 1024,
            transcendentals=HEADS * LEVELS * ROWS * ROWS,
        ),
    )(parents.transpose(0, 2, 1), queries, keys_values, grad_out)


def solution(mesh):
    in_specs = (
        P("depth", "seg", None, None),
        P("depth", "seg", None, None, None),
        P("depth", "seg", None, None),
        P(),
    )
    out_specs = (P("depth", "seg", None, None), P("depth", "seg", None, None, None))
    return jax.shard_map(shards, mesh=mesh, in_specs=in_specs, out_specs=out_specs, check_vma=False)
```

```python
import functools

import jax
import jax.numpy as jnp
from jax import lax
from jax.experimental import pallas as pl
from jax.experimental.pallas import tpu as pltpu
from jax.sharding import PartitionSpec as P

HEADS = 20
KV_HEADS = 4
HEAD_DIM = 128
GROUP = HEADS // KV_HEADS
ROWS = 128
LEVELS = 8
SEGS = 16
PIECE = 16
PIECES_PER_PART = ROWS // PIECE
STACK = GROUP * ROWS
PAIR = 2 * ROWS
TILE = SEGS * PIECE
OWNERS = SEGS // 2

NEG_FILL = -1e30
SCALE = HEAD_DIM ** -0.5
EXP2_SCALE = SCALE * 1.4426950408889634
MESH = pl.DeviceIdType.MESH
BF16 = jnp.bfloat16
F32 = jnp.float32


def half(value):
    return lax.div(value, 2)


def odd(value):
    return lax.rem(value, 2)


def wrapped(index):
    return jnp.where(index >= SEGS, index - SEGS, index)


def lanes(index, count=1):
    width = count * HEAD_DIM
    return pl.ds(pl.multiple_of(index * width, width), width)


def rows_of(index, count):
    return pl.ds(pl.multiple_of(index * count, count), count)


def owner_column(owner, parity):
    z = half(owner)
    return 4 * z + 2 * odd(owner) + odd(z + parity)


def fold(tile):
    return tile.reshape(tile.shape[0] // 8, 8, tile.shape[1])


def kernel(
    parents, queries, keys_values, grad_out, grad_queries, grad_kv,
    anc, pick, spread, kv_in, q_in, g_in, kv_stage, pieces, chosen, blocks,
    terms, term_pieces, own, stacks, turned, query_sum, logits, grad_probs,
    probs, grad_logits, final_out, final_in,
    kv_sem, q_sem, g_sem, ready, p1_send, p1_recv, p3_send, p3_recv, b1_send, b1_recv,
    f_send, f_recv,
):
    level = lax.axis_index("depth")
    me = lax.axis_index("seg")
    below = LEVELS - 1 - level
    my_z, my_x = lax.div(me, 4), lax.rem(me, 4)
    my_parity = odd(my_z + my_x)
    my_owner = 2 * my_z + half(my_x)

    def remote(src, dst, send_sem, recv_sem, device):
        return pltpu.make_async_remote_copy(
            src_ref=src, dst_ref=dst, send_sem=send_sem, recv_sem=recv_sem,
            device_id=device, device_id_type=MESH,
        )

    def wait_bytes(ref, sem):
        pltpu.make_async_copy(ref, ref, sem).wait()

    def per_count(which, action):
        for count in range(1, LEVELS):
            pl.when(which == count)(functools.partial(action, count))

    load_kv = pltpu.make_async_copy(keys_values, kv_in, kv_sem)
    load_q = pltpu.make_async_copy(queries, q_in, q_sem)
    load_g = pltpu.make_async_copy(grad_out, g_in, g_sem)
    load_kv.start()
    load_q.start()
    load_g.start()

    barrier = pltpu.get_barrier_semaphore()

    def in_line(step):
        other = level + step
        return (jnp.where(other >= LEVELS, other - LEVELS, other), me)

    @pl.loop(1, SEGS)
    def _(step):
        pl.semaphore_signal(
            barrier, inc=1, device_id=(level, wrapped(me + step)), device_id_type=MESH
        )

    @pl.loop(1, LEVELS)
    def _(step):
        pl.semaphore_signal(barrier, inc=1, device_id=in_line(step), device_id_type=MESH)

    @pl.loop(0, SEGS)
    def _(column):
        anc[0, column] = column

    @pl.loop(1, below + 1)
    def _(offset):
        @pl.loop(0, SEGS)
        def _(column):
            anc[offset, column] = anc[offset - 1, parents[level + offset - 1, 0, column]]

    load_kv.wait()
    for head in range(KV_HEADS):
        for part in range(2):
            kv_stage[head, pl.ds(part * PIECES_PER_PART, PIECES_PER_PART)] = kv_in[
                0, 0, part, :, head * HEAD_DIM:(head + 1) * HEAD_DIM
            ].reshape(PIECES_PER_PART, PIECE, HEAD_DIM)
    pl.semaphore_wait(barrier, SEGS - 1 + LEVELS - 1)

    def spread_out(head):
        for turn in range(1, SEGS):
            peer = wrapped(me + turn)
            remote(
                kv_stage.at[head, peer], pieces.at[head, me],
                p1_send.at[head], p1_recv.at[head], (level, peer),
            ).start()
        pltpu.make_async_copy(
            kv_stage.at[head, me], pieces.at[head, me], p1_recv.at[head]
        ).start()

    spread_out(0)

    @pl.loop(1, LEVELS)
    def _(step):
        pl.semaphore_signal(ready, inc=1, device_id=in_line(step), device_id_type=MESH)

    @pl.loop(1, below + 1)
    def _(offset):
        lane = lax.broadcasted_iota(jnp.int32, (PIECE, TILE), 1)
        row = lax.broadcasted_iota(jnp.int32, (PIECE, TILE), 0)
        ahead = lane - row
        for column in range(SEGS):
            pick[offset - 1, rows_of(column, PIECE), :] = jnp.where(
                ahead == anc[offset, column] * PIECE, 1.0, 0.0
            ).astype(BF16)

    def batch_left(head, offset):
        wait_bytes(chosen.at[head, offset - 1], p3_send.at[odd(head), offset - 1])

    def pick_and_send(head):
        wait_bytes(pieces.at[head], p1_recv.at[head])
        pl.when(head < KV_HEADS - 1)(lambda: spread_out(head + 1))

        @pl.loop(1, below + 1)
        def _(step):
            offset = jnp.where(head == 0, below + 1 - step, step)
            found = jnp.dot(
                pick[offset - 1], pieces[head].reshape(TILE, HEAD_DIM),
                preferred_element_type=F32,
            )
            chosen[head, offset - 1] = found.astype(BF16).reshape(SEGS, PIECE, HEAD_DIM)
            pl.when(head > 0)(lambda: batch_left(head - 1, offset))
            for turn in range(SEGS):
                column = wrapped(me + turn)
                remote(
                    chosen.at[head, offset - 1, column], blocks.at[head, offset, me],
                    p3_send.at[odd(head), offset - 1], p3_recv.at[head],
                    (level + offset, column),
                ).start()

    pl.semaphore_wait(ready, LEVELS - 1)

    @pl.loop(0, KV_HEADS)
    def _(head):
        blocks[head, 0] = kv_stage[head]

        @pl.when(odd(level) == 0)
        def _():
            blocks[head, level + 1] = jnp.zeros((SEGS, PIECE, HEAD_DIM), BF16)

    def make_spread():
        @pl.loop(1, below + 1)
        def _(offset):
            lane = lax.broadcasted_iota(jnp.int32, (PIECE, TILE), 1)
            row = lax.broadcasted_iota(jnp.int32, (PIECE, TILE), 0)
            lane_column = lane >> 4
            span = pl.ds(pl.multiple_of((offset - 1) * TILE, TILE), TILE)
            target = (lane & (PIECE - 1)) - row
            for column in range(SEGS):
                target = jnp.where(
                    lane_column == column, target + anc[offset, column] * PIECE, target
                )
            for column in range(SEGS):
                spread[rows_of(column, PIECE), span] = jnp.where(
                    target == column * PIECE, 1.0, 0.0
                ).astype(BF16)

        @pl.loop(below, LEVELS - 1)
        def _(index):
            spread[:, pl.ds(pl.multiple_of(index * TILE, TILE), TILE)] = jnp.zeros(
                (TILE, TILE), BF16
            )
            for slot in range(2):
                term_pieces[slot, index] = jnp.zeros((SEGS, 2, PIECE, HEAD_DIM), BF16)

    halves = [pl.ds(part * PIECES_PER_PART, PIECES_PER_PART) for part in range(2)]

    def attend(head, pairs):
        span_all = [pl.ds(group * ROWS, ROWS) for group in range(GROUP)]

        def block_pair(pair, part):
            return blocks[head, 2 * pair:2 * pair + 2, halves[part]].reshape(PAIR, HEAD_DIM)

        for index in range(2):
            for group, span in enumerate(span_all):
                tile = (q_in, g_in)[index][0, 0, :, lanes(head * GROUP + group)]
                stacks[index, span, :] = tile
                turned[index, :, span] = tile.T
        u_row = lax.broadcasted_iota(jnp.int32, (ROWS, ROWS), 0)
        t_row = lax.broadcasted_iota(jnp.int32, (ROWS, ROWS), 1)
        last_seen = odd(level) == 1
        best = [jnp.full((8, ROWS), NEG_FILL, F32) for group in range(GROUP)]
        for pair in range(pairs):
            raw = jnp.dot(block_pair(pair, 0), turned[0], preferred_element_type=F32)
            for group, span in enumerate(span_all):
                first = raw[0:ROWS, group * ROWS:(group + 1) * ROWS]
                second = raw[ROWS:PAIR, group * ROWS:(group + 1) * ROWS]
                if pair == 0:
                    first = jnp.where(u_row <= t_row, first, NEG_FILL)
                if pair == pairs - 1:
                    second = jnp.where(last_seen, second, NEG_FILL)
                logits[pair * PAIR:pair * PAIR + ROWS, span] = first
                logits[pair * PAIR + ROWS:(pair + 1) * PAIR, span] = second
                best[group] = jnp.maximum(
                    best[group], jnp.maximum(fold(first).max(0), fold(second).max(0))
                )
        top = [value.max(0, keepdims=True) for value in best]
        total = [jnp.zeros((8, ROWS), F32) for group in range(GROUP)]
        delta = [jnp.zeros((8, ROWS), F32) for group in range(GROUP)]
        for pair in range(pairs):
            rows = slice(pair * PAIR, (pair + 1) * PAIR)
            raw = jnp.dot(block_pair(pair, 1), turned[1], preferred_element_type=F32)
            for group, span in enumerate(span_all):
                tile = jnp.exp2((logits[rows, span] - top[group]) * EXP2_SCALE)
                part = raw[:, group * ROWS:(group + 1) * ROWS]
                logits[rows, span] = tile
                grad_probs[rows, span] = part
                total[group] += fold(tile).sum(0)
                delta[group] += fold(tile * part).sum(0)
        inverse = [1.0 / value.sum(0, keepdims=True) for value in total]
        delta = [value.sum(0, keepdims=True) * by for value, by in zip(delta, inverse)]
        for pair in range(pairs):
            rows = slice(pair * PAIR, (pair + 1) * PAIR)
            for group, span in enumerate(span_all):
                exact = logits[rows, span] * inverse[group]
                probs[rows, span] = exact.astype(BF16)
                grad_logits[rows, span] = (
                    exact * (grad_probs[rows, span] - delta[group])
                ).astype(BF16)
            value_term = jnp.dot(probs[rows, :], stacks[1], preferred_element_type=F32)
            key_term = SCALE * jnp.dot(
                grad_logits[rows, :], stacks[0], preferred_element_type=F32
            )
            for part, term in enumerate((key_term, value_term)):
                terms[head, 2 * pair:2 * pair + 2, halves[part]] = term.astype(BF16).reshape(
                    2, PIECES_PER_PART, PIECE, HEAD_DIM
                )
                if pair == 0:
                    own[head, part] = term[0:ROWS]
            moved = lax.dot_general(
                block_pair(pair, 0), grad_logits[rows, :], (((0,), (0,)), ((), ())),
                preferred_element_type=F32,
            )
            if pair == 0:
                query_sum[...] = moved
            else:
                query_sum[...] += moved
        for group, span in enumerate(span_all):
            grad_queries[0, 0, :, lanes(head * GROUP + group)] = (
                SCALE * query_sum[:, span].T
            ).astype(BF16)

    def terms_left(head, offset):
        wait_bytes(terms.at[head, offset], b1_send.at[odd(head), offset - 1])

    def send_terms(head):
        targets = []
        for turn in range(OWNERS):
            owner = my_owner + turn
            owner = jnp.where(owner >= OWNERS, owner - OWNERS, owner)
            targets.append((owner, owner_column(owner, odd(head))))

        @pl.loop(1, level + 1)
        def _(offset):
            pl.when(head > 0)(lambda: terms_left(head - 1, offset))
            for owner, column in targets:
                remote(
                    terms.at[head, offset, pl.ds(2 * owner, 2)],
                    term_pieces.at[half(head), offset - 1, me],
                    b1_send.at[odd(head), offset - 1], b1_recv.at[half(head)],
                    (level - offset, column),
                ).start()

    def sum_and_return(head):
        slot = half(head)

        @pl.when((level < LEVELS - 1) & (odd(head) == my_parity))
        def _():
            per_count(
                below,
                lambda count: wait_bytes(
                    term_pieces.at[slot, pl.ds(0, count)], b1_recv.at[slot]
                ),
            )

            def add_up(count):
                received = term_pieces[slot, 0:count]
                total = jnp.dot(
                    spread[:, 0:count * TILE],
                    jnp.concatenate(
                        [
                            received[:, :, index].reshape(count * TILE, HEAD_DIM)
                            for index in range(2)
                        ],
                        axis=1,
                    ),
                    preferred_element_type=F32,
                )
                for index in range(2):
                    final_out[slot, :, index] = total[
                        :, index * HEAD_DIM:(index + 1) * HEAD_DIM
                    ].astype(BF16).reshape(SEGS, PIECE, HEAD_DIM)

            pl.when(below <= 2)(lambda: add_up(2))
            pl.when((below > 2) & (below <= 4))(lambda: add_up(4))
            pl.when(below > 4)(lambda: add_up(LEVELS - 1))
            landing = final_in.at[head, pl.ds(2 * my_owner, 2)]
            for turn in range(1, SEGS):
                peer = wrapped(me + turn)
                remote(
                    final_out.at[slot, peer], landing,
                    f_send.at[slot], f_recv.at[head], (level, peer),
                ).start()
            pltpu.make_async_copy(final_out.at[slot, me], landing, f_recv.at[head]).start()

    def store(head):
        @pl.when(level < LEVELS - 1)
        def _():
            wait_bytes(final_in.at[head], f_recv.at[head])
            for part in range(2):
                own[head, part] += final_in[head, halves[part]].reshape(
                    ROWS, HEAD_DIM
                ).astype(F32)

        grad_kv[0, 0, :, :, lanes(head)] = own[head].astype(BF16)

    @pl.loop(0, KV_HEADS + 4)
    def _(tick):
        @pl.when(tick < KV_HEADS)
        def _():
            pick_and_send(tick)

        @pl.when(tick == 0)
        def _():
            make_spread()
            load_q.wait()
            load_g.wait()

        @pl.when((tick >= 3) & (tick < KV_HEADS + 3))
        def _():
            sum_and_return(tick - 3)

        @pl.when(tick >= 4)
        def _():
            store(tick - 4)

        @pl.when((tick >= 1) & (tick < KV_HEADS + 1))
        def _():
            head = tick - 1
            per_count(
                level,
                lambda count: wait_bytes(blocks.at[head, pl.ds(1, count)], p3_recv.at[head]),
            )
            for pairs in range(1, LEVELS // 2 + 1):
                pl.when(half(level) == pairs - 1)(functools.partial(attend, head, pairs))
            send_terms(head)

    @pl.loop(0, KV_HEADS)
    def _(head):
        wait_bytes(pieces.at[head, pl.ds(1, SEGS - 1)], p1_send.at[head])

    @pl.loop(1, below + 1)
    def _(offset):
        batch_left(KV_HEADS - 1, offset)

    @pl.loop(1, level + 1)
    def _(offset):
        terms_left(KV_HEADS - 1, offset)

    @pl.when(level < LEVELS - 1)
    def _():
        for slot in range(2):
            wait_bytes(final_out.at[slot, pl.ds(1, SEGS - 1)], f_send.at[slot])


def shards(queries, keys_values, grad_out, parents):
    vmem = pl.BlockSpec(memory_space=pltpu.VMEM)
    smem = pl.BlockSpec(memory_space=pltpu.SMEM)
    hbm = pl.BlockSpec(memory_space=pltpu.HBM)
    dma = pltpu.SemaphoreType.DMA
    tile = (SEGS, PIECE, HEAD_DIM)
    keys_count = LEVELS * ROWS
    scratch = [
        pltpu.SMEM((LEVELS, SEGS), jnp.int32),
        pltpu.VMEM((LEVELS - 1, TILE, TILE), BF16),
        pltpu.VMEM((TILE, (LEVELS - 1) * TILE), BF16),
        pltpu.VMEM(keys_values.shape, BF16),
        pltpu.VMEM(queries.shape, BF16),
        pltpu.VMEM(queries.shape, BF16),
        pltpu.VMEM((KV_HEADS,) + tile, BF16),
        pltpu.VMEM((KV_HEADS,) + tile, BF16),
        pltpu.VMEM((KV_HEADS, LEVELS - 1) + tile, BF16),
        pltpu.VMEM((KV_HEADS, LEVELS) + tile, BF16),
        pltpu.VMEM((KV_HEADS, LEVELS) + tile, BF16),
        pltpu.VMEM((2, LEVELS - 1, SEGS, 2, PIECE, HEAD_DIM), BF16),
        pltpu.VMEM((KV_HEADS, 2, ROWS, HEAD_DIM), F32),
        pltpu.VMEM((2, STACK, HEAD_DIM), BF16),
        pltpu.VMEM((2, HEAD_DIM, STACK), BF16),
        pltpu.VMEM((HEAD_DIM, STACK), F32),
        pltpu.VMEM((keys_count, STACK), F32),
        pltpu.VMEM((keys_count, STACK), F32),
        pltpu.VMEM((keys_count, STACK), BF16),
        pltpu.VMEM((keys_count, STACK), BF16),
        pltpu.VMEM((2, SEGS, 2, PIECE, HEAD_DIM), BF16),
        pltpu.VMEM((KV_HEADS,) + tile, BF16),
        dma, dma, dma,
        pltpu.SemaphoreType.REGULAR,
        dma((KV_HEADS,)), dma((KV_HEADS,)),
        dma((2, LEVELS - 1)), dma((KV_HEADS,)),
        dma((2, LEVELS - 1)), dma((2,)),
        dma((2,)), dma((KV_HEADS,)),
    ]
    return pl.pallas_call(
        kernel,
        out_shape=(
            jax.ShapeDtypeStruct(queries.shape, BF16),
            jax.ShapeDtypeStruct(keys_values.shape, BF16),
        ),
        in_specs=[smem, hbm, hbm, hbm],
        out_specs=(vmem, vmem),
        scratch_shapes=scratch,
        compiler_params=pltpu.CompilerParams(
            collective_id=0, has_side_effects=True, vmem_limit_bytes=56 * 1024 * 1024
        ),
        cost_estimate=pl.CostEstimate(
            flops=5 * 2 * HEADS * LEVELS * ROWS * ROWS * HEAD_DIM,
            bytes_accessed=8 * 1024 * 1024,
            transcendentals=HEADS * LEVELS * ROWS * ROWS,
        ),
    )(parents.transpose(0, 2, 1), queries, keys_values, grad_out)


def solution(mesh):
    in_specs = (
        P("depth", "seg", None, None),
        P("depth", "seg", None, None, None),
        P("depth", "seg", None, None),
        P(),
    )
    out_specs = (P("depth", "seg", None, None), P("depth", "seg", None, None, None))
    return jax.shard_map(shards, mesh=mesh, in_specs=in_specs, out_specs=out_specs, check_vma=False)
```

```python
import functools

import jax
import jax.numpy as jnp
from jax import lax
from jax.experimental import pallas as pl
from jax.experimental.pallas import tpu as pltpu
from jax.sharding import PartitionSpec as P

HEADS = 20
KV_HEADS = 4
HEAD_DIM = 128
GROUP = HEADS // KV_HEADS
ROWS = 128
LEVELS = 8
SEGS = 16
PIECE = 16
PIECES_PER_PART = ROWS // PIECE
STACK = GROUP * ROWS
PAIR = 2 * ROWS
TILE = SEGS * PIECE
OWNERS = SEGS // 2

NEG_FILL = -1e30
SCALE = HEAD_DIM ** -0.5
EXP2_SCALE = SCALE * 1.4426950408889634
MESH = pl.DeviceIdType.MESH
BF16 = jnp.bfloat16
F32 = jnp.float32


def half(value):
    return lax.div(value, 2)


def odd(value):
    return lax.rem(value, 2)


def wrapped(index):
    return jnp.where(index >= SEGS, index - SEGS, index)


def lanes(index, count=1):
    width = count * HEAD_DIM
    return pl.ds(pl.multiple_of(index * width, width), width)


def rows_of(index, count):
    return pl.ds(pl.multiple_of(index * count, count), count)


def owner_column(owner, parity):
    z = half(owner)
    return 4 * z + 2 * odd(owner) + odd(z + parity)


def fold(tile):
    return tile.reshape(tile.shape[0] // 8, 8, tile.shape[1])


def kernel(
    parents, queries, keys_values, grad_out, grad_queries, grad_kv,
    anc, pick, spread, kv_in, q_in, g_in, kv_stage, pieces, chosen, blocks,
    terms, term_pieces, own, stacks, turned, query_sum, logits, grad_probs,
    probs, grad_logits, final_out, final_in,
    kv_sem, q_sem, g_sem, ready, p1_send, p1_recv, p3_send, p3_recv, b1_send, b1_recv,
    f_send, f_recv,
):
    level = lax.axis_index("depth")
    me = lax.axis_index("seg")
    below = LEVELS - 1 - level
    my_z, my_x = lax.div(me, 4), lax.rem(me, 4)
    my_parity = odd(my_z + my_x)
    my_owner = 2 * my_z + half(my_x)

    def remote(src, dst, send_sem, recv_sem, device):
        return pltpu.make_async_remote_copy(
            src_ref=src, dst_ref=dst, send_sem=send_sem, recv_sem=recv_sem,
            device_id=device, device_id_type=MESH,
        )

    def wait_bytes(ref, sem):
        pltpu.make_async_copy(ref, ref, sem).wait()

    def per_count(which, action):
        for count in range(1, LEVELS):
            pl.when(which == count)(functools.partial(action, count))

    load_kv = pltpu.make_async_copy(keys_values, kv_in, kv_sem)
    load_q = pltpu.make_async_copy(queries, q_in, q_sem)
    load_g = pltpu.make_async_copy(grad_out, g_in, g_sem)
    load_kv.start()
    load_q.start()
    load_g.start()

    barrier = pltpu.get_barrier_semaphore()

    def in_line(step):
        other = level + step
        return (jnp.where(other >= LEVELS, other - LEVELS, other), me)

    @pl.loop(1, SEGS)
    def _(step):
        pl.semaphore_signal(
            barrier, inc=1, device_id=(level, wrapped(me + step)), device_id_type=MESH
        )

    @pl.loop(1, LEVELS)
    def _(step):
        pl.semaphore_signal(barrier, inc=1, device_id=in_line(step), device_id_type=MESH)

    @pl.loop(0, SEGS)
    def _(column):
        anc[0, column] = column

    @pl.loop(1, below + 1)
    def _(offset):
        @pl.loop(0, SEGS)
        def _(column):
            anc[offset, column] = anc[offset - 1, parents[level + offset - 1, 0, column]]

    load_kv.wait()
    for head in range(KV_HEADS):
        for part in range(2):
            kv_stage[head, pl.ds(part * PIECES_PER_PART, PIECES_PER_PART)] = kv_in[
                0, 0, part, :, head * HEAD_DIM:(head + 1) * HEAD_DIM
            ].reshape(PIECES_PER_PART, PIECE, HEAD_DIM)
    pl.semaphore_wait(barrier, SEGS - 1 + LEVELS - 1)

    def spread_out(head):
        for turn in range(1, SEGS):
            peer = wrapped(me + turn)
            remote(
                kv_stage.at[head, peer], pieces.at[head, me],
                p1_send.at[head], p1_recv.at[head], (level, peer),
            ).start()
        pltpu.make_async_copy(
            kv_stage.at[head, me], pieces.at[head, me], p1_recv.at[head]
        ).start()

    spread_out(0)

    @pl.loop(1, LEVELS)
    def _(step):
        pl.semaphore_signal(ready, inc=1, device_id=in_line(step), device_id_type=MESH)

    @pl.loop(1, below + 1)
    def _(offset):
        lane = lax.broadcasted_iota(jnp.int32, (PIECE, TILE), 1)
        row = lax.broadcasted_iota(jnp.int32, (PIECE, TILE), 0)
        ahead = lane - row
        for column in range(SEGS):
            pick[offset - 1, rows_of(column, PIECE), :] = jnp.where(
                ahead == anc[offset, column] * PIECE, 1.0, 0.0
            ).astype(BF16)

    def batch_left(head, offset):
        wait_bytes(chosen.at[head, offset - 1], p3_send.at[odd(head), offset - 1])

    def pick_and_send(head):
        wait_bytes(pieces.at[head], p1_recv.at[head])
        pl.when(head < KV_HEADS - 1)(lambda: spread_out(head + 1))

        @pl.loop(1, below + 1)
        def _(step):
            offset = jnp.where(head == 0, below + 1 - step, step)
            found = jnp.dot(
                pick[offset - 1], pieces[head].reshape(TILE, HEAD_DIM),
                preferred_element_type=F32,
            )
            chosen[head, offset - 1] = found.astype(BF16).reshape(SEGS, PIECE, HEAD_DIM)
            pl.when(head > 0)(lambda: batch_left(head - 1, offset))
            for turn in range(SEGS):
                column = wrapped(me + turn)
                remote(
                    chosen.at[head, offset - 1, column], blocks.at[head, offset, me],
                    p3_send.at[odd(head), offset - 1], p3_recv.at[head],
                    (level + offset, column),
                ).start()

    pl.semaphore_wait(ready, LEVELS - 1)

    @pl.loop(0, KV_HEADS)
    def _(head):
        blocks[head, 0] = kv_stage[head]

        @pl.when(odd(level) == 0)
        def _():
            blocks[head, level + 1] = jnp.zeros((SEGS, PIECE, HEAD_DIM), BF16)

    def make_spread():
        @pl.loop(1, below + 1)
        def _(offset):
            lane = lax.broadcasted_iota(jnp.int32, (PIECE, TILE), 1)
            row = lax.broadcasted_iota(jnp.int32, (PIECE, TILE), 0)
            lane_column = lane >> 4
            span = pl.ds(pl.multiple_of((offset - 1) * TILE, TILE), TILE)
            target = (lane & (PIECE - 1)) - row
            for column in range(SEGS):
                target = jnp.where(
                    lane_column == column, target + anc[offset, column] * PIECE, target
                )
            for column in range(SEGS):
                spread[rows_of(column, PIECE), span] = jnp.where(
                    target == column * PIECE, 1.0, 0.0
                ).astype(BF16)

        @pl.loop(below, LEVELS - 1)
        def _(index):
            spread[:, pl.ds(pl.multiple_of(index * TILE, TILE), TILE)] = jnp.zeros(
                (TILE, TILE), BF16
            )
            for slot in range(2):
                term_pieces[slot, index] = jnp.zeros((SEGS, 2, PIECE, HEAD_DIM), BF16)

    halves = [pl.ds(part * PIECES_PER_PART, PIECES_PER_PART) for part in range(2)]

    def attend(head, pairs):
        span_all = [pl.ds(group * ROWS, ROWS) for group in range(GROUP)]

        def block_pair(pair, part):
            return blocks[head, 2 * pair:2 * pair + 2, halves[part]].reshape(PAIR, HEAD_DIM)

        for index in range(2):
            for group, span in enumerate(span_all):
                tile = (q_in, g_in)[index][0, 0, :, lanes(head * GROUP + group)]
                stacks[index, span, :] = tile
                turned[index, :, span] = tile.T
        u_row = lax.broadcasted_iota(jnp.int32, (ROWS, ROWS), 0)
        t_row = lax.broadcasted_iota(jnp.int32, (ROWS, ROWS), 1)
        last_seen = odd(level) == 1
        best = [jnp.full((8, ROWS), NEG_FILL, F32) for group in range(GROUP)]
        for pair in range(pairs):
            raw = jnp.dot(block_pair(pair, 0), turned[0], preferred_element_type=F32)
            for group, span in enumerate(span_all):
                first = raw[0:ROWS, group * ROWS:(group + 1) * ROWS]
                second = raw[ROWS:PAIR, group * ROWS:(group + 1) * ROWS]
                if pair == 0:
                    first = jnp.where(u_row <= t_row, first, NEG_FILL)
                if pair == pairs - 1:
                    second = jnp.where(last_seen, second, NEG_FILL)
                logits[pair * PAIR:pair * PAIR + ROWS, span] = first
                logits[pair * PAIR + ROWS:(pair + 1) * PAIR, span] = second
                best[group] = jnp.maximum(
                    best[group], jnp.maximum(fold(first).max(0), fold(second).max(0))
                )
        top = [value.max(0, keepdims=True) for value in best]
        total = [jnp.zeros((8, ROWS), F32) for group in range(GROUP)]
        delta = [jnp.zeros((8, ROWS), F32) for group in range(GROUP)]
        for pair in range(pairs):
            rows = slice(pair * PAIR, (pair + 1) * PAIR)
            raw = jnp.dot(block_pair(pair, 1), turned[1], preferred_element_type=F32)
            for group, span in enumerate(span_all):
                tile = jnp.exp2((logits[rows, span] - top[group]) * EXP2_SCALE)
                part = raw[:, group * ROWS:(group + 1) * ROWS]
                logits[rows, span] = tile
                grad_probs[rows, span] = part
                total[group] += fold(tile).sum(0)
                delta[group] += fold(tile * part).sum(0)
        inverse = [1.0 / value.sum(0, keepdims=True) for value in total]
        delta = [value.sum(0, keepdims=True) * by for value, by in zip(delta, inverse)]
        for pair in range(pairs):
            rows = slice(pair * PAIR, (pair + 1) * PAIR)
            for group, span in enumerate(span_all):
                exact = logits[rows, span] * inverse[group]
                probs[rows, span] = exact.astype(BF16)
                grad_logits[rows, span] = (
                    exact * (grad_probs[rows, span] - delta[group])
                ).astype(BF16)
            value_term = jnp.dot(probs[rows, :], stacks[1], preferred_element_type=F32)
            key_term = SCALE * jnp.dot(
                grad_logits[rows, :], stacks[0], preferred_element_type=F32
            )
            for part, term in enumerate((key_term, value_term)):
                terms[head, 2 * pair:2 * pair + 2, halves[part]] = term.astype(BF16).reshape(
                    2, PIECES_PER_PART, PIECE, HEAD_DIM
                )
                if pair == 0:
                    own[head, part] = term[0:ROWS]
            moved = lax.dot_general(
                block_pair(pair, 0), grad_logits[rows, :], (((0,), (0,)), ((), ())),
                preferred_element_type=F32,
            )
            if pair == 0:
                query_sum[...] = moved
            else:
                query_sum[...] += moved
        for group, span in enumerate(span_all):
            grad_queries[0, 0, :, lanes(head * GROUP + group)] = (
                SCALE * query_sum[:, span].T
            ).astype(BF16)

    def terms_left(head, offset):
        wait_bytes(terms.at[head, offset], b1_send.at[odd(head), offset - 1])

    def send_terms(head):
        targets = []
        for turn in range(OWNERS):
            owner = my_owner + turn
            owner = jnp.where(owner >= OWNERS, owner - OWNERS, owner)
            targets.append((owner, owner_column(owner, odd(head))))

        @pl.loop(1, level + 1)
        def _(offset):
            pl.when(head > 0)(lambda: terms_left(head - 1, offset))
            for owner, column in targets:
                remote(
                    terms.at[head, offset, pl.ds(2 * owner, 2)],
                    term_pieces.at[half(head), offset - 1, me],
                    b1_send.at[odd(head), offset - 1], b1_recv.at[half(head)],
                    (level - offset, column),
                ).start()

    def sum_and_return(head):
        slot = half(head)

        @pl.when((level < LEVELS - 1) & (odd(head) == my_parity))
        def _():
            per_count(
                below,
                lambda count: wait_bytes(
                    term_pieces.at[slot, pl.ds(0, count)], b1_recv.at[slot]
                ),
            )

            def add_up(count):
                received = term_pieces[slot, 0:count]
                total = jnp.dot(
                    spread[:, 0:count * TILE],
                    jnp.concatenate(
                        [
                            received[:, :, index].reshape(count * TILE, HEAD_DIM)
                            for index in range(2)
                        ],
                        axis=1,
                    ),
                    preferred_element_type=F32,
                )
                for index in range(2):
                    final_out[slot, :, index] = total[
                        :, index * HEAD_DIM:(index + 1) * HEAD_DIM
                    ].astype(BF16).reshape(SEGS, PIECE, HEAD_DIM)

            pl.when(below <= 2)(lambda: add_up(2))
            pl.when((below > 2) & (below <= 4))(lambda: add_up(4))
            pl.when(below > 4)(lambda: add_up(LEVELS - 1))
            landing = final_in.at[head, pl.ds(2 * my_owner, 2)]
            for turn in range(1, SEGS):
                peer = wrapped(me + turn)
                remote(
                    final_out.at[slot, peer], landing,
                    f_send.at[slot], f_recv.at[head], (level, peer),
                ).start()
            pltpu.make_async_copy(final_out.at[slot, me], landing, f_recv.at[head]).start()

    def store(head):
        @pl.when(level < LEVELS - 1)
        def _():
            wait_bytes(final_in.at[head], f_recv.at[head])
            for part in range(2):
                own[head, part] += final_in[head, halves[part]].reshape(
                    ROWS, HEAD_DIM
                ).astype(F32)

        grad_kv[0, 0, :, :, lanes(head)] = own[head].astype(BF16)

    lag = jnp.where(level <= 2, KV_HEADS, 1)

    @pl.loop(0, KV_HEADS + lag + 3)
    def _(tick):
        @pl.when(tick < KV_HEADS)
        def _():
            pick_and_send(tick)

        @pl.when(tick == 0)
        def _():
            load_q.wait()
            load_g.wait()

        @pl.when(tick == KV_HEADS - 1)
        def _():
            make_spread()

        @pl.when((tick >= lag) & (tick < KV_HEADS + lag))
        def _():
            head = tick - lag
            per_count(
                level,
                lambda count: wait_bytes(blocks.at[head, pl.ds(1, count)], p3_recv.at[head]),
            )
            for pairs in range(1, LEVELS // 2 + 1):
                pl.when(half(level) == pairs - 1)(functools.partial(attend, head, pairs))
            send_terms(head)

        @pl.when((tick >= lag + 2) & (tick < KV_HEADS + lag + 2))
        def _():
            sum_and_return(tick - lag - 2)

        @pl.when(tick >= lag + 3)
        def _():
            store(tick - lag - 3)

    @pl.loop(0, KV_HEADS)
    def _(head):
        wait_bytes(pieces.at[head, pl.ds(1, SEGS - 1)], p1_send.at[head])

    @pl.loop(1, below + 1)
    def _(offset):
        batch_left(KV_HEADS - 1, offset)

    @pl.loop(1, level + 1)
    def _(offset):
        terms_left(KV_HEADS - 1, offset)

    @pl.when(level < LEVELS - 1)
    def _():
        for slot in range(2):
            wait_bytes(final_out.at[slot, pl.ds(1, SEGS - 1)], f_send.at[slot])


def shards(queries, keys_values, grad_out, parents):
    vmem = pl.BlockSpec(memory_space=pltpu.VMEM)
    smem = pl.BlockSpec(memory_space=pltpu.SMEM)
    hbm = pl.BlockSpec(memory_space=pltpu.HBM)
    dma = pltpu.SemaphoreType.DMA
    tile = (SEGS, PIECE, HEAD_DIM)
    keys_count = LEVELS * ROWS
    scratch = [
        pltpu.SMEM((LEVELS, SEGS), jnp.int32),
        pltpu.VMEM((LEVELS - 1, TILE, TILE), BF16),
        pltpu.VMEM((TILE, (LEVELS - 1) * TILE), BF16),
        pltpu.VMEM(keys_values.shape, BF16),
        pltpu.VMEM(queries.shape, BF16),
        pltpu.VMEM(queries.shape, BF16),
        pltpu.VMEM((KV_HEADS,) + tile, BF16),
        pltpu.VMEM((KV_HEADS,) + tile, BF16),
        pltpu.VMEM((KV_HEADS, LEVELS - 1) + tile, BF16),
        pltpu.VMEM((KV_HEADS, LEVELS) + tile, BF16),
        pltpu.VMEM((KV_HEADS, LEVELS) + tile, BF16),
        pltpu.VMEM((2, LEVELS - 1, SEGS, 2, PIECE, HEAD_DIM), BF16),
        pltpu.VMEM((KV_HEADS, 2, ROWS, HEAD_DIM), F32),
        pltpu.VMEM((2, STACK, HEAD_DIM), BF16),
        pltpu.VMEM((2, HEAD_DIM, STACK), BF16),
        pltpu.VMEM((HEAD_DIM, STACK), F32),
        pltpu.VMEM((keys_count, STACK), F32),
        pltpu.VMEM((keys_count, STACK), F32),
        pltpu.VMEM((keys_count, STACK), BF16),
        pltpu.VMEM((keys_count, STACK), BF16),
        pltpu.VMEM((2, SEGS, 2, PIECE, HEAD_DIM), BF16),
        pltpu.VMEM((KV_HEADS,) + tile, BF16),
        dma, dma, dma,
        pltpu.SemaphoreType.REGULAR,
        dma((KV_HEADS,)), dma((KV_HEADS,)),
        dma((2, LEVELS - 1)), dma((KV_HEADS,)),
        dma((2, LEVELS - 1)), dma((2,)),
        dma((2,)), dma((KV_HEADS,)),
    ]
    return pl.pallas_call(
        kernel,
        out_shape=(
            jax.ShapeDtypeStruct(queries.shape, BF16),
            jax.ShapeDtypeStruct(keys_values.shape, BF16),
        ),
        in_specs=[smem, hbm, hbm, hbm],
        out_specs=(vmem, vmem),
        scratch_shapes=scratch,
        compiler_params=pltpu.CompilerParams(
            collective_id=0, has_side_effects=True, vmem_limit_bytes=56 * 1024 * 1024
        ),
        cost_estimate=pl.CostEstimate(
            flops=5 * 2 * HEADS * LEVELS * ROWS * ROWS * HEAD_DIM,
            bytes_accessed=8 * 1024 * 1024,
            transcendentals=HEADS * LEVELS * ROWS * ROWS,
        ),
    )(parents.transpose(0, 2, 1), queries, keys_values, grad_out)


def solution(mesh):
    in_specs = (
        P("depth", "seg", None, None),
        P("depth", "seg", None, None, None),
        P("depth", "seg", None, None),
        P(),
    )
    out_specs = (P("depth", "seg", None, None), P("depth", "seg", None, None, None))
    return jax.shard_map(shards, mesh=mesh, in_specs=in_specs, out_specs=out_specs, check_vma=False)
```

```python
import functools

import jax
import jax.numpy as jnp
from jax import lax
from jax.experimental import pallas as pl
from jax.experimental.pallas import tpu as pltpu
from jax.sharding import PartitionSpec as P

HEADS = 20
KV_HEADS = 4
HEAD_DIM = 128
GROUP = HEADS // KV_HEADS
ROWS = 128
LEVELS = 8
SEGS = 16
PIECE = 16
PIECES_PER_PART = ROWS // PIECE
STACK = GROUP * ROWS
PAIR = 2 * ROWS
TILE = SEGS * PIECE
OWNERS = SEGS // 2

NEG_FILL = -1e30
SCALE = HEAD_DIM ** -0.5
EXP2_SCALE = SCALE * 1.4426950408889634
MESH = pl.DeviceIdType.MESH
BF16 = jnp.bfloat16
F32 = jnp.float32


def half(value):
    return lax.div(value, 2)


def odd(value):
    return lax.rem(value, 2)


def wrapped(index):
    return jnp.where(index >= SEGS, index - SEGS, index)


def lanes(index, count=1):
    width = count * HEAD_DIM
    return pl.ds(pl.multiple_of(index * width, width), width)


def rows_of(index, count):
    return pl.ds(pl.multiple_of(index * count, count), count)


def owner_column(owner, parity):
    z = half(owner)
    return 4 * z + 2 * odd(owner) + odd(z + parity)


def fold(tile):
    return tile.reshape(tile.shape[0] // 8, 8, tile.shape[1])


def kernel(
    parents, queries, keys_values, grad_out, grad_queries, grad_kv,
    anc, pick, spread, kv_in, q_in, g_in, kv_stage, pieces, chosen, blocks,
    terms, term_pieces, own, stacks, turned, query_sum, logits, grad_probs,
    probs, grad_logits, final_out, final_in,
    kv_sem, q_sem, g_sem, ready, p1_send, p1_recv, p3_send, p3_recv, b1_send, b1_recv,
    f_send, f_recv,
):
    level = lax.axis_index("depth")
    me = lax.axis_index("seg")
    below = LEVELS - 1 - level
    mirror = LEVELS - 1 - level
    my_z, my_x = lax.div(me, 4), lax.rem(me, 4)
    my_parity = odd(my_z + my_x)
    my_owner = 2 * my_z + half(my_x)

    def remote(src, dst, send_sem, recv_sem, device):
        return pltpu.make_async_remote_copy(
            src_ref=src, dst_ref=dst, send_sem=send_sem, recv_sem=recv_sem,
            device_id=device, device_id_type=MESH,
        )

    def wait_bytes(ref, sem):
        pltpu.make_async_copy(ref, ref, sem).wait()

    def per_count(which, action):
        for count in range(1, LEVELS):
            pl.when(which == count)(functools.partial(action, count))

    load_kv = pltpu.make_async_copy(keys_values, kv_in, kv_sem)
    load_q = pltpu.make_async_copy(queries, q_in, q_sem)
    load_g = pltpu.make_async_copy(grad_out, g_in, g_sem)
    load_kv.start()
    load_q.start()
    load_g.start()

    barrier = pltpu.get_barrier_semaphore()

    def in_line(step):
        other = level + step
        return (jnp.where(other >= LEVELS, other - LEVELS, other), me)

    @pl.loop(1, SEGS)
    def _(step):
        pl.semaphore_signal(
            barrier, inc=1, device_id=(level, wrapped(me + step)), device_id_type=MESH
        )

        pl.semaphore_signal(
            barrier, inc=1, device_id=(mirror, wrapped(me + step)), device_id_type=MESH
        )

    @pl.loop(1, LEVELS)
    def _(step):
        pl.semaphore_signal(barrier, inc=1, device_id=in_line(step), device_id_type=MESH)

    served = (mirror, level)
    for index, base in enumerate(served):
        @pl.loop(0, SEGS)
        def _(column):
            anc[index, 0, column] = column

        @pl.loop(1, LEVELS - base)
        def _(offset):
            @pl.loop(0, SEGS)
            def _(column):
                anc[index, offset, column] = anc[
                    index, offset - 1, parents[base + offset - 1, 0, column]
                ]

    load_kv.wait()
    for head in range(KV_HEADS):
        for part in range(2):
            kv_stage[head, pl.ds(part * PIECES_PER_PART, PIECES_PER_PART)] = kv_in[
                0, 0, part, :, head * HEAD_DIM:(head + 1) * HEAD_DIM
            ].reshape(PIECES_PER_PART, PIECE, HEAD_DIM)
    pl.semaphore_wait(barrier, 2 * (SEGS - 1) + LEVELS - 1)

    def spread_out(head):
        host = jnp.where(head == 0, mirror, level)

        def copy_to(peer):
            return remote(
                kv_stage.at[head, peer], pieces.at[head, me],
                p1_send.at[head], p1_recv.at[head], (host, peer),
            )

        for turn in range(1, SEGS):
            copy_to(wrapped(me + turn)).start()
        pl.when(head == 0)(lambda: copy_to(me).start())
        pl.when(head > 0)(
            lambda: pltpu.make_async_copy(
                kv_stage.at[head, me], pieces.at[head, me], p1_recv.at[head]
            ).start()
        )

    pl.loop(0, 2)(spread_out)

    @pl.loop(1, LEVELS)
    def _(step):
        pl.semaphore_signal(ready, inc=1, device_id=in_line(step), device_id_type=MESH)

    for index, base in enumerate(served):
        @pl.loop(1, LEVELS - base)
        def _(offset):
            lane = lax.broadcasted_iota(jnp.int32, (PIECE, TILE), 1)
            row = lax.broadcasted_iota(jnp.int32, (PIECE, TILE), 0)
            ahead = lane - row
            for column in range(SEGS):
                pick[index, offset - 1, rows_of(column, PIECE), :] = jnp.where(
                    ahead == anc[index, offset, column] * PIECE, 1.0, 0.0
                ).astype(BF16)

    def batch_left(head, offset):
        wait_bytes(chosen.at[head, offset - 1], p3_send.at[head, offset - 1])

    def pick_and_send(head):
        wait_bytes(pieces.at[head], p1_recv.at[head])
        pl.when((head > 0) & (head < KV_HEADS - 1))(lambda: spread_out(head + 1))
        base = jnp.where(head == 0, mirror, level)
        index = jnp.where(head == 0, 0, 1)

        @pl.loop(1, LEVELS - base)
        def _(offset):
            found = jnp.dot(
                pick[index, offset - 1], pieces[head].reshape(TILE, HEAD_DIM),
                preferred_element_type=F32,
            )
            chosen[head, offset - 1] = found.astype(BF16).reshape(SEGS, PIECE, HEAD_DIM)
            pl.when(head > 1)(lambda: batch_left(head - 1, offset))
            target = base + offset

            def copy_to(column):
                return remote(
                    chosen.at[head, offset - 1, column], blocks.at[head, offset, me],
                    p3_send.at[head, offset - 1], p3_recv.at[head], (target, column),
                )

            for turn in range(1, SEGS):
                copy_to(wrapped(me + turn)).start()
            pl.when(target != level)(lambda: copy_to(me).start())
            pl.when(target == level)(
                lambda: pltpu.make_async_copy(
                    chosen.at[head, offset - 1, me], blocks.at[head, offset, me],
                    p3_recv.at[head],
                ).start()
            )

    pl.semaphore_wait(ready, LEVELS - 1)

    @pl.loop(0, KV_HEADS)
    def _(head):
        blocks[head, 0] = kv_stage[head]

        @pl.when(odd(level) == 0)
        def _():
            blocks[head, level + 1] = jnp.zeros((SEGS, PIECE, HEAD_DIM), BF16)

    def make_spread():
        @pl.loop(1, below + 1)
        def _(offset):
            lane = lax.broadcasted_iota(jnp.int32, (PIECE, TILE), 1)
            row = lax.broadcasted_iota(jnp.int32, (PIECE, TILE), 0)
            lane_column = lane >> 4
            span = pl.ds(pl.multiple_of((offset - 1) * TILE, TILE), TILE)
            target = (lane & (PIECE - 1)) - row
            for column in range(SEGS):
                target = jnp.where(
                    lane_column == column, target + anc[1, offset, column] * PIECE, target
                )
            for column in range(SEGS):
                spread[rows_of(column, PIECE), span] = jnp.where(
                    target == column * PIECE, 1.0, 0.0
                ).astype(BF16)

        @pl.loop(below, LEVELS - 1)
        def _(index):
            spread[:, pl.ds(pl.multiple_of(index * TILE, TILE), TILE)] = jnp.zeros(
                (TILE, TILE), BF16
            )
            for slot in range(2):
                term_pieces[slot, index] = jnp.zeros((SEGS, 2, PIECE, HEAD_DIM), BF16)

    halves = [pl.ds(part * PIECES_PER_PART, PIECES_PER_PART) for part in range(2)]

    def attend(head, pairs):
        span_all = [pl.ds(group * ROWS, ROWS) for group in range(GROUP)]

        def block_pair(pair, part):
            return blocks[head, 2 * pair:2 * pair + 2, halves[part]].reshape(PAIR, HEAD_DIM)

        for index in range(2):
            for group, span in enumerate(span_all):
                tile = (q_in, g_in)[index][0, 0, :, lanes(head * GROUP + group)]
                stacks[index, span, :] = tile
                turned[index, :, span] = tile.T
        u_row = lax.broadcasted_iota(jnp.int32, (ROWS, ROWS), 0)
        t_row = lax.broadcasted_iota(jnp.int32, (ROWS, ROWS), 1)
        last_seen = odd(level) == 1
        best = [jnp.full((8, ROWS), NEG_FILL, F32) for group in range(GROUP)]
        for pair in range(pairs):
            raw = jnp.dot(block_pair(pair, 0), turned[0], preferred_element_type=F32)
            for group, span in enumerate(span_all):
                first = raw[0:ROWS, group * ROWS:(group + 1) * ROWS]
                second = raw[ROWS:PAIR, group * ROWS:(group + 1) * ROWS]
                if pair == 0:
                    first = jnp.where(u_row <= t_row, first, NEG_FILL)
                if pair == pairs - 1:
                    second = jnp.where(last_seen, second, NEG_FILL)
                logits[pair * PAIR:pair * PAIR + ROWS, span] = first
                logits[pair * PAIR + ROWS:(pair + 1) * PAIR, span] = second
                best[group] = jnp.maximum(
                    best[group], jnp.maximum(fold(first).max(0), fold(second).max(0))
                )
        top = [value.max(0, keepdims=True) for value in best]
        total = [jnp.zeros((8, ROWS), F32) for group in range(GROUP)]
        delta = [jnp.zeros((8, ROWS), F32) for group in range(GROUP)]
        for pair in range(pairs):
            rows = slice(pair * PAIR, (pair + 1) * PAIR)
            raw = jnp.dot(block_pair(pair, 1), turned[1], preferred_element_type=F32)
            for group, span in enumerate(span_all):
                tile = jnp.exp2((logits[rows, span] - top[group]) * EXP2_SCALE)
                part = raw[:, group * ROWS:(group + 1) * ROWS]
                logits[rows, span] = tile
                grad_probs[rows, span] = part
                total[group] += fold(tile).sum(0)
                delta[group] += fold(tile * part).sum(0)
        inverse = [1.0 / value.sum(0, keepdims=True) for value in total]
        delta = [value.sum(0, keepdims=True) * by for value, by in zip(delta, inverse)]
        for pair in range(pairs):
            rows = slice(pair * PAIR, (pair + 1) * PAIR)
            for group, span in enumerate(span_all):
                exact = logits[rows, span] * inverse[group]
                probs[rows, span] = exact.astype(BF16)
                grad_logits[rows, span] = (
                    exact * (grad_probs[rows, span] - delta[group])
                ).astype(BF16)
            value_term = jnp.dot(probs[rows, :], stacks[1], preferred_element_type=F32)
            key_term = SCALE * jnp.dot(
                grad_logits[rows, :], stacks[0], preferred_element_type=F32
            )
            for part, term in enumerate((key_term, value_term)):
                terms[head, 2 * pair:2 * pair + 2, halves[part]] = term.astype(BF16).reshape(
                    2, PIECES_PER_PART, PIECE, HEAD_DIM
                )
                if pair == 0:
                    own[head, part] = term[0:ROWS]
            moved = lax.dot_general(
                block_pair(pair, 0), grad_logits[rows, :], (((0,), (0,)), ((), ())),
                preferred_element_type=F32,
            )
            if pair == 0:
                query_sum[...] = moved
            else:
                query_sum[...] += moved
        for group, span in enumerate(span_all):
            grad_queries[0, 0, :, lanes(head * GROUP + group)] = (
                SCALE * query_sum[:, span].T
            ).astype(BF16)

    def terms_left(head, offset):
        wait_bytes(terms.at[head, offset], b1_send.at[odd(head), offset - 1])

    def send_terms(head):
        targets = []
        for turn in range(OWNERS):
            owner = my_owner + turn
            owner = jnp.where(owner >= OWNERS, owner - OWNERS, owner)
            targets.append((owner, owner_column(owner, odd(head))))

        @pl.loop(1, level + 1)
        def _(offset):
            pl.when(head > 0)(lambda: terms_left(head - 1, offset))
            for owner, column in targets:
                remote(
                    terms.at[head, offset, pl.ds(2 * owner, 2)],
                    term_pieces.at[half(head), offset - 1, me],
                    b1_send.at[odd(head), offset - 1], b1_recv.at[half(head)],
                    (level - offset, column),
                ).start()

    def sum_and_return(head):
        slot = half(head)

        @pl.when((level < LEVELS - 1) & (odd(head) == my_parity))
        def _():
            per_count(
                below,
                lambda count: wait_bytes(
                    term_pieces.at[slot, pl.ds(0, count)], b1_recv.at[slot]
                ),
            )

            def add_up(count):
                received = term_pieces[slot, 0:count]
                total = jnp.dot(
                    spread[:, 0:count * TILE],
                    jnp.concatenate(
                        [
                            received[:, :, index].reshape(count * TILE, HEAD_DIM)
                            for index in range(2)
                        ],
                        axis=1,
                    ),
                    preferred_element_type=F32,
                )
                for index in range(2):
                    final_out[slot, :, index] = total[
                        :, index * HEAD_DIM:(index + 1) * HEAD_DIM
                    ].astype(BF16).reshape(SEGS, PIECE, HEAD_DIM)

            pl.when(below <= 2)(lambda: add_up(2))
            pl.when((below > 2) & (below <= 4))(lambda: add_up(4))
            pl.when(below > 4)(lambda: add_up(LEVELS - 1))
            landing = final_in.at[head, pl.ds(2 * my_owner, 2)]
            for turn in range(1, SEGS):
                peer = wrapped(me + turn)
                remote(
                    final_out.at[slot, peer], landing,
                    f_send.at[slot], f_recv.at[head], (level, peer),
                ).start()
            pltpu.make_async_copy(final_out.at[slot, me], landing, f_recv.at[head]).start()

    def store(head):
        @pl.when(level < LEVELS - 1)
        def _():
            wait_bytes(final_in.at[head], f_recv.at[head])
            for part in range(2):
                own[head, part] += final_in[head, halves[part]].reshape(
                    ROWS, HEAD_DIM
                ).astype(F32)

        grad_kv[0, 0, :, :, lanes(head)] = own[head].astype(BF16)

    @pl.loop(0, KV_HEADS + 4)
    def _(tick):
        pl.when(tick == 0)(lambda: pick_and_send(0))
        pl.when(tick < KV_HEADS - 1)(lambda: pick_and_send(tick + 1))

        @pl.when(tick == 0)
        def _():
            make_spread()
            load_q.wait()
            load_g.wait()

        @pl.when((tick >= 3) & (tick < KV_HEADS + 3))
        def _():
            sum_and_return(tick - 3)

        @pl.when(tick >= 4)
        def _():
            store(tick - 4)

        @pl.when((tick >= 1) & (tick < KV_HEADS + 1))
        def _():
            head = tick - 1
            per_count(
                level,
                lambda count: wait_bytes(blocks.at[head, pl.ds(1, count)], p3_recv.at[head]),
            )
            for pairs in range(1, LEVELS // 2 + 1):
                pl.when(half(level) == pairs - 1)(functools.partial(attend, head, pairs))
            send_terms(head)

    @pl.loop(0, KV_HEADS)
    def _(head):
        wait_bytes(pieces.at[head, pl.ds(1, SEGS - 1)], p1_send.at[head])
        pl.when(head == 0)(lambda: wait_bytes(pieces.at[0, 0], p1_send.at[0]))

    @pl.loop(1, LEVELS - mirror)
    def _(offset):
        wait_bytes(chosen.at[0, offset - 1, pl.ds(1, SEGS - 1)], p3_send.at[0, offset - 1])
        pl.when(mirror + offset != level)(
            lambda: wait_bytes(chosen.at[0, offset - 1, 0], p3_send.at[0, offset - 1])
        )

    @pl.loop(1, below + 1)
    def _(offset):
        batch_left(KV_HEADS - 1, offset)

    @pl.loop(1, level + 1)
    def _(offset):
        terms_left(KV_HEADS - 1, offset)

    @pl.when(level < LEVELS - 1)
    def _():
        for slot in range(2):
            wait_bytes(final_out.at[slot, pl.ds(1, SEGS - 1)], f_send.at[slot])


def shards(queries, keys_values, grad_out, parents):
    vmem = pl.BlockSpec(memory_space=pltpu.VMEM)
    smem = pl.BlockSpec(memory_space=pltpu.SMEM)
    hbm = pl.BlockSpec(memory_space=pltpu.HBM)
    dma = pltpu.SemaphoreType.DMA
    tile = (SEGS, PIECE, HEAD_DIM)
    keys_count = LEVELS * ROWS
    scratch = [
        pltpu.SMEM((2, LEVELS, SEGS), jnp.int32),
        pltpu.VMEM((2, LEVELS - 1, TILE, TILE), BF16),
        pltpu.VMEM((TILE, (LEVELS - 1) * TILE), BF16),
        pltpu.VMEM(keys_values.shape, BF16),
        pltpu.VMEM(queries.shape, BF16),
        pltpu.VMEM(queries.shape, BF16),
        pltpu.VMEM((KV_HEADS,) + tile, BF16),
        pltpu.VMEM((KV_HEADS,) + tile, BF16),
        pltpu.VMEM((KV_HEADS, LEVELS - 1) + tile, BF16),
        pltpu.VMEM((KV_HEADS, LEVELS) + tile, BF16),
        pltpu.VMEM((KV_HEADS, LEVELS) + tile, BF16),
        pltpu.VMEM((2, LEVELS - 1, SEGS, 2, PIECE, HEAD_DIM), BF16),
        pltpu.VMEM((KV_HEADS, 2, ROWS, HEAD_DIM), F32),
        pltpu.VMEM((2, STACK, HEAD_DIM), BF16),
        pltpu.VMEM((2, HEAD_DIM, STACK), BF16),
        pltpu.VMEM((HEAD_DIM, STACK), F32),
        pltpu.VMEM((keys_count, STACK), F32),
        pltpu.VMEM((keys_count, STACK), F32),
        pltpu.VMEM((keys_count, STACK), BF16),
        pltpu.VMEM((keys_count, STACK), BF16),
        pltpu.VMEM((2, SEGS, 2, PIECE, HEAD_DIM), BF16),
        pltpu.VMEM((KV_HEADS,) + tile, BF16),
        dma, dma, dma,
        pltpu.SemaphoreType.REGULAR,
        dma((KV_HEADS,)), dma((KV_HEADS,)),
        dma((KV_HEADS, LEVELS - 1)), dma((KV_HEADS,)),
        dma((2, LEVELS - 1)), dma((2,)),
        dma((2,)), dma((KV_HEADS,)),
    ]
    return pl.pallas_call(
        kernel,
        out_shape=(
            jax.ShapeDtypeStruct(queries.shape, BF16),
            jax.ShapeDtypeStruct(keys_values.shape, BF16),
        ),
        in_specs=[smem, hbm, hbm, hbm],
        out_specs=(vmem, vmem),
        scratch_shapes=scratch,
        compiler_params=pltpu.CompilerParams(
            collective_id=0, has_side_effects=True, vmem_limit_bytes=56 * 1024 * 1024
        ),
        cost_estimate=pl.CostEstimate(
            flops=5 * 2 * HEADS * LEVELS * ROWS * ROWS * HEAD_DIM,
            bytes_accessed=8 * 1024 * 1024,
            transcendentals=HEADS * LEVELS * ROWS * ROWS,
        ),
    )(parents.transpose(0, 2, 1), queries, keys_values, grad_out)


def solution(mesh):
    in_specs = (
        P("depth", "seg", None, None),
        P("depth", "seg", None, None, None),
        P("depth", "seg", None, None),
        P(),
    )
    out_specs = (P("depth", "seg", None, None), P("depth", "seg", None, None, None))
    return jax.shard_map(shards, mesh=mesh, in_specs=in_specs, out_specs=out_specs, check_vma=False)
```

```python
import functools

import jax
import jax.numpy as jnp
from jax import lax
from jax.experimental import pallas as pl
from jax.experimental.pallas import tpu as pltpu
from jax.sharding import PartitionSpec as P

HEADS = 20
KV_HEADS = 4
HEAD_DIM = 128
GROUP = HEADS // KV_HEADS
ROWS = 128
LEVELS = 8
SEGS = 16
PIECE = 16
PIECES_PER_PART = ROWS // PIECE
STACK = GROUP * ROWS
PAIR = 2 * ROWS
TILE = SEGS * PIECE
OWNERS = SEGS // 2

NEG_FILL = -1e30
SCALE = HEAD_DIM ** -0.5
EXP2_SCALE = SCALE * 1.4426950408889634
MESH = pl.DeviceIdType.MESH
BF16 = jnp.bfloat16
F32 = jnp.float32


def half(value):
    return lax.div(value, 2)


def odd(value):
    return lax.rem(value, 2)


def wrapped(index):
    return jnp.where(index >= SEGS, index - SEGS, index)


def lanes(index, count=1):
    width = count * HEAD_DIM
    return pl.ds(pl.multiple_of(index * width, width), width)


def rows_of(index, count):
    return pl.ds(pl.multiple_of(index * count, count), count)


def owner_column(owner, parity):
    z = half(owner)
    return 4 * z + 2 * odd(owner) + odd(z + parity)


def fold(tile):
    return tile.reshape(tile.shape[0] // 8, 8, tile.shape[1])


def kernel(
    parents, queries, keys_values, grad_out, grad_queries, grad_kv,
    anc, pick, spread, kv_in, q_in, g_in, kv_stage, pieces, chosen, blocks,
    terms, term_pieces, own, stacks, turned, query_sum, logits, grad_probs,
    probs, grad_logits, total, final_out, final_in, q_out, kv_out,
    kv_sem, q_sem, g_sem, ready, p1_send, p1_recv, p3_send, p3_recv, b1_send, b1_recv,
    f_send, f_recv, q_out_sem, kv_out_sem,
):
    level = lax.axis_index("depth")
    me = lax.axis_index("seg")
    below = LEVELS - 1 - level
    my_z, my_x = lax.div(me, 4), lax.rem(me, 4)
    my_parity = odd(my_z + my_x)
    my_owner = 2 * my_z + half(my_x)

    def remote(src, dst, send_sem, recv_sem, device):
        return pltpu.make_async_remote_copy(
            src_ref=src, dst_ref=dst, send_sem=send_sem, recv_sem=recv_sem,
            device_id=device, device_id_type=MESH,
        )

    def wait_bytes(ref, sem):
        pltpu.make_async_copy(ref, ref, sem).wait()

    def per_count(which, action):
        for count in range(1, LEVELS):
            pl.when(which == count)(functools.partial(action, count))

    load_kv = pltpu.make_async_copy(keys_values, kv_in, kv_sem)
    load_q = pltpu.make_async_copy(queries, q_in, q_sem)
    load_g = pltpu.make_async_copy(grad_out, g_in, g_sem)
    load_kv.start()
    load_q.start()
    load_g.start()

    barrier = pltpu.get_barrier_semaphore()

    def in_line(step):
        other = level + step
        return (jnp.where(other >= LEVELS, other - LEVELS, other), me)

    @pl.loop(1, SEGS)
    def _(step):
        pl.semaphore_signal(
            barrier, inc=1, device_id=(level, wrapped(me + step)), device_id_type=MESH
        )

    @pl.loop(1, LEVELS)
    def _(step):
        pl.semaphore_signal(barrier, inc=1, device_id=in_line(step), device_id_type=MESH)

    @pl.loop(0, SEGS)
    def _(column):
        anc[0, column] = column

    @pl.loop(1, below + 1)
    def _(offset):
        @pl.loop(0, SEGS)
        def _(column):
            anc[offset, column] = anc[offset - 1, parents[level + offset - 1, 0, column]]

    load_kv.wait()
    for head in range(KV_HEADS):
        for part in range(2):
            kv_stage[head, pl.ds(part * PIECES_PER_PART, PIECES_PER_PART)] = kv_in[
                0, 0, part, :, head * HEAD_DIM:(head + 1) * HEAD_DIM
            ].reshape(PIECES_PER_PART, PIECE, HEAD_DIM)
    pl.semaphore_wait(barrier, SEGS - 1 + LEVELS - 1)

    def spread_out(head):
        for turn in range(1, SEGS):
            peer = wrapped(me + turn)
            remote(
                kv_stage.at[head, peer], pieces.at[head, me],
                p1_send.at[head], p1_recv.at[head], (level, peer),
            ).start()
        pltpu.make_async_copy(
            kv_stage.at[head, me], pieces.at[head, me], p1_recv.at[head]
        ).start()

    spread_out(0)

    @pl.loop(1, LEVELS)
    def _(step):
        pl.semaphore_signal(ready, inc=1, device_id=in_line(step), device_id_type=MESH)

    @pl.loop(1, below + 1)
    def _(offset):
        lane = lax.broadcasted_iota(jnp.int32, (PIECE, TILE), 1)
        row = lax.broadcasted_iota(jnp.int32, (PIECE, TILE), 0)
        ahead = lane - row
        for column in range(SEGS):
            pick[offset - 1, rows_of(column, PIECE), :] = jnp.where(
                ahead == anc[offset, column] * PIECE, 1.0, 0.0
            ).astype(BF16)

    def batch_left(head, offset):
        wait_bytes(chosen.at[head, offset - 1], p3_send.at[odd(head), offset - 1])

    def pick_and_send(head):
        wait_bytes(pieces.at[head], p1_recv.at[head])
        pl.when(head < KV_HEADS - 1)(lambda: spread_out(head + 1))

        @pl.loop(1, below + 1)
        def _(step):
            offset = jnp.where(head == 0, below + 1 - step, step)
            found = jnp.dot(
                pick[offset - 1], pieces[head].reshape(TILE, HEAD_DIM),
                preferred_element_type=F32,
            )
            chosen[head, offset - 1] = found.astype(BF16).reshape(SEGS, PIECE, HEAD_DIM)
            pl.when(head > 0)(lambda: batch_left(head - 1, offset))
            for turn in range(SEGS):
                column = wrapped(me + turn)
                remote(
                    chosen.at[head, offset - 1, column], blocks.at[head, offset, me],
                    p3_send.at[odd(head), offset - 1], p3_recv.at[head],
                    (level + offset, column),
                ).start()

    pl.semaphore_wait(ready, LEVELS - 1)

    @pl.loop(0, KV_HEADS)
    def _(head):
        blocks[head, 0] = kv_stage[head]

        @pl.when(odd(level) == 0)
        def _():
            blocks[head, level + 1] = jnp.zeros((SEGS, PIECE, HEAD_DIM), BF16)

    def make_spread():
        @pl.loop(1, below + 1)
        def _(offset):
            lane = lax.broadcasted_iota(jnp.int32, (PIECE, TILE), 1)
            row = lax.broadcasted_iota(jnp.int32, (PIECE, TILE), 0)
            lane_column = lane >> 4
            span = pl.ds(pl.multiple_of((offset - 1) * TILE, TILE), TILE)
            target = (lane & (PIECE - 1)) - row
            for column in range(SEGS):
                target = jnp.where(
                    lane_column == column, target + anc[offset, column] * PIECE, target
                )
            for column in range(SEGS):
                spread[rows_of(column, PIECE), span] = jnp.where(
                    target == column * PIECE, 1.0, 0.0
                ).astype(BF16)

    halves = [pl.ds(part * PIECES_PER_PART, PIECES_PER_PART) for part in range(2)]

    def query_copy(head):
        span = lanes(head, GROUP)
        return pltpu.make_async_copy(
            q_out.at[:, span], grad_queries.at[0, 0, :, span], q_out_sem.at[head]
        )

    def kv_copy(head):
        return pltpu.make_async_copy(
            kv_out.at[:, :, lanes(head)], grad_kv.at[0, 0, :, :, lanes(head)], kv_out_sem.at[head]
        )

    def attend(head, pairs):
        span_all = [pl.ds(group * ROWS, ROWS) for group in range(GROUP)]

        def block_pair(pair, part):
            return blocks[head, 2 * pair:2 * pair + 2, halves[part]].reshape(PAIR, HEAD_DIM)

        for index in range(2):
            for group, span in enumerate(span_all):
                tile = (q_in, g_in)[index][0, 0, :, lanes(head * GROUP + group)]
                stacks[index, span, :] = tile
                turned[index, :, span] = tile.T
        u_row = lax.broadcasted_iota(jnp.int32, (ROWS, ROWS), 0)
        t_row = lax.broadcasted_iota(jnp.int32, (ROWS, ROWS), 1)
        last_seen = odd(level) == 1
        best = [jnp.full((8, ROWS), NEG_FILL, F32) for group in range(GROUP)]
        for pair in range(pairs):
            raw = jnp.dot(block_pair(pair, 0), turned[0], preferred_element_type=F32)
            for group, span in enumerate(span_all):
                first = raw[0:ROWS, group * ROWS:(group + 1) * ROWS]
                second = raw[ROWS:PAIR, group * ROWS:(group + 1) * ROWS]
                if pair == 0:
                    first = jnp.where(u_row <= t_row, first, NEG_FILL)
                if pair == pairs - 1:
                    second = jnp.where(last_seen, second, NEG_FILL)
                logits[pair * PAIR:pair * PAIR + ROWS, span] = first
                logits[pair * PAIR + ROWS:(pair + 1) * PAIR, span] = second
                best[group] = jnp.maximum(
                    best[group], jnp.maximum(fold(first).max(0), fold(second).max(0))
                )
        top = [value.max(0, keepdims=True) for value in best]
        total = [jnp.zeros((8, ROWS), F32) for group in range(GROUP)]
        delta = [jnp.zeros((8, ROWS), F32) for group in range(GROUP)]
        for pair in range(pairs):
            rows = slice(pair * PAIR, (pair + 1) * PAIR)
            raw = jnp.dot(block_pair(pair, 1), turned[1], preferred_element_type=F32)
            for group, span in enumerate(span_all):
                tile = jnp.exp2((logits[rows, span] - top[group]) * EXP2_SCALE)
                part = raw[:, group * ROWS:(group + 1) * ROWS]
                logits[rows, span] = tile
                grad_probs[rows, span] = part
                total[group] += fold(tile).sum(0)
                delta[group] += fold(tile * part).sum(0)
        inverse = [1.0 / value.sum(0, keepdims=True) for value in total]
        delta = [value.sum(0, keepdims=True) * by for value, by in zip(delta, inverse)]
        for pair in range(pairs):
            rows = slice(pair * PAIR, (pair + 1) * PAIR)
            for group, span in enumerate(span_all):
                exact = logits[rows, span] * inverse[group]
                probs[rows, span] = exact.astype(BF16)
                grad_logits[rows, span] = (
                    exact * (grad_probs[rows, span] - delta[group])
                ).astype(BF16)
            value_term = jnp.dot(probs[rows, :], stacks[1], preferred_element_type=F32)
            key_term = SCALE * jnp.dot(
                grad_logits[rows, :], stacks[0], preferred_element_type=F32
            )
            for part, term in enumerate((key_term, value_term)):
                terms[head, 2 * pair:2 * pair + 2, halves[part]] = term.astype(BF16).reshape(
                    2, PIECES_PER_PART, PIECE, HEAD_DIM
                )
                if pair == 0:
                    own[head, part] = term[0:ROWS]
            moved = lax.dot_general(
                block_pair(pair, 0), grad_logits[rows, :], (((0,), (0,)), ((), ())),
                preferred_element_type=F32,
            )
            if pair == 0:
                query_sum[...] = moved
            else:
                query_sum[...] += moved
        for group, span in enumerate(span_all):
            q_out[:, lanes(head * GROUP + group)] = (SCALE * query_sum[:, span].T).astype(BF16)
        query_copy(head).start()

    def terms_left(head, offset):
        wait_bytes(terms.at[head, offset], b1_send.at[odd(head), offset - 1])

    def send_terms(head):
        targets = []
        for turn in range(OWNERS):
            owner = my_owner + turn
            owner = jnp.where(owner >= OWNERS, owner - OWNERS, owner)
            targets.append((owner, owner_column(owner, odd(head))))

        @pl.loop(1, level + 1)
        def _(offset):
            pl.when(head > 0)(lambda: terms_left(head - 1, offset))
            for owner, column in targets:
                remote(
                    terms.at[head, offset, pl.ds(2 * owner, 2)],
                    term_pieces.at[half(head), offset - 1, me],
                    b1_send.at[odd(head), offset - 1], b1_recv.at[half(head), offset - 1],
                    (level - offset, column),
                ).start()

    def sum_and_return(head):
        slot = half(head)

        @pl.when((level < LEVELS - 1) & (odd(head) == my_parity))
        def _():
            total[...] = jnp.zeros((TILE, 2 * HEAD_DIM), F32)

            @pl.loop(1, below + 1)
            def _(offset):
                wait_bytes(term_pieces.at[slot, offset - 1], b1_recv.at[slot, offset - 1])
                total[...] += jnp.dot(
                    spread[:, pl.ds(pl.multiple_of((offset - 1) * TILE, TILE), TILE)],
                    jnp.concatenate(
                        [
                            term_pieces[slot, offset - 1, :, index].reshape(TILE, HEAD_DIM)
                            for index in range(2)
                        ],
                        axis=1,
                    ),
                    preferred_element_type=F32,
                )

            for index in range(2):
                final_out[slot, :, index] = total[
                    :, index * HEAD_DIM:(index + 1) * HEAD_DIM
                ].astype(BF16).reshape(SEGS, PIECE, HEAD_DIM)
            landing = final_in.at[head, pl.ds(2 * my_owner, 2)]
            for turn in range(1, SEGS):
                peer = wrapped(me + turn)
                remote(
                    final_out.at[slot, peer], landing,
                    f_send.at[slot], f_recv.at[head], (level, peer),
                ).start()
            pltpu.make_async_copy(final_out.at[slot, me], landing, f_recv.at[head]).start()

    def store(head):
        @pl.when(level < LEVELS - 1)
        def _():
            wait_bytes(final_in.at[head], f_recv.at[head])
            for part in range(2):
                own[head, part] += final_in[head, halves[part]].reshape(
                    ROWS, HEAD_DIM
                ).astype(F32)

        kv_out[:, :, lanes(head)] = own[head].astype(BF16)
        kv_copy(head).start()

    @pl.loop(0, KV_HEADS + 4)
    def _(tick):
        @pl.when(tick < KV_HEADS)
        def _():
            pick_and_send(tick)

        @pl.when(tick == 0)
        def _():
            make_spread()
            load_q.wait()
            load_g.wait()

        @pl.when((tick >= 3) & (tick < KV_HEADS + 3))
        def _():
            sum_and_return(tick - 3)

        @pl.when(tick >= 4)
        def _():
            store(tick - 4)

        @pl.when((tick >= 1) & (tick < KV_HEADS + 1))
        def _():
            head = tick - 1
            per_count(
                level,
                lambda count: wait_bytes(blocks.at[head, pl.ds(1, count)], p3_recv.at[head]),
            )
            for pairs in range(1, LEVELS // 2 + 1):
                pl.when(half(level) == pairs - 1)(functools.partial(attend, head, pairs))
            send_terms(head)

    @pl.loop(0, KV_HEADS)
    def _(head):
        wait_bytes(pieces.at[head, pl.ds(1, SEGS - 1)], p1_send.at[head])
        query_copy(head).wait()
        kv_copy(head).wait()

    @pl.loop(1, below + 1)
    def _(offset):
        batch_left(KV_HEADS - 1, offset)

    @pl.loop(1, level + 1)
    def _(offset):
        terms_left(KV_HEADS - 1, offset)

    @pl.when(level < LEVELS - 1)
    def _():
        for slot in range(2):
            wait_bytes(final_out.at[slot, pl.ds(1, SEGS - 1)], f_send.at[slot])


def shards(queries, keys_values, grad_out, parents):
    smem = pl.BlockSpec(memory_space=pltpu.SMEM)
    hbm = pl.BlockSpec(memory_space=pltpu.HBM)
    dma = pltpu.SemaphoreType.DMA
    tile = (SEGS, PIECE, HEAD_DIM)
    keys_count = LEVELS * ROWS
    scratch = [
        pltpu.SMEM((LEVELS, SEGS), jnp.int32),
        pltpu.VMEM((LEVELS - 1, TILE, TILE), BF16),
        pltpu.VMEM((TILE, (LEVELS - 1) * TILE), BF16),
        pltpu.VMEM(keys_values.shape, BF16),
        pltpu.VMEM(queries.shape, BF16),
        pltpu.VMEM(queries.shape, BF16),
        pltpu.VMEM((KV_HEADS,) + tile, BF16),
        pltpu.VMEM((KV_HEADS,) + tile, BF16),
        pltpu.VMEM((KV_HEADS, LEVELS - 1) + tile, BF16),
        pltpu.VMEM((KV_HEADS, LEVELS) + tile, BF16),
        pltpu.VMEM((KV_HEADS, LEVELS) + tile, BF16),
        pltpu.VMEM((2, LEVELS - 1, SEGS, 2, PIECE, HEAD_DIM), BF16),
        pltpu.VMEM((KV_HEADS, 2, ROWS, HEAD_DIM), F32),
        pltpu.VMEM((2, STACK, HEAD_DIM), BF16),
        pltpu.VMEM((2, HEAD_DIM, STACK), BF16),
        pltpu.VMEM((HEAD_DIM, STACK), F32),
        pltpu.VMEM((keys_count, STACK), F32),
        pltpu.VMEM((keys_count, STACK), F32),
        pltpu.VMEM((keys_count, STACK), BF16),
        pltpu.VMEM((keys_count, STACK), BF16),
        pltpu.VMEM((TILE, 2 * HEAD_DIM), F32),
        pltpu.VMEM((2, SEGS, 2, PIECE, HEAD_DIM), BF16),
        pltpu.VMEM((KV_HEADS,) + tile, BF16),
        pltpu.VMEM((ROWS, HEADS * HEAD_DIM), BF16),
        pltpu.VMEM((2, ROWS, KV_HEADS * HEAD_DIM), BF16),
        dma, dma, dma,
        pltpu.SemaphoreType.REGULAR,
        dma((KV_HEADS,)), dma((KV_HEADS,)),
        dma((2, LEVELS - 1)), dma((KV_HEADS,)),
        dma((2, LEVELS - 1)), dma((2, LEVELS - 1)),
        dma((2,)), dma((KV_HEADS,)),
        dma((KV_HEADS,)), dma((KV_HEADS,)),
    ]
    return pl.pallas_call(
        kernel,
        out_shape=(
            jax.ShapeDtypeStruct(queries.shape, BF16),
            jax.ShapeDtypeStruct(keys_values.shape, BF16),
        ),
        in_specs=[smem, hbm, hbm, hbm],
        out_specs=(hbm, hbm),
        scratch_shapes=scratch,
        compiler_params=pltpu.CompilerParams(
            collective_id=0, has_side_effects=True, vmem_limit_bytes=56 * 1024 * 1024
        ),
        cost_estimate=pl.CostEstimate(
            flops=5 * 2 * HEADS * LEVELS * ROWS * ROWS * HEAD_DIM,
            bytes_accessed=8 * 1024 * 1024,
            transcendentals=HEADS * LEVELS * ROWS * ROWS,
        ),
    )(parents.transpose(0, 2, 1), queries, keys_values, grad_out)


def solution(mesh):
    in_specs = (
        P("depth", "seg", None, None),
        P("depth", "seg", None, None, None),
        P("depth", "seg", None, None),
        P(),
    )
    out_specs = (P("depth", "seg", None, None), P("depth", "seg", None, None, None))
    return jax.shard_map(shards, mesh=mesh, in_specs=in_specs, out_specs=out_specs, check_vma=False)
```

```python
import functools

import jax
import jax.numpy as jnp
from jax import lax
from jax.experimental import pallas as pl
from jax.experimental.pallas import tpu as pltpu
from jax.sharding import PartitionSpec as P

HEADS = 20
KV_HEADS = 4
HEAD_DIM = 128
GROUP = HEADS // KV_HEADS
ROWS = 128
LEVELS = 8
SEGS = 16
PIECE = 16
PIECES_PER_PART = ROWS // PIECE
STACK = GROUP * ROWS
PAIR = 2 * ROWS
TILE = SEGS * PIECE
OWNERS = SEGS // 2

NEG_FILL = -1e30
SCALE = HEAD_DIM ** -0.5
EXP2_SCALE = SCALE * 1.4426950408889634
MESH = pl.DeviceIdType.MESH
BF16 = jnp.bfloat16
F32 = jnp.float32


def half(value):
    return lax.div(value, 2)


def odd(value):
    return lax.rem(value, 2)


def wrapped(index):
    return jnp.where(index >= SEGS, index - SEGS, index)


def lanes(index, count=1):
    width = count * HEAD_DIM
    return pl.ds(pl.multiple_of(index * width, width), width)


def rows_of(index, count):
    return pl.ds(pl.multiple_of(index * count, count), count)


def owner_column(owner, parity):
    z = half(owner)
    return 4 * z + 2 * odd(owner) + odd(z + parity)


def fold(tile):
    return tile.reshape(tile.shape[0] // 8, 8, tile.shape[1])


def kernel(
    parents, queries, keys_values, grad_out, grad_queries, grad_kv,
    anc, pick, spread, kv_in, q_in, g_in, kv_stage, pieces, chosen, blocks,
    terms, term_pieces, own, stacks, turned, query_sum, logits, grad_probs,
    probs, grad_logits, total, final_out, final_in, q_out, kv_out,
    kv_sem, q_sem, g_sem, ready, p1_send, p1_recv, p3_send, p3_recv, b1_send, b1_recv,
    f_send, f_recv, q_out_sem, kv_out_sem,
):
    level = lax.axis_index("depth")
    me = lax.axis_index("seg")
    below = LEVELS - 1 - level
    my_z, my_x = lax.div(me, 4), lax.rem(me, 4)
    my_parity = odd(my_z + my_x)
    my_owner = 2 * my_z + half(my_x)
    summed_level = jnp.where(my_parity == 1, LEVELS - 1 - level, level)

    def remote(src, dst, send_sem, recv_sem, device):
        return pltpu.make_async_remote_copy(
            src_ref=src, dst_ref=dst, send_sem=send_sem, recv_sem=recv_sem,
            device_id=device, device_id_type=MESH,
        )

    def wait_bytes(ref, sem):
        pltpu.make_async_copy(ref, ref, sem).wait()

    def per_count(which, action):
        for count in range(1, LEVELS):
            pl.when(which == count)(functools.partial(action, count))

    load_kv = pltpu.make_async_copy(keys_values, kv_in, kv_sem)
    load_q = pltpu.make_async_copy(queries, q_in, q_sem)
    load_g = pltpu.make_async_copy(grad_out, g_in, g_sem)
    load_kv.start()
    load_q.start()
    load_g.start()

    barrier = pltpu.get_barrier_semaphore()

    def in_line(step):
        other = level + step
        return (jnp.where(other >= LEVELS, other - LEVELS, other), me)

    @pl.loop(1, SEGS)
    def _(step):
        pl.semaphore_signal(
            barrier, inc=1, device_id=(level, wrapped(me + step)), device_id_type=MESH
        )

    @pl.loop(1, LEVELS)
    def _(step):
        pl.semaphore_signal(barrier, inc=1, device_id=in_line(step), device_id_type=MESH)

    for index, base in enumerate((level, summed_level)):
        @pl.loop(0, SEGS)
        def _(column):
            anc[index, 0, column] = column

        @pl.loop(1, LEVELS - base)
        def _(offset):
            @pl.loop(0, SEGS)
            def _(column):
                anc[index, offset, column] = anc[
                    index, offset - 1, parents[base + offset - 1, 0, column]
                ]

    load_kv.wait()
    for head in range(KV_HEADS):
        for part in range(2):
            kv_stage[head, pl.ds(part * PIECES_PER_PART, PIECES_PER_PART)] = kv_in[
                0, 0, part, :, head * HEAD_DIM:(head + 1) * HEAD_DIM
            ].reshape(PIECES_PER_PART, PIECE, HEAD_DIM)
    pl.semaphore_wait(barrier, SEGS - 1 + LEVELS - 1)

    def spread_out(head):
        for turn in range(1, SEGS):
            peer = wrapped(me + turn)
            remote(
                kv_stage.at[head, peer], pieces.at[head, me],
                p1_send.at[head], p1_recv.at[head], (level, peer),
            ).start()
        pltpu.make_async_copy(
            kv_stage.at[head, me], pieces.at[head, me], p1_recv.at[head]
        ).start()

    spread_out(0)

    @pl.loop(1, LEVELS)
    def _(step):
        pl.semaphore_signal(ready, inc=1, device_id=in_line(step), device_id_type=MESH)

    @pl.loop(1, below + 1)
    def _(offset):
        lane = lax.broadcasted_iota(jnp.int32, (PIECE, TILE), 1)
        row = lax.broadcasted_iota(jnp.int32, (PIECE, TILE), 0)
        ahead = lane - row
        for column in range(SEGS):
            pick[offset - 1, rows_of(column, PIECE), :] = jnp.where(
                ahead == anc[0, offset, column] * PIECE, 1.0, 0.0
            ).astype(BF16)

    def batch_left(head, offset):
        wait_bytes(chosen.at[head, offset - 1], p3_send.at[odd(head), offset - 1])

    def pick_and_send(head):
        wait_bytes(pieces.at[head], p1_recv.at[head])
        pl.when(head < KV_HEADS - 1)(lambda: spread_out(head + 1))

        @pl.loop(1, below + 1)
        def _(step):
            offset = jnp.where(head == 0, below + 1 - step, step)
            found = jnp.dot(
                pick[offset - 1], pieces[head].reshape(TILE, HEAD_DIM),
                preferred_element_type=F32,
            )
            chosen[head, offset - 1] = found.astype(BF16).reshape(SEGS, PIECE, HEAD_DIM)
            pl.when(head > 0)(lambda: batch_left(head - 1, offset))
            for turn in range(SEGS):
                column = wrapped(me + turn)
                remote(
                    chosen.at[head, offset - 1, column], blocks.at[head, offset, me],
                    p3_send.at[odd(head), offset - 1], p3_recv.at[head],
                    (level + offset, column),
                ).start()

    pl.semaphore_wait(ready, LEVELS - 1)

    @pl.loop(0, KV_HEADS)
    def _(head):
        blocks[head, 0] = kv_stage[head]

        @pl.when(odd(level) == 0)
        def _():
            blocks[head, level + 1] = jnp.zeros((SEGS, PIECE, HEAD_DIM), BF16)

    def make_spread():
        @pl.loop(1, LEVELS - summed_level)
        def _(offset):
            lane = lax.broadcasted_iota(jnp.int32, (PIECE, TILE), 1)
            row = lax.broadcasted_iota(jnp.int32, (PIECE, TILE), 0)
            lane_column = lane >> 4
            span = pl.ds(pl.multiple_of((offset - 1) * TILE, TILE), TILE)
            target = (lane & (PIECE - 1)) - row
            for column in range(SEGS):
                target = jnp.where(
                    lane_column == column, target + anc[1, offset, column] * PIECE, target
                )
            for column in range(SEGS):
                spread[rows_of(column, PIECE), span] = jnp.where(
                    target == column * PIECE, 1.0, 0.0
                ).astype(BF16)

    halves = [pl.ds(part * PIECES_PER_PART, PIECES_PER_PART) for part in range(2)]

    def query_copy(head):
        span = lanes(head, GROUP)
        return pltpu.make_async_copy(
            q_out.at[:, span], grad_queries.at[0, 0, :, span], q_out_sem.at[head]
        )

    def kv_copy(head):
        return pltpu.make_async_copy(
            kv_out.at[:, :, lanes(head)], grad_kv.at[0, 0, :, :, lanes(head)], kv_out_sem.at[head]
        )

    def attend(head, pairs):
        span_all = [pl.ds(group * ROWS, ROWS) for group in range(GROUP)]

        def block_pair(pair, part):
            return blocks[head, 2 * pair:2 * pair + 2, halves[part]].reshape(PAIR, HEAD_DIM)

        for index in range(2):
            for group, span in enumerate(span_all):
                tile = (q_in, g_in)[index][0, 0, :, lanes(head * GROUP + group)]
                stacks[index, span, :] = tile
                turned[index, :, span] = tile.T
        u_row = lax.broadcasted_iota(jnp.int32, (ROWS, ROWS), 0)
        t_row = lax.broadcasted_iota(jnp.int32, (ROWS, ROWS), 1)
        last_seen = odd(level) == 1
        best = [jnp.full((8, ROWS), NEG_FILL, F32) for group in range(GROUP)]
        for pair in range(pairs):
            raw = jnp.dot(block_pair(pair, 0), turned[0], preferred_element_type=F32)
            for group, span in enumerate(span_all):
                first = raw[0:ROWS, group * ROWS:(group + 1) * ROWS]
                second = raw[ROWS:PAIR, group * ROWS:(group + 1) * ROWS]
                if pair == 0:
                    first = jnp.where(u_row <= t_row, first, NEG_FILL)
                if pair == pairs - 1:
                    second = jnp.where(last_seen, second, NEG_FILL)
                logits[pair * PAIR:pair * PAIR + ROWS, span] = first
                logits[pair * PAIR + ROWS:(pair + 1) * PAIR, span] = second
                best[group] = jnp.maximum(
                    best[group], jnp.maximum(fold(first).max(0), fold(second).max(0))
                )
        top = [value.max(0, keepdims=True) for value in best]
        total = [jnp.zeros((8, ROWS), F32) for group in range(GROUP)]
        delta = [jnp.zeros((8, ROWS), F32) for group in range(GROUP)]
        for pair in range(pairs):
            rows = slice(pair * PAIR, (pair + 1) * PAIR)
            raw = jnp.dot(block_pair(pair, 1), turned[1], preferred_element_type=F32)
            for group, span in enumerate(span_all):
                tile = jnp.exp2((logits[rows, span] - top[group]) * EXP2_SCALE)
                part = raw[:, group * ROWS:(group + 1) * ROWS]
                logits[rows, span] = tile
                grad_probs[rows, span] = part
                total[group] += fold(tile).sum(0)
                delta[group] += fold(tile * part).sum(0)
        inverse = [1.0 / value.sum(0, keepdims=True) for value in total]
        delta = [value.sum(0, keepdims=True) * by for value, by in zip(delta, inverse)]
        for pair in range(pairs):
            rows = slice(pair * PAIR, (pair + 1) * PAIR)
            for group, span in enumerate(span_all):
                exact = logits[rows, span] * inverse[group]
                probs[rows, span] = exact.astype(BF16)
                grad_logits[rows, span] = (
                    exact * (grad_probs[rows, span] - delta[group])
                ).astype(BF16)
            value_term = jnp.dot(probs[rows, :], stacks[1], preferred_element_type=F32)
            key_term = SCALE * jnp.dot(
                grad_logits[rows, :], stacks[0], preferred_element_type=F32
            )
            for part, term in enumerate((key_term, value_term)):
                terms[head, 2 * pair:2 * pair + 2, halves[part]] = term.astype(BF16).reshape(
                    2, PIECES_PER_PART, PIECE, HEAD_DIM
                )
                if pair == 0:
                    own[head, part] = term[0:ROWS]
            moved = lax.dot_general(
                block_pair(pair, 0), grad_logits[rows, :], (((0,), (0,)), ((), ())),
                preferred_element_type=F32,
            )
            if pair == 0:
                query_sum[...] = moved
            else:
                query_sum[...] += moved
        for group, span in enumerate(span_all):
            q_out[:, lanes(head * GROUP + group)] = (SCALE * query_sum[:, span].T).astype(BF16)
        query_copy(head).start()

    def summing_level(head, offset):
        target = level - offset
        return jnp.where(odd(head) == 1, LEVELS - 1 - target, target)

    def stays(head, offset):
        return (summing_level(head, offset) == level) & (my_parity == odd(head))

    def terms_left(head, offset):
        sem = b1_send.at[odd(head), offset - 1]
        local = stays(head, offset)
        pl.when(local)(lambda: wait_bytes(terms.at[head, offset, pl.ds(2, SEGS - 2)], sem))
        pl.when(~local)(lambda: wait_bytes(terms.at[head, offset], sem))

    def send_terms(head):
        targets = []
        for turn in range(OWNERS):
            owner = my_owner + turn
            owner = jnp.where(owner >= OWNERS, owner - OWNERS, owner)
            targets.append((owner, owner_column(owner, odd(head))))

        @pl.loop(1, level + 1)
        def _(offset):
            pl.when(head > 0)(lambda: terms_left(head - 1, offset))
            host = summing_level(head, offset)
            local = stays(head, offset)
            landing = term_pieces.at[half(head), offset - 1, me]
            arrival = b1_recv.at[half(head), offset - 1]
            for turn, (owner, column) in enumerate(targets):
                source = terms.at[head, offset, pl.ds(2 * owner, 2)]
                copy = remote(
                    source, landing, b1_send.at[odd(head), offset - 1], arrival, (host, column)
                )
                if turn > 0:
                    copy.start()
                else:
                    pl.when(~local)(copy.start)
                    pl.when(local)(pltpu.make_async_copy(source, landing, arrival).start)

    def sum_and_return(head):
        slot = half(head)

        @pl.when((summed_level < LEVELS - 1) & (odd(head) == my_parity))
        def _():
            total[...] = jnp.zeros((TILE, 2 * HEAD_DIM), F32)

            @pl.loop(1, LEVELS - summed_level)
            def _(offset):
                wait_bytes(term_pieces.at[slot, offset - 1], b1_recv.at[slot, offset - 1])
                total[...] += jnp.dot(
                    spread[:, pl.ds(pl.multiple_of((offset - 1) * TILE, TILE), TILE)],
                    jnp.concatenate(
                        [
                            term_pieces[slot, offset - 1, :, index].reshape(TILE, HEAD_DIM)
                            for index in range(2)
                        ],
                        axis=1,
                    ),
                    preferred_element_type=F32,
                )

            for index in range(2):
                final_out[slot, :, index] = total[
                    :, index * HEAD_DIM:(index + 1) * HEAD_DIM
                ].astype(BF16).reshape(SEGS, PIECE, HEAD_DIM)
            landing = final_in.at[head, pl.ds(2 * my_owner, 2)]

            def copy_to(peer):
                return remote(
                    final_out.at[slot, peer], landing,
                    f_send.at[slot], f_recv.at[head], (summed_level, peer),
                )

            for turn in range(1, SEGS):
                copy_to(wrapped(me + turn)).start()
            pl.when(my_parity == 1)(lambda: copy_to(me).start())
            pl.when(my_parity == 0)(
                lambda: pltpu.make_async_copy(
                    final_out.at[slot, me], landing, f_recv.at[head]
                ).start()
            )

    def store(head):
        @pl.when(level < LEVELS - 1)
        def _():
            wait_bytes(final_in.at[head], f_recv.at[head])
            for part in range(2):
                own[head, part] += final_in[head, halves[part]].reshape(
                    ROWS, HEAD_DIM
                ).astype(F32)

        kv_out[:, :, lanes(head)] = own[head].astype(BF16)
        kv_copy(head).start()

    @pl.loop(0, KV_HEADS + 4)
    def _(tick):
        @pl.when(tick < KV_HEADS)
        def _():
            pick_and_send(tick)

        @pl.when(tick == 0)
        def _():
            make_spread()
            load_q.wait()
            load_g.wait()

        @pl.when((tick >= 1) & (tick < KV_HEADS + 1))
        def _():
            head = tick - 1
            per_count(
                level,
                lambda count: wait_bytes(blocks.at[head, pl.ds(1, count)], p3_recv.at[head]),
            )
            for pairs in range(1, LEVELS // 2 + 1):
                pl.when(half(level) == pairs - 1)(functools.partial(attend, head, pairs))
            send_terms(head)

        @pl.when((tick >= 3) & (tick < KV_HEADS + 3))
        def _():
            sum_and_return(tick - 3)

        @pl.when(tick >= 4)
        def _():
            store(tick - 4)

    @pl.loop(0, KV_HEADS)
    def _(head):
        wait_bytes(pieces.at[head, pl.ds(1, SEGS - 1)], p1_send.at[head])
        query_copy(head).wait()
        kv_copy(head).wait()

    @pl.loop(1, below + 1)
    def _(offset):
        batch_left(KV_HEADS - 1, offset)

    @pl.loop(1, level + 1)
    def _(offset):
        terms_left(KV_HEADS - 1, offset)

    @pl.when(summed_level < LEVELS - 1)
    def _():
        for slot in range(2):
            wait_bytes(final_out.at[slot, pl.ds(1, SEGS - 1)], f_send.at[slot])
            pl.when(my_parity == 1)(
                functools.partial(wait_bytes, final_out.at[slot, 0], f_send.at[slot])
            )


def shards(queries, keys_values, grad_out, parents):
    smem = pl.BlockSpec(memory_space=pltpu.SMEM)
    hbm = pl.BlockSpec(memory_space=pltpu.HBM)
    dma = pltpu.SemaphoreType.DMA
    tile = (SEGS, PIECE, HEAD_DIM)
    keys_count = LEVELS * ROWS
    scratch = [
        pltpu.SMEM((2, LEVELS, SEGS), jnp.int32),
        pltpu.VMEM((LEVELS - 1, TILE, TILE), BF16),
        pltpu.VMEM((TILE, (LEVELS - 1) * TILE), BF16),
        pltpu.VMEM(keys_values.shape, BF16),
        pltpu.VMEM(queries.shape, BF16),
        pltpu.VMEM(queries.shape, BF16),
        pltpu.VMEM((KV_HEADS,) + tile, BF16),
        pltpu.VMEM((KV_HEADS,) + tile, BF16),
        pltpu.VMEM((KV_HEADS, LEVELS - 1) + tile, BF16),
        pltpu.VMEM((KV_HEADS, LEVELS) + tile, BF16),
        pltpu.VMEM((KV_HEADS, LEVELS) + tile, BF16),
        pltpu.VMEM((2, LEVELS - 1, SEGS, 2, PIECE, HEAD_DIM), BF16),
        pltpu.VMEM((KV_HEADS, 2, ROWS, HEAD_DIM), F32),
        pltpu.VMEM((2, STACK, HEAD_DIM), BF16),
        pltpu.VMEM((2, HEAD_DIM, STACK), BF16),
        pltpu.VMEM((HEAD_DIM, STACK), F32),
        pltpu.VMEM((keys_count, STACK), F32),
        pltpu.VMEM((keys_count, STACK), F32),
        pltpu.VMEM((keys_count, STACK), BF16),
        pltpu.VMEM((keys_count, STACK), BF16),
        pltpu.VMEM((TILE, 2 * HEAD_DIM), F32),
        pltpu.VMEM((2, SEGS, 2, PIECE, HEAD_DIM), BF16),
        pltpu.VMEM((KV_HEADS,) + tile, BF16),
        pltpu.VMEM((ROWS, HEADS * HEAD_DIM), BF16),
        pltpu.VMEM((2, ROWS, KV_HEADS * HEAD_DIM), BF16),
        dma, dma, dma,
        pltpu.SemaphoreType.REGULAR,
        dma((KV_HEADS,)), dma((KV_HEADS,)),
        dma((2, LEVELS - 1)), dma((KV_HEADS,)),
        dma((2, LEVELS - 1)), dma((2, LEVELS - 1)),
        dma((2,)), dma((KV_HEADS,)),
        dma((KV_HEADS,)), dma((KV_HEADS,)),
    ]
    return pl.pallas_call(
        kernel,
        out_shape=(
            jax.ShapeDtypeStruct(queries.shape, BF16),
            jax.ShapeDtypeStruct(keys_values.shape, BF16),
        ),
        in_specs=[smem, hbm, hbm, hbm],
        out_specs=(hbm, hbm),
        scratch_shapes=scratch,
        compiler_params=pltpu.CompilerParams(
            collective_id=0, has_side_effects=True, vmem_limit_bytes=56 * 1024 * 1024
        ),
        cost_estimate=pl.CostEstimate(
            flops=5 * 2 * HEADS * LEVELS * ROWS * ROWS * HEAD_DIM,
            bytes_accessed=8 * 1024 * 1024,
            transcendentals=HEADS * LEVELS * ROWS * ROWS,
        ),
    )(parents.transpose(0, 2, 1), queries, keys_values, grad_out)


def solution(mesh):
    in_specs = (
        P("depth", "seg", None, None),
        P("depth", "seg", None, None, None),
        P("depth", "seg", None, None),
        P(),
    )
    out_specs = (P("depth", "seg", None, None), P("depth", "seg", None, None, None))
    return jax.shard_map(shards, mesh=mesh, in_specs=in_specs, out_specs=out_specs, check_vma=False)
```

```python
import functools

import jax
import jax.numpy as jnp
from jax import lax
from jax.experimental import pallas as pl
from jax.experimental.pallas import tpu as pltpu
from jax.sharding import PartitionSpec as P

HEADS = 20
KV_HEADS = 4
HEAD_DIM = 128
GROUP = HEADS // KV_HEADS
ROWS = 128
LEVELS = 8
SEGS = 16
PIECE = 16
PIECES_PER_PART = ROWS // PIECE
STACK = GROUP * ROWS
PAIR = 2 * ROWS
TILE = SEGS * PIECE
OWNERS = SEGS // 2

NEG_FILL = -1e30
SCALE = HEAD_DIM ** -0.5
EXP2_SCALE = SCALE * 1.4426950408889634
MESH = pl.DeviceIdType.MESH
BF16 = jnp.bfloat16
F32 = jnp.float32


def half(value):
    return lax.div(value, 2)


def odd(value):
    return lax.rem(value, 2)


def wrapped(index):
    return jnp.where(index >= SEGS, index - SEGS, index)


def lanes(index, count=1):
    width = count * HEAD_DIM
    return pl.ds(pl.multiple_of(index * width, width), width)


def rows_of(index, count):
    return pl.ds(pl.multiple_of(index * count, count), count)


def owner_column(owner, parity):
    z = half(owner)
    return 4 * z + 2 * odd(owner) + odd(z + parity)


def fold(tile):
    return tile.reshape(tile.shape[0] // 8, 8, tile.shape[1])


def kernel(
    parents, queries, keys_values, grad_out, grad_queries, grad_kv,
    anc, pick, spread, kv_in, q_in, g_in, kv_stage, pieces, chosen, blocks,
    terms, term_pieces, own, stacks, turned, query_sum, logits, grad_probs,
    probs, grad_logits, total, final_out, final_in,
    kv_sem, q_sem, g_sem, ready, p1_send, p1_recv, p3_send, p3_recv, b1_send, b1_recv,
    f_send, f_recv,
):
    level = lax.axis_index("depth")
    me = lax.axis_index("seg")
    below = LEVELS - 1 - level
    my_z, my_x = lax.div(me, 4), lax.rem(me, 4)
    my_parity = odd(my_z + my_x)
    my_owner = 2 * my_z + half(my_x)

    def remote(src, dst, send_sem, recv_sem, device):
        return pltpu.make_async_remote_copy(
            src_ref=src, dst_ref=dst, send_sem=send_sem, recv_sem=recv_sem,
            device_id=device, device_id_type=MESH,
        )

    def wait_bytes(ref, sem):
        pltpu.make_async_copy(ref, ref, sem).wait()

    def per_count(which, action):
        for count in range(1, LEVELS):
            pl.when(which == count)(functools.partial(action, count))

    load_kv = pltpu.make_async_copy(keys_values, kv_in, kv_sem)
    load_q = pltpu.make_async_copy(queries, q_in, q_sem)
    load_g = pltpu.make_async_copy(grad_out, g_in, g_sem)
    load_kv.start()
    load_q.start()
    load_g.start()

    barrier = pltpu.get_barrier_semaphore()

    def in_line(step):
        other = level + step
        return (jnp.where(other >= LEVELS, other - LEVELS, other), me)

    @pl.loop(1, SEGS)
    def _(step):
        pl.semaphore_signal(
            barrier, inc=1, device_id=(level, wrapped(me + step)), device_id_type=MESH
        )

    @pl.loop(1, LEVELS)
    def _(step):
        pl.semaphore_signal(barrier, inc=1, device_id=in_line(step), device_id_type=MESH)

    @pl.loop(0, SEGS)
    def _(column):
        anc[0, column] = column

    @pl.loop(1, below + 1)
    def _(offset):
        @pl.loop(0, SEGS)
        def _(column):
            anc[offset, column] = anc[offset - 1, parents[level + offset - 1, 0, column]]

    load_kv.wait()
    for head in range(KV_HEADS):
        for part in range(2):
            kv_stage[head, pl.ds(part * PIECES_PER_PART, PIECES_PER_PART)] = kv_in[
                0, 0, part, :, head * HEAD_DIM:(head + 1) * HEAD_DIM
            ].reshape(PIECES_PER_PART, PIECE, HEAD_DIM)
    pl.semaphore_wait(barrier, SEGS - 1 + LEVELS - 1)

    def spread_out(head):
        for turn in range(1, SEGS):
            peer = wrapped(me + turn)
            remote(
                kv_stage.at[head, peer], pieces.at[head, me],
                p1_send.at[head], p1_recv.at[head], (level, peer),
            ).start()
        pltpu.make_async_copy(
            kv_stage.at[head, me], pieces.at[head, me], p1_recv.at[head]
        ).start()

    spread_out(0)

    @pl.loop(1, LEVELS)
    def _(step):
        pl.semaphore_signal(ready, inc=1, device_id=in_line(step), device_id_type=MESH)

    @pl.loop(1, below + 1)
    def _(offset):
        lane = lax.broadcasted_iota(jnp.int32, (PIECE, TILE), 1)
        row = lax.broadcasted_iota(jnp.int32, (PIECE, TILE), 0)
        ahead = lane - row
        for column in range(SEGS):
            pick[offset - 1, rows_of(column, PIECE), :] = jnp.where(
                ahead == anc[offset, column] * PIECE, 1.0, 0.0
            ).astype(BF16)

    def batch_left(head, offset):
        wait_bytes(chosen.at[head, offset - 1], p3_send.at[odd(head), offset - 1])

    def pick_and_send(head):
        wait_bytes(pieces.at[head], p1_recv.at[head])
        pl.when(head < KV_HEADS - 1)(lambda: spread_out(head + 1))

        @pl.loop(1, below + 1)
        def _(step):
            offset = jnp.where(head == 0, below + 1 - step, step)
            found = jnp.dot(
                pick[offset - 1], pieces[head].reshape(TILE, HEAD_DIM),
                preferred_element_type=F32,
            )
            chosen[head, offset - 1] = found.astype(BF16).reshape(SEGS, PIECE, HEAD_DIM)
            pl.when(head > 0)(lambda: batch_left(head - 1, offset))
            for turn in range(SEGS):
                column = wrapped(me + turn)
                remote(
                    chosen.at[head, offset - 1, column], blocks.at[head, offset, me],
                    p3_send.at[odd(head), offset - 1], p3_recv.at[head],
                    (level + offset, column),
                ).start()

    pl.semaphore_wait(ready, LEVELS - 1)

    @pl.loop(0, KV_HEADS)
    def _(head):
        blocks[head, 0] = kv_stage[head]

        @pl.when(odd(level) == 0)
        def _():
            blocks[head, level + 1] = jnp.zeros((SEGS, PIECE, HEAD_DIM), BF16)

    def make_spread():
        @pl.loop(1, below + 1)
        def _(offset):
            lane = lax.broadcasted_iota(jnp.int32, (PIECE, TILE), 1)
            row = lax.broadcasted_iota(jnp.int32, (PIECE, TILE), 0)
            lane_column = lane >> 4
            span = pl.ds(pl.multiple_of((offset - 1) * TILE, TILE), TILE)
            target = (lane & (PIECE - 1)) - row
            for column in range(SEGS):
                target = jnp.where(
                    lane_column == column, target + anc[offset, column] * PIECE, target
                )
            for column in range(SEGS):
                spread[rows_of(column, PIECE), span] = jnp.where(
                    target == column * PIECE, 1.0, 0.0
                ).astype(BF16)

    halves = [pl.ds(part * PIECES_PER_PART, PIECES_PER_PART) for part in range(2)]

    def attend(head, pairs):
        span_all = [pl.ds(group * ROWS, ROWS) for group in range(GROUP)]

        def block_pair(pair, part):
            return blocks[head, 2 * pair:2 * pair + 2, halves[part]].reshape(PAIR, HEAD_DIM)

        for index in range(2):
            for group, span in enumerate(span_all):
                tile = (q_in, g_in)[index][0, 0, :, lanes(head * GROUP + group)]
                stacks[index, span, :] = tile
                turned[index, :, span] = tile.T
        u_row = lax.broadcasted_iota(jnp.int32, (ROWS, ROWS), 0)
        t_row = lax.broadcasted_iota(jnp.int32, (ROWS, ROWS), 1)
        last_seen = odd(level) == 1
        best = [jnp.full((8, ROWS), NEG_FILL, F32) for group in range(GROUP)]
        for pair in range(pairs):
            raw = jnp.dot(block_pair(pair, 0), turned[0], preferred_element_type=F32)
            for group, span in enumerate(span_all):
                first = raw[0:ROWS, group * ROWS:(group + 1) * ROWS]
                second = raw[ROWS:PAIR, group * ROWS:(group + 1) * ROWS]
                if pair == 0:
                    first = jnp.where(u_row <= t_row, first, NEG_FILL)
                if pair == pairs - 1:
                    second = jnp.where(last_seen, second, NEG_FILL)
                logits[pair * PAIR:pair * PAIR + ROWS, span] = first
                logits[pair * PAIR + ROWS:(pair + 1) * PAIR, span] = second
                best[group] = jnp.maximum(
                    best[group], jnp.maximum(fold(first).max(0), fold(second).max(0))
                )
        top = [value.max(0, keepdims=True) for value in best]
        total = [jnp.zeros((8, ROWS), F32) for group in range(GROUP)]
        delta = [jnp.zeros((8, ROWS), F32) for group in range(GROUP)]
        for pair in range(pairs):
            rows = slice(pair * PAIR, (pair + 1) * PAIR)
            raw = jnp.dot(block_pair(pair, 1), turned[1], preferred_element_type=F32)
            for group, span in enumerate(span_all):
                tile = jnp.exp2((logits[rows, span] - top[group]) * EXP2_SCALE)
                part = raw[:, group * ROWS:(group + 1) * ROWS]
                logits[rows, span] = tile
                grad_probs[rows, span] = part
                total[group] += fold(tile).sum(0)
                delta[group] += fold(tile * part).sum(0)
        inverse = [1.0 / value.sum(0, keepdims=True) for value in total]
        delta = [value.sum(0, keepdims=True) * by for value, by in zip(delta, inverse)]
        for pair in range(pairs):
            rows = slice(pair * PAIR, (pair + 1) * PAIR)
            for group, span in enumerate(span_all):
                exact = logits[rows, span] * inverse[group]
                probs[rows, span] = exact.astype(BF16)
                grad_logits[rows, span] = (
                    exact * (grad_probs[rows, span] - delta[group])
                ).astype(BF16)
            value_term = jnp.dot(probs[rows, :], stacks[1], preferred_element_type=F32)
            key_term = SCALE * jnp.dot(
                grad_logits[rows, :], stacks[0], preferred_element_type=F32
            )
            for part, term in enumerate((key_term, value_term)):
                terms[head, 2 * pair:2 * pair + 2, halves[part]] = term.astype(BF16).reshape(
                    2, PIECES_PER_PART, PIECE, HEAD_DIM
                )
                if pair == 0:
                    own[head, part] = term[0:ROWS]
            moved = lax.dot_general(
                block_pair(pair, 0), grad_logits[rows, :], (((0,), (0,)), ((), ())),
                preferred_element_type=F32,
            )
            if pair == 0:
                query_sum[...] = moved
            else:
                query_sum[...] += moved
        for group, span in enumerate(span_all):
            grad_queries[0, 0, :, lanes(head * GROUP + group)] = (
                SCALE * query_sum[:, span].T
            ).astype(BF16)

    def terms_left(head, offset):
        wait_bytes(terms.at[head, offset], b1_send.at[odd(head), offset - 1])

    def send_terms(head):
        targets = []
        for turn in range(OWNERS):
            owner = my_owner + turn
            owner = jnp.where(owner >= OWNERS, owner - OWNERS, owner)
            targets.append((owner, owner_column(owner, odd(head))))

        @pl.loop(1, level + 1)
        def _(offset):
            pl.when(head > 0)(lambda: terms_left(head - 1, offset))
            for owner, column in targets:
                remote(
                    terms.at[head, offset, pl.ds(2 * owner, 2)],
                    term_pieces.at[half(head), offset - 1, me],
                    b1_send.at[odd(head), offset - 1], b1_recv.at[half(head), offset - 1],
                    (level - offset, column),
                ).start()

    def sum_and_return(head):
        slot = half(head)

        @pl.when((level < LEVELS - 1) & (odd(head) == my_parity))
        def _():
            total[...] = jnp.zeros((TILE, 2 * HEAD_DIM), F32)

            @pl.loop(1, below + 1)
            def _(offset):
                wait_bytes(term_pieces.at[slot, offset - 1], b1_recv.at[slot, offset - 1])
                total[...] += jnp.dot(
                    spread[:, pl.ds(pl.multiple_of((offset - 1) * TILE, TILE), TILE)],
                    jnp.concatenate(
                        [
                            term_pieces[slot, offset - 1, :, index].reshape(TILE, HEAD_DIM)
                            for index in range(2)
                        ],
                        axis=1,
                    ),
                    preferred_element_type=F32,
                )

            for index in range(2):
                final_out[slot, :, index] = total[
                    :, index * HEAD_DIM:(index + 1) * HEAD_DIM
                ].astype(BF16).reshape(SEGS, PIECE, HEAD_DIM)
            landing = final_in.at[head, pl.ds(2 * my_owner, 2)]
            for turn in range(1, SEGS):
                peer = wrapped(me + turn)
                remote(
                    final_out.at[slot, peer], landing,
                    f_send.at[slot], f_recv.at[head], (level, peer),
                ).start()
            pltpu.make_async_copy(final_out.at[slot, me], landing, f_recv.at[head]).start()

    def store(head):
        @pl.when(level < LEVELS - 1)
        def _():
            wait_bytes(final_in.at[head], f_recv.at[head])
            for part in range(2):
                own[head, part] += final_in[head, halves[part]].reshape(
                    ROWS, HEAD_DIM
                ).astype(F32)

        grad_kv[0, 0, :, :, lanes(head)] = own[head].astype(BF16)

    @pl.loop(0, KV_HEADS + 4)
    def _(tick):
        @pl.when(tick < KV_HEADS)
        def _():
            pick_and_send(tick)

        @pl.when(tick == 0)
        def _():
            make_spread()
            load_q.wait()
            load_g.wait()

        @pl.when((tick >= 3) & (tick < KV_HEADS + 3))
        def _():
            sum_and_return(tick - 3)

        @pl.when(tick >= 4)
        def _():
            store(tick - 4)

        @pl.when((tick >= 1) & (tick < KV_HEADS + 1))
        def _():
            head = tick - 1
            per_count(
                level,
                lambda count: wait_bytes(blocks.at[head, pl.ds(1, count)], p3_recv.at[head]),
            )
            for pairs in range(1, LEVELS // 2 + 1):
                pl.when(half(level) == pairs - 1)(functools.partial(attend, head, pairs))
            send_terms(head)

    @pl.loop(0, KV_HEADS)
    def _(head):
        wait_bytes(pieces.at[head, pl.ds(1, SEGS - 1)], p1_send.at[head])

    @pl.loop(1, below + 1)
    def _(offset):
        batch_left(KV_HEADS - 1, offset)

    @pl.loop(1, level + 1)
    def _(offset):
        terms_left(KV_HEADS - 1, offset)

    @pl.when(level < LEVELS - 1)
    def _():
        for slot in range(2):
            wait_bytes(final_out.at[slot, pl.ds(1, SEGS - 1)], f_send.at[slot])


def shards(queries, keys_values, grad_out, parents):
    smem = pl.BlockSpec(memory_space=pltpu.SMEM)
    vmem = pl.BlockSpec(memory_space=pltpu.VMEM)
    hbm = pl.BlockSpec(memory_space=pltpu.HBM)
    dma = pltpu.SemaphoreType.DMA
    tile = (SEGS, PIECE, HEAD_DIM)
    keys_count = LEVELS * ROWS
    scratch = [
        pltpu.SMEM((LEVELS, SEGS), jnp.int32),
        pltpu.VMEM((LEVELS - 1, TILE, TILE), BF16),
        pltpu.VMEM((TILE, (LEVELS - 1) * TILE), BF16),
        pltpu.VMEM(keys_values.shape, BF16),
        pltpu.VMEM(queries.shape, BF16),
        pltpu.VMEM(queries.shape, BF16),
        pltpu.VMEM((KV_HEADS,) + tile, BF16),
        pltpu.VMEM((KV_HEADS,) + tile, BF16),
        pltpu.VMEM((KV_HEADS, LEVELS - 1) + tile, BF16),
        pltpu.VMEM((KV_HEADS, LEVELS) + tile, BF16),
        pltpu.VMEM((KV_HEADS, LEVELS) + tile, BF16),
        pltpu.VMEM((2, LEVELS - 1, SEGS, 2, PIECE, HEAD_DIM), BF16),
        pltpu.VMEM((KV_HEADS, 2, ROWS, HEAD_DIM), F32),
        pltpu.VMEM((2, STACK, HEAD_DIM), BF16),
        pltpu.VMEM((2, HEAD_DIM, STACK), BF16),
        pltpu.VMEM((HEAD_DIM, STACK), F32),
        pltpu.VMEM((keys_count, STACK), F32),
        pltpu.VMEM((keys_count, STACK), F32),
        pltpu.VMEM((keys_count, STACK), BF16),
        pltpu.VMEM((keys_count, STACK), BF16),
        pltpu.VMEM((TILE, 2 * HEAD_DIM), F32),
        pltpu.VMEM((2, SEGS, 2, PIECE, HEAD_DIM), BF16),
        pltpu.VMEM((KV_HEADS,) + tile, BF16),
        dma, dma, dma,
        pltpu.SemaphoreType.REGULAR,
        dma((KV_HEADS,)), dma((KV_HEADS,)),
        dma((2, LEVELS - 1)), dma((KV_HEADS,)),
        dma((2, LEVELS - 1)), dma((2, LEVELS - 1)),
        dma((2,)), dma((KV_HEADS,)),
    ]
    return pl.pallas_call(
        kernel,
        out_shape=(
            jax.ShapeDtypeStruct(queries.shape, BF16),
            jax.ShapeDtypeStruct(keys_values.shape, BF16),
        ),
        in_specs=[smem, hbm, hbm, hbm],
        out_specs=(vmem, vmem),
        scratch_shapes=scratch,
        compiler_params=pltpu.CompilerParams(
            collective_id=0, has_side_effects=True, vmem_limit_bytes=105 * 512 * 1024
        ),
        cost_estimate=pl.CostEstimate(
            flops=5 * 2 * HEADS * LEVELS * ROWS * ROWS * HEAD_DIM,
            bytes_accessed=8 * 1024 * 1024,
            transcendentals=HEADS * LEVELS * ROWS * ROWS,
        ),
    )(parents.transpose(0, 2, 1), queries, keys_values, grad_out)


def solution(mesh):
    in_specs = (
        P("depth", "seg", None, None),
        P("depth", "seg", None, None, None),
        P("depth", "seg", None, None),
        P(),
    )
    out_specs = (P("depth", "seg", None, None), P("depth", "seg", None, None, None))
    return jax.shard_map(shards, mesh=mesh, in_specs=in_specs, out_specs=out_specs, check_vma=False)
```

```python
import functools

import jax
import jax.numpy as jnp
from jax import lax
from jax.experimental import pallas as pl
from jax.experimental.pallas import tpu as pltpu
from jax.sharding import PartitionSpec as P

HEADS = 20
KV_HEADS = 4
HEAD_DIM = 128
GROUP = HEADS // KV_HEADS
ROWS = 128
LEVELS = 8
SEGS = 16
PIECE = 16
PIECES_PER_PART = ROWS // PIECE
STACK = GROUP * ROWS
PAIR = 2 * ROWS
TILE = SEGS * PIECE
OWNERS = SEGS // 2

NEG_FILL = -1e30
SCALE = HEAD_DIM ** -0.5
EXP2_SCALE = SCALE * 1.4426950408889634
MESH = pl.DeviceIdType.MESH
BF16 = jnp.bfloat16
F32 = jnp.float32


def half(value):
    return lax.div(value, 2)


def odd(value):
    return lax.rem(value, 2)


def wrapped(index):
    return jnp.where(index >= SEGS, index - SEGS, index)


def lanes(index, count=1):
    width = count * HEAD_DIM
    return pl.ds(pl.multiple_of(index * width, width), width)


def rows_of(index, count):
    return pl.ds(pl.multiple_of(index * count, count), count)


def owner_column(owner, parity):
    z = half(owner)
    return 4 * z + 2 * odd(owner) + odd(z + parity)


def fold(tile):
    return tile.reshape(tile.shape[0] // 8, 8, tile.shape[1])


def kernel(
    parents, queries, keys_values, grad_out, grad_queries, grad_kv,
    anc, pick, spread, kv_in, q_in, g_in, kv_stage, pieces, chosen, blocks,
    terms, term_pieces, own, stacks, turned, query_sum, logits, grad_probs,
    probs, grad_logits, total, final_out, final_in,
    kv_sem, q_sem, g_sem, ready, p1_send, p1_recv, p3_send, p3_recv, b1_send, b1_recv,
    f_send, f_recv,
):
    level = lax.axis_index("depth")
    me = lax.axis_index("seg")
    below = LEVELS - 1 - level
    my_z, my_x = lax.div(me, 4), lax.rem(me, 4)
    my_parity = odd(my_z + my_x)
    my_owner = 2 * my_z + half(my_x)

    def remote(src, dst, send_sem, recv_sem, device):
        return pltpu.make_async_remote_copy(
            src_ref=src, dst_ref=dst, send_sem=send_sem, recv_sem=recv_sem,
            device_id=device, device_id_type=MESH,
        )

    def wait_bytes(ref, sem):
        pltpu.make_async_copy(ref, ref, sem).wait()

    def per_count(which, action):
        for count in range(1, LEVELS):
            pl.when(which == count)(functools.partial(action, count))

    load_kv = pltpu.make_async_copy(keys_values, kv_in, kv_sem)
    load_q = pltpu.make_async_copy(queries, q_in, q_sem)
    load_g = pltpu.make_async_copy(grad_out, g_in, g_sem)
    load_kv.start()
    load_q.start()
    load_g.start()

    barrier = pltpu.get_barrier_semaphore()

    def in_line(step):
        other = level + step
        return (jnp.where(other >= LEVELS, other - LEVELS, other), me)

    @pl.loop(1, SEGS)
    def _(step):
        pl.semaphore_signal(
            barrier, inc=1, device_id=(level, wrapped(me + step)), device_id_type=MESH
        )

    @pl.loop(1, LEVELS)
    def _(step):
        pl.semaphore_signal(barrier, inc=1, device_id=in_line(step), device_id_type=MESH)

    @pl.loop(0, SEGS)
    def _(column):
        anc[0, column] = column

    @pl.loop(1, below + 1)
    def _(offset):
        @pl.loop(0, SEGS)
        def _(column):
            anc[offset, column] = anc[offset - 1, parents[level + offset - 1, 0, column]]

    load_kv.wait()
    for head in range(KV_HEADS):
        for part in range(2):
            kv_stage[head, pl.ds(part * PIECES_PER_PART, PIECES_PER_PART)] = kv_in[
                0, 0, part, :, head * HEAD_DIM:(head + 1) * HEAD_DIM
            ].reshape(PIECES_PER_PART, PIECE, HEAD_DIM)
    pl.semaphore_wait(barrier, SEGS - 1 + LEVELS - 1)

    def spread_out(head):
        for turn in range(1, SEGS):
            peer = wrapped(me + turn)
            remote(
                kv_stage.at[head, peer], pieces.at[head, me],
                p1_send.at[head], p1_recv.at[head], (level, peer),
            ).start()
        pltpu.make_async_copy(
            kv_stage.at[head, me], pieces.at[head, me], p1_recv.at[head]
        ).start()

    spread_out(0)

    @pl.loop(1, LEVELS)
    def _(step):
        pl.semaphore_signal(ready, inc=1, device_id=in_line(step), device_id_type=MESH)

    @pl.loop(1, below + 1)
    def _(offset):
        lane = lax.broadcasted_iota(jnp.int32, (PIECE, TILE), 1)
        row = lax.broadcasted_iota(jnp.int32, (PIECE, TILE), 0)
        ahead = lane - row
        for column in range(SEGS):
            pick[offset - 1, rows_of(column, PIECE), :] = jnp.where(
                ahead == anc[offset, column] * PIECE, 1.0, 0.0
            ).astype(BF16)

    def batch_left(head, offset):
        wait_bytes(chosen.at[head, offset - 1], p3_send.at[odd(head), offset - 1])

    def pick_up(head):
        wait_bytes(pieces.at[head], p1_recv.at[head])
        pl.when(head < KV_HEADS - 1)(lambda: spread_out(head + 1))

        def products(count):
            found = jnp.dot(
                pick[0:count].reshape(count * TILE, TILE),
                pieces[head].reshape(TILE, HEAD_DIM), preferred_element_type=F32,
            )
            chosen[head, 0:count] = found.astype(BF16).reshape(count, SEGS, PIECE, HEAD_DIM)

        pl.when((below > 0) & (below <= 2))(lambda: products(2))
        pl.when((below > 2) & (below <= 4))(lambda: products(4))
        pl.when(below > 4)(lambda: products(LEVELS - 1))

    def send_pieces(head):
        @pl.when(head == 0)
        def _():
            wait_bytes(pieces.at[0], p1_recv.at[0])
            spread_out(1)

        @pl.loop(1, below + 1)
        def _(step):
            offset = jnp.where(head == 0, below + 1 - step, step)

            @pl.when(head == 0)
            def _():
                found = jnp.dot(
                    pick[offset - 1], pieces[0].reshape(TILE, HEAD_DIM),
                    preferred_element_type=F32,
                )
                chosen[0, offset - 1] = found.astype(BF16).reshape(SEGS, PIECE, HEAD_DIM)

            pl.when(head > 0)(lambda: batch_left(head - 1, offset))
            for turn in range(SEGS):
                column = wrapped(me + turn)
                remote(
                    chosen.at[head, offset - 1, column], blocks.at[head, offset, me],
                    p3_send.at[odd(head), offset - 1], p3_recv.at[head],
                    (level + offset, column),
                ).start()

    pl.semaphore_wait(ready, LEVELS - 1)

    @pl.loop(0, KV_HEADS)
    def _(head):
        blocks[head, 0] = kv_stage[head]

        @pl.when(odd(level) == 0)
        def _():
            blocks[head, level + 1] = jnp.zeros((SEGS, PIECE, HEAD_DIM), BF16)

    def make_spread():
        @pl.loop(1, below + 1)
        def _(offset):
            lane = lax.broadcasted_iota(jnp.int32, (PIECE, TILE), 1)
            row = lax.broadcasted_iota(jnp.int32, (PIECE, TILE), 0)
            lane_column = lane >> 4
            span = pl.ds(pl.multiple_of((offset - 1) * TILE, TILE), TILE)
            target = (lane & (PIECE - 1)) - row
            for column in range(SEGS):
                target = jnp.where(
                    lane_column == column, target + anc[offset, column] * PIECE, target
                )
            for column in range(SEGS):
                spread[rows_of(column, PIECE), span] = jnp.where(
                    target == column * PIECE, 1.0, 0.0
                ).astype(BF16)

    halves = [pl.ds(part * PIECES_PER_PART, PIECES_PER_PART) for part in range(2)]

    def attend(head, pairs):
        span_all = [pl.ds(group * ROWS, ROWS) for group in range(GROUP)]

        def block_pair(pair, part):
            return blocks[head, 2 * pair:2 * pair + 2, halves[part]].reshape(PAIR, HEAD_DIM)

        for index in range(2):
            for group, span in enumerate(span_all):
                tile = (q_in, g_in)[index][0, 0, :, lanes(head * GROUP + group)]
                stacks[index, span, :] = tile
                turned[index, :, span] = tile.T
        u_row = lax.broadcasted_iota(jnp.int32, (ROWS, ROWS), 0)
        t_row = lax.broadcasted_iota(jnp.int32, (ROWS, ROWS), 1)
        last_seen = odd(level) == 1
        best = [jnp.full((8, ROWS), NEG_FILL, F32) for group in range(GROUP)]
        for pair in range(pairs):
            raw = jnp.dot(block_pair(pair, 0), turned[0], preferred_element_type=F32)
            for group, span in enumerate(span_all):
                first = raw[0:ROWS, group * ROWS:(group + 1) * ROWS]
                second = raw[ROWS:PAIR, group * ROWS:(group + 1) * ROWS]
                if pair == 0:
                    first = jnp.where(u_row <= t_row, first, NEG_FILL)
                if pair == pairs - 1:
                    second = jnp.where(last_seen, second, NEG_FILL)
                logits[pair * PAIR:pair * PAIR + ROWS, span] = first
                logits[pair * PAIR + ROWS:(pair + 1) * PAIR, span] = second
                best[group] = jnp.maximum(
                    best[group], jnp.maximum(fold(first).max(0), fold(second).max(0))
                )
        top = [value.max(0, keepdims=True) for value in best]
        total = [jnp.zeros((8, ROWS), F32) for group in range(GROUP)]
        delta = [jnp.zeros((8, ROWS), F32) for group in range(GROUP)]
        for pair in range(pairs):
            rows = slice(pair * PAIR, (pair + 1) * PAIR)
            raw = jnp.dot(block_pair(pair, 1), turned[1], preferred_element_type=F32)
            for group, span in enumerate(span_all):
                tile = jnp.exp2((logits[rows, span] - top[group]) * EXP2_SCALE)
                part = raw[:, group * ROWS:(group + 1) * ROWS]
                logits[rows, span] = tile
                grad_probs[rows, span] = part
                total[group] += fold(tile).sum(0)
                delta[group] += fold(tile * part).sum(0)
        inverse = [1.0 / value.sum(0, keepdims=True) for value in total]
        delta = [value.sum(0, keepdims=True) * by for value, by in zip(delta, inverse)]
        for pair in range(pairs):
            rows = slice(pair * PAIR, (pair + 1) * PAIR)
            for group, span in enumerate(span_all):
                exact = logits[rows, span] * inverse[group]
                probs[rows, span] = exact.astype(BF16)
                grad_logits[rows, span] = (
                    exact * (grad_probs[rows, span] - delta[group])
                ).astype(BF16)
            value_term = jnp.dot(probs[rows, :], stacks[1], preferred_element_type=F32)
            key_term = SCALE * jnp.dot(
                grad_logits[rows, :], stacks[0], preferred_element_type=F32
            )
            for part, term in enumerate((key_term, value_term)):
                terms[head, 2 * pair:2 * pair + 2, halves[part]] = term.astype(BF16).reshape(
                    2, PIECES_PER_PART, PIECE, HEAD_DIM
                )
                if pair == 0:
                    own[head, part] = term[0:ROWS]
            moved = lax.dot_general(
                block_pair(pair, 0), grad_logits[rows, :], (((0,), (0,)), ((), ())),
                preferred_element_type=F32,
            )
            if pair == 0:
                query_sum[...] = moved
            else:
                query_sum[...] += moved
        for group, span in enumerate(span_all):
            grad_queries[0, 0, :, lanes(head * GROUP + group)] = (
                SCALE * query_sum[:, span].T
            ).astype(BF16)

    def terms_left(head, offset):
        wait_bytes(terms.at[head, offset], b1_send.at[odd(head), offset - 1])

    def send_terms(head):
        targets = []
        for turn in range(OWNERS):
            owner = my_owner + turn
            owner = jnp.where(owner >= OWNERS, owner - OWNERS, owner)
            targets.append((owner, owner_column(owner, odd(head))))

        @pl.loop(1, level + 1)
        def _(offset):
            pl.when(head > 0)(lambda: terms_left(head - 1, offset))
            for owner, column in targets:
                remote(
                    terms.at[head, offset, pl.ds(2 * owner, 2)],
                    term_pieces.at[half(head), offset - 1, me],
                    b1_send.at[odd(head), offset - 1], b1_recv.at[half(head), offset - 1],
                    (level - offset, column),
                ).start()

    def sum_and_return(head):
        slot = half(head)

        @pl.when((level < LEVELS - 1) & (odd(head) == my_parity))
        def _():
            total[...] = jnp.zeros((TILE, 2 * HEAD_DIM), F32)

            @pl.loop(1, below + 1)
            def _(offset):
                wait_bytes(term_pieces.at[slot, offset - 1], b1_recv.at[slot, offset - 1])
                total[...] += jnp.dot(
                    spread[:, pl.ds(pl.multiple_of((offset - 1) * TILE, TILE), TILE)],
                    jnp.concatenate(
                        [
                            term_pieces[slot, offset - 1, :, index].reshape(TILE, HEAD_DIM)
                            for index in range(2)
                        ],
                        axis=1,
                    ),
                    preferred_element_type=F32,
                )

            for index in range(2):
                final_out[slot, :, index] = total[
                    :, index * HEAD_DIM:(index + 1) * HEAD_DIM
                ].astype(BF16).reshape(SEGS, PIECE, HEAD_DIM)
            landing = final_in.at[head, pl.ds(2 * my_owner, 2)]
            for turn in range(1, SEGS):
                peer = wrapped(me + turn)
                remote(
                    final_out.at[slot, peer], landing,
                    f_send.at[slot], f_recv.at[head], (level, peer),
                ).start()
            pltpu.make_async_copy(final_out.at[slot, me], landing, f_recv.at[head]).start()

    def store(head):
        @pl.when(level < LEVELS - 1)
        def _():
            wait_bytes(final_in.at[head], f_recv.at[head])
            for part in range(2):
                own[head, part] += final_in[head, halves[part]].reshape(
                    ROWS, HEAD_DIM
                ).astype(F32)

        grad_kv[0, 0, :, :, lanes(head)] = own[head].astype(BF16)

    @pl.loop(0, KV_HEADS + 4)
    def _(tick):
        @pl.when(tick < KV_HEADS)
        def _():
            send_pieces(tick)

        @pl.when(tick == 0)
        def _():
            make_spread()
            load_q.wait()
            load_g.wait()

        @pl.when((tick >= 3) & (tick < KV_HEADS + 3))
        def _():
            sum_and_return(tick - 3)

        @pl.when(tick >= 4)
        def _():
            store(tick - 4)

        @pl.when((tick >= 1) & (tick < KV_HEADS + 1))
        def _():
            head = tick - 1
            per_count(
                level,
                lambda count: wait_bytes(blocks.at[head, pl.ds(1, count)], p3_recv.at[head]),
            )
            for pairs in range(1, LEVELS // 2 + 1):
                pl.when(half(level) == pairs - 1)(functools.partial(attend, head, pairs))
            send_terms(head)

        @pl.when(tick < KV_HEADS - 1)
        def _():
            pick_up(tick + 1)

    @pl.loop(0, KV_HEADS)
    def _(head):
        wait_bytes(pieces.at[head, pl.ds(1, SEGS - 1)], p1_send.at[head])

    @pl.loop(1, below + 1)
    def _(offset):
        batch_left(KV_HEADS - 1, offset)

    @pl.loop(1, level + 1)
    def _(offset):
        terms_left(KV_HEADS - 1, offset)

    @pl.when(level < LEVELS - 1)
    def _():
        for slot in range(2):
            wait_bytes(final_out.at[slot, pl.ds(1, SEGS - 1)], f_send.at[slot])


def shards(queries, keys_values, grad_out, parents):
    smem = pl.BlockSpec(memory_space=pltpu.SMEM)
    vmem = pl.BlockSpec(memory_space=pltpu.VMEM)
    hbm = pl.BlockSpec(memory_space=pltpu.HBM)
    dma = pltpu.SemaphoreType.DMA
    tile = (SEGS, PIECE, HEAD_DIM)
    keys_count = LEVELS * ROWS
    scratch = [
        pltpu.SMEM((LEVELS, SEGS), jnp.int32),
        pltpu.VMEM((LEVELS - 1, TILE, TILE), BF16),
        pltpu.VMEM((TILE, (LEVELS - 1) * TILE), BF16),
        pltpu.VMEM(keys_values.shape, BF16),
        pltpu.VMEM(queries.shape, BF16),
        pltpu.VMEM(queries.shape, BF16),
        pltpu.VMEM((KV_HEADS,) + tile, BF16),
        pltpu.VMEM((KV_HEADS,) + tile, BF16),
        pltpu.VMEM((KV_HEADS, LEVELS - 1) + tile, BF16),
        pltpu.VMEM((KV_HEADS, LEVELS) + tile, BF16),
        pltpu.VMEM((KV_HEADS, LEVELS) + tile, BF16),
        pltpu.VMEM((2, LEVELS - 1, SEGS, 2, PIECE, HEAD_DIM), BF16),
        pltpu.VMEM((KV_HEADS, 2, ROWS, HEAD_DIM), F32),
        pltpu.VMEM((2, STACK, HEAD_DIM), BF16),
        pltpu.VMEM((2, HEAD_DIM, STACK), BF16),
        pltpu.VMEM((HEAD_DIM, STACK), F32),
        pltpu.VMEM((keys_count, STACK), F32),
        pltpu.VMEM((keys_count, STACK), F32),
        pltpu.VMEM((keys_count, STACK), BF16),
        pltpu.VMEM((keys_count, STACK), BF16),
        pltpu.VMEM((TILE, 2 * HEAD_DIM), F32),
        pltpu.VMEM((2, SEGS, 2, PIECE, HEAD_DIM), BF16),
        pltpu.VMEM((KV_HEADS,) + tile, BF16),
        dma, dma, dma,
        pltpu.SemaphoreType.REGULAR,
        dma((KV_HEADS,)), dma((KV_HEADS,)),
        dma((2, LEVELS - 1)), dma((KV_HEADS,)),
        dma((2, LEVELS - 1)), dma((2, LEVELS - 1)),
        dma((2,)), dma((KV_HEADS,)),
    ]
    return pl.pallas_call(
        kernel,
        out_shape=(
            jax.ShapeDtypeStruct(queries.shape, BF16),
            jax.ShapeDtypeStruct(keys_values.shape, BF16),
        ),
        in_specs=[smem, hbm, hbm, hbm],
        out_specs=(vmem, vmem),
        scratch_shapes=scratch,
        compiler_params=pltpu.CompilerParams(
            collective_id=0, has_side_effects=True, vmem_limit_bytes=105 * 512 * 1024
        ),
        cost_estimate=pl.CostEstimate(
            flops=5 * 2 * HEADS * LEVELS * ROWS * ROWS * HEAD_DIM,
            bytes_accessed=8 * 1024 * 1024,
            transcendentals=HEADS * LEVELS * ROWS * ROWS,
        ),
    )(parents.transpose(0, 2, 1), queries, keys_values, grad_out)


def solution(mesh):
    in_specs = (
        P("depth", "seg", None, None),
        P("depth", "seg", None, None, None),
        P("depth", "seg", None, None),
        P(),
    )
    out_specs = (P("depth", "seg", None, None), P("depth", "seg", None, None, None))
    return jax.shard_map(shards, mesh=mesh, in_specs=in_specs, out_specs=out_specs, check_vma=False)
```

```python
import functools

import jax
import jax.numpy as jnp
from jax import lax
from jax.experimental import pallas as pl
from jax.experimental.pallas import tpu as pltpu
from jax.sharding import PartitionSpec as P

HEADS = 20
KV_HEADS = 4
HEAD_DIM = 128
GROUP = HEADS // KV_HEADS
ROWS = 128
LEVELS = 8
SEGS = 16
PIECE = 16
PIECES_PER_PART = ROWS // PIECE
STACK = GROUP * ROWS
PAIR = 2 * ROWS
TILE = SEGS * PIECE
OWNERS = SEGS // 2

NEG_FILL = -1e30
SCALE = HEAD_DIM ** -0.5
EXP2_SCALE = SCALE * 1.4426950408889634
MESH = pl.DeviceIdType.MESH
BF16 = jnp.bfloat16
F32 = jnp.float32


def half(value):
    return lax.div(value, 2)


def odd(value):
    return lax.rem(value, 2)


def wrapped(index):
    return jnp.where(index >= SEGS, index - SEGS, index)


def lanes(index, count=1):
    width = count * HEAD_DIM
    return pl.ds(pl.multiple_of(index * width, width), width)


def rows_of(index, count):
    return pl.ds(pl.multiple_of(index * count, count), count)


def owner_column(owner, parity):
    z = half(owner)
    return 4 * z + 2 * odd(owner) + odd(z + parity)


def fold(tile):
    return tile.reshape(tile.shape[0] // 8, 8, tile.shape[1])


def kernel(
    parents, queries, keys_values, grad_out, grad_queries, grad_kv,
    anc, pick, spread, kv_in, q_in, g_in, kv_stage, pieces, chosen, blocks,
    terms, term_pieces, own, stacks, turned, query_sum, logits, grad_probs,
    probs, grad_logits, total, final_out, final_in,
    kv_sem, q_sem, g_sem, ready, p1_send, p1_recv, p3_send, p3_recv, b1_send, b1_recv,
    f_send, f_recv,
):
    level = lax.axis_index("depth")
    me = lax.axis_index("seg")
    below = LEVELS - 1 - level
    my_z, my_x = lax.div(me, 4), lax.rem(me, 4)
    my_parity = odd(my_z + my_x)
    my_owner = 2 * my_z + half(my_x)

    def remote(src, dst, send_sem, recv_sem, device):
        return pltpu.make_async_remote_copy(
            src_ref=src, dst_ref=dst, send_sem=send_sem, recv_sem=recv_sem,
            device_id=device, device_id_type=MESH,
        )

    def wait_bytes(ref, sem):
        pltpu.make_async_copy(ref, ref, sem).wait()

    def per_count(which, action):
        for count in range(1, LEVELS):
            pl.when(which == count)(functools.partial(action, count))

    load_kv = pltpu.make_async_copy(keys_values, kv_in, kv_sem)
    load_q = pltpu.make_async_copy(queries, q_in, q_sem)
    load_g = pltpu.make_async_copy(grad_out, g_in, g_sem)
    load_kv.start()
    load_q.start()
    load_g.start()

    barrier = pltpu.get_barrier_semaphore()

    def in_line(step):
        other = level + step
        return (jnp.where(other >= LEVELS, other - LEVELS, other), me)

    @pl.loop(1, SEGS)
    def _(step):
        pl.semaphore_signal(
            barrier, inc=1, device_id=(level, wrapped(me + step)), device_id_type=MESH
        )

    @pl.loop(1, LEVELS)
    def _(step):
        pl.semaphore_signal(barrier, inc=1, device_id=in_line(step), device_id_type=MESH)

    @pl.loop(0, SEGS)
    def _(column):
        anc[0, column] = column

    @pl.loop(1, below + 1)
    def _(offset):
        @pl.loop(0, SEGS)
        def _(column):
            anc[offset, column] = anc[offset - 1, parents[level + offset - 1, 0, column]]

    load_kv.wait()
    for head in range(KV_HEADS):
        for part in range(2):
            kv_stage[head, pl.ds(part * PIECES_PER_PART, PIECES_PER_PART)] = kv_in[
                0, 0, part, :, head * HEAD_DIM:(head + 1) * HEAD_DIM
            ].reshape(PIECES_PER_PART, PIECE, HEAD_DIM)
    pl.semaphore_wait(barrier, SEGS - 1 + LEVELS - 1)

    def spread_out(head):
        for turn in range(1, SEGS):
            peer = wrapped(me + turn)
            remote(
                kv_stage.at[head, peer], pieces.at[head, me],
                p1_send.at[head], p1_recv.at[head], (level, peer),
            ).start()
        pltpu.make_async_copy(
            kv_stage.at[head, me], pieces.at[head, me], p1_recv.at[head]
        ).start()

    spread_out(0)

    @pl.loop(1, LEVELS)
    def _(step):
        pl.semaphore_signal(ready, inc=1, device_id=in_line(step), device_id_type=MESH)

    @pl.loop(1, below + 1)
    def _(offset):
        lane = lax.broadcasted_iota(jnp.int32, (PIECE, TILE), 1)
        row = lax.broadcasted_iota(jnp.int32, (PIECE, TILE), 0)
        ahead = lane - row
        for column in range(SEGS):
            pick[offset - 1, rows_of(column, PIECE), :] = jnp.where(
                ahead == anc[offset, column] * PIECE, 1.0, 0.0
            ).astype(BF16)

    def batch_left(head, offset):
        wait_bytes(chosen.at[head, offset - 1], p3_send.at[odd(head), offset - 1])

    def pick_and_send(head):
        wait_bytes(pieces.at[head], p1_recv.at[head])
        pl.when(head < KV_HEADS - 1)(lambda: spread_out(head + 1))

        @pl.loop(1, below + 1)
        def _(step):
            offset = jnp.where(head == 0, below + 1 - step, step)
            found = jnp.dot(
                pick[offset - 1], pieces[head].reshape(TILE, HEAD_DIM),
                preferred_element_type=F32,
            )
            chosen[head, offset - 1] = found.astype(BF16).reshape(SEGS, PIECE, HEAD_DIM)
            pl.when(head > 1)(lambda: batch_left(head - 2, offset))
            for turn in range(SEGS):
                column = wrapped(me + turn)
                remote(
                    chosen.at[head, offset - 1, column], blocks.at[head, offset, me],
                    p3_send.at[odd(head), offset - 1], p3_recv.at[head],
                    (level + offset, column),
                ).start()

    pl.semaphore_wait(ready, LEVELS - 1)

    @pl.loop(0, KV_HEADS)
    def _(head):
        blocks[head, 0] = kv_stage[head]

        @pl.when(odd(level) == 0)
        def _():
            blocks[head, level + 1] = jnp.zeros((SEGS, PIECE, HEAD_DIM), BF16)

    def make_spread():
        @pl.loop(1, below + 1)
        def _(offset):
            lane = lax.broadcasted_iota(jnp.int32, (PIECE, TILE), 1)
            row = lax.broadcasted_iota(jnp.int32, (PIECE, TILE), 0)
            lane_column = lane >> 4
            span = pl.ds(pl.multiple_of((offset - 1) * TILE, TILE), TILE)
            target = (lane & (PIECE - 1)) - row
            for column in range(SEGS):
                target = jnp.where(
                    lane_column == column, target + anc[offset, column] * PIECE, target
                )
            for column in range(SEGS):
                spread[rows_of(column, PIECE), span] = jnp.where(
                    target == column * PIECE, 1.0, 0.0
                ).astype(BF16)

    halves = [pl.ds(part * PIECES_PER_PART, PIECES_PER_PART) for part in range(2)]

    def attend(head, pairs):
        span_all = [pl.ds(group * ROWS, ROWS) for group in range(GROUP)]

        def block_pair(pair, part):
            return blocks[head, 2 * pair:2 * pair + 2, halves[part]].reshape(PAIR, HEAD_DIM)

        for index in range(2):
            for group, span in enumerate(span_all):
                tile = (q_in, g_in)[index][0, 0, :, lanes(head * GROUP + group)]
                stacks[index, span, :] = tile
                turned[index, :, span] = tile.T
        u_row = lax.broadcasted_iota(jnp.int32, (ROWS, ROWS), 0)
        t_row = lax.broadcasted_iota(jnp.int32, (ROWS, ROWS), 1)
        last_seen = odd(level) == 1
        best = [jnp.full((8, ROWS), NEG_FILL, F32) for group in range(GROUP)]
        for pair in range(pairs):
            raw = jnp.dot(block_pair(pair, 0), turned[0], preferred_element_type=F32)
            for group, span in enumerate(span_all):
                first = raw[0:ROWS, group * ROWS:(group + 1) * ROWS]
                second = raw[ROWS:PAIR, group * ROWS:(group + 1) * ROWS]
                if pair == 0:
                    first = jnp.where(u_row <= t_row, first, NEG_FILL)
                if pair == pairs - 1:
                    second = jnp.where(last_seen, second, NEG_FILL)
                logits[pair * PAIR:pair * PAIR + ROWS, span] = first
                logits[pair * PAIR + ROWS:(pair + 1) * PAIR, span] = second
                best[group] = jnp.maximum(
                    best[group], jnp.maximum(fold(first).max(0), fold(second).max(0))
                )
        top = [value.max(0, keepdims=True) for value in best]
        total = [jnp.zeros((8, ROWS), F32) for group in range(GROUP)]
        delta = [jnp.zeros((8, ROWS), F32) for group in range(GROUP)]
        for pair in range(pairs):
            rows = slice(pair * PAIR, (pair + 1) * PAIR)
            raw = jnp.dot(block_pair(pair, 1), turned[1], preferred_element_type=F32)
            for group, span in enumerate(span_all):
                tile = jnp.exp2((logits[rows, span] - top[group]) * EXP2_SCALE)
                part = raw[:, group * ROWS:(group + 1) * ROWS]
                logits[rows, span] = tile
                grad_probs[rows, span] = part
                total[group] += fold(tile).sum(0)
                delta[group] += fold(tile * part).sum(0)
        inverse = [1.0 / value.sum(0, keepdims=True) for value in total]
        delta = [value.sum(0, keepdims=True) * by for value, by in zip(delta, inverse)]
        for pair in range(pairs):
            rows = slice(pair * PAIR, (pair + 1) * PAIR)
            for group, span in enumerate(span_all):
                exact = logits[rows, span] * inverse[group]
                probs[rows, span] = exact.astype(BF16)
                grad_logits[rows, span] = (
                    exact * (grad_probs[rows, span] - delta[group])
                ).astype(BF16)
            value_term = jnp.dot(probs[rows, :], stacks[1], preferred_element_type=F32)
            key_term = SCALE * jnp.dot(
                grad_logits[rows, :], stacks[0], preferred_element_type=F32
            )
            for part, term in enumerate((key_term, value_term)):
                terms[head, 2 * pair:2 * pair + 2, halves[part]] = term.astype(BF16).reshape(
                    2, PIECES_PER_PART, PIECE, HEAD_DIM
                )
                if pair == 0:
                    own[head, part] = term[0:ROWS]
            moved = lax.dot_general(
                block_pair(pair, 0), grad_logits[rows, :], (((0,), (0,)), ((), ())),
                preferred_element_type=F32,
            )
            if pair == 0:
                query_sum[...] = moved
            else:
                query_sum[...] += moved
        for group, span in enumerate(span_all):
            grad_queries[0, 0, :, lanes(head * GROUP + group)] = (
                SCALE * query_sum[:, span].T
            ).astype(BF16)

    def terms_left(head, offset):
        wait_bytes(terms.at[head, offset], b1_send.at[odd(head), offset - 1])

    def send_terms(head):
        targets = []
        for turn in range(OWNERS):
            owner = my_owner + turn
            owner = jnp.where(owner >= OWNERS, owner - OWNERS, owner)
            targets.append((owner, owner_column(owner, odd(head))))

        @pl.loop(1, level + 1)
        def _(offset):
            pl.when(head > 0)(lambda: terms_left(head - 1, offset))
            for owner, column in targets:
                remote(
                    terms.at[head, offset, pl.ds(2 * owner, 2)],
                    term_pieces.at[half(head), offset - 1, me],
                    b1_send.at[odd(head), offset - 1], b1_recv.at[half(head), offset - 1],
                    (level - offset, column),
                ).start()

    def sum_and_return(head):
        slot = half(head)

        @pl.when((level < LEVELS - 1) & (odd(head) == my_parity))
        def _():
            total[...] = jnp.zeros((TILE, 2 * HEAD_DIM), F32)

            @pl.loop(1, below + 1)
            def _(offset):
                wait_bytes(term_pieces.at[slot, offset - 1], b1_recv.at[slot, offset - 1])
                total[...] += jnp.dot(
                    spread[:, pl.ds(pl.multiple_of((offset - 1) * TILE, TILE), TILE)],
                    jnp.concatenate(
                        [
                            term_pieces[slot, offset - 1, :, index].reshape(TILE, HEAD_DIM)
                            for index in range(2)
                        ],
                        axis=1,
                    ),
                    preferred_element_type=F32,
                )

            for index in range(2):
                final_out[slot, :, index] = total[
                    :, index * HEAD_DIM:(index + 1) * HEAD_DIM
                ].astype(BF16).reshape(SEGS, PIECE, HEAD_DIM)
            landing = final_in.at[head, pl.ds(2 * my_owner, 2)]
            for turn in range(1, SEGS):
                peer = wrapped(me + turn)
                remote(
                    final_out.at[slot, peer], landing,
                    f_send.at[slot], f_recv.at[head], (level, peer),
                ).start()
            pltpu.make_async_copy(final_out.at[slot, me], landing, f_recv.at[head]).start()

    def store(head):
        @pl.when(level < LEVELS - 1)
        def _():
            wait_bytes(final_in.at[head], f_recv.at[head])
            for part in range(2):
                own[head, part] += final_in[head, halves[part]].reshape(
                    ROWS, HEAD_DIM
                ).astype(F32)

        grad_kv[0, 0, :, :, lanes(head)] = own[head].astype(BF16)

    @pl.loop(0, KV_HEADS + 4)
    def _(tick):
        @pl.when(tick < KV_HEADS)
        def _():
            pick_and_send(tick)

        @pl.when(tick == 0)
        def _():
            make_spread()
            load_q.wait()
            load_g.wait()

        @pl.when((tick >= 3) & (tick < KV_HEADS + 3))
        def _():
            sum_and_return(tick - 3)

        @pl.when(tick >= 4)
        def _():
            store(tick - 4)

        @pl.when((tick >= 1) & (tick < KV_HEADS + 1))
        def _():
            head = tick - 1
            per_count(
                level,
                lambda count: wait_bytes(blocks.at[head, pl.ds(1, count)], p3_recv.at[head]),
            )
            for pairs in range(1, LEVELS // 2 + 1):
                pl.when(half(level) == pairs - 1)(functools.partial(attend, head, pairs))
            send_terms(head)

    @pl.loop(0, KV_HEADS)
    def _(head):
        wait_bytes(pieces.at[head, pl.ds(1, SEGS - 1)], p1_send.at[head])

    @pl.loop(1, below + 1)
    def _(offset):
        batch_left(KV_HEADS - 2, offset)
        batch_left(KV_HEADS - 1, offset)

    @pl.loop(1, level + 1)
    def _(offset):
        terms_left(KV_HEADS - 1, offset)

    @pl.when(level < LEVELS - 1)
    def _():
        for slot in range(2):
            wait_bytes(final_out.at[slot, pl.ds(1, SEGS - 1)], f_send.at[slot])


def shards(queries, keys_values, grad_out, parents):
    smem = pl.BlockSpec(memory_space=pltpu.SMEM)
    vmem = pl.BlockSpec(memory_space=pltpu.VMEM)
    hbm = pl.BlockSpec(memory_space=pltpu.HBM)
    dma = pltpu.SemaphoreType.DMA
    tile = (SEGS, PIECE, HEAD_DIM)
    keys_count = LEVELS * ROWS
    scratch = [
        pltpu.SMEM((LEVELS, SEGS), jnp.int32),
        pltpu.VMEM((LEVELS - 1, TILE, TILE), BF16),
        pltpu.VMEM((TILE, (LEVELS - 1) * TILE), BF16),
        pltpu.VMEM(keys_values.shape, BF16),
        pltpu.VMEM(queries.shape, BF16),
        pltpu.VMEM(queries.shape, BF16),
        pltpu.VMEM((KV_HEADS,) + tile, BF16),
        pltpu.VMEM((KV_HEADS,) + tile, BF16),
        pltpu.VMEM((KV_HEADS, LEVELS - 1) + tile, BF16),
        pltpu.VMEM((KV_HEADS, LEVELS) + tile, BF16),
        pltpu.VMEM((KV_HEADS, LEVELS) + tile, BF16),
        pltpu.VMEM((2, LEVELS - 1, SEGS, 2, PIECE, HEAD_DIM), BF16),
        pltpu.VMEM((KV_HEADS, 2, ROWS, HEAD_DIM), F32),
        pltpu.VMEM((2, STACK, HEAD_DIM), BF16),
        pltpu.VMEM((2, HEAD_DIM, STACK), BF16),
        pltpu.VMEM((HEAD_DIM, STACK), F32),
        pltpu.VMEM((keys_count, STACK), F32),
        pltpu.VMEM((keys_count, STACK), F32),
        pltpu.VMEM((keys_count, STACK), BF16),
        pltpu.VMEM((keys_count, STACK), BF16),
        pltpu.VMEM((TILE, 2 * HEAD_DIM), F32),
        pltpu.VMEM((2, SEGS, 2, PIECE, HEAD_DIM), BF16),
        pltpu.VMEM((KV_HEADS,) + tile, BF16),
        dma, dma, dma,
        pltpu.SemaphoreType.REGULAR,
        dma((KV_HEADS,)), dma((KV_HEADS,)),
        dma((2, LEVELS - 1)), dma((KV_HEADS,)),
        dma((2, LEVELS - 1)), dma((2, LEVELS - 1)),
        dma((2,)), dma((KV_HEADS,)),
    ]
    return pl.pallas_call(
        kernel,
        out_shape=(
            jax.ShapeDtypeStruct(queries.shape, BF16),
            jax.ShapeDtypeStruct(keys_values.shape, BF16),
        ),
        in_specs=[smem, hbm, hbm, hbm],
        out_specs=(vmem, vmem),
        scratch_shapes=scratch,
        compiler_params=pltpu.CompilerParams(
            collective_id=0, has_side_effects=True, vmem_limit_bytes=105 * 512 * 1024
        ),
        cost_estimate=pl.CostEstimate(
            flops=5 * 2 * HEADS * LEVELS * ROWS * ROWS * HEAD_DIM,
            bytes_accessed=8 * 1024 * 1024,
            transcendentals=HEADS * LEVELS * ROWS * ROWS,
        ),
    )(parents.transpose(0, 2, 1), queries, keys_values, grad_out)


def solution(mesh):
    in_specs = (
        P("depth", "seg", None, None),
        P("depth", "seg", None, None, None),
        P("depth", "seg", None, None),
        P(),
    )
    out_specs = (P("depth", "seg", None, None), P("depth", "seg", None, None, None))
    return jax.shard_map(shards, mesh=mesh, in_specs=in_specs, out_specs=out_specs, check_vma=False)
```

```python
import functools

import jax
import jax.numpy as jnp
from jax import lax
from jax.experimental import pallas as pl
from jax.experimental.pallas import tpu as pltpu
from jax.sharding import PartitionSpec as P

HEADS = 20
KV_HEADS = 4
HEAD_DIM = 128
GROUP = HEADS // KV_HEADS
ROWS = 128
LEVELS = 8
SEGS = 16
PIECE = 16
PIECES_PER_PART = ROWS // PIECE
STACK = GROUP * ROWS
PAIR = 2 * ROWS
TILE = SEGS * PIECE
OWNERS = SEGS // 2

NEG_FILL = -1e30
SCALE = HEAD_DIM ** -0.5
EXP2_SCALE = SCALE * 1.4426950408889634
MESH = pl.DeviceIdType.MESH
BF16 = jnp.bfloat16
F32 = jnp.float32


def half(value):
    return lax.div(value, 2)


def odd(value):
    return lax.rem(value, 2)


def wrapped(index):
    return jnp.where(index >= SEGS, index - SEGS, index)


def lanes(index, count=1):
    width = count * HEAD_DIM
    return pl.ds(pl.multiple_of(index * width, width), width)


def rows_of(index, count):
    return pl.ds(pl.multiple_of(index * count, count), count)


def fold(tile):
    return tile.reshape(tile.shape[0] // 8, 8, tile.shape[1])


def kernel(
    parents, queries, keys_values, grad_out, grad_queries, grad_kv,
    anc, pick, spread, kv_in, q_in, g_in, kv_stage, pieces, chosen, blocks,
    terms, term_pieces, own, stacks, turned, query_sum, logits, grad_probs,
    probs, grad_logits, total, final_out, final_in,
    kv_sem, q_sem, g_sem, ready, p1_send, p1_recv, p3_send, p3_recv, b1_send, b1_recv,
    f_send, f_recv,
):
    level = lax.axis_index("depth")
    me = lax.axis_index("seg")
    below = LEVELS - 1 - level
    my_z, my_x = lax.div(me, 4), lax.rem(me, 4)
    my_parity = odd(my_z + my_x)
    my_owner = 2 * my_z + half(my_x)

    def around(index):
        return jnp.where(index >= 4, index - 4, index)

    def shifted(dz, dx):
        return 4 * around(my_z + dz) + around(my_x + dx)

    def remote(src, dst, send_sem, recv_sem, device):
        return pltpu.make_async_remote_copy(
            src_ref=src, dst_ref=dst, send_sem=send_sem, recv_sem=recv_sem,
            device_id=device, device_id_type=MESH,
        )

    def wait_bytes(ref, sem):
        pltpu.make_async_copy(ref, ref, sem).wait()

    def per_count(which, action):
        for count in range(1, LEVELS):
            pl.when(which == count)(functools.partial(action, count))

    load_kv = pltpu.make_async_copy(keys_values, kv_in, kv_sem)
    load_q = pltpu.make_async_copy(queries, q_in, q_sem)
    load_g = pltpu.make_async_copy(grad_out, g_in, g_sem)
    load_kv.start()
    load_q.start()
    load_g.start()

    barrier = pltpu.get_barrier_semaphore()

    def in_line(step):
        other = level + step
        return (jnp.where(other >= LEVELS, other - LEVELS, other), me)

    @pl.loop(1, SEGS)
    def _(step):
        pl.semaphore_signal(
            barrier, inc=1, device_id=(level, wrapped(me + step)), device_id_type=MESH
        )

    @pl.loop(1, LEVELS)
    def _(step):
        pl.semaphore_signal(barrier, inc=1, device_id=in_line(step), device_id_type=MESH)

    @pl.loop(0, SEGS)
    def _(column):
        anc[0, column] = column

    @pl.loop(1, below + 1)
    def _(offset):
        @pl.loop(0, SEGS)
        def _(column):
            anc[offset, column] = anc[offset - 1, parents[level + offset - 1, 0, column]]

    load_kv.wait()
    for head in range(KV_HEADS):
        for part in range(2):
            kv_stage[head, pl.ds(part * PIECES_PER_PART, PIECES_PER_PART)] = kv_in[
                0, 0, part, :, head * HEAD_DIM:(head + 1) * HEAD_DIM
            ].reshape(PIECES_PER_PART, PIECE, HEAD_DIM)
    pl.semaphore_wait(barrier, SEGS - 1 + LEVELS - 1)

    def spread_out(head):
        for turn in range(1, SEGS):
            peer = shifted(turn // 4, turn % 4)
            remote(
                kv_stage.at[head, peer], pieces.at[head, me],
                p1_send.at[head], p1_recv.at[head], (level, peer),
            ).start()
        pltpu.make_async_copy(
            kv_stage.at[head, me], pieces.at[head, me], p1_recv.at[head]
        ).start()

    spread_out(0)

    @pl.loop(1, LEVELS)
    def _(step):
        pl.semaphore_signal(ready, inc=1, device_id=in_line(step), device_id_type=MESH)

    @pl.loop(1, below + 1)
    def _(offset):
        lane = lax.broadcasted_iota(jnp.int32, (PIECE, TILE), 1)
        row = lax.broadcasted_iota(jnp.int32, (PIECE, TILE), 0)
        ahead = lane - row
        for column in range(SEGS):
            pick[offset - 1, rows_of(column, PIECE), :] = jnp.where(
                ahead == anc[offset, column] * PIECE, 1.0, 0.0
            ).astype(BF16)

    def batch_left(head, offset):
        wait_bytes(chosen.at[head, offset - 1], p3_send.at[odd(head), offset - 1])

    def pick_and_send(head):
        wait_bytes(pieces.at[head], p1_recv.at[head])
        pl.when(head < KV_HEADS - 1)(lambda: spread_out(head + 1))

        @pl.loop(1, below + 1)
        def _(step):
            offset = jnp.where(head == 0, below + 1 - step, step)
            found = jnp.dot(
                pick[offset - 1], pieces[head].reshape(TILE, HEAD_DIM),
                preferred_element_type=F32,
            )
            chosen[head, offset - 1] = found.astype(BF16).reshape(SEGS, PIECE, HEAD_DIM)
            pl.when(head > 0)(lambda: batch_left(head - 1, offset))
            for turn in range(SEGS):
                column = shifted(turn // 4, turn % 4)
                remote(
                    chosen.at[head, offset - 1, column], blocks.at[head, offset, me],
                    p3_send.at[odd(head), offset - 1], p3_recv.at[head],
                    (level + offset, column),
                ).start()

    pl.semaphore_wait(ready, LEVELS - 1)

    @pl.loop(0, KV_HEADS)
    def _(head):
        blocks[head, 0] = kv_stage[head]

        @pl.when(odd(level) == 0)
        def _():
            blocks[head, level + 1] = jnp.zeros((SEGS, PIECE, HEAD_DIM), BF16)

    def make_spread():
        @pl.loop(1, below + 1)
        def _(offset):
            lane = lax.broadcasted_iota(jnp.int32, (PIECE, TILE), 1)
            row = lax.broadcasted_iota(jnp.int32, (PIECE, TILE), 0)
            lane_column = lane >> 4
            span = pl.ds(pl.multiple_of((offset - 1) * TILE, TILE), TILE)
            target = (lane & (PIECE - 1)) - row
            for column in range(SEGS):
                target = jnp.where(
                    lane_column == column, target + anc[offset, column] * PIECE, target
                )
            for column in range(SEGS):
                spread[rows_of(column, PIECE), span] = jnp.where(
                    target == column * PIECE, 1.0, 0.0
                ).astype(BF16)

    halves = [pl.ds(part * PIECES_PER_PART, PIECES_PER_PART) for part in range(2)]

    def attend(head, pairs):
        span_all = [pl.ds(group * ROWS, ROWS) for group in range(GROUP)]

        def block_pair(pair, part):
            return blocks[head, 2 * pair:2 * pair + 2, halves[part]].reshape(PAIR, HEAD_DIM)

        for index in range(2):
            for group, span in enumerate(span_all):
                tile = (q_in, g_in)[index][0, 0, :, lanes(head * GROUP + group)]
                stacks[index, span, :] = tile
                turned[index, :, span] = tile.T
        u_row = lax.broadcasted_iota(jnp.int32, (ROWS, ROWS), 0)
        t_row = lax.broadcasted_iota(jnp.int32, (ROWS, ROWS), 1)
        last_seen = odd(level) == 1
        best = [jnp.full((8, ROWS), NEG_FILL, F32) for group in range(GROUP)]
        for pair in range(pairs):
            raw = jnp.dot(block_pair(pair, 0), turned[0], preferred_element_type=F32)
            for group, span in enumerate(span_all):
                first = raw[0:ROWS, group * ROWS:(group + 1) * ROWS]
                second = raw[ROWS:PAIR, group * ROWS:(group + 1) * ROWS]
                if pair == 0:
                    first = jnp.where(u_row <= t_row, first, NEG_FILL)
                if pair == pairs - 1:
                    second = jnp.where(last_seen, second, NEG_FILL)
                logits[pair * PAIR:pair * PAIR + ROWS, span] = first
                logits[pair * PAIR + ROWS:(pair + 1) * PAIR, span] = second
                best[group] = jnp.maximum(
                    best[group], jnp.maximum(fold(first).max(0), fold(second).max(0))
                )
        top = [value.max(0, keepdims=True) for value in best]
        total = [jnp.zeros((8, ROWS), F32) for group in range(GROUP)]
        delta = [jnp.zeros((8, ROWS), F32) for group in range(GROUP)]
        for pair in range(pairs):
            rows = slice(pair * PAIR, (pair + 1) * PAIR)
            raw = jnp.dot(block_pair(pair, 1), turned[1], preferred_element_type=F32)
            for group, span in enumerate(span_all):
                tile = jnp.exp2((logits[rows, span] - top[group]) * EXP2_SCALE)
                part = raw[:, group * ROWS:(group + 1) * ROWS]
                logits[rows, span] = tile
                grad_probs[rows, span] = part
                total[group] += fold(tile).sum(0)
                delta[group] += fold(tile * part).sum(0)
        inverse = [1.0 / value.sum(0, keepdims=True) for value in total]
        delta = [value.sum(0, keepdims=True) * by for value, by in zip(delta, inverse)]
        for pair in range(pairs):
            rows = slice(pair * PAIR, (pair + 1) * PAIR)
            for group, span in enumerate(span_all):
                exact = logits[rows, span] * inverse[group]
                probs[rows, span] = exact.astype(BF16)
                grad_logits[rows, span] = (
                    exact * (grad_probs[rows, span] - delta[group])
                ).astype(BF16)
            value_term = jnp.dot(probs[rows, :], stacks[1], preferred_element_type=F32)
            key_term = SCALE * jnp.dot(
                grad_logits[rows, :], stacks[0], preferred_element_type=F32
            )
            for part, term in enumerate((key_term, value_term)):
                terms[head, 2 * pair:2 * pair + 2, halves[part]] = term.astype(BF16).reshape(
                    2, PIECES_PER_PART, PIECE, HEAD_DIM
                )
                if pair == 0:
                    own[head, part] = term[0:ROWS]
            moved = lax.dot_general(
                block_pair(pair, 0), grad_logits[rows, :], (((0,), (0,)), ((), ())),
                preferred_element_type=F32,
            )
            if pair == 0:
                query_sum[...] = moved
            else:
                query_sum[...] += moved
        for group, span in enumerate(span_all):
            grad_queries[0, 0, :, lanes(head * GROUP + group)] = (
                SCALE * query_sum[:, span].T
            ).astype(BF16)

    def terms_left(head, offset):
        wait_bytes(terms.at[head, offset], b1_send.at[odd(head), offset - 1])

    def send_terms(head):
        targets = []
        skew = jnp.where(my_parity == odd(head), 0, 1)
        for turn in range(OWNERS):
            z = around(my_z + turn // 2)
            x = around(my_x + (0, 2, 1, 3)[turn % 4] + skew)
            targets.append((2 * z + half(x), 4 * z + x))

        @pl.loop(1, level + 1)
        def _(offset):
            pl.when(head > 0)(lambda: terms_left(head - 1, offset))
            for owner, column in targets:
                remote(
                    terms.at[head, offset, pl.ds(2 * owner, 2)],
                    term_pieces.at[half(head), offset - 1, me],
                    b1_send.at[odd(head), offset - 1], b1_recv.at[half(head), offset - 1],
                    (level - offset, column),
                ).start()

    def sum_and_return(head):
        slot = half(head)

        @pl.when((level < LEVELS - 1) & (odd(head) == my_parity))
        def _():
            total[...] = jnp.zeros((TILE, 2 * HEAD_DIM), F32)

            @pl.loop(1, below + 1)
            def _(offset):
                wait_bytes(term_pieces.at[slot, offset - 1], b1_recv.at[slot, offset - 1])
                total[...] += jnp.dot(
                    spread[:, pl.ds(pl.multiple_of((offset - 1) * TILE, TILE), TILE)],
                    jnp.concatenate(
                        [
                            term_pieces[slot, offset - 1, :, index].reshape(TILE, HEAD_DIM)
                            for index in range(2)
                        ],
                        axis=1,
                    ),
                    preferred_element_type=F32,
                )

            for index in range(2):
                final_out[slot, :, index] = total[
                    :, index * HEAD_DIM:(index + 1) * HEAD_DIM
                ].astype(BF16).reshape(SEGS, PIECE, HEAD_DIM)
            landing = final_in.at[head, pl.ds(2 * my_owner, 2)]
            for turn in range(1, SEGS):
                peer = shifted(turn // 4, turn % 4)
                remote(
                    final_out.at[slot, peer], landing,
                    f_send.at[slot], f_recv.at[head], (level, peer),
                ).start()
            pltpu.make_async_copy(final_out.at[slot, me], landing, f_recv.at[head]).start()

    def store(head):
        @pl.when(level < LEVELS - 1)
        def _():
            wait_bytes(final_in.at[head], f_recv.at[head])
            for part in range(2):
                own[head, part] += final_in[head, halves[part]].reshape(
                    ROWS, HEAD_DIM
                ).astype(F32)

        grad_kv[0, 0, :, :, lanes(head)] = own[head].astype(BF16)

    @pl.loop(0, KV_HEADS + 4)
    def _(tick):
        @pl.when(tick < KV_HEADS)
        def _():
            pick_and_send(tick)

        @pl.when(tick == 0)
        def _():
            make_spread()
            load_q.wait()
            load_g.wait()

        @pl.when((tick >= 3) & (tick < KV_HEADS + 3))
        def _():
            sum_and_return(tick - 3)

        @pl.when(tick >= 4)
        def _():
            store(tick - 4)

        @pl.when((tick >= 1) & (tick < KV_HEADS + 1))
        def _():
            head = tick - 1
            per_count(
                level,
                lambda count: wait_bytes(blocks.at[head, pl.ds(1, count)], p3_recv.at[head]),
            )
            for pairs in range(1, LEVELS // 2 + 1):
                pl.when(half(level) == pairs - 1)(functools.partial(attend, head, pairs))
            send_terms(head)

    @pl.loop(0, KV_HEADS)
    def _(head):
        wait_bytes(pieces.at[head, pl.ds(1, SEGS - 1)], p1_send.at[head])

    @pl.loop(1, below + 1)
    def _(offset):
        batch_left(KV_HEADS - 1, offset)

    @pl.loop(1, level + 1)
    def _(offset):
        terms_left(KV_HEADS - 1, offset)

    @pl.when(level < LEVELS - 1)
    def _():
        for slot in range(2):
            wait_bytes(final_out.at[slot, pl.ds(1, SEGS - 1)], f_send.at[slot])


def shards(queries, keys_values, grad_out, parents):
    smem = pl.BlockSpec(memory_space=pltpu.SMEM)
    vmem = pl.BlockSpec(memory_space=pltpu.VMEM)
    hbm = pl.BlockSpec(memory_space=pltpu.HBM)
    dma = pltpu.SemaphoreType.DMA
    tile = (SEGS, PIECE, HEAD_DIM)
    keys_count = LEVELS * ROWS
    scratch = [
        pltpu.SMEM((LEVELS, SEGS), jnp.int32),
        pltpu.VMEM((LEVELS - 1, TILE, TILE), BF16),
        pltpu.VMEM((TILE, (LEVELS - 1) * TILE), BF16),
        pltpu.VMEM(keys_values.shape, BF16),
        pltpu.VMEM(queries.shape, BF16),
        pltpu.VMEM(queries.shape, BF16),
        pltpu.VMEM((KV_HEADS,) + tile, BF16),
        pltpu.VMEM((KV_HEADS,) + tile, BF16),
        pltpu.VMEM((KV_HEADS, LEVELS - 1) + tile, BF16),
        pltpu.VMEM((KV_HEADS, LEVELS) + tile, BF16),
        pltpu.VMEM((KV_HEADS, LEVELS) + tile, BF16),
        pltpu.VMEM((2, LEVELS - 1, SEGS, 2, PIECE, HEAD_DIM), BF16),
        pltpu.VMEM((KV_HEADS, 2, ROWS, HEAD_DIM), F32),
        pltpu.VMEM((2, STACK, HEAD_DIM), BF16),
        pltpu.VMEM((2, HEAD_DIM, STACK), BF16),
        pltpu.VMEM((HEAD_DIM, STACK), F32),
        pltpu.VMEM((keys_count, STACK), F32),
        pltpu.VMEM((keys_count, STACK), F32),
        pltpu.VMEM((keys_count, STACK), BF16),
        pltpu.VMEM((keys_count, STACK), BF16),
        pltpu.VMEM((TILE, 2 * HEAD_DIM), F32),
        pltpu.VMEM((2, SEGS, 2, PIECE, HEAD_DIM), BF16),
        pltpu.VMEM((KV_HEADS,) + tile, BF16),
        dma, dma, dma,
        pltpu.SemaphoreType.REGULAR,
        dma((KV_HEADS,)), dma((KV_HEADS,)),
        dma((2, LEVELS - 1)), dma((KV_HEADS,)),
        dma((2, LEVELS - 1)), dma((2, LEVELS - 1)),
        dma((2,)), dma((KV_HEADS,)),
    ]
    return pl.pallas_call(
        kernel,
        out_shape=(
            jax.ShapeDtypeStruct(queries.shape, BF16),
            jax.ShapeDtypeStruct(keys_values.shape, BF16),
        ),
        in_specs=[smem, hbm, hbm, hbm],
        out_specs=(vmem, vmem),
        scratch_shapes=scratch,
        compiler_params=pltpu.CompilerParams(
            collective_id=0, has_side_effects=True, vmem_limit_bytes=105 * 512 * 1024
        ),
        cost_estimate=pl.CostEstimate(
            flops=5 * 2 * HEADS * LEVELS * ROWS * ROWS * HEAD_DIM,
            bytes_accessed=8 * 1024 * 1024,
            transcendentals=HEADS * LEVELS * ROWS * ROWS,
        ),
    )(parents.transpose(0, 2, 1), queries, keys_values, grad_out)


def solution(mesh):
    in_specs = (
        P("depth", "seg", None, None),
        P("depth", "seg", None, None, None),
        P("depth", "seg", None, None),
        P(),
    )
    out_specs = (P("depth", "seg", None, None), P("depth", "seg", None, None, None))
    return jax.shard_map(shards, mesh=mesh, in_specs=in_specs, out_specs=out_specs, check_vma=False)
```

```python
import functools

import jax
import jax.numpy as jnp
from jax import lax
from jax.experimental import pallas as pl
from jax.experimental.pallas import tpu as pltpu
from jax.sharding import PartitionSpec as P

HEADS = 20
KV_HEADS = 4
HEAD_DIM = 128
GROUP = HEADS // KV_HEADS
ROWS = 128
LEVELS = 8
SEGS = 16
PIECE = 16
PIECES_PER_PART = ROWS // PIECE
STACK = GROUP * ROWS
PAIR = 2 * ROWS
TILE = SEGS * PIECE
OWNERS = SEGS // 2

NEG_FILL = -1e30
SCALE = HEAD_DIM ** -0.5
EXP2_SCALE = SCALE * 1.4426950408889634
MESH = pl.DeviceIdType.MESH
BF16 = jnp.bfloat16
F32 = jnp.float32


def half(value):
    return lax.div(value, 2)


def odd(value):
    return lax.rem(value, 2)


def wrapped(index):
    return jnp.where(index >= SEGS, index - SEGS, index)


def lanes(index, count=1):
    width = count * HEAD_DIM
    return pl.ds(pl.multiple_of(index * width, width), width)


def rows_of(index, count):
    return pl.ds(pl.multiple_of(index * count, count), count)


def fold(tile):
    return tile.reshape(tile.shape[0] // 8, 8, tile.shape[1])


def kernel(
    parents, queries, keys_values, grad_out, grad_queries, grad_kv,
    anc, pick, spread, kv_in, q_in, g_in, kv_stage, pieces, chosen, blocks,
    terms, term_pieces, own, stacks, turned, query_sum, logits, grad_probs,
    probs, grad_logits, total, final_out, final_in,
    kv_sem, q_sem, g_sem, ready, p1_send, p1_recv, p3_send, p3_recv, b1_send, b1_recv,
    f_send, f_recv,
):
    level = lax.axis_index("depth")
    me = lax.axis_index("seg")
    below = LEVELS - 1 - level
    my_z, my_x = lax.div(me, 4), lax.rem(me, 4)
    my_parity = odd(my_z + my_x)
    my_owner = 2 * my_z + half(my_x)

    def around(index):
        return jnp.where(index >= 4, index - 4, index)

    def shifted(dz, dx):
        return 4 * around(my_z + dz) + around(my_x + dx)

    def remote(src, dst, send_sem, recv_sem, device):
        return pltpu.make_async_remote_copy(
            src_ref=src, dst_ref=dst, send_sem=send_sem, recv_sem=recv_sem,
            device_id=device, device_id_type=MESH,
        )

    def wait_bytes(ref, sem):
        pltpu.make_async_copy(ref, ref, sem).wait()

    def per_count(which, action):
        for count in range(1, LEVELS):
            pl.when(which == count)(functools.partial(action, count))

    load_kv = pltpu.make_async_copy(keys_values, kv_in, kv_sem)
    load_q = pltpu.make_async_copy(queries, q_in, q_sem)
    load_g = pltpu.make_async_copy(grad_out, g_in, g_sem)
    load_kv.start()
    load_q.start()
    load_g.start()

    barrier = pltpu.get_barrier_semaphore()

    def in_line(step):
        other = level + step
        return (jnp.where(other >= LEVELS, other - LEVELS, other), me)

    @pl.loop(1, SEGS)
    def _(step):
        pl.semaphore_signal(
            barrier, inc=1, device_id=(level, wrapped(me + step)), device_id_type=MESH
        )

    @pl.loop(1, LEVELS)
    def _(step):
        pl.semaphore_signal(barrier, inc=1, device_id=in_line(step), device_id_type=MESH)

    @pl.loop(0, SEGS)
    def _(column):
        anc[0, column] = column

    @pl.loop(1, below + 1)
    def _(offset):
        @pl.loop(0, SEGS)
        def _(column):
            anc[offset, column] = anc[offset - 1, parents[level + offset - 1, 0, column]]

    load_kv.wait()
    for head in range(KV_HEADS):
        for part in range(2):
            kv_stage[head, pl.ds(part * PIECES_PER_PART, PIECES_PER_PART)] = kv_in[
                0, 0, part, :, head * HEAD_DIM:(head + 1) * HEAD_DIM
            ].reshape(PIECES_PER_PART, PIECE, HEAD_DIM)
    pl.semaphore_wait(barrier, SEGS - 1 + LEVELS - 1)

    def spread_out(head):
        for turn in range(1, SEGS):
            peer = shifted(turn // 4, turn % 4)
            remote(
                kv_stage.at[head, peer], pieces.at[head, me],
                p1_send.at[head], p1_recv.at[head], (level, peer),
            ).start()
        pltpu.make_async_copy(
            kv_stage.at[head, me], pieces.at[head, me], p1_recv.at[head]
        ).start()

    spread_out(0)

    @pl.loop(1, LEVELS)
    def _(step):
        pl.semaphore_signal(ready, inc=1, device_id=in_line(step), device_id_type=MESH)

    @pl.loop(1, below + 1)
    def _(offset):
        lane = lax.broadcasted_iota(jnp.int32, (PIECE, TILE), 1)
        row = lax.broadcasted_iota(jnp.int32, (PIECE, TILE), 0)
        ahead = lane - row
        for column in range(SEGS):
            pick[offset - 1, rows_of(column, PIECE), :] = jnp.where(
                ahead == anc[offset, column] * PIECE, 1.0, 0.0
            ).astype(BF16)

    def batch_left(head, offset):
        wait_bytes(chosen.at[head, offset - 1], p3_send.at[odd(head), offset - 1])

    def pick_and_send(head):
        wait_bytes(pieces.at[head], p1_recv.at[head])
        pl.when(head < KV_HEADS - 1)(lambda: spread_out(head + 1))

        @pl.loop(1, below + 1)
        def _(step):
            offset = jnp.where(head == 0, below + 1 - step, step)
            found = jnp.dot(
                pick[offset - 1], pieces[head].reshape(TILE, HEAD_DIM),
                preferred_element_type=F32,
            )
            chosen[head, offset - 1] = found.astype(BF16).reshape(SEGS, PIECE, HEAD_DIM)
            pl.when(head > 0)(lambda: batch_left(head - 1, offset))
            for turn in range(SEGS):
                column = shifted(turn // 4, turn % 4)
                remote(
                    chosen.at[head, offset - 1, column], blocks.at[head, offset, me],
                    p3_send.at[odd(head), offset - 1], p3_recv.at[head],
                    (level + offset, column),
                ).start()

    pl.semaphore_wait(ready, LEVELS - 1)

    @pl.loop(0, KV_HEADS)
    def _(head):
        blocks[head, 0] = kv_stage[head]

        @pl.when(odd(level) == 0)
        def _():
            blocks[head, level + 1] = jnp.zeros((SEGS, PIECE, HEAD_DIM), BF16)

    def make_spread():
        @pl.loop(1, below + 1)
        def _(offset):
            lane = lax.broadcasted_iota(jnp.int32, (PIECE, TILE), 1)
            row = lax.broadcasted_iota(jnp.int32, (PIECE, TILE), 0)
            lane_column = lane >> 4
            span = pl.ds(pl.multiple_of((offset - 1) * TILE, TILE), TILE)
            target = (lane & (PIECE - 1)) - row
            for column in range(SEGS):
                target = jnp.where(
                    lane_column == column, target + anc[offset, column] * PIECE, target
                )
            for column in range(SEGS):
                spread[rows_of(column, PIECE), span] = jnp.where(
                    target == column * PIECE, 1.0, 0.0
                ).astype(BF16)

    halves = [pl.ds(part * PIECES_PER_PART, PIECES_PER_PART) for part in range(2)]

    def attend(head, pairs):
        span_all = [pl.ds(group * ROWS, ROWS) for group in range(GROUP)]

        def block_pair(pair, part):
            return blocks[head, 2 * pair:2 * pair + 2, halves[part]].reshape(PAIR, HEAD_DIM)

        for index in range(2):
            for group, span in enumerate(span_all):
                tile = (q_in, g_in)[index][0, 0, :, lanes(head * GROUP + group)]
                stacks[index, span, :] = tile
                turned[index, :, span] = tile.T
        u_row = lax.broadcasted_iota(jnp.int32, (ROWS, ROWS), 0)
        t_row = lax.broadcasted_iota(jnp.int32, (ROWS, ROWS), 1)
        last_seen = odd(level) == 1
        best = [jnp.full((8, ROWS), NEG_FILL, F32) for group in range(GROUP)]
        for pair in range(pairs):
            raw = jnp.dot(block_pair(pair, 0), turned[0], preferred_element_type=F32)
            for group, span in enumerate(span_all):
                first = raw[0:ROWS, group * ROWS:(group + 1) * ROWS]
                second = raw[ROWS:PAIR, group * ROWS:(group + 1) * ROWS]
                if pair == 0:
                    first = jnp.where(u_row <= t_row, first, NEG_FILL)
                if pair == pairs - 1:
                    second = jnp.where(last_seen, second, NEG_FILL)
                logits[pair * PAIR:pair * PAIR + ROWS, span] = first
                logits[pair * PAIR + ROWS:(pair + 1) * PAIR, span] = second
                best[group] = jnp.maximum(
                    best[group], jnp.maximum(fold(first).max(0), fold(second).max(0))
                )
        top = [value.max(0, keepdims=True) for value in best]
        total = [jnp.zeros((8, ROWS), F32) for group in range(GROUP)]
        delta = [jnp.zeros((8, ROWS), F32) for group in range(GROUP)]
        for pair in range(pairs):
            rows = slice(pair * PAIR, (pair + 1) * PAIR)
            raw = jnp.dot(block_pair(pair, 1), turned[1], preferred_element_type=F32)
            for group, span in enumerate(span_all):
                tile = jnp.exp2((logits[rows, span] - top[group]) * EXP2_SCALE)
                part = raw[:, group * ROWS:(group + 1) * ROWS]
                logits[rows, span] = tile
                grad_probs[rows, span] = part
                total[group] += fold(tile).sum(0)
                delta[group] += fold(tile * part).sum(0)
        inverse = [1.0 / value.sum(0, keepdims=True) for value in total]
        delta = [value.sum(0, keepdims=True) * by for value, by in zip(delta, inverse)]
        for pair in range(pairs):
            rows = slice(pair * PAIR, (pair + 1) * PAIR)
            for group, span in enumerate(span_all):
                exact = logits[rows, span] * inverse[group]
                probs[rows, span] = exact.astype(BF16)
                grad_logits[rows, span] = (
                    exact * (grad_probs[rows, span] - delta[group])
                ).astype(BF16)
            value_term = jnp.dot(probs[rows, :], stacks[1], preferred_element_type=F32)
            key_term = SCALE * jnp.dot(
                grad_logits[rows, :], stacks[0], preferred_element_type=F32
            )
            for part, term in enumerate((key_term, value_term)):
                terms[head, 2 * pair:2 * pair + 2, halves[part]] = term.astype(BF16).reshape(
                    2, PIECES_PER_PART, PIECE, HEAD_DIM
                )
                if pair == 0:
                    own[head, part] = term[0:ROWS]
            moved = lax.dot_general(
                block_pair(pair, 0), grad_logits[rows, :], (((0,), (0,)), ((), ())),
                preferred_element_type=F32,
            )
            if pair == 0:
                query_sum[...] = moved
            else:
                query_sum[...] += moved
        for group, span in enumerate(span_all):
            grad_queries[0, 0, :, lanes(head * GROUP + group)] = (
                SCALE * query_sum[:, span].T
            ).astype(BF16)

    def terms_left(head, offset):
        wait_bytes(terms.at[head, offset], b1_send.at[odd(head), offset - 1])

    def send_terms(head):
        targets = []
        skew = jnp.where(my_parity == odd(head), 0, 1)
        for turn in range(OWNERS):
            z = around(my_z + turn // 2)
            x = around(my_x + (0, 2, 1, 3)[turn % 4] + skew)
            targets.append((2 * z + half(x), 4 * z + x))

        @pl.loop(1, level + 1)
        def _(offset):
            pl.when(head > 0)(lambda: terms_left(head - 1, offset))
            for owner, column in targets:
                remote(
                    terms.at[head, offset, pl.ds(2 * owner, 2)],
                    term_pieces.at[half(head), offset - 1, me],
                    b1_send.at[odd(head), offset - 1], b1_recv.at[half(head), offset - 1],
                    (level - offset, column),
                ).start()

    def sum_and_return(head):
        slot = half(head)

        @pl.when((level < LEVELS - 1) & (odd(head) == my_parity))
        def _():
            total[...] = jnp.zeros((TILE, 2 * HEAD_DIM), F32)

            @pl.loop(1, below + 1)
            def _(offset):
                wait_bytes(term_pieces.at[slot, offset - 1], b1_recv.at[slot, offset - 1])
                total[...] += jnp.dot(
                    spread[:, pl.ds(pl.multiple_of((offset - 1) * TILE, TILE), TILE)],
                    jnp.concatenate(
                        [
                            term_pieces[slot, offset - 1, :, index].reshape(TILE, HEAD_DIM)
                            for index in range(2)
                        ],
                        axis=1,
                    ),
                    preferred_element_type=F32,
                )

            for index in range(2):
                final_out[slot, :, index] = total[
                    :, index * HEAD_DIM:(index + 1) * HEAD_DIM
                ].astype(BF16).reshape(SEGS, PIECE, HEAD_DIM)
            landing = final_in.at[head, pl.ds(2 * my_owner, 2)]
            for turn in range(1, SEGS):
                peer = shifted(turn // 4, turn % 4)
                remote(
                    final_out.at[slot, peer], landing,
                    f_send.at[slot], f_recv.at[head], (level, peer),
                ).start()
            pltpu.make_async_copy(final_out.at[slot, me], landing, f_recv.at[head]).start()

    def store(head):
        @pl.when(level < LEVELS - 1)
        def _():
            wait_bytes(final_in.at[head], f_recv.at[head])
            for part in range(2):
                own[head, part] += final_in[head, halves[part]].reshape(
                    ROWS, HEAD_DIM
                ).astype(F32)

        grad_kv[0, 0, :, :, lanes(head)] = own[head].astype(BF16)

    @pl.loop(0, KV_HEADS + 4)
    def _(tick):
        @pl.when(tick < KV_HEADS)
        def _():
            pick_and_send(tick)

        @pl.when(tick == 0)
        def _():
            make_spread()
            load_q.wait()
            load_g.wait()

        @pl.when((tick >= 1) & (tick < KV_HEADS + 1))
        def _():
            head = tick - 1
            per_count(
                level,
                lambda count: wait_bytes(blocks.at[head, pl.ds(1, count)], p3_recv.at[head]),
            )
            for pairs in range(1, LEVELS // 2 + 1):
                pl.when(half(level) == pairs - 1)(functools.partial(attend, head, pairs))
            send_terms(head)

        @pl.when((tick >= 3) & (tick < KV_HEADS + 3))
        def _():
            sum_and_return(tick - 3)

        @pl.when(tick >= 4)
        def _():
            store(tick - 4)

    @pl.loop(0, KV_HEADS)
    def _(head):
        wait_bytes(pieces.at[head, pl.ds(1, SEGS - 1)], p1_send.at[head])

    @pl.loop(1, below + 1)
    def _(offset):
        batch_left(KV_HEADS - 1, offset)

    @pl.loop(1, level + 1)
    def _(offset):
        terms_left(KV_HEADS - 1, offset)

    @pl.when(level < LEVELS - 1)
    def _():
        for slot in range(2):
            wait_bytes(final_out.at[slot, pl.ds(1, SEGS - 1)], f_send.at[slot])


def shards(queries, keys_values, grad_out, parents):
    smem = pl.BlockSpec(memory_space=pltpu.SMEM)
    vmem = pl.BlockSpec(memory_space=pltpu.VMEM)
    hbm = pl.BlockSpec(memory_space=pltpu.HBM)
    dma = pltpu.SemaphoreType.DMA
    tile = (SEGS, PIECE, HEAD_DIM)
    keys_count = LEVELS * ROWS
    scratch = [
        pltpu.SMEM((LEVELS, SEGS), jnp.int32),
        pltpu.VMEM((LEVELS - 1, TILE, TILE), BF16),
        pltpu.VMEM((TILE, (LEVELS - 1) * TILE), BF16),
        pltpu.VMEM(keys_values.shape, BF16),
        pltpu.VMEM(queries.shape, BF16),
        pltpu.VMEM(queries.shape, BF16),
        pltpu.VMEM((KV_HEADS,) + tile, BF16),
        pltpu.VMEM((KV_HEADS,) + tile, BF16),
        pltpu.VMEM((KV_HEADS, LEVELS - 1) + tile, BF16),
        pltpu.VMEM((KV_HEADS, LEVELS) + tile, BF16),
        pltpu.VMEM((KV_HEADS, LEVELS) + tile, BF16),
        pltpu.VMEM((2, LEVELS - 1, SEGS, 2, PIECE, HEAD_DIM), BF16),
        pltpu.VMEM((KV_HEADS, 2, ROWS, HEAD_DIM), F32),
        pltpu.VMEM((2, STACK, HEAD_DIM), BF16),
        pltpu.VMEM((2, HEAD_DIM, STACK), BF16),
        pltpu.VMEM((HEAD_DIM, STACK), F32),
        pltpu.VMEM((keys_count, STACK), F32),
        pltpu.VMEM((keys_count, STACK), F32),
        pltpu.VMEM((keys_count, STACK), BF16),
        pltpu.VMEM((keys_count, STACK), BF16),
        pltpu.VMEM((TILE, 2 * HEAD_DIM), F32),
        pltpu.VMEM((2, SEGS, 2, PIECE, HEAD_DIM), BF16),
        pltpu.VMEM((KV_HEADS,) + tile, BF16),
        dma, dma, dma,
        pltpu.SemaphoreType.REGULAR,
        dma((KV_HEADS,)), dma((KV_HEADS,)),
        dma((2, LEVELS - 1)), dma((KV_HEADS,)),
        dma((2, LEVELS - 1)), dma((2, LEVELS - 1)),
        dma((2,)), dma((KV_HEADS,)),
    ]
    return pl.pallas_call(
        kernel,
        out_shape=(
            jax.ShapeDtypeStruct(queries.shape, BF16),
            jax.ShapeDtypeStruct(keys_values.shape, BF16),
        ),
        in_specs=[smem, hbm, hbm, hbm],
        out_specs=(vmem, vmem),
        scratch_shapes=scratch,
        compiler_params=pltpu.CompilerParams(
            collective_id=0, has_side_effects=True, vmem_limit_bytes=105 * 512 * 1024
        ),
        cost_estimate=pl.CostEstimate(
            flops=5 * 2 * HEADS * LEVELS * ROWS * ROWS * HEAD_DIM,
            bytes_accessed=8 * 1024 * 1024,
            transcendentals=HEADS * LEVELS * ROWS * ROWS,
        ),
    )(parents.transpose(0, 2, 1), queries, keys_values, grad_out)


def solution(mesh):
    in_specs = (
        P("depth", "seg", None, None),
        P("depth", "seg", None, None, None),
        P("depth", "seg", None, None),
        P(),
    )
    out_specs = (P("depth", "seg", None, None), P("depth", "seg", None, None, None))
    return jax.shard_map(shards, mesh=mesh, in_specs=in_specs, out_specs=out_specs, check_vma=False)
```
